32 devices in a mesh: seq: 2 (over x), batch: 16 (over z, y, core).
Axes of the slice: x: 2, y: 2, z: 4, core: 2. Of those that a mesh axis runs over, the one named last changes fastest.
Arguments:
- tokens: bfloat16 [32, 2048, 1024], P('batch', 'seq'), may hold values from -6 to 6
- cotangent: bfloat16 [32, 2048, 1024], P('batch', 'seq'), may hold values from -6 to 6
- lengths: int32 [32], P('batch'), may hold values from 256 to 2048, as said below
- routed: int32 [32, 256], P('batch'), may hold values from -1 to 2047, as said below
- w_qkv: bfloat16 [1024, 3072], P(('seq', 'batch')), may hold values from -0.1875 to 0.1875
- w_out: bfloat16 [1024, 1024], P(('seq', 'batch')), may hold values from -0.75 to 0.75
- w_up: bfloat16 [1024, 4096], P(('seq', 'batch')), may hold values from -0.1875 to 0.1875
- w_down: bfloat16 [4096, 1024], P(('seq', 'batch')), may hold values from -0.09375 to 0.09375
- gain_attn: bfloat16 [1024], P(('seq', 'batch')), may hold values from 0.099609375 to 1.8984375
- gain_mlp: bfloat16 [1024], P(('seq', 'batch')), may hold values from 0.099609375 to 1.8984375
- router: bfloat16 [1024], P(('seq', 'batch')), may hold values from -0.1875 to 0.1875
Outputs:
- output: bfloat16 [32, 2048, 1024], P('batch', 'seq')
- input_grad: bfloat16 [32, 2048, 1024], P('batch', 'seq')
- grad_qkv: float32 [1024, 3072], P(('seq', 'batch'))
- grad_out: float32 [1024, 1024], P(('seq', 'batch'))
- grad_up: float32 [1024, 4096], P(('seq', 'batch'))
- grad_down: float32 [4096, 1024], P(('seq', 'batch'))
- grad_gain_attn: float32 [1024], P(('seq', 'batch'))
- grad_gain_mlp: float32 [1024], P(('seq', 'batch'))
- grad_router: float32 [1024], P(('seq', 'batch'))
The draws below stay inside these ranges and needn't reach their ends.
Inputs may be any that keep to these rules, and one draw needn't show every extreme that they name: `lengths`: multiples of 8; in every run of 2 slots along the first dimension one slot has length 2048. `routed`: for a slot of length n, entries 0 to n // 8 - 1 are distinct positions below n in rising order; the others are -1.
All inputs are finite; a program needn't handle non-finite values.
Results may differ from the reference program's by a relative error of at most 0.014.
Values may be sent and summed in bfloat16 or wider, within the bound.
A program may use at most 192 MiB of HBM per device.

```python
import math
import jax
import jax.numpy as jnp
from jax import lax

D = 1024
FF = 4096
HEADS = 16
HEAD_DIM = 64
L = 2048
MIN_LEN = 256
SLOT_DEV = 2
ROUTED = 256
SLOTS = 32


def slot_lengths(key):
    drawn = jax.random.randint(key, (SLOTS,), MIN_LEN // 8, L // 8 + 1) * 8
    key_full = jax.random.fold_in(key, 11)
    full_at = jax.random.randint(key_full, (SLOTS // SLOT_DEV,), 0, SLOT_DEV)
    slot_ids = jnp.arange(SLOTS, dtype=jnp.int32)
    is_full = slot_ids % SLOT_DEV == full_at[slot_ids // SLOT_DEV]
    return jnp.where(is_full, L, drawn).astype(jnp.int32)


def draw_lengths(key, part):
    return slot_lengths(key)


def draw_routed(key, part):
    sizes_now = slot_lengths(key)
    key = jax.random.fold_in(key, 5)
    slot_keys = jax.random.split(key, SLOTS)

    def draw_one(slot_key, length_now):
        shuffled = jax.random.permutation(slot_key, L).astype(jnp.int32)
        position = jnp.arange(L, dtype=jnp.int32)
        ranking = jnp.where(position < length_now, shuffled, L + position)
        ordered = jnp.argsort(ranking)[:ROUTED].astype(jnp.int32)
        in_use = jnp.arange(ROUTED, dtype=jnp.int32) < length_now // 8
        chosen = jnp.sort(jnp.where(in_use, ordered, L))
        return jnp.where(in_use, chosen, -1).astype(jnp.int32)
    return jax.vmap(draw_one)(slot_keys, sizes_now)


def block_scale(key, extent, pieces, low, largest):
    loudness = 1.0
    for axis_at, parts in pieces:
        heights = jax.random.uniform(jax.random.fold_in(jax.random.fold_in(key, 6), axis_at), (parts,), jnp.float32, low / len(pieces), largest / len(pieces))
        loudness = loudness * jnp.repeat(jnp.exp(heights), extent[axis_at] // parts).reshape((-1,) + (1,) * (len(extent) - 1 - axis_at))
    return loudness


def centred(key, shape, deviation, reach, pieces=(), held_as=jnp.bfloat16):
    values = deviation * jax.random.normal(key, shape, jnp.float32)
    if pieces:
        values = values * block_scale(key, shape, pieces, -0.22, 0.18)
    return jnp.clip(values, -reach, reach).astype(held_as)


def setup_inputs(seed: int = 0) -> dict:
    keys = jax.random.split(jax.random.key(seed), 12)
    return {
        "tokens": centred(keys[0], (SLOTS, L, D), 1.0, 6.0, ((0, 16), (1, 2))),
        "cotangent": centred(keys[1], (SLOTS, L, D), 1.0, 6.0, ((0, 16), (1, 2))),
        "lengths": draw_lengths(jax.random.fold_in(keys[11], 71), 0),
        "routed": draw_routed(jax.random.fold_in(keys[11], 71), 0),
        "w_qkv": centred(keys[4], (D, 3 * D), D ** -0.5, 0.1875, ((0, 32),)),
        "w_out": centred(keys[5], (D, D), (D // 16) ** -0.5, 0.75, ((0, 32),)),
        "w_up": centred(keys[6], (D, FF), D ** -0.5, 0.1875, ((0, 32),)),
        "w_down": centred(keys[7], (FF, D), FF ** -0.5, 0.09375, ((0, 32),)),
        "gain_attn": jnp.clip(1.0 + 0.18 * jax.random.normal(keys[8], (D,), jnp.float32), 0.099609375, 1.8984375).astype(jnp.bfloat16),
        "gain_mlp": jnp.clip(1.0 + 0.18 * jax.random.normal(keys[9], (D,), jnp.float32), 0.099609375, 1.8984375).astype(jnp.bfloat16),
        "router": centred(keys[10], (D,), D ** -0.5, 0.1875, ((0, 32),)),
    }


@jax.custom_vjp
def low(v):
    return lax.optimization_barrier(v.astype(jnp.bfloat16)).astype(jnp.float32)

@jax.custom_vjp
def low_back(v):
    return v

def low_keep(v):
    return (low(v), None)

def low_pass(kept, grad):
    return (grad,)

def back_keep(v):
    return (v, None)

def back_low(kept, grad):
    return (low(grad),)
low.defvjp(low_keep, low_pass)
low_back.defvjp(back_keep, back_low)
epsilon = 1e-05
highest = lax.Precision.HIGHEST

def rms_norm(values_in, gain_vec):
    return values_in * lax.rsqrt(lax.optimization_barrier(jnp.mean(values_in * values_in, axis=-1, keepdims=True)) + epsilon) * gain_vec

def block_forward(tokens, lengths, routed, w_qkv, w_out, w_up, w_down, gain_attn, gain_mlp, router):
    group_size = tokens.shape[0]
    counts = lengths // 8
    rank_all = jnp.arange(ROUTED, dtype=jnp.int32)
    live_rows = rank_all[None, :] < counts[:, None]
    safe_index = jnp.where(live_rows, routed, 0).astype(jnp.int32)
    picked = jnp.take_along_axis(tokens, safe_index[:, :, None], axis=1)
    picked = low_back(picked)
    normed = low(rms_norm(picked, gain_attn))
    joined = low(low_back(jnp.einsum('gcd,de->gce', normed, w_qkv, precision=highest)))
    query_rows = joined[..., :D].reshape(group_size, ROUTED, HEADS, HEAD_DIM)
    key_rows = joined[..., D:2 * D].reshape(group_size, ROUTED, HEADS, HEAD_DIM)
    value_rows = joined[..., 2 * D:].reshape(group_size, ROUTED, HEADS, HEAD_DIM)
    scores = jnp.einsum('gqha,gkha->ghqk', query_rows, key_rows, precision=highest) * HEAD_DIM ** (-0.5)
    scores = low_back(scores)
    causal = rank_all[None, :] <= rank_all[:, None]
    allowed = causal[None, :, :] & (rank_all[None, None, :] < counts[:, None, None])
    scores = jnp.where(allowed[:, None], scores, -1000000000.0)
    row_max = lax.optimization_barrier(jnp.max(scores, axis=-1, keepdims=True))
    weights_f = jnp.exp(scores - row_max)
    row_total = lax.optimization_barrier(jnp.sum(weights_f, axis=-1, keepdims=True))
    mixture = jnp.einsum('ghqk,gkha->gqha', low(weights_f), value_rows, precision=highest)
    mixture = mixture / jnp.transpose(row_total, (0, 2, 1, 3))
    attended = low(low_back(mixture.reshape(group_size, ROUTED, D)))
    branch_a = low_back(jnp.einsum('gcd,de->gce', attended, w_out, precision=highest))
    hidden = picked + branch_a
    normed_two = low(rms_norm(hidden, gain_mlp))
    up_proj = low_back(jnp.einsum('gcd,df->gcf', normed_two, w_up, precision=highest))
    activated = low(jax.nn.gelu(up_proj, approximate=True))
    branch_m = low_back(jnp.einsum('gcf,fd->gcd', activated, w_down, precision=highest))
    gate_prob = jax.nn.sigmoid(jnp.einsum('gcd,d->gc', picked, router, precision=highest))
    update = gate_prob[..., None] * (branch_a + branch_m) * live_rows[..., None].astype(jnp.float32)
    update = low(update)
    slot_ids = jnp.arange(group_size, dtype=jnp.int32)[:, None]
    return tokens.at[slot_ids, safe_index].add(update)

def reference(tokens, cotangent, lengths, routed, w_qkv, w_out, w_up, w_down, gain_attn, gain_mlp, router):
    weights = tuple((matrix.astype(jnp.float32) for matrix in (w_qkv, w_out, w_up, w_down, gain_attn, gain_mlp, router)))
    group_size = math.gcd(SLOTS, max(1, 4096 // L))
    group_count = SLOTS // group_size

    def group_step(summed, inputs):
        tok_group, cot_group, len_group, idx_group = inputs

        def forward(tok_in, *params):
            return block_forward(tok_in, len_group, idx_group, *params)
        result, pullback = jax.vjp(forward, tok_group.astype(jnp.float32), *weights)
        grads = pullback(cot_group.astype(jnp.float32))
        summed = jax.tree.map(jnp.add, summed, tuple(grads[1:]))
        return (summed, (result.astype(jnp.bfloat16), grads[0].astype(jnp.bfloat16)))
    start = tuple((jnp.zeros_like(matrix) for matrix in weights))
    inputs = (tokens.reshape(group_count, group_size, L, D), cotangent.reshape(group_count, group_size, L, D), lengths.reshape(group_count, group_size), routed.reshape(group_count, group_size, ROUTED))
    summed, (output, input_grad) = lax.scan(group_step, start, inputs)
    output = output.reshape(SLOTS, L, D)
    input_grad = input_grad.reshape(SLOTS, L, D)
    return (output, input_grad, summed[0], summed[1], summed[2], summed[3], summed[4], summed[5], summed[6])
```

```python
import jax
import jax.numpy as jnp
from jax import lax
from jax.sharding import PartitionSpec as P

HEAD_DIM = 64


epsilon = 1e-05
highest = lax.Precision.HIGHEST


def norm_apply(values_in, gain_vec):
    return (
        values_in
        * lax.rsqrt(jnp.mean(values_in * values_in, axis=-1, keepdims=True) + epsilon)
        * gain_vec
    )


def gelu_tanh(values_in):
    return jax.nn.gelu(values_in, approximate=True)


def per_device(
    tokens, cotangent, lengths, routed, w_qkv, w_out, w_up, w_down, gain_attn, gain_mlp, router
):
    slot_count, local_len, model_width = tokens.shape
    capacity = routed.shape[1]
    seq_devices = lax.axis_size("seq")
    own_count = capacity // seq_devices
    head_count = model_width // HEAD_DIM
    row_count = own_count * slot_count
    score_scale = HEAD_DIM ** (-0.5)
    f32 = jnp.float32
    bf16 = jnp.bfloat16
    gathered = (
        lax.all_gather(w_qkv, ("seq", "batch"), axis=0, tiled=True),
        lax.all_gather(w_out, ("seq", "batch"), axis=0, tiled=True),
        lax.all_gather(w_up, ("seq", "batch"), axis=0, tiled=True),
        lax.all_gather(w_down, ("seq", "batch"), axis=0, tiled=True),
        lax.all_gather(gain_attn, ("seq", "batch"), axis=0, tiled=True),
        lax.all_gather(gain_mlp, ("seq", "batch"), axis=0, tiled=True),
        lax.all_gather(router, ("seq", "batch"), axis=0, tiled=True),
    )
    full_qkv, full_out, full_up, full_down, full_ga, full_gm, full_router = gathered
    gain_one = full_ga.astype(f32)
    gain_two = full_gm.astype(f32)
    router_vec = full_router.astype(f32)
    counts = lengths // 8
    seq_place = lax.axis_index("seq")
    positions = seq_place * local_len + jnp.arange(local_len, dtype=jnp.int32)
    rank_all = jnp.arange(capacity, dtype=jnp.int32)
    live_all = rank_all[None, :] < counts[:, None]
    chooser = ((routed[:, :, None] == positions[None, None, :]) & live_all[:, :, None]).astype(bf16)
    pick_in = jnp.einsum("scp,spd->csd", chooser, tokens, preferred_element_type=f32)
    pick_cot = jnp.einsum("scp,spd->csd", chooser, cotangent, preferred_element_type=f32)
    picked, picked_cot = (
        lax.psum_scatter(
            pick_in.astype(jnp.bfloat16), "seq", scatter_dimension=0, tiled=True
        ).astype(jnp.float32),
        lax.psum_scatter(
            pick_cot.astype(jnp.bfloat16), "seq", scatter_dimension=0, tiled=True
        ).astype(jnp.float32),
    )
    own_rank = seq_place * own_count + jnp.arange(own_count, dtype=jnp.int32)
    live_own = own_rank[:, None] < counts[None, :]
    live_mask = live_own.reshape(row_count, 1).astype(f32)
    routed_in = picked.reshape(row_count, model_width)
    normed_one = norm_apply(routed_in, gain_one).astype(bf16)
    joined = jnp.dot(normed_one, full_qkv, preferred_element_type=f32).astype(bf16)
    query_rows = joined[:, :model_width].reshape(own_count, slot_count, head_count, HEAD_DIM)
    key_own = joined[:, model_width : 2 * model_width].reshape(own_count, slot_count, model_width)
    value_own = joined[:, 2 * model_width :].reshape(own_count, slot_count, model_width)
    key_every, value_every = (
        lax.all_gather(key_own, "seq", axis=0, tiled=True),
        lax.all_gather(value_own, "seq", axis=0, tiled=True),
    )
    key_rows = key_every.reshape(capacity, slot_count, head_count, HEAD_DIM)
    value_rows = value_every.reshape(capacity, slot_count, head_count, HEAD_DIM)
    scores = (
        jnp.einsum("qsha,ksha->shqk", query_rows, key_rows, preferred_element_type=f32)
        * score_scale
    )
    causal = rank_all[None, :] <= own_rank[:, None]
    allowed = causal[None, :, :] & (rank_all[None, None, :] < counts[:, None, None])
    scores = jnp.where(allowed[:, None], scores, -1000000000.0)
    row_max = jnp.max(scores, axis=-1, keepdims=True)
    weights_f = jnp.exp(scores - row_max)
    row_total = jnp.sum(weights_f, axis=-1, keepdims=True)
    weights_low = weights_f.astype(bf16)
    mixture = jnp.einsum("shqk,ksha->qsha", weights_low, value_rows, preferred_element_type=f32)
    mixture = mixture / jnp.transpose(row_total, (2, 0, 1, 3))
    attended = mixture.reshape(row_count, model_width).astype(bf16)
    branch_a = jnp.dot(attended, full_out, preferred_element_type=f32)
    hidden = routed_in + branch_a
    normed_two = norm_apply(hidden, gain_two).astype(bf16)
    up_proj = jnp.dot(normed_two, full_up, preferred_element_type=f32)
    activated = gelu_tanh(up_proj).astype(bf16)
    branch_m = jnp.dot(activated, full_down, preferred_element_type=f32)
    gate_prob = jax.nn.sigmoid(jnp.dot(routed_in, router_vec, precision=highest))
    branch = branch_a + branch_m
    update = (
        (gate_prob[:, None] * branch * live_mask)
        .astype(bf16)
        .reshape(own_count, slot_count, model_width)
    )
    update_every = lax.all_gather(update, "seq", axis=0, tiled=True)
    output = (
        tokens.astype(f32)
        + jnp.einsum("scp,csd->spd", chooser, update_every, preferred_element_type=f32)
    ).astype(bf16)
    cot_rows = picked_cot.reshape(row_count, model_width)
    grad_gate = jnp.sum(cot_rows * branch, axis=-1)
    grad_logit = grad_gate * gate_prob * (1.0 - gate_prob)
    grad_branch = gate_prob[:, None] * cot_rows
    grad_m = grad_branch.astype(bf16)
    grad_act = jnp.einsum("rd,fd->rf", grad_m, full_down, preferred_element_type=f32)
    unused_up, gelu_pull = jax.vjp(gelu_tanh, up_proj)
    grad_u = gelu_pull(grad_act)[0].astype(bf16)
    grad_n2 = jnp.einsum("rf,df->rd", grad_u, full_up, preferred_element_type=f32)
    unused_two, norm_pull_two = jax.vjp(norm_apply, hidden, gain_two)
    grad_hidden, grad_gm = norm_pull_two(grad_n2)
    grad_a = (grad_branch + grad_hidden).astype(bf16)
    grad_att = jnp.einsum("rd,ed->re", grad_a, full_out, preferred_element_type=f32).astype(bf16)
    grad_att4 = grad_att.reshape(own_count, slot_count, head_count, HEAD_DIM)
    delta_rows = jnp.sum(grad_att4.astype(f32) * mixture, axis=-1)
    delta = jnp.transpose(delta_rows, (1, 2, 0))[..., None]
    grad_p = jnp.einsum("qsha,ksha->shqk", grad_att4, value_rows, preferred_element_type=f32)
    probs = weights_f / row_total
    grad_s = (probs * (grad_p - delta)).astype(bf16)
    grad_q = (
        jnp.einsum("shqk,ksha->qsha", grad_s, key_rows, preferred_element_type=f32) * score_scale
    )
    grad_k = (
        jnp.einsum("shqk,qsha->ksha", grad_s, query_rows, preferred_element_type=f32) * score_scale
    )
    scaled_low = weights_low.astype(f32) / row_total
    grad_v = jnp.einsum("shqk,qsha->ksha", scaled_low, grad_att4.astype(f32), precision=highest)
    grad_k_own, grad_v_own = (
        lax.psum_scatter(
            grad_k.reshape(capacity, slot_count, model_width).astype(jnp.bfloat16),
            "seq",
            scatter_dimension=0,
            tiled=True,
        ).astype(jnp.float32),
        lax.psum_scatter(
            grad_v.reshape(capacity, slot_count, model_width).astype(jnp.bfloat16),
            "seq",
            scatter_dimension=0,
            tiled=True,
        ).astype(jnp.float32),
    )
    grad_joined = jnp.concatenate(
        [
            grad_q.reshape(row_count, model_width),
            grad_k_own.reshape(row_count, model_width),
            grad_v_own.reshape(row_count, model_width),
        ],
        axis=-1,
    ).astype(bf16)
    grad_n1 = jnp.einsum("re,de->rd", grad_joined, full_qkv, preferred_element_type=f32)
    unused_one, norm_pull_one = jax.vjp(norm_apply, routed_in, gain_one)
    grad_x1, grad_ga = norm_pull_one(grad_n1)
    grad_router = jnp.sum(routed_in * grad_logit[:, None], axis=0)
    grad_rows = (grad_hidden + grad_x1 + grad_logit[:, None] * router_vec[None, :]).astype(bf16)
    grad_rows = grad_rows.reshape(own_count, slot_count, model_width)
    grad_every = lax.all_gather(grad_rows, "seq", axis=0, tiled=True)
    input_grad = (
        cotangent.astype(f32)
        + jnp.einsum("scp,csd->spd", chooser, grad_every, preferred_element_type=f32)
    ).astype(bf16)
    part_qkv = jnp.einsum("rd,re->de", normed_one, grad_joined, preferred_element_type=f32)
    part_out = jnp.einsum("re,rd->ed", attended, grad_a, preferred_element_type=f32)
    part_up = jnp.einsum("rd,rf->df", normed_two, grad_u, preferred_element_type=f32)
    part_down = jnp.einsum("rf,rd->fd", activated, grad_m, preferred_element_type=f32)

    def sum_rows(part):
        return lax.psum_scatter(
            part.astype(bf16), ("seq", "batch"), scatter_dimension=0, tiled=True
        ).astype(f32)

    down_sum = sum_rows(part_down)
    grad_up = sum_rows(part_up)
    grad_out = sum_rows(part_out)
    grad_qkv = sum_rows(part_qkv)
    small_ga, small_gm, small_router = (
        lax.psum_scatter(grad_ga, ("seq", "batch"), scatter_dimension=0, tiled=True),
        lax.psum_scatter(grad_gm, ("seq", "batch"), scatter_dimension=0, tiled=True),
        lax.psum_scatter(grad_router, ("seq", "batch"), scatter_dimension=0, tiled=True),
    )
    return (
        output,
        input_grad,
        grad_qkv,
        grad_out,
        grad_up,
        down_sum,
        small_ga,
        small_gm,
        small_router,
    )


def solution(mesh):
    in_specs = (
        P("batch", "seq", None),
        P("batch", "seq", None),
        P("batch"),
        P("batch", None),
        P(("seq", "batch"), None),
        P(("seq", "batch"), None),
        P(("seq", "batch"), None),
        P(("seq", "batch"), None),
        P(("seq", "batch")),
        P(("seq", "batch")),
        P(("seq", "batch")),
    )
    out_specs = (
        P("batch", "seq", None),
        P("batch", "seq", None),
        P(("seq", "batch"), None),
        P(("seq", "batch"), None),
        P(("seq", "batch"), None),
        P(("seq", "batch"), None),
        P(("seq", "batch")),
        P(("seq", "batch")),
        P(("seq", "batch")),
    )
    return jax.shard_map(
        per_device, mesh=mesh, in_specs=in_specs, out_specs=out_specs, check_vma=False
    )
```

```python
import functools

import jax
import jax.numpy as jnp
from jax import lax
from jax.experimental import pallas as pl
from jax.experimental.pallas import tpu as pltpu
from jax.sharding import PartitionSpec as P

HEAD_DIM = 64
MESH = pl.DeviceIdType.MESH


epsilon = 1e-05
highest = lax.Precision.HIGHEST
f32 = jnp.float32
bf16 = jnp.bfloat16

LINE = 4
GELU_C = 0.7978845608
GELU_K = 0.044715


def dot_nn(a, b):
    return lax.dot_general(a, b, (((1,), (0,)), ((), ())), preferred_element_type=f32)


def dot_nt(a, b):
    return lax.dot_general(a, b, (((1,), (1,)), ((), ())), preferred_element_type=f32)


def dot_tn(a, b):
    return lax.dot_general(a, b, (((0,), (0,)), ((), ())), preferred_element_type=f32)


def place():
    s = lax.axis_index("seq")
    b = lax.axis_index("batch")
    return s, b // 4, lax.rem(b // 2, 2), lax.rem(b, 2)


def device(s, z, y, c):
    return (s, z * 4 + y * 2 + c)


def remote(src, dst, send, recv, target):
    return pltpu.make_async_remote_copy(
        src_ref=src, dst_ref=dst, send_sem=send, recv_sem=recv, device_id=target, device_id_type=MESH
    )


def greet(targets):
    barrier = pltpu.get_barrier_semaphore()
    for target in targets:
        pl.semaphore_signal(barrier, inc=1, device_id=target, device_id_type=MESH)
    pl.semaphore_wait(barrier, len(targets))


def inverse_rms(values):
    return lax.rsqrt(jnp.mean(values * values, axis=-1, keepdims=True) + epsilon)


def head_mask(parity):
    lane = lax.broadcasted_iota(jnp.int32, (1, 128), 1)
    return jnp.where(lane // HEAD_DIM == parity, 1.0, 0.0).astype(f32)


def allowed_pairs(bias_row):
    count = bias_row.shape[-1]
    query = lax.broadcasted_iota(jnp.int32, (count, count), 0)
    key = lax.broadcasted_iota(jnp.int32, (count, count), 1)
    return (key <= query) & (bias_row > -1.0)


def norm_apply(values_in, gain_vec):
    return (
        values_in
        * lax.rsqrt(jnp.mean(values_in * values_in, axis=-1, keepdims=True) + epsilon)
        * gain_vec
    )


def gelu_tanh(values_in):
    return jax.nn.gelu(values_in, approximate=True)


def general_device(
    tokens, cotangent, lengths, routed, w_qkv, w_out, w_up, w_down, gain_attn, gain_mlp, router
):
    slot_count, local_len, model_width = tokens.shape
    capacity = routed.shape[1]
    seq_devices = lax.axis_size("seq")
    own_count = capacity // seq_devices
    head_count = model_width // HEAD_DIM
    row_count = own_count * slot_count
    score_scale = HEAD_DIM ** (-0.5)
    gathered = (
        lax.all_gather(w_qkv, ("seq", "batch"), axis=0, tiled=True),
        lax.all_gather(w_out, ("seq", "batch"), axis=0, tiled=True),
        lax.all_gather(w_up, ("seq", "batch"), axis=0, tiled=True),
        lax.all_gather(w_down, ("seq", "batch"), axis=0, tiled=True),
        lax.all_gather(gain_attn, ("seq", "batch"), axis=0, tiled=True),
        lax.all_gather(gain_mlp, ("seq", "batch"), axis=0, tiled=True),
        lax.all_gather(router, ("seq", "batch"), axis=0, tiled=True),
    )
    full_qkv, full_out, full_up, full_down, full_ga, full_gm, full_router = gathered
    gain_one = full_ga.astype(f32)
    gain_two = full_gm.astype(f32)
    router_vec = full_router.astype(f32)
    counts = lengths // 8
    seq_place = lax.axis_index("seq")
    positions = seq_place * local_len + jnp.arange(local_len, dtype=jnp.int32)
    rank_all = jnp.arange(capacity, dtype=jnp.int32)
    live_all = rank_all[None, :] < counts[:, None]
    chooser = ((routed[:, :, None] == positions[None, None, :]) & live_all[:, :, None]).astype(bf16)
    pick_in = jnp.einsum("scp,spd->csd", chooser, tokens, preferred_element_type=f32)
    pick_cot = jnp.einsum("scp,spd->csd", chooser, cotangent, preferred_element_type=f32)
    picked, picked_cot = (
        lax.psum_scatter(
            pick_in.astype(jnp.bfloat16), "seq", scatter_dimension=0, tiled=True
        ).astype(jnp.float32),
        lax.psum_scatter(
            pick_cot.astype(jnp.bfloat16), "seq", scatter_dimension=0, tiled=True
        ).astype(jnp.float32),
    )
    own_rank = seq_place * own_count + jnp.arange(own_count, dtype=jnp.int32)
    live_own = own_rank[:, None] < counts[None, :]
    live_mask = live_own.reshape(row_count, 1).astype(f32)
    routed_in = picked.reshape(row_count, model_width)
    normed_one = norm_apply(routed_in, gain_one).astype(bf16)
    joined = jnp.dot(normed_one, full_qkv, preferred_element_type=f32).astype(bf16)
    query_rows = joined[:, :model_width].reshape(own_count, slot_count, head_count, HEAD_DIM)
    key_own = joined[:, model_width : 2 * model_width].reshape(own_count, slot_count, model_width)
    value_own = joined[:, 2 * model_width :].reshape(own_count, slot_count, model_width)
    key_every, value_every = (
        lax.all_gather(key_own, "seq", axis=0, tiled=True),
        lax.all_gather(value_own, "seq", axis=0, tiled=True),
    )
    key_rows = key_every.reshape(capacity, slot_count, head_count, HEAD_DIM)
    value_rows = value_every.reshape(capacity, slot_count, head_count, HEAD_DIM)
    scores = (
        jnp.einsum("qsha,ksha->shqk", query_rows, key_rows, preferred_element_type=f32)
        * score_scale
    )
    causal = rank_all[None, :] <= own_rank[:, None]
    allowed = causal[None, :, :] & (rank_all[None, None, :] < counts[:, None, None])
    scores = jnp.where(allowed[:, None], scores, -1000000000.0)
    row_max = jnp.max(scores, axis=-1, keepdims=True)
    weights_f = jnp.exp(scores - row_max)
    row_total = jnp.sum(weights_f, axis=-1, keepdims=True)
    weights_low = weights_f.astype(bf16)
    mixture = jnp.einsum("shqk,ksha->qsha", weights_low, value_rows, preferred_element_type=f32)
    mixture = mixture / jnp.transpose(row_total, (2, 0, 1, 3))
    attended = mixture.reshape(row_count, model_width).astype(bf16)
    branch_a = jnp.dot(attended, full_out, preferred_element_type=f32)
    hidden = routed_in + branch_a
    normed_two = norm_apply(hidden, gain_two).astype(bf16)
    up_proj = jnp.dot(normed_two, full_up, preferred_element_type=f32)
    activated = gelu_tanh(up_proj).astype(bf16)
    branch_m = jnp.dot(activated, full_down, preferred_element_type=f32)
    gate_prob = jax.nn.sigmoid(jnp.dot(routed_in, router_vec, precision=highest))
    branch = branch_a + branch_m
    update = (
        (gate_prob[:, None] * branch * live_mask)
        .astype(bf16)
        .reshape(own_count, slot_count, model_width)
    )
    update_every = lax.all_gather(update, "seq", axis=0, tiled=True)
    output = (
        tokens.astype(f32)
        + jnp.einsum("scp,csd->spd", chooser, update_every, preferred_element_type=f32)
    ).astype(bf16)
    cot_rows = picked_cot.reshape(row_count, model_width)
    grad_gate = jnp.sum(cot_rows * branch, axis=-1)
    grad_logit = grad_gate * gate_prob * (1.0 - gate_prob)
    grad_branch = gate_prob[:, None] * cot_rows
    grad_m = grad_branch.astype(bf16)
    grad_act = jnp.einsum("rd,fd->rf", grad_m, full_down, preferred_element_type=f32)
    unused_up, gelu_pull = jax.vjp(gelu_tanh, up_proj)
    grad_u = gelu_pull(grad_act)[0].astype(bf16)
    grad_n2 = jnp.einsum("rf,df->rd", grad_u, full_up, preferred_element_type=f32)
    unused_two, norm_pull_two = jax.vjp(norm_apply, hidden, gain_two)
    grad_hidden, grad_gm = norm_pull_two(grad_n2)
    grad_a = (grad_branch + grad_hidden).astype(bf16)
    grad_att = jnp.einsum("rd,ed->re", grad_a, full_out, preferred_element_type=f32).astype(bf16)
    grad_att4 = grad_att.reshape(own_count, slot_count, head_count, HEAD_DIM)
    delta_rows = jnp.sum(grad_att4.astype(f32) * mixture, axis=-1)
    delta = jnp.transpose(delta_rows, (1, 2, 0))[..., None]
    grad_p = jnp.einsum("qsha,ksha->shqk", grad_att4, value_rows, preferred_element_type=f32)
    probs = weights_f / row_total
    grad_s = (probs * (grad_p - delta)).astype(bf16)
    grad_q = (
        jnp.einsum("shqk,ksha->qsha", grad_s, key_rows, preferred_element_type=f32) * score_scale
    )
    grad_k = (
        jnp.einsum("shqk,qsha->ksha", grad_s, query_rows, preferred_element_type=f32) * score_scale
    )
    scaled_low = weights_low.astype(f32) / row_total
    grad_v = jnp.einsum("shqk,qsha->ksha", scaled_low, grad_att4.astype(f32), precision=highest)
    grad_k_own, grad_v_own = (
        lax.psum_scatter(
            grad_k.reshape(capacity, slot_count, model_width).astype(jnp.bfloat16),
            "seq",
            scatter_dimension=0,
            tiled=True,
        ).astype(jnp.float32),
        lax.psum_scatter(
            grad_v.reshape(capacity, slot_count, model_width).astype(jnp.bfloat16),
            "seq",
            scatter_dimension=0,
            tiled=True,
        ).astype(jnp.float32),
    )
    grad_joined = jnp.concatenate(
        [
            grad_q.reshape(row_count, model_width),
            grad_k_own.reshape(row_count, model_width),
            grad_v_own.reshape(row_count, model_width),
        ],
        axis=-1,
    ).astype(bf16)
    grad_n1 = jnp.einsum("re,de->rd", grad_joined, full_qkv, preferred_element_type=f32)
    unused_one, norm_pull_one = jax.vjp(norm_apply, routed_in, gain_one)
    grad_x1, grad_ga = norm_pull_one(grad_n1)
    grad_router = jnp.sum(routed_in * grad_logit[:, None], axis=0)
    grad_rows = (grad_hidden + grad_x1 + grad_logit[:, None] * router_vec[None, :]).astype(bf16)
    grad_rows = grad_rows.reshape(own_count, slot_count, model_width)
    grad_every = lax.all_gather(grad_rows, "seq", axis=0, tiled=True)
    input_grad = (
        cotangent.astype(f32)
        + jnp.einsum("scp,csd->spd", chooser, grad_every, preferred_element_type=f32)
    ).astype(bf16)
    part_qkv = jnp.einsum("rd,re->de", normed_one, grad_joined, preferred_element_type=f32)
    part_out = jnp.einsum("re,rd->ed", attended, grad_a, preferred_element_type=f32)
    part_up = jnp.einsum("rd,rf->df", normed_two, grad_u, preferred_element_type=f32)
    part_down = jnp.einsum("rf,rd->fd", activated, grad_m, preferred_element_type=f32)

    def sum_rows(part):
        return lax.psum_scatter(
            part.astype(bf16), ("seq", "batch"), scatter_dimension=0, tiled=True
        ).astype(f32)

    down_sum = sum_rows(part_down)
    grad_up = sum_rows(part_up)
    grad_out = sum_rows(part_out)
    grad_qkv = sum_rows(part_qkv)
    small_ga, small_gm, small_router = (
        lax.psum_scatter(grad_ga, ("seq", "batch"), scatter_dimension=0, tiled=True),
        lax.psum_scatter(grad_gm, ("seq", "batch"), scatter_dimension=0, tiled=True),
        lax.psum_scatter(grad_router, ("seq", "batch"), scatter_dimension=0, tiled=True),
    )
    return (
        output,
        input_grad,
        grad_qkv,
        grad_out,
        grad_up,
        down_sum,
        small_ga,
        small_gm,
        small_router,
    )


def first_kernel(
    tok_hbm, cot_hbm, vec_hbm, wq_hbm, wo_hbm, wu_hbm, wd_hbm, pos_ref, bias_ref,
    xr_out, dr_out, h_out, qkv_out, o_out, wq_out, wo_out, gains_out, gd_out, gu_out, d2s_out, d2r_out, ms_out,
    tok, cot, wq, wo, wu, wd, gv, stq, stu, stv, rcv,
    xs, xr, ds, dr, a_s, a_r, hid, n2, qkv, att, act, gp, m_s, d2s, d2r, dm, gd, gu, gains,
    loc, out_sem, sz, rz, sy, ry, sc, rc, sx, rx,
):
    s, z, y, c = place()
    xdev, ydev, cdev = device(1 - s, z, y, c), device(s, z, 1 - y, c), device(s, z, y, 1 - c)
    zdev = [device(s, lax.rem(z + i + 1, LINE), y, c) for i in range(3)]
    zsrc = [lax.rem(z + 3 - i, LINE) for i in range(3)]
    half_q, half_u = stq.shape[1] // 3, stu.shape[1]
    model = xr.shape[2]

    local = []

    def fetch(src, dst):
        copy = pltpu.make_async_copy(src, dst, loc.at[len(local)])
        copy.start()
        local.append(copy)
        return copy

    stage = [fetch(vec_hbm, stv)]
    for j in range(3):
        stage.append(fetch(wq_hbm.at[:, pl.ds(j * 2 * half_q + (1 - s) * half_q, half_q)], stq.at[:, pl.ds(j * half_q, half_q)]))
    own_q = [
        fetch(wq_hbm.at[:, pl.ds(j * 2 * half_q + s * half_q, half_q)], wq.at[s, z, y, c, :, pl.ds(j * half_q, half_q)])
        for j in range(3)
    ]
    stage.append(fetch(wu_hbm.at[:, pl.ds((1 - s) * half_u, half_u)], stu))
    own_o = fetch(wo_hbm, wo.at[z, y, c])
    own_u = fetch(wu_hbm.at[:, pl.ds(s * half_u, half_u)], wu.at[s, z, y, c])
    own_d = fetch(wd_hbm, wd.at[z, y, c])
    get_tok = [fetch(tok_hbm.at[i], tok.at[i]) for i in range(2)]
    get_cot = [fetch(cot_hbm.at[i], cot.at[i]) for i in range(2)]

    blocks = [
        lambda zz, yy, cc: wq.at[s, zz, yy, cc],
        lambda zz, yy, cc: wq.at[1 - s, zz, yy, cc],
        lambda zz, yy, cc: gv.at[zz, yy, cc],
        lambda zz, yy, cc: wo.at[zz, yy, cc],
        lambda zz, yy, cc: wu.at[s, zz, yy, cc],
        lambda zz, yy, cc: wu.at[1 - s, zz, yy, cc],
        lambda zz, yy, cc: wd.at[zz, yy, cc],
    ]
    lines = [
        lambda yy, cc: wq.at[s, :, yy, cc],
        lambda yy, cc: wq.at[1 - s, :, yy, cc],
        lambda yy, cc: gv.at[:, yy, cc],
        lambda yy, cc: wo.at[:, yy, cc],
        lambda yy, cc: wu.at[s, :, yy, cc],
        lambda yy, cc: wu.at[1 - s, :, yy, cc],
        lambda yy, cc: wd.at[:, yy, cc],
    ]
    sent = []

    def send(src, dst, send_sem, recv_sem, target):
        copy = remote(src, dst, send_sem, recv_sem, target)
        copy.start()
        sent.append(copy)
        return copy

    def spread(p):
        own = blocks[p](z, y, c)
        for i in range(3):
            send(own, own, sz.at[p, i], rz.at[p, i], zdev[i])
        send(own, own, sy.at[p, 3], ry.at[p, 3], ydev)

    def after_z(p):
        for i in range(3):
            ref = blocks[p](zsrc[i], y, c)
            remote(ref, ref, sz.at[p, i], rz.at[p, i], zdev[i]).wait_recv()
            send(ref, ref, sy.at[p, i], ry.at[p, i], ydev)
        line = lines[p](y, c)
        send(line, line, sc.at[p, 0], rc.at[p, 0], cdev)

    def after_y(p):
        for i, zz in enumerate([z] + zsrc):
            ref = blocks[p](zz, 1 - y, c)
            remote(ref, ref, sy.at[p, (i + 3) % 4], ry.at[p, (i + 3) % 4], ydev).wait_recv()
        line = lines[p](1 - y, c)
        send(line, line, sc.at[p, 1], rc.at[p, 1], cdev)

    def after_c(p):
        for i, yy in enumerate([y, 1 - y]):
            ref = lines[p](yy, 1 - c)
            remote(ref, ref, sc.at[p, i], rc.at[p, i], cdev).wait_recv()

    outs = []

    def put(src, dst):
        copy = pltpu.make_async_copy(src, dst, out_sem.at[len(outs)])
        copy.start()
        outs.append(copy)

    greet([xdev, ydev, cdev] + zdev)
    for copy in stage:
        copy.wait()
    swap_v = send(stv, rcv, sx.at[0], rx.at[0], xdev)
    swap_q = send(stq, wq.at[s, z, y, c], sx.at[1], rx.at[1], xdev)
    for copy in own_q:
        copy.wait()
    spread(0)
    swap_u = send(stu, wu.at[s, z, y, c], sx.at[2], rx.at[2], xdev)
    own_o.wait()
    spread(3)

    position = lax.broadcasted_iota(jnp.int32, (pos_ref.shape[1], tok.shape[1]), 1) + s * tok.shape[1]

    def chooser(i):
        return jnp.where(position == pos_ref[i], 1.0, 0.0).astype(bf16)

    get_tok[0].wait()
    xs[0] = dot_nn(chooser(0), tok[0]).astype(bf16)
    x_swap = [send(xs.at[0], xr.at[0], sx.at[3], rx.at[3], xdev)]
    get_tok[1].wait()
    xs[1] = dot_nn(chooser(1), tok[1]).astype(bf16)
    x_swap.append(send(xs.at[1], xr.at[1], sx.at[4], rx.at[4], xdev))

    swap_v.wait_recv()
    gv[z, y, c] = stv[...] + rcv[...]
    spread(2)
    remote(wq.at[1 - s, z, y, c], wq.at[1 - s, z, y, c], sx.at[1], rx.at[1], xdev).wait_recv()
    spread(1)
    for i in range(2):
        get_cot[i].wait()
        ds[i] = dot_nn(chooser(i), cot[i]).astype(bf16)
    own_u.wait()
    after_z(0)
    spread(4)
    after_z(3)
    after_z(2)
    remote(wu.at[1 - s, z, y, c], wu.at[1 - s, z, y, c], sx.at[2], rx.at[2], xdev).wait_recv()
    spread(5)
    after_y(0)
    after_z(1)
    own_d.wait()
    spread(6)
    after_y(3)
    after_y(2)
    after_y(1)
    after_c(0)
    after_c(3)
    after_c(2)
    after_c(1)

    gains[...] = jnp.sum(gv[...].astype(f32).reshape(16, 16, model), axis=0)
    gain_one, gain_two, router = gains[0:1], gains[1:2], gains[2:3]
    put(wq, wq_out)
    put(wo, wo_out)
    put(gains, gains_out)

    def attend(i):
        ok = allowed_pairs(bias_ref[i])

        def pair(j, carry):
            q2 = qkv[i, :, pl.ds(j * 128, 128)].astype(f32)
            k2 = qkv[i, :, pl.ds(half_q + j * 128, 128)]
            v2 = qkv[i, :, pl.ds(2 * half_q + j * 128, 128)]
            mixed = jnp.zeros(q2.shape, f32)
            for parity in range(2):
                mask = head_mask(parity)
                score = dot_nt((q2 * mask).astype(bf16), k2) * (HEAD_DIM**-0.5)
                score = jnp.where(ok, score, -1000000000.0)
                weight = jnp.exp(score - jnp.max(score, axis=-1, keepdims=True))
                total = jnp.sum(weight, axis=-1, keepdims=True)
                mixed += dot_nn(weight.astype(bf16), v2) / total * mask
            att[i, :, pl.ds(j * 128, 128)] = mixed.astype(bf16)
            return carry

        lax.fori_loop(0, half_q // 128, pair, 0)

    d_swap, a_swap = [], []
    for i in range(2):
        x_swap[i].wait()
        row = xr[i].astype(f32) + xs[i].astype(f32)
        xr[i] = row.astype(bf16)
        normed = (row * inverse_rms(row) * gain_one).astype(bf16)
        for j in range(3):
            qkv[i, :, pl.ds(j * half_q, half_q)] = dot_nn(
                normed, wq[:, :, :, :, :, pl.ds(j * half_q, half_q)].reshape(model, half_q)
            ).astype(bf16)
        attend(i)
        for j in range(2):
            cols = pl.ds(j * (model // 2), model // 2)
            a_s[i, :, cols] = dot_nn(att[i], wo[:, :, :, :, cols].reshape(half_q, model // 2)).astype(bf16)
        a_swap.append(send(a_s.at[i], a_r.at[i], sx.at[5 + i], rx.at[5 + i], xdev))
        if i == 0:
            after_z(4)
            after_z(5)
            after_y(4)
    for i in range(2):
        d_swap.append(send(ds.at[i], dr.at[i], sx.at[7 + i], rx.at[7 + i], xdev))
    put(xr, xr_out)
    put(qkv, qkv_out)
    put(att, o_out)
    after_z(6)
    after_y(5)
    after_c(4)
    after_c(5)

    def mlp_up(i):
        a_swap[i].wait()
        row = xr[i].astype(f32) + (a_s[i].astype(f32) + a_r[i].astype(f32))
        hid[i] = row
        n2[i] = (row * inverse_rms(row) * gain_two).astype(bf16)

        def tile(t, carry):
            cols = pl.ds(t * 512, 512)
            up = dot_nn(n2[i], wu[:, :, :, :, :, cols].reshape(model, 512))
            curve = jnp.tanh(GELU_C * (up + GELU_K * up * up * up))
            act[i, :, cols] = (0.5 * up * (1.0 + curve)).astype(bf16)
            slope = 0.5 * (1.0 + curve) + 0.5 * up * (1.0 - curve * curve) * (
                GELU_C * (1.0 + 3.0 * GELU_K * up * up)
            )
            gp[i, :, cols] = slope.astype(bf16)
            return carry

        lax.fori_loop(0, half_u // 512, tile, 0)

    mlp_up(0)
    after_y(6)
    mlp_up(1)
    put(hid, h_out)
    after_c(6)

    def mlp_back(i):
        d_swap[i].wait()
        cot_row = dr[i].astype(f32) + ds[i].astype(f32)
        dr[i] = cot_row.astype(bf16)
        gate = jax.nn.sigmoid(jnp.sum(xr[i].astype(f32) * router, axis=-1, keepdims=True))
        dm[i] = (gate * cot_row).astype(bf16)

        def tile(t, carry):
            cols = pl.ds(t * 512, 512)
            back = dot_nt(dm[i], wd[t].reshape(512, model))
            gp[i, :, cols] = (back * gp[i, :, cols].astype(f32)).astype(bf16)
            return carry

        lax.fori_loop(0, half_u // 512, tile, 0)
        for j in range(2):
            cols = pl.ds(j * (model // 2), model // 2)
            d2s[i, :, cols] = dot_nt(gp[i], wu[j].reshape(model // 2, half_u)).astype(bf16)
        return send(d2s.at[i], d2r.at[i], sx.at[9 + i], rx.at[9 + i], xdev)

    d2_swap = [mlp_back(0), mlp_back(1)]
    put(dr, dr_out)
    put(d2s, d2s_out)
    rows = act.shape[0] * act.shape[1]

    def down_tile(t, carry):
        part = dot_tn(act[:, :, pl.ds(t * 512, 512)].reshape(rows, 512), dm[...].reshape(rows, model))
        gd[t] = part.astype(bf16).reshape(gd.shape[1:])
        return carry

    lax.fori_loop(0, half_u // 512, down_tile, 0)
    put(gd, gd_out)

    def up_tile(t, carry):
        cols = pl.ds(t * 512, 512)
        part = dot_tn(n2[...].reshape(rows, model), gp[:, :, cols].reshape(rows, 512))
        gu[:, :, :, :, :, cols] = part.astype(bf16).reshape(gu.shape[:5] + (512,))
        return carry

    lax.fori_loop(0, half_u // 512, up_tile, 0)
    put(gu, gu_out)
    for i in range(2):
        for j in range(2):
            cols = pl.ds(j * (model // 2), model // 2)
            m_s[i, :, cols] = dot_nn(act[i], wd[:, :, :, :, cols].reshape(half_u, model // 2)).astype(bf16)
    put(m_s, ms_out)
    for copy in d2_swap:
        copy.wait_recv()
    put(d2r, d2r_out)
    waited = x_swap + a_swap + d_swap
    for copy in sent:
        if not any(copy is other for other in waited):
            copy.wait_send()
    for copy in outs:
        copy.wait()


def second_kernel(
    xr_in, dr_in, h_in, qkv_in, o_in, wq_in, wo_in, gains_in, gd_in, gu_in, d2s_in, d2r_in, ms_in, live_ref, bias_ref,
    upd_out, dx_out, fq_out, fo_out, fu_out, fd_out, vec_out,
    xr, dr, hid, qkv, att, wq, wo, gains, d2s, d2r, m_s, m_r, n1, dh, da, do, dqkv, d1s, d1r, upd, dx, logit,
    go, gq, lcd, lcu, rcd, rcu, rco, rcq, ryd, ryu, ryo, ryq, rzd, rzu, rzo, rzq,
    fq, fo, fu, fd, suq, suu, ruq, ruu, vs, vr, v_all,
    loc, out_sem, sc, rc, sy, ry, sz, rz, sx, rx,
):
    s, z, y, c = place()
    xdev, ydev, cdev = device(1 - s, z, y, c), device(s, z, 1 - y, c), device(s, z, y, 1 - c)
    zdev = [device(s, lax.rem(z + i + 1, LINE), y, c) for i in range(3)]
    model, half_q, half_u = xr.shape[2], att.shape[2], fu.shape[2]
    rows = xr.shape[0] * xr.shape[1]
    local, sent, outs = [], [], []

    def fetch(src, dst):
        copy = pltpu.make_async_copy(src, dst, loc.at[len(local)])
        copy.start()
        local.append(copy)
        return copy

    def send(src, dst, send_sem, recv_sem, target):
        copy = remote(src, dst, send_sem, recv_sem, target)
        copy.start()
        sent.append(copy)
        return copy

    def put(src, dst):
        copy = pltpu.make_async_copy(src, dst, out_sem.at[len(outs)])
        copy.start()
        outs.append(copy)

    half_d = lcd.shape[3]
    other = [
        lambda cc, i=i: gd_in.at[:, :, cc, pl.ds(half_d * i, half_d)] for i in range(2)
    ] + [lambda cc, i=i: gu_in.at[i, :, :, cc] for i in range(2)] + [lambda cc: go.at[:, :, cc]] + [
        lambda cc, i=i: gq.at[i, :, :, cc] for i in range(2)
    ]
    land_c = [rcd.at[0], rcd.at[1], rcu.at[0], rcu.at[1], rco.at[0], rcq.at[0], rcq.at[1]]
    land_y = [ryd.at[0], ryd.at[1], ryu.at[0], ryu.at[1], ryo.at[0], ryq.at[0], ryq.at[1]]
    land_z = [rzd.at[0], rzd.at[1], rzu.at[0], rzu.at[1], rzo.at[0], rzq.at[0], rzq.at[1]]

    def c_start(k):
        return send(other[k](1 - c), land_c[k], sc.at[k], rc.at[k], cdev)

    def c_end(k, own):
        remote(land_c[k], land_c[k], sc.at[k], rc.at[k], cdev).wait_recv()
        ref = land_c[k]

        def add(i, carry):
            ref[i] = (ref[i].astype(f32) + own(i).astype(f32)).astype(bf16)
            return carry

        lax.fori_loop(0, LINE, add, 0)
        send(ref.at[:, 1 - y], land_y[k], sy.at[k], ry.at[k], ydev)

    def y_end(k):
        ref = land_y[k]
        remote(ref, ref, sy.at[k], ry.at[k], ydev).wait_recv()

        def add(i, carry):
            ref[i] = (ref[i].astype(f32) + land_c[k][i, y].astype(f32)).astype(bf16)
            return carry

        lax.fori_loop(0, LINE, add, 0)
        for i in range(3):
            send(ref.at[lax.rem(z + i + 1, LINE)], land_z[k].at[i], sz.at[k, i], rz.at[k, i], zdev[i])

    def z_end(k):
        total = land_y[k][z].astype(f32)
        for i in range(3):
            remote(land_z[k].at[i], land_z[k].at[i], sz.at[k, i], rz.at[k, i], zdev[i]).wait_recv()
            total += land_z[k][i].astype(f32)
        return total

    get_d2 = [fetch(d2s_in, d2s), fetch(d2r_in, d2r), fetch(h_in, hid), fetch(gains_in, gains), fetch(dr_in, dr), fetch(xr_in, xr)]
    get_m = fetch(ms_in, m_s)
    get_own = [fetch(other[k](c), (lcd.at[k] if k < 2 else lcu.at[k - 2])) for k in range(4)]
    get_att = [fetch(wo_in, wo), fetch(o_in, att), fetch(qkv_in, qkv)]
    get_wq = fetch(wq_in, wq)
    greet([xdev, ydev, cdev] + zdev)
    for k in range(4):
        c_start(k)
    get_m.wait()
    m_swap = [send(m_s.at[i], m_r.at[i], sx.at[i], rx.at[i], xdev) for i in range(2)]
    for k in range(2):
        get_own[k].wait()
        c_end(k, lambda i, k=k: lcd[k, i])
    for copy in get_d2:
        copy.wait()
    gain_one, gain_two, router = gains[0:1], gains[1:2], gains[2:3]

    def gate_of(i):
        return jax.nn.sigmoid(jnp.sum(xr[i].astype(f32) * router, axis=-1, keepdims=True))

    def hidden_back(i):
        back = d2s[i].astype(f32) + d2r[i].astype(f32)
        row = hid[i]
        r2 = inverse_rms(row)
        scaled = back * gain_two
        step = r2 * scaled - row * (r2 * r2 * r2 * jnp.mean(scaled * row, axis=-1, keepdims=True))
        dh[i] = step
        da[i] = (gate_of(i) * dr[i].astype(f32) + step).astype(bf16)
        for j in range(1):
            do[i] = dot_nt(da[i], wo[...].reshape(half_q, model)).astype(bf16)
        return jnp.sum(d2s[i].astype(f32) * row * r2, axis=0, keepdims=True)

    def attend_back(i):
        ok = allowed_pairs(bias_ref[i])
        scale = HEAD_DIM**-0.5

        def pair(j, carry):
            q2 = qkv[i, :, pl.ds(j * 128, 128)]
            k2 = qkv[i, :, pl.ds(half_q + j * 128, 128)]
            v2 = qkv[i, :, pl.ds(2 * half_q + j * 128, 128)]
            g2 = do[i, :, pl.ds(j * 128, 128)].astype(f32)
            q2f = q2.astype(f32)
            dq2 = jnp.zeros(q2.shape, f32)
            dk2 = jnp.zeros(q2.shape, f32)
            dv2 = jnp.zeros(q2.shape, f32)
            for parity in range(2):
                mask = head_mask(parity)
                score = dot_nt((q2f * mask).astype(bf16), k2) * scale
                score = jnp.where(ok, score, -1000000000.0)
                weight = jnp.exp(score - jnp.max(score, axis=-1, keepdims=True))
                over = 1.0 / jnp.sum(weight, axis=-1, keepdims=True)
                gh = g2 * mask
                dp = dot_nt(gh.astype(bf16), v2)
                prob = weight * over
                delta = jnp.sum(prob * dp, axis=-1, keepdims=True)
                dscore = (prob * (dp - delta)).astype(bf16)
                dq2 += dot_nn(dscore, k2) * mask
                dk2 += dot_tn(dscore, q2) * mask
                dv2 += dot_tn(weight.astype(bf16), (gh * over).astype(bf16))
            dqkv[i, :, pl.ds(j * 128, 128)] = (dq2 * scale).astype(bf16)
            dqkv[i, :, pl.ds(half_q + j * 128, 128)] = (dk2 * scale).astype(bf16)
            dqkv[i, :, pl.ds(2 * half_q + j * 128, 128)] = dv2.astype(bf16)
            return carry

        lax.fori_loop(0, half_q // 128, pair, 0)

    def inner_back(i):
        row = xr[i].astype(f32)
        r1 = inverse_rms(row)
        n1[i] = (row * r1 * gain_one).astype(bf16)
        grad = jnp.zeros((1, model // 2), f32)
        parts = []
        for j in range(2):
            cols = pl.ds(j * (model // 2), model // 2)
            part = dot_nt(dqkv[i], wq[j].reshape(model // 2, 3 * half_q))
            d1s[i, :, cols] = part.astype(bf16)
            parts.append(jnp.sum(part * xr[i, :, cols].astype(f32) * r1, axis=0, keepdims=True))
        swap = send(d1s.at[i], d1r.at[i], sx.at[2 + i], rx.at[2 + i], xdev)
        return swap, parts

    for copy in get_att:
        copy.wait()
    grad_gm = hidden_back(0)
    get_own[2].wait()
    c_end(2, lambda i: lcu[0, i])
    attend_back(0)
    get_own[3].wait()
    c_end(3, lambda i: lcu[1, i])
    get_wq.wait()
    swap_0, parts_0 = inner_back(0)
    y_end(0)
    grad_gm += hidden_back(1)
    attend_back(1)
    swap_1, parts_1 = inner_back(1)
    d1_swap = [swap_0, swap_1]
    y_end(1)

    for j in range(2):
        cols = pl.ds(j * (model // 2), model // 2)
        vs[0:1, cols] = parts_0[j] + parts_1[j]
    vs[1:2] = grad_gm

    for t in range(2):
        cols = pl.ds(t * (model // 2), model // 2)
        part = dot_tn(att[...].reshape(rows, half_q), da[:, :, cols].reshape(rows, model // 2))
        go[:, :, :, :, cols] = part.astype(bf16).reshape(go.shape[:4] + (model // 2,))
    c_start(4)

    def qkv_tile(t, carry):
        cols = pl.ds(t * half_q, half_q)
        part = dot_tn(n1[...].reshape(rows, model), dqkv[:, :, cols].reshape(rows, half_q))
        gq[:, :, :, :, :, cols] = part.astype(bf16).reshape(gq.shape[:5] + (half_q,))
        return carry

    lax.fori_loop(0, 3, qkv_tile, 0)
    c_start(5)
    c_start(6)
    c_end(4, lambda i: go[i, :, c])

    grad_router = jnp.zeros((1, model), f32)
    for i in range(2):
        m_swap[i].wait()
        row = xr[i].astype(f32)
        gate = gate_of(i)
        branch = (hid[i] - row) + (m_s[i].astype(f32) + m_r[i].astype(f32))
        upd[i] = (gate * branch * live_ref[i]).astype(bf16)
        slope = jnp.sum(dr[i].astype(f32) * branch, axis=-1, keepdims=True) * gate * (1.0 - gate)
        logit[i] = slope
        grad_router += jnp.sum(row * slope, axis=0, keepdims=True)
    put(upd, upd_out)
    vs[2:3] = 0.5 * grad_router
    vs[3:8] = jnp.zeros((5, model), f32)
    send(vs, vr.at[0], sc.at[7], rc.at[7], cdev)
    c_end(5, lambda i: gq[0, i, :, c])
    c_end(6, lambda i: gq[1, i, :, c])

    y_end(2)
    fd[0:half_d] = z_end(0)
    y_end(3)
    fd[half_d:] = z_end(1)
    put(fd, fd_out)
    remote(vs, vr.at[0], sc.at[7], rc.at[7], cdev).wait_recv()
    v_all[0] = vs[...] + vr[0]
    send(v_all.at[0], vr.at[1], sy.at[7], ry.at[7], ydev)
    y_end(4)
    fu[0] = z_end(2)

    for i in range(2):
        d1_swap[i].wait()
        row = xr[i].astype(f32)
        r1 = inverse_rms(row)
        scaled = (d1s[i].astype(f32) + d1r[i].astype(f32)) * gain_one
        step = r1 * scaled - row * (r1 * r1 * r1 * jnp.mean(scaled * row, axis=-1, keepdims=True))
        dx[i] = (dh[i] + step + logit[i] * router).astype(bf16)
    put(dx, dx_out)

    fu[1] = z_end(3)
    suu[...] = fu[1 - s].astype(bf16)
    send(suu, ruu, sx.at[4], rx.at[4], xdev)
    remote(vs, vr.at[1], sy.at[7], ry.at[7], ydev).wait_recv()
    v_all[1] = v_all[0] + vr[1]
    for i in range(3):
        send(v_all.at[1], vr.at[2 + i], sz.at[7, i], rz.at[7, i], zdev[i])
    y_end(5)
    fo[...] = z_end(4)
    put(fo, fo_out)
    y_end(6)
    for i in range(3):
        remote(vs, vr.at[2 + i], sz.at[7, i], rz.at[7, i], zdev[i]).wait_recv()
    v_all[2] = v_all[1] + vr[2] + vr[3] + vr[4]
    send(v_all.at[2], vr.at[5], sx.at[6], rx.at[6], xdev)
    put(fu.at[s], fu_out.at[:, pl.ds(s * half_u, half_u)])
    fq[0] = z_end(5)
    remote(ruu, ruu, sx.at[4], rx.at[4], xdev).wait_recv()
    fu[1 - s] = ruu[...].astype(f32)
    put(fu.at[1 - s], fu_out.at[:, pl.ds((1 - s) * half_u, half_u)])
    fq[1] = z_end(6)
    suq[...] = fq[1 - s].astype(bf16)
    send(suq, ruq, sx.at[5], rx.at[5], xdev)
    for j in range(3):
        put(fq.at[s, :, pl.ds(j * half_q, half_q)], fq_out.at[:, pl.ds(2 * j * half_q + s * half_q, half_q)])
    remote(vs, vr.at[5], sx.at[6], rx.at[6], xdev).wait_recv()
    v_all[3] = v_all[2] + vr[5]
    put(v_all.at[3], vec_out)
    remote(ruq, ruq, sx.at[5], rx.at[5], xdev).wait_recv()
    fq[1 - s] = ruq[...].astype(f32)
    for j in range(3):
        put(fq.at[1 - s, :, pl.ds(j * half_q, half_q)], fq_out.at[:, pl.ds(2 * j * half_q + (1 - s) * half_q, half_q)])
    waited = m_swap + d1_swap
    for copy in sent:
        if not any(copy is item for item in waited):
            copy.wait_send()
    for copy in outs:
        copy.wait()


def split_device(
    tokens, cotangent, lengths, routed, w_qkv, w_out, w_up, w_down, gain_attn, gain_mlp, router
):
    slots, local_len, model = tokens.shape
    ranks = routed.shape[1]
    half_q, half_u = w_qkv.shape[1] // 6, w_up.shape[1] // 2
    part, down = w_qkv.shape[0], w_down.shape[0]
    s = lax.axis_index("seq")
    flat = s * lax.axis_size("batch") + lax.axis_index("batch")
    rank_all = jnp.arange(ranks, dtype=jnp.int32)
    live = rank_all[None, :] < (lengths // 8)[:, None]
    where_live = jnp.where(live, routed, -1)
    bias = jnp.where(live, 0.0, -1000000000.0).astype(f32)[:, None, :]
    lane = jnp.arange(model, dtype=jnp.int32)
    small = jnp.stack([gain_attn, gain_mlp, router])
    vec = jnp.where(lane[None, :] // part == flat, jnp.tile(small, (1, model // part)), 0)
    vec = jnp.pad(vec, ((0, 13), (0, 0)))

    hbm = pl.BlockSpec(memory_space=pl.ANY)
    vmem = pl.BlockSpec(memory_space=pltpu.VMEM)
    sds = jax.ShapeDtypeStruct
    dma = pltpu.SemaphoreType.DMA
    rows = (slots, ranks, model)
    grid = (LINE, 2, 2)
    wq_shape, wo_shape = (2,) + grid + (part, 3 * half_q), grid + (part, model)
    wu_shape, wd_shape = (2,) + grid + (part, half_u), grid + (down, model)
    first = pl.pallas_call(
        first_kernel,
        out_shape=(
            sds(rows, bf16), sds(rows, bf16), sds(rows, f32), sds((slots, ranks, 3 * half_q), bf16),
            sds((slots, ranks, half_q), bf16), sds(wq_shape, bf16), sds(wo_shape, bf16), sds((16, model), f32),
            sds(wd_shape, bf16), sds(wu_shape, bf16), sds(rows, bf16), sds(rows, bf16), sds(rows, bf16),
        ),
        in_specs=[hbm] * 7 + [vmem] * 2,
        out_specs=[hbm] * 13,
        scratch_shapes=[
            pltpu.VMEM(tokens.shape, bf16), pltpu.VMEM(tokens.shape, bf16),
            pltpu.VMEM(wq_shape, bf16), pltpu.VMEM(wo_shape, bf16), pltpu.VMEM(wu_shape, bf16), pltpu.VMEM(wd_shape, bf16),
            pltpu.VMEM(grid + (16, model), bf16),
            pltpu.VMEM((part, 3 * half_q), bf16), pltpu.VMEM((part, half_u), bf16),
            pltpu.VMEM((16, model), bf16), pltpu.VMEM((16, model), bf16),
            pltpu.VMEM(rows, bf16), pltpu.VMEM(rows, bf16), pltpu.VMEM(rows, bf16), pltpu.VMEM(rows, bf16),
            pltpu.VMEM(rows, bf16), pltpu.VMEM(rows, bf16), pltpu.VMEM(rows, f32), pltpu.VMEM(rows, bf16),
            pltpu.VMEM((slots, ranks, 3 * half_q), bf16), pltpu.VMEM((slots, ranks, half_q), bf16),
            pltpu.VMEM((slots, ranks, half_u), bf16), pltpu.VMEM((slots, ranks, half_u), bf16),
            pltpu.VMEM(rows, bf16), pltpu.VMEM(rows, bf16), pltpu.VMEM(rows, bf16), pltpu.VMEM(rows, bf16),
            pltpu.VMEM(wd_shape, bf16), pltpu.VMEM(wu_shape, bf16), pltpu.VMEM((16, model), f32),
            dma((16,)), dma((13,)), dma((7, 3)), dma((7, 3)), dma((7, 4)), dma((7, 4)), dma((7, 2)), dma((7, 2)),
            dma((11,)), dma((11,)),
        ],
        compiler_params=pltpu.CompilerParams(collective_id=1, has_side_effects=True, vmem_limit_bytes=60 << 20),
        name="gather_and_forward",
    )
    xr, dr, hid, qkv, att, wq, wo, gains, gd, gu, d2s, d2r, m_s = first(
        tokens, cotangent, vec, w_qkv, w_out, w_up, w_down, where_live[:, :, None], bias
    )
    land = lambda chunks, tall, wide: [
        pltpu.VMEM((chunks, LINE, 2, tall, wide), bf16),
        pltpu.VMEM((chunks, LINE, tall, wide), bf16),
        pltpu.VMEM((chunks, 3, tall, wide), bf16),
    ]
    on_d, on_u, on_o, on_q = (
        land(2, down // 2, model), land(2, part, half_u), land(1, part, model), land(2, part, 3 * half_q)
    )
    upd, dxr, grad_qkv, grad_out, grad_up, grad_down, vec_sum = pl.pallas_call(
        second_kernel,
        out_shape=(
            sds(rows, bf16), sds(rows, bf16), sds((part, 6 * half_q), f32), sds((part, model), f32),
            sds((part, 2 * half_u), f32), sds((down, model), f32), sds((8, model), f32),
        ),
        in_specs=[hbm] * 13 + [vmem] * 2,
        out_specs=[hbm] * 7,
        scratch_shapes=[
            pltpu.VMEM(rows, bf16), pltpu.VMEM(rows, bf16), pltpu.VMEM(rows, f32),
            pltpu.VMEM((slots, ranks, 3 * half_q), bf16), pltpu.VMEM((slots, ranks, half_q), bf16),
            pltpu.VMEM(wq_shape, bf16), pltpu.VMEM(wo_shape, bf16), pltpu.VMEM((16, model), f32),
            pltpu.VMEM(rows, bf16), pltpu.VMEM(rows, bf16), pltpu.VMEM(rows, bf16), pltpu.VMEM(rows, bf16),
            pltpu.VMEM(rows, bf16), pltpu.VMEM(rows, f32), pltpu.VMEM(rows, bf16),
            pltpu.VMEM((slots, ranks, half_q), bf16), pltpu.VMEM((slots, ranks, 3 * half_q), bf16),
            pltpu.VMEM(rows, bf16), pltpu.VMEM(rows, bf16), pltpu.VMEM(rows, bf16), pltpu.VMEM(rows, bf16),
            pltpu.VMEM((slots, ranks, 1), f32),
            pltpu.VMEM(wo_shape, bf16), pltpu.VMEM(wq_shape, bf16), on_d[0], on_u[0],
            on_d[0], on_u[0], on_o[0], on_q[0], on_d[1], on_u[1], on_o[1], on_q[1], on_d[2], on_u[2], on_o[2], on_q[2],
            pltpu.VMEM((2, part, 3 * half_q), f32), pltpu.VMEM((part, model), f32),
            pltpu.VMEM((2, part, half_u), f32), pltpu.VMEM((down, model), f32),
            pltpu.VMEM((part, 3 * half_q), bf16), pltpu.VMEM((part, half_u), bf16),
            pltpu.VMEM((part, 3 * half_q), bf16), pltpu.VMEM((part, half_u), bf16),
            pltpu.VMEM((8, model), f32), pltpu.VMEM((6, 8, model), f32), pltpu.VMEM((4, 8, model), f32),
            dma((16,)), dma((13,)), dma((8,)), dma((8,)), dma((8,)), dma((8,)), dma((8, 3)), dma((8, 3)),
            dma((7,)), dma((7,)),
        ],
        compiler_params=pltpu.CompilerParams(collective_id=2, has_side_effects=True, vmem_limit_bytes=60 << 20),
        name="backward_and_sum",
    )(xr, dr, hid, qkv, att, wq, wo, gains, gd, gu, d2s, d2r, m_s, live[:, :, None].astype(f32), bias)

    positions = s * local_len + jnp.arange(local_len, dtype=jnp.int32)
    chooser = (where_live[:, :, None] == positions[None, None, :]).astype(bf16)

    def place_rows(base, moved):
        return (
            base.astype(f32) + jnp.einsum("scp,scd->spd", chooser, moved, preferred_element_type=f32)
        ).astype(bf16)

    mine = lax.dynamic_slice(vec_sum, (0, flat * part), (8, part))
    return (
        place_rows(tokens, upd), place_rows(cotangent, dxr), grad_qkv, grad_out, grad_up, grad_down,
        mine[0], mine[1], mine[2],
    )


def solution(mesh):
    in_specs = (
        P("batch", "seq", None),
        P("batch", "seq", None),
        P("batch"),
        P("batch", None),
        P(("seq", "batch"), None),
        P(("seq", "batch"), None),
        P(("seq", "batch"), None),
        P(("seq", "batch"), None),
        P(("seq", "batch")),
        P(("seq", "batch")),
        P(("seq", "batch")),
    )
    out_specs = (
        P("batch", "seq", None),
        P("batch", "seq", None),
        P(("seq", "batch"), None),
        P(("seq", "batch"), None),
        P(("seq", "batch"), None),
        P(("seq", "batch"), None),
        P(("seq", "batch")),
        P(("seq", "batch")),
        P(("seq", "batch")),
    )
    small_slice = mesh.shape["seq"] == 2 and mesh.shape["batch"] == 4 * LINE
    body = split_device if small_slice else general_device
    return jax.shard_map(body, mesh=mesh, in_specs=in_specs, out_specs=out_specs, check_vma=False)
```

```python
import functools

import jax
import jax.numpy as jnp
from jax import lax
from jax.experimental import pallas as pl
from jax.experimental.pallas import tpu as pltpu
from jax.sharding import PartitionSpec as P

HEAD_DIM = 64
MESH = pl.DeviceIdType.MESH


epsilon = 1e-05
highest = lax.Precision.HIGHEST
f32 = jnp.float32
bf16 = jnp.bfloat16

LINE = 4
GELU_C = 0.7978845608
GELU_K = 0.044715


def dot_nn(a, b):
    return lax.dot_general(a, b, (((1,), (0,)), ((), ())), preferred_element_type=f32)


def dot_nt(a, b):
    return lax.dot_general(a, b, (((1,), (1,)), ((), ())), preferred_element_type=f32)


def dot_tn(a, b):
    return lax.dot_general(a, b, (((0,), (0,)), ((), ())), preferred_element_type=f32)


def place():
    s = lax.axis_index("seq")
    b = lax.axis_index("batch")
    return s, b // 4, lax.rem(b // 2, 2), lax.rem(b, 2)


def device(s, z, y, c):
    return (s, z * 4 + y * 2 + c)


def remote(src, dst, send, recv, target):
    return pltpu.make_async_remote_copy(
        src_ref=src, dst_ref=dst, send_sem=send, recv_sem=recv, device_id=target, device_id_type=MESH
    )


def greet(targets):
    barrier = pltpu.get_barrier_semaphore()
    for target in targets:
        pl.semaphore_signal(barrier, inc=1, device_id=target, device_id_type=MESH)
    pl.semaphore_wait(barrier, len(targets))


def inverse_rms(values):
    return lax.rsqrt(jnp.mean(values * values, axis=-1, keepdims=True) + epsilon)


def head_mask(parity):
    lane = lax.broadcasted_iota(jnp.int32, (1, 128), 1)
    return jnp.where(lane // HEAD_DIM == parity, 1.0, 0.0).astype(f32)


def norm_apply(values_in, gain_vec):
    return (
        values_in
        * lax.rsqrt(jnp.mean(values_in * values_in, axis=-1, keepdims=True) + epsilon)
        * gain_vec
    )


def gelu_tanh(values_in):
    return jax.nn.gelu(values_in, approximate=True)


def general_device(
    tokens, cotangent, lengths, routed, w_qkv, w_out, w_up, w_down, gain_attn, gain_mlp, router
):
    slot_count, local_len, model_width = tokens.shape
    capacity = routed.shape[1]
    seq_devices = lax.axis_size("seq")
    own_count = capacity // seq_devices
    head_count = model_width // HEAD_DIM
    row_count = own_count * slot_count
    score_scale = HEAD_DIM ** (-0.5)
    gathered = (
        lax.all_gather(w_qkv, ("seq", "batch"), axis=0, tiled=True),
        lax.all_gather(w_out, ("seq", "batch"), axis=0, tiled=True),
        lax.all_gather(w_up, ("seq", "batch"), axis=0, tiled=True),
        lax.all_gather(w_down, ("seq", "batch"), axis=0, tiled=True),
        lax.all_gather(gain_attn, ("seq", "batch"), axis=0, tiled=True),
        lax.all_gather(gain_mlp, ("seq", "batch"), axis=0, tiled=True),
        lax.all_gather(router, ("seq", "batch"), axis=0, tiled=True),
    )
    full_qkv, full_out, full_up, full_down, full_ga, full_gm, full_router = gathered
    gain_one = full_ga.astype(f32)
    gain_two = full_gm.astype(f32)
    router_vec = full_router.astype(f32)
    counts = lengths // 8
    seq_place = lax.axis_index("seq")
    positions = seq_place * local_len + jnp.arange(local_len, dtype=jnp.int32)
    rank_all = jnp.arange(capacity, dtype=jnp.int32)
    live_all = rank_all[None, :] < counts[:, None]
    chooser = ((routed[:, :, None] == positions[None, None, :]) & live_all[:, :, None]).astype(bf16)
    pick_in = jnp.einsum("scp,spd->csd", chooser, tokens, preferred_element_type=f32)
    pick_cot = jnp.einsum("scp,spd->csd", chooser, cotangent, preferred_element_type=f32)
    picked, picked_cot = (
        lax.psum_scatter(
            pick_in.astype(jnp.bfloat16), "seq", scatter_dimension=0, tiled=True
        ).astype(jnp.float32),
        lax.psum_scatter(
            pick_cot.astype(jnp.bfloat16), "seq", scatter_dimension=0, tiled=True
        ).astype(jnp.float32),
    )
    own_rank = seq_place * own_count + jnp.arange(own_count, dtype=jnp.int32)
    live_own = own_rank[:, None] < counts[None, :]
    live_mask = live_own.reshape(row_count, 1).astype(f32)
    routed_in = picked.reshape(row_count, model_width)
    normed_one = norm_apply(routed_in, gain_one).astype(bf16)
    joined = jnp.dot(normed_one, full_qkv, preferred_element_type=f32).astype(bf16)
    query_rows = joined[:, :model_width].reshape(own_count, slot_count, head_count, HEAD_DIM)
    key_own = joined[:, model_width : 2 * model_width].reshape(own_count, slot_count, model_width)
    value_own = joined[:, 2 * model_width :].reshape(own_count, slot_count, model_width)
    key_every, value_every = (
        lax.all_gather(key_own, "seq", axis=0, tiled=True),
        lax.all_gather(value_own, "seq", axis=0, tiled=True),
    )
    key_rows = key_every.reshape(capacity, slot_count, head_count, HEAD_DIM)
    value_rows = value_every.reshape(capacity, slot_count, head_count, HEAD_DIM)
    scores = (
        jnp.einsum("qsha,ksha->shqk", query_rows, key_rows, preferred_element_type=f32)
        * score_scale
    )
    causal = rank_all[None, :] <= own_rank[:, None]
    allowed = causal[None, :, :] & (rank_all[None, None, :] < counts[:, None, None])
    scores = jnp.where(allowed[:, None], scores, -1000000000.0)
    row_max = jnp.max(scores, axis=-1, keepdims=True)
    weights_f = jnp.exp(scores - row_max)
    row_total = jnp.sum(weights_f, axis=-1, keepdims=True)
    weights_low = weights_f.astype(bf16)
    mixture = jnp.einsum("shqk,ksha->qsha", weights_low, value_rows, preferred_element_type=f32)
    mixture = mixture / jnp.transpose(row_total, (2, 0, 1, 3))
    attended = mixture.reshape(row_count, model_width).astype(bf16)
    branch_a = jnp.dot(attended, full_out, preferred_element_type=f32)
    hidden = routed_in + branch_a
    normed_two = norm_apply(hidden, gain_two).astype(bf16)
    up_proj = jnp.dot(normed_two, full_up, preferred_element_type=f32)
    activated = gelu_tanh(up_proj).astype(bf16)
    branch_m = jnp.dot(activated, full_down, preferred_element_type=f32)
    gate_prob = jax.nn.sigmoid(jnp.dot(routed_in, router_vec, precision=highest))
    branch = branch_a + branch_m
    update = (
        (gate_prob[:, None] * branch * live_mask)
        .astype(bf16)
        .reshape(own_count, slot_count, model_width)
    )
    update_every = lax.all_gather(update, "seq", axis=0, tiled=True)
    output = (
        tokens.astype(f32)
        + jnp.einsum("scp,csd->spd", chooser, update_every, preferred_element_type=f32)
    ).astype(bf16)
    cot_rows = picked_cot.reshape(row_count, model_width)
    grad_gate = jnp.sum(cot_rows * branch, axis=-1)
    grad_logit = grad_gate * gate_prob * (1.0 - gate_prob)
    grad_branch = gate_prob[:, None] * cot_rows
    grad_m = grad_branch.astype(bf16)
    grad_act = jnp.einsum("rd,fd->rf", grad_m, full_down, preferred_element_type=f32)
    unused_up, gelu_pull = jax.vjp(gelu_tanh, up_proj)
    grad_u = gelu_pull(grad_act)[0].astype(bf16)
    grad_n2 = jnp.einsum("rf,df->rd", grad_u, full_up, preferred_element_type=f32)
    unused_two, norm_pull_two = jax.vjp(norm_apply, hidden, gain_two)
    grad_hidden, grad_gm = norm_pull_two(grad_n2)
    grad_a = (grad_branch + grad_hidden).astype(bf16)
    grad_att = jnp.einsum("rd,ed->re", grad_a, full_out, preferred_element_type=f32).astype(bf16)
    grad_att4 = grad_att.reshape(own_count, slot_count, head_count, HEAD_DIM)
    delta_rows = jnp.sum(grad_att4.astype(f32) * mixture, axis=-1)
    delta = jnp.transpose(delta_rows, (1, 2, 0))[..., None]
    grad_p = jnp.einsum("qsha,ksha->shqk", grad_att4, value_rows, preferred_element_type=f32)
    probs = weights_f / row_total
    grad_s = (probs * (grad_p - delta)).astype(bf16)
    grad_q = (
        jnp.einsum("shqk,ksha->qsha", grad_s, key_rows, preferred_element_type=f32) * score_scale
    )
    grad_k = (
        jnp.einsum("shqk,qsha->ksha", grad_s, query_rows, preferred_element_type=f32) * score_scale
    )
    scaled_low = weights_low.astype(f32) / row_total
    grad_v = jnp.einsum("shqk,qsha->ksha", scaled_low, grad_att4.astype(f32), precision=highest)
    grad_k_own, grad_v_own = (
        lax.psum_scatter(
            grad_k.reshape(capacity, slot_count, model_width).astype(jnp.bfloat16),
            "seq",
            scatter_dimension=0,
            tiled=True,
        ).astype(jnp.float32),
        lax.psum_scatter(
            grad_v.reshape(capacity, slot_count, model_width).astype(jnp.bfloat16),
            "seq",
            scatter_dimension=0,
            tiled=True,
        ).astype(jnp.float32),
    )
    grad_joined = jnp.concatenate(
        [
            grad_q.reshape(row_count, model_width),
            grad_k_own.reshape(row_count, model_width),
            grad_v_own.reshape(row_count, model_width),
        ],
        axis=-1,
    ).astype(bf16)
    grad_n1 = jnp.einsum("re,de->rd", grad_joined, full_qkv, preferred_element_type=f32)
    unused_one, norm_pull_one = jax.vjp(norm_apply, routed_in, gain_one)
    grad_x1, grad_ga = norm_pull_one(grad_n1)
    grad_router = jnp.sum(routed_in * grad_logit[:, None], axis=0)
    grad_rows = (grad_hidden + grad_x1 + grad_logit[:, None] * router_vec[None, :]).astype(bf16)
    grad_rows = grad_rows.reshape(own_count, slot_count, model_width)
    grad_every = lax.all_gather(grad_rows, "seq", axis=0, tiled=True)
    input_grad = (
        cotangent.astype(f32)
        + jnp.einsum("scp,csd->spd", chooser, grad_every, preferred_element_type=f32)
    ).astype(bf16)
    part_qkv = jnp.einsum("rd,re->de", normed_one, grad_joined, preferred_element_type=f32)
    part_out = jnp.einsum("re,rd->ed", attended, grad_a, preferred_element_type=f32)
    part_up = jnp.einsum("rd,rf->df", normed_two, grad_u, preferred_element_type=f32)
    part_down = jnp.einsum("rf,rd->fd", activated, grad_m, preferred_element_type=f32)

    def sum_rows(part):
        return lax.psum_scatter(
            part.astype(bf16), ("seq", "batch"), scatter_dimension=0, tiled=True
        ).astype(f32)

    down_sum = sum_rows(part_down)
    grad_up = sum_rows(part_up)
    grad_out = sum_rows(part_out)
    grad_qkv = sum_rows(part_qkv)
    small_ga, small_gm, small_router = (
        lax.psum_scatter(grad_ga, ("seq", "batch"), scatter_dimension=0, tiled=True),
        lax.psum_scatter(grad_gm, ("seq", "batch"), scatter_dimension=0, tiled=True),
        lax.psum_scatter(grad_router, ("seq", "batch"), scatter_dimension=0, tiled=True),
    )
    return (
        output,
        input_grad,
        grad_qkv,
        grad_out,
        grad_up,
        down_sum,
        small_ga,
        small_gm,
        small_router,
    )


def block_kernel(
    tok_hbm, cot_hbm, wq_hbm, wo_hbm, wu_hbm, wd_hbm, small_ref, routed_ref, len_ref,
    upd_out, dx_out, fq_out, fo_out, fu_out, fd_out, vec_out,
    wq, wo, wu, wd, gv, stq, stu, stv, rcv,
    xs, xr, ds, dr, a_s, a_r, d2s, d2r, d1r, m_s, m_r, hid, dh, qkv, att, act, gp, logit, gains,
    gd, gu, rcd, rcu, ryd, ryu, rzd, rzu,
    fqk, fv, fo, fu, fd, sqk, sv, suu, rqk, rv, ruu, vs, vr, v_all,
    loc, out_sem, wz, vz, wy, vy, wc, vc, sx, rx, gc, hc, gy, hy, gz, hz, free,
):
    s, z, y, c = place()
    near, far = z + 1 - 2 * lax.rem(z, 2), LINE - 1 - z
    xdev, ydev, cdev = device(1 - s, z, y, c), device(s, z, 1 - y, c), device(s, z, y, 1 - c)
    ndev, fdev = device(s, near, y, c), device(s, far, y, c)
    model, half_q, half_u = xr.shape[2], att.shape[2], act.shape[2]
    ranks, half = xr.shape[1], xr.shape[2] // 2
    rows = xr.shape[0] * ranks
    part, half_d = stq.shape[0], wd.shape[3] // 2
    local, sent, outs = [], [], []

    def fetch(src, dst):
        copy = pltpu.make_async_copy(src, dst, loc.at[len(local)])
        copy.start()
        local.append(copy)
        return copy

    def send(src, dst, send_sem, recv_sem, target):
        copy = remote(src, dst, send_sem, recv_sem, target)
        copy.start()
        sent.append(copy)
        return copy

    def gone(copy):
        copy.wait_send()
        sent[:] = [other for other in sent if other is not copy]

    def arrive(ref, send_sem, recv_sem, target):
        remote(ref, ref, send_sem, recv_sem, target).wait_recv()

    def put(src, dst):
        copy = pltpu.make_async_copy(src, dst, out_sem.at[len(outs)])
        copy.start()
        outs.append(copy)

    stage, own_q = [], []
    for j in range(3):
        base, dst = 2 * j * half_q, pl.ds(j * half_q, half_q)
        stage.append(fetch(wq_hbm.at[:, pl.ds(base + (1 - s) * half_q, half_q)], stq.at[:, dst]))
        own_q.append(fetch(wq_hbm.at[:, pl.ds(base + s * half_q, half_q)], wq.at[s, z, y, c, :, dst]))
    get_tok = [fetch(tok_hbm.at[i], gd.at[pl.ds(2 * i, 2)]) for i in range(2)]
    own_o = fetch(wo_hbm, wo.at[z, y, c])
    stage_u = fetch(wu_hbm.at[:, pl.ds((1 - s) * half_u, half_u)], stu)
    own_u = fetch(wu_hbm.at[:, pl.ds(s * half_u, half_u)], wu.at[s, z, y, c])
    own_d = fetch(wd_hbm, wd.at[z, y, c])

    def down_half(i):
        return pl.ds(half_d * i, half_d)

    blocks = [
        lambda zz, yy, cc: wq.at[s, zz, yy, cc],
        lambda zz, yy, cc: wq.at[1 - s, zz, yy, cc],
        lambda zz, yy, cc: gv.at[zz, yy, cc],
        lambda zz, yy, cc: wo.at[zz, yy, cc],
        lambda zz, yy, cc: wu.at[s, zz, yy, cc],
        lambda zz, yy, cc: wu.at[1 - s, zz, yy, cc],
        lambda zz, yy, cc: wd.at[zz, yy, cc, down_half(0)],
        lambda zz, yy, cc: wd.at[zz, yy, cc, down_half(1)],
    ]
    lines = [
        lambda yy, cc: wq.at[s, :, yy, cc],
        lambda yy, cc: wq.at[1 - s, :, yy, cc],
        lambda yy, cc: gv.at[:, yy, cc],
        lambda yy, cc: wo.at[:, yy, cc],
        lambda yy, cc: wu.at[s, :, yy, cc],
        lambda yy, cc: wu.at[1 - s, :, yy, cc],
        lambda yy, cc: wd.at[:, yy, cc, down_half(0)],
        lambda yy, cc: wd.at[:, yy, cc, down_half(1)],
    ]
    Q_OWN, Q_SWAP, VEC, OUT, U_OWN, U_SWAP, D_0, D_1 = range(8)

    def spread(p):
        own = blocks[p](z, y, c)
        send(own, own, wz.at[p, 0], vz.at[p, 0], fdev)
        send(own, own, wz.at[p, 1], vz.at[p, 1], ndev)
        send(own, own, wy.at[p, 0], vy.at[p, 0], ydev)

    def after_far(p):
        ref = blocks[p](far, y, c)
        arrive(ref, wz.at[p, 0], vz.at[p, 0], fdev)
        send(ref, ref, wz.at[p, 2], vz.at[p, 2], ndev)
        send(ref, ref, wy.at[p, 1], vy.at[p, 1], ydev)

    def after_near(p):
        for i, zz in ((1, near), (2, LINE - 1 - near)):
            ref = blocks[p](zz, y, c)
            arrive(ref, wz.at[p, i], vz.at[p, i], ndev)
            send(ref, ref, wy.at[p, i + 1], vy.at[p, i + 1], ydev)
        line = lines[p](y, c)
        send(line, line, wc.at[p, 0], vc.at[p, 0], cdev)

    def after_y(p):
        for i, zz in enumerate((z, far, near, LINE - 1 - near)):
            arrive(blocks[p](zz, 1 - y, c), wy.at[p, i], vy.at[p, i], ydev)
        line = lines[p](1 - y, c)
        send(line, line, wc.at[p, 1], vc.at[p, 1], cdev)

    def after_c(p):
        for i, yy in enumerate((y, 1 - y)):
            arrive(lines[p](yy, 1 - c), wc.at[p, i], vc.at[p, i], cdev)

    parts = [
        lambda cc: gd.at[:, :, cc, down_half(0)],
        lambda cc: gd.at[:, :, cc, down_half(1)],
        lambda cc: gu.at[0, :, :, cc],
        lambda cc: gu.at[1, :, :, cc],
    ]
    parts += parts[:2]
    land_c = [rcd.at[0], rcd.at[1], rcu.at[0], rcu.at[1], rcd.at[0], rcd.at[1]]
    land_y = [ryd.at[0], ryd.at[1], ryu.at[0], ryu.at[1], ryd.at[0], ryd.at[1]]
    land_z = [rzd.at[0], rzd.at[1], rzu.at[0], rzu.at[1], rzd.at[0], rzd.at[1]]

    def c_start(k):
        return send(parts[k](1 - c), land_c[k], gc.at[k], hc.at[k], cdev)

    def c_end(k):
        ref, own = land_c[k], parts[k](c)
        arrive(ref, gc.at[k], hc.at[k], cdev)

        def add(i, carry):
            ref[i] = (ref[i].astype(f32) + own[i].astype(f32)).astype(bf16)
            return carry

        lax.fori_loop(0, LINE, add, 0)
        return send(ref.at[:, 1 - y], land_y[k], gy.at[k], hy.at[k], ydev)

    def y_end(k):
        ref, own = land_y[k], land_c[k]
        arrive(ref, gy.at[k], hy.at[k], ydev)

        def add(i, carry):
            ref[i] = (ref[i].astype(f32) + own[i, y].astype(f32)).astype(bf16)
            return carry

        lax.fori_loop(0, LINE, add, 0)
        return [
            send(ref.at[LINE - 1 - near], land_z[k].at[1], gz.at[k, 1], hz.at[k, 1], ndev),
            send(ref.at[near], land_z[k].at[0], gz.at[k, 0], hz.at[k, 0], ndev),
        ]

    def z_mid(k):
        ref = land_z[k].at[1]
        arrive(ref, gz.at[k, 1], hz.at[k, 1], ndev)
        ref[...] = (ref[...].astype(f32) + land_y[k][far].astype(f32)).astype(bf16)
        return send(ref, land_z[k].at[2], gz.at[k, 2], hz.at[k, 2], fdev)

    def z_end(k):
        arrive(land_z[k].at[0], gz.at[k, 0], hz.at[k, 0], ndev)
        arrive(land_z[k].at[2], gz.at[k, 2], hz.at[k, 2], fdev)
        return land_y[k][z].astype(f32) + land_z[k][0].astype(f32) + land_z[k][2].astype(f32)

    lane = lax.broadcasted_iota(jnp.int32, (part, model), 1)
    fits = (lax.rem(lane, part) == lax.broadcasted_iota(jnp.int32, (part, model), 0)) & (
        lane // part == s * 4 * LINE + z * 4 + y * 2 + c
    )
    stv[...] = dot_nn(small_ref[...], jnp.where(fits, 1.0, 0.0).astype(bf16)).astype(bf16)

    def chooser(i):
        count = len_ref[i] // 8
        rank = lax.broadcasted_iota(jnp.int32, (1, ranks), 1)
        row = jnp.where(rank < count, routed_ref[i : i + 1], -1).astype(f32)
        eye = lax.broadcasted_iota(jnp.int32, (ranks, ranks), 0) == lax.broadcasted_iota(
            jnp.int32, (ranks, ranks), 1
        )
        column = jnp.sum(jnp.where(eye, row, 0.0), axis=1, keepdims=True).astype(jnp.int32)
        count_here = tok_hbm.shape[1] * 512
        position = lax.broadcasted_iota(jnp.int32, (ranks, count_here), 1) + s * count_here
        return jnp.where(position == column, 1.0, 0.0).astype(bf16)

    def pick(i, dst):
        dst[i] = dot_nn(chooser(i), gd[2 * i : 2 * i + 2].reshape(tok_hbm.shape[1] * 512, model)).astype(bf16)

    def live_column(i):
        rank = lax.broadcasted_iota(jnp.int32, (ranks, 1), 0)
        return jnp.where(rank < len_ref[i] // 8, 1.0, 0.0).astype(f32)

    def allowed(i):
        query = lax.broadcasted_iota(jnp.int32, (ranks, ranks), 0)
        key = lax.broadcasted_iota(jnp.int32, (ranks, ranks), 1)
        return (key <= query) & (key < len_ref[i] // 8)

    greet([xdev, ydev, cdev, ndev, fdev])
    swap_v = send(stv, rcv, sx.at[0], rx.at[0], xdev)
    for copy in stage:
        copy.wait()
    send(stq, wq.at[s, z, y, c], sx.at[1], rx.at[1], xdev)
    for copy in own_q:
        copy.wait()
    spread(Q_OWN)
    x_swap = []
    get_tok[0].wait()
    pick(0, xs)
    x_swap.append(send(xs.at[0], xr.at[0], sx.at[3], rx.at[3], xdev))
    get_cot = [fetch(cot_hbm.at[0], gd.at[pl.ds(0, 2)])]
    stage_u.wait()
    send(stu, wu.at[s, z, y, c], sx.at[2], rx.at[2], xdev)
    get_tok[1].wait()
    pick(1, xs)
    x_swap.append(send(xs.at[1], xr.at[1], sx.at[4], rx.at[4], xdev))
    get_cot.append(fetch(cot_hbm.at[1], gd.at[pl.ds(2, 2)]))
    swap_v.wait_recv()
    gv[z, y, c] = stv[...] + rcv[...]
    spread(VEC)
    arrive(wq.at[1 - s, z, y, c], sx.at[1], rx.at[1], xdev)
    spread(Q_SWAP)
    own_o.wait()
    spread(OUT)
    own_u.wait()
    spread(U_OWN)
    own_d.wait()
    get_cot[0].wait()
    pick(0, ds)
    d_swap = [send(ds.at[0], dr.at[0], sx.at[7], rx.at[7], xdev)]
    after_far(Q_OWN)
    get_cot[1].wait()
    pick(1, ds)
    after_near(Q_OWN)
    after_far(VEC)
    after_far(Q_SWAP)
    after_near(VEC)
    after_near(Q_SWAP)
    arrive(wu.at[1 - s, z, y, c], sx.at[2], rx.at[2], xdev)
    spread(U_SWAP)
    spread(D_0)
    spread(D_1)
    after_far(OUT)
    after_y(Q_OWN)
    after_near(OUT)
    after_y(VEC)
    after_y(Q_SWAP)
    after_far(U_OWN)
    after_c(Q_OWN)
    after_c(VEC)
    after_c(Q_SWAP)

    gains[...] = jnp.sum(gv[...].astype(f32).reshape(4 * LINE, 16, model), axis=0)
    gain_one, gain_two, router = gains[0:1], gains[1:2], gains[2:3]

    def enter(i):
        x_swap[i].wait()
        row = xr[i].astype(f32) + xs[i].astype(f32)
        xr[i] = row.astype(bf16)
        xs[i] = (row * inverse_rms(row) * gain_one).astype(bf16)
        for j in range(3):
            cols = pl.ds(j * half_q, half_q)
            qkv[i, :, cols] = dot_nn(xs[i], wq[:, :, :, :, :, cols].reshape(model, half_q)).astype(bf16)

    def attend(i):
        ok = allowed(i)

        def pair(j, carry):
            q2 = qkv[i, :, pl.ds(j * 128, 128)].astype(f32)
            k2 = qkv[i, :, pl.ds(half_q + j * 128, 128)]
            v2 = qkv[i, :, pl.ds(2 * half_q + j * 128, 128)]
            mixed = jnp.zeros(q2.shape, f32)
            for parity in range(2):
                mask = head_mask(parity)
                score = dot_nt((q2 * mask).astype(bf16), k2) * (HEAD_DIM**-0.5)
                score = jnp.where(ok, score, -1000000000.0)
                weight = jnp.exp(score - jnp.max(score, axis=-1, keepdims=True))
                total = jnp.sum(weight, axis=-1, keepdims=True)
                mixed += dot_nn(weight.astype(bf16), v2) / total * mask
            att[i, :, pl.ds(j * 128, 128)] = mixed.astype(bf16)
            return carry

        lax.fori_loop(0, half_q // 128, pair, 0)

    def leave(i):
        for j in range(2):
            cols = pl.ds(j * half, half)
            a_s[i, :, cols] = dot_nn(att[i], wo[:, :, :, :, cols].reshape(half_q, half)).astype(bf16)
        return send(a_s.at[i], a_r.at[i], sx.at[5 + i], rx.at[5 + i], xdev)

    enter(0)
    after_y(OUT)
    after_near(U_OWN)
    attend(0)
    after_c(OUT)
    a_swap = [leave(0)]
    after_far(U_SWAP)
    enter(1)
    after_y(U_OWN)
    after_near(U_SWAP)
    attend(1)
    after_far(D_0)
    a_swap.append(leave(1))
    d_swap.append(send(ds.at[1], dr.at[1], sx.at[8], rx.at[8], xdev))
    after_y(U_SWAP)
    after_near(D_0)
    after_c(U_OWN)
    after_c(U_SWAP)

    def mlp_up(i):
        a_swap[i].wait()
        row = xr[i].astype(f32) + (a_s[i].astype(f32) + a_r[i].astype(f32))
        hid[i] = row
        a_s[i] = (row * inverse_rms(row) * gain_two).astype(bf16)

        def tile(t, carry):
            cols = pl.ds(t * 512, 512)
            up = dot_nn(a_s[i], wu[:, :, :, :, :, cols].reshape(model, 512))
            curve = jnp.tanh(GELU_C * (up + GELU_K * up * up * up))
            act[i, :, cols] = (0.5 * up * (1.0 + curve)).astype(bf16)
            slope = 0.5 * (1.0 + curve) + 0.5 * up * (1.0 - curve * curve) * (
                GELU_C * (1.0 + 3.0 * GELU_K * up * up)
            )
            gp[i, :, cols] = slope.astype(bf16)
            return carry

        lax.fori_loop(0, half_u // 512, tile, 0)

    def gate_of(i):
        return jax.nn.sigmoid(jnp.sum(xr[i].astype(f32) * router, axis=-1, keepdims=True))

    def cotangent_rows(i):
        d_swap[i].wait()
        row = dr[i].astype(f32) + ds[i].astype(f32)
        dr[i] = row.astype(bf16)
        ds[i] = (gate_of(i) * row).astype(bf16)

    def mlp_back(i):
        def tile(t, carry):
            cols = pl.ds(t * 512, 512)
            back = dot_nt(ds[i], wd[t].reshape(512, model))
            gp[i, :, cols] = (back * gp[i, :, cols].astype(f32)).astype(bf16)
            return carry

        lax.fori_loop(0, half_u // 512, tile, 0)
        for j in range(2):
            cols = pl.ds(j * half, half)
            d2s[i, :, cols] = dot_nt(gp[i], wu[j].reshape(half, half_u)).astype(bf16)
        return send(d2s.at[i], d2r.at[i], sx.at[9 + i], rx.at[9 + i], xdev)

    def mlp_out(i):
        for j in range(2):
            cols = pl.ds(j * half, half)
            m_s[i, :, cols] = dot_nn(act[i], wd[:, :, :, :, cols].reshape(half_u, half)).astype(bf16)
        return send(m_s.at[i], m_r.at[i], sx.at[11 + i], rx.at[11 + i], xdev)

    mlp_up(0)
    after_far(D_1)
    after_y(D_0)
    after_near(D_1)
    cotangent_rows(0)
    mlp_up(1)
    after_y(D_1)
    after_c(D_0)
    after_c(D_1)
    d2_swap = [mlp_back(0)]
    cotangent_rows(1)

    def down_tile(t, carry):
        grad = dot_tn(act[:, :, pl.ds(t * 512, 512)].reshape(rows, 512), ds[...].reshape(rows, model))
        gd[t] = grad.astype(bf16).reshape(gd.shape[1:])
        return carry

    lax.fori_loop(0, half_u // 512, down_tile, 0)
    c_down = [c_start(0), c_start(1)]
    d2_swap.append(mlp_back(1))
    y_down = [c_end(0)]

    def up_tile(t, carry):
        cols = pl.ds(t * 512, 512)
        grad = dot_tn(a_s[...].reshape(rows, model), gp[:, :, cols].reshape(rows, 512))
        gu[:, :, :, :, :, cols] = grad.astype(bf16).reshape(gu.shape[:5] + (512,))
        return carry

    lax.fori_loop(0, half_u // 512, up_tile, 0)
    c_start(2)
    c_start(3)
    y_down.append(c_end(1))
    m_swap = [mlp_out(0), mlp_out(1)]
    c_end(2)
    c_end(3)

    def hidden_back(i):
        d2_swap[i].wait()
        back = d2s[i].astype(f32) + d2r[i].astype(f32)
        row = hid[i]
        r2 = inverse_rms(row)
        scaled = back * gain_two
        step = r2 * scaled - row * (r2 * r2 * r2 * jnp.mean(scaled * row, axis=-1, keepdims=True))
        dh[i] = step
        gp[i, :, 0:model] = (gate_of(i) * dr[i].astype(f32) + step).astype(bf16)
        gp[i, :, model : model + half_q] = dot_nt(gp[i, :, 0:model], wo[...].reshape(half_q, model)).astype(bf16)
        return jnp.sum(d2s[i].astype(f32) * row * r2, axis=0, keepdims=True)

    def attend_back(i):
        ok = allowed(i)
        scale = HEAD_DIM**-0.5

        def pair(j, carry):
            q2 = qkv[i, :, pl.ds(j * 128, 128)]
            k2 = qkv[i, :, pl.ds(half_q + j * 128, 128)]
            v2 = qkv[i, :, pl.ds(2 * half_q + j * 128, 128)]
            g2 = gp[i, :, pl.ds(model + j * 128, 128)].astype(f32)
            q2f = q2.astype(f32)
            dq2 = jnp.zeros(q2.shape, f32)
            dk2 = jnp.zeros(q2.shape, f32)
            dv2 = jnp.zeros(q2.shape, f32)
            for parity in range(2):
                mask = head_mask(parity)
                score = dot_nt((q2f * mask).astype(bf16), k2) * scale
                score = jnp.where(ok, score, -1000000000.0)
                weight = jnp.exp(score - jnp.max(score, axis=-1, keepdims=True))
                over = 1.0 / jnp.sum(weight, axis=-1, keepdims=True)
                gh = g2 * mask
                dp = dot_nt(gh.astype(bf16), v2)
                prob = weight * over
                delta = jnp.sum(prob * dp, axis=-1, keepdims=True)
                dscore = (prob * (dp - delta)).astype(bf16)
                dq2 += dot_nn(dscore, k2) * mask
                dk2 += dot_tn(dscore, q2) * mask
                dv2 += dot_tn(weight.astype(bf16), (gh * over).astype(bf16))
            act[i, :, pl.ds(j * 128, 128)] = (dq2 * scale).astype(bf16)
            act[i, :, pl.ds(half_q + j * 128, 128)] = (dk2 * scale).astype(bf16)
            act[i, :, pl.ds(2 * half_q + j * 128, 128)] = dv2.astype(bf16)
            return carry

        lax.fori_loop(0, half_q // 128, pair, 0)

    def inner_back(i):
        r1 = inverse_rms(xr[i].astype(f32))
        sums = []
        for j in range(2):
            cols = pl.ds(j * half, half)
            step = dot_nt(act[i, :, 0 : 3 * half_q], wq[j].reshape(half, 3 * half_q))
            d2s[i, :, cols] = step.astype(bf16)
            sums.append(jnp.sum(step * xr[i, :, cols].astype(f32) * r1, axis=0, keepdims=True))
        return send(d2s.at[i], d1r.at[i], sx.at[13 + i], rx.at[13 + i], xdev), sums

    z_down = []
    grad_gm = hidden_back(0)
    attend_back(0)
    z_down += y_end(0)
    swap_0, sums_0 = inner_back(0)
    grad_gm += hidden_back(1)
    z_down += y_end(1)
    z_down.append(z_mid(0))
    attend_back(1)
    z_down.append(z_mid(1))
    fd[0:half_d] = z_end(0)
    y_end(2)
    fd[half_d:] = z_end(1)
    put(fd, fd_out)
    for copy in c_down + y_down + z_down:
        gone(copy)
    for target in (ydev, cdev, ndev, fdev):
        pl.semaphore_signal(free, inc=1, device_id=target, device_id_type=MESH)

    def out_tile(t):
        cols = pl.ds(t * half, half)
        grad = dot_tn(att[...].reshape(rows, half_q), gp[:, :, cols].reshape(rows, half))
        gd[:, :, :, 3 * part :, cols] = grad.astype(bf16).reshape(wo.shape[:4] + (half,))

    def qkv_tile(t):
        grad = dot_tn(xs[...].reshape(rows, model), act[:, :, t * half_q : (t + 1) * half_q].reshape(rows, half_q))
        grad = grad.astype(bf16).reshape(wq.shape[:5] + (half_q,))
        if t < 2:
            gd[:, :, :, 0:part, t * half_q : (t + 1) * half_q] = grad[0]
            gd[:, :, :, part : 2 * part, t * half_q : (t + 1) * half_q] = grad[1]
        else:
            gd[:, :, :, 2 * part : 3 * part, 0:half_q] = grad[0]
            gd[:, :, :, 2 * part : 3 * part, half_q:] = grad[1]

    qkv_tile(0)
    qkv_tile(1)
    pl.semaphore_wait(free, 4)
    c_start(4)
    out_tile(0)
    out_tile(1)
    qkv_tile(2)
    c_start(5)
    c_end(4)
    swap_1, sums_1 = inner_back(1)
    d1_swap = [swap_0, swap_1]
    for j in range(2):
        vs[0:1, j * half : (j + 1) * half] = sums_0[j] + sums_1[j]
    vs[1:2] = grad_gm
    c_end(5)
    z_mid(2)
    y_end(3)

    grad_router = jnp.zeros((1, model), f32)
    for i in range(2):
        m_swap[i].wait()
        row = xr[i].astype(f32)
        gate = gate_of(i)
        branch = (hid[i] - row) + (m_s[i].astype(f32) + m_r[i].astype(f32))
        m_s[i] = (gate * branch * live_column(i)).astype(bf16)
        slope = jnp.sum(dr[i].astype(f32) * branch, axis=-1, keepdims=True) * gate * (1.0 - gate)
        logit[i] = slope
        grad_router += jnp.sum(row * slope, axis=0, keepdims=True)
    put(m_s, upd_out)
    vs[2:3] = 0.5 * grad_router
    vs[3:8] = jnp.zeros((5, model), f32)
    send(vs, vr.at[0], gc.at[6], hc.at[6], cdev)
    fu[0] = z_end(2)
    z_mid(3)
    arrive(vr.at[0], gc.at[6], hc.at[6], cdev)
    v_all[0] = vs[...] + vr[0]
    send(v_all.at[0], vr.at[1], gy.at[6], hy.at[6], ydev)
    y_end(4)
    fu[1] = z_end(3)
    suu[...] = fu[1 - s].astype(bf16)
    send(suu, ruu, sx.at[15], rx.at[15], xdev)
    put(fu.at[s], fu_out.at[:, pl.ds(s * half_u, half_u)])
    arrive(vr.at[1], gy.at[6], hy.at[6], ydev)
    v_all[1] = v_all[0] + vr[1]
    send(v_all.at[1], vr.at[2], gz.at[6, 0], hz.at[6, 0], ndev)
    z_mid(4)

    for i in range(2):
        d1_swap[i].wait()
        row = xr[i].astype(f32)
        r1 = inverse_rms(row)
        scaled = (d2s[i].astype(f32) + d1r[i].astype(f32)) * gain_one
        step = r1 * scaled - row * (r1 * r1 * r1 * jnp.mean(scaled * row, axis=-1, keepdims=True))
        d2s[i] = (dh[i] + step + logit[i] * router).astype(bf16)
    put(d2s, dx_out)

    y_end(5)
    arrive(vr.at[2], gz.at[6, 0], hz.at[6, 0], ndev)
    v_all[2] = v_all[1] + vr[2]
    send(v_all.at[2], vr.at[3], gz.at[6, 1], hz.at[6, 1], fdev)
    fqk[...] = z_end(4).reshape(fqk.shape)
    sqk[...] = fqk[1 - s].astype(bf16)
    send(sqk, rqk, sx.at[16], rx.at[16], xdev)
    z_mid(5)
    arrive(ruu, sx.at[15], rx.at[15], xdev)
    fu[1 - s] = ruu[...].astype(f32)
    put(fu.at[1 - s], fu_out.at[:, pl.ds((1 - s) * half_u, half_u)])
    for j in range(2):
        put(fqk.at[s, :, pl.ds(j * half_q, half_q)], fq_out.at[:, pl.ds(2 * j * half_q + s * half_q, half_q)])
    arrive(vr.at[3], gz.at[6, 1], hz.at[6, 1], fdev)
    v_all[3] = v_all[2] + vr[3]
    send(v_all.at[3], vr.at[4], sx.at[18], rx.at[18], xdev)
    last = z_end(5)
    fv[...] = last[0:part]
    sv[...] = fv[:, pl.ds((1 - s) * half_q, half_q)].astype(bf16)
    send(sv, rv, sx.at[17], rx.at[17], xdev)
    fo[...] = last[part:]
    put(fo, fo_out)
    put(fv.at[:, pl.ds(s * half_q, half_q)], fq_out.at[:, pl.ds(4 * half_q + s * half_q, half_q)])
    arrive(rqk, sx.at[16], rx.at[16], xdev)
    fqk[1 - s] = rqk[...].astype(f32)
    for j in range(2):
        put(
            fqk.at[1 - s, :, pl.ds(j * half_q, half_q)],
            fq_out.at[:, pl.ds(2 * j * half_q + (1 - s) * half_q, half_q)],
        )
    arrive(vr.at[4], sx.at[18], rx.at[18], xdev)
    v_all[4] = v_all[3] + vr[4]
    put(v_all.at[4], vec_out)
    arrive(rv, sx.at[17], rx.at[17], xdev)
    fv[:, pl.ds((1 - s) * half_q, half_q)] = rv[...].astype(f32)
    put(
        fv.at[:, pl.ds((1 - s) * half_q, half_q)],
        fq_out.at[:, pl.ds(4 * half_q + (1 - s) * half_q, half_q)],
    )
    waited = x_swap + a_swap + d_swap + d2_swap + m_swap + d1_swap
    for copy in list(sent):
        if not any(copy is other for other in waited):
            copy.wait_send()
    for copy in outs:
        copy.wait()


def rows_kernel(
    len_ref, routed_ref, tok_ref, cot_ref, upd_ref, dx_ref, fq_ref, fo_ref, fu_ref, fd_ref, vec_ref,
    out_ref, grad_ref, fq_out, fo_out, fu_out, fd_out, one_out, two_out, three_out,
):
    slot, step = pl.program_id(0), pl.program_id(1)
    s = lax.axis_index("seq")
    tall, model = tok_ref.shape[1:]
    ranks = upd_ref.shape[1]
    rank = lax.broadcasted_iota(jnp.int32, (1, ranks), 1)
    routed = jnp.where(rank < len_ref[slot] // 8, routed_ref[pl.ds(slot, 1)], -1)
    first = (s * pl.num_programs(1) + step) * tall
    position = lax.broadcasted_iota(jnp.int32, (tall, ranks), 0) + first
    chooser = jnp.where(position == routed, 1.0, 0.0).astype(bf16)
    out_ref[0] = (tok_ref[0].astype(f32) + dot_nn(chooser, upd_ref[0])).astype(bf16)
    grad_ref[0] = (cot_ref[0].astype(f32) + dot_nn(chooser, dx_ref[0])).astype(bf16)

    @pl.when((slot == 0) & (step == 0))
    def _():
        fq_out[...] = fq_ref[...]
        fo_out[...] = fo_ref[...]
        fu_out[...] = fu_ref[...]
        fd_out[...] = fd_ref[...]
        part = one_out.shape[1]
        flat = s * lax.axis_size("batch") + lax.axis_index("batch")
        lane = lax.broadcasted_iota(jnp.int32, (part, model), 1)
        here = (lane // part == flat) & (
            lax.rem(lane, part) == lax.broadcasted_iota(jnp.int32, (part, model), 0)
        )
        eye = lax.broadcasted_iota(jnp.int32, (part, part), 0) == lax.broadcasted_iota(
            jnp.int32, (part, part), 1
        )
        for j, ref in enumerate((one_out, two_out, three_out)):
            column = jnp.sum(jnp.where(here, vec_ref[j : j + 1], 0.0), axis=1, keepdims=True)
            ref[...] = jnp.sum(jnp.where(eye, column, 0.0), axis=0, keepdims=True)


def split_device(
    tokens, cotangent, lengths, routed, w_qkv, w_out, w_up, w_down, gain_attn, gain_mlp, router
):
    slots, local_len, model = tokens.shape
    ranks = routed.shape[1]
    half_q, half_u = w_qkv.shape[1] // 6, w_up.shape[1] // 2
    part, down = w_qkv.shape[0], w_down.shape[0]
    small = jnp.concatenate(
        [gain_attn[None], gain_mlp[None], router[None], jnp.zeros((13, part), bf16)], axis=0
    )
    hbm = pl.BlockSpec(memory_space=pl.ANY)
    vmem = pl.BlockSpec(memory_space=pltpu.VMEM)
    smem = pl.BlockSpec(memory_space=pltpu.SMEM)
    sds, space, dma = jax.ShapeDtypeStruct, pltpu.VMEM, pltpu.SemaphoreType.DMA
    rows = (slots, ranks, model)
    grid = (LINE, 2, 2)
    wq_shape, wo_shape = (2,) + grid + (part, 3 * half_q), grid + (part, model)
    wu_shape, wd_shape = (2,) + grid + (part, half_u), grid + (down, model)
    blocked = (slots, local_len // 512, 2, 2, 128, model)
    row_bf16 = space(rows, bf16)

    def land(tall, wide):
        return [
            space((2, LINE, 2, tall, wide), bf16),
            space((2, LINE, tall, wide), bf16),
            space((2, 3, tall, wide), bf16),
        ]

    on_d, on_u = land(down // 2, model), land(part, half_u)
    grad_shapes = (
        sds((part, 6 * half_q), f32), sds((part, model), f32), sds((part, 2 * half_u), f32), sds((down, model), f32),
    )
    upd, dxr, *sums, vec = pl.pallas_call(
        block_kernel,
        out_shape=(sds(rows, bf16), sds(rows, bf16)) + grad_shapes + (sds((8, model), f32),),
        in_specs=[hbm] * 6 + [vmem] * 2 + [smem],
        out_specs=[hbm] * 7,
        scratch_shapes=[
            space(wq_shape, bf16), space(wo_shape, bf16), space(wu_shape, bf16), space(wd_shape, bf16),
            space(grid + (16, model), bf16),
            space((part, 3 * half_q), bf16), space((part, half_u), bf16), space((16, model), bf16), space((16, model), bf16),
            *[row_bf16] * 11, space(rows, f32), space(rows, f32),
            space((slots, ranks, 3 * half_q), bf16), space((slots, ranks, half_q), bf16),
            space((slots, ranks, half_u), bf16), space((slots, ranks, half_u), bf16),
            space((slots, ranks, 1), f32), space((16, model), f32),
            space(wd_shape, bf16), space(wu_shape, bf16),
            on_d[0], on_u[0], on_d[1], on_u[1], on_d[2], on_u[2],
            space((2, part, model), f32), space((part, model), f32), space((part, model), f32),
            space((2, part, half_u), f32), space((down, model), f32),
            space((part, model), bf16), space((part, half_q), bf16), space((part, half_u), bf16),
            space((part, model), bf16), space((part, half_q), bf16), space((part, half_u), bf16),
            space((8, model), f32), space((5, 8, model), f32), space((5, 8, model), f32),
            dma((16,)), dma((16,)), dma((8, 3)), dma((8, 3)), dma((8, 4)), dma((8, 4)), dma((8, 2)), dma((8, 2)),
            dma((19,)), dma((19,)), dma((7,)), dma((7,)), dma((7,)), dma((7,)), dma((7, 3)), dma((7, 3)),
            pltpu.SemaphoreType.REGULAR,
        ],
        compiler_params=pltpu.CompilerParams(collective_id=1, has_side_effects=True, vmem_limit_bytes=60 << 20),
        name="block",
    )(tokens.reshape(blocked), cotangent.reshape(blocked), w_qkv, w_out, w_up, w_down, small, routed, lengths)

    tall = 512
    big = pl.BlockSpec((1, tall, model), lambda i, j: (i, j, 0))
    moved = pl.BlockSpec((1, ranks, model), lambda i, j: (i, 0, 0))

    def whole(shape):
        return pl.BlockSpec(shape, lambda i, j: (0, 0))

    whole_grads = [whole(g.shape) for g in grad_shapes]
    vectors = (sds((1, part), f32),) * 3
    output, input_grad, g_qkv, g_out, g_up, g_down, g_one, g_two, g_three = pl.pallas_call(
        rows_kernel,
        grid=(slots, local_len // tall),
        out_shape=(sds(tokens.shape, bf16), sds(tokens.shape, bf16)) + grad_shapes + vectors,
        in_specs=[smem, whole(routed.shape), big, big, moved, moved] + whole_grads + [whole((8, model))],
        out_specs=[big, big] + whole_grads + [whole((1, part))] * 3,
        compiler_params=pltpu.CompilerParams(vmem_limit_bytes=40 << 20),
        name="rows",
    )(lengths, routed, tokens, cotangent, upd, dxr, *sums, vec)
    return (
        output, input_grad, g_qkv, g_out, g_up, g_down,
        g_one.reshape(part), g_two.reshape(part), g_three.reshape(part),
    )


def solution(mesh):
    in_specs = (
        P("batch", "seq", None),
        P("batch", "seq", None),
        P("batch"),
        P("batch", None),
        P(("seq", "batch"), None),
        P(("seq", "batch"), None),
        P(("seq", "batch"), None),
        P(("seq", "batch"), None),
        P(("seq", "batch")),
        P(("seq", "batch")),
        P(("seq", "batch")),
    )
    out_specs = (
        P("batch", "seq", None),
        P("batch", "seq", None),
        P(("seq", "batch"), None),
        P(("seq", "batch"), None),
        P(("seq", "batch"), None),
        P(("seq", "batch"), None),
        P(("seq", "batch")),
        P(("seq", "batch")),
        P(("seq", "batch")),
    )
    small_slice = mesh.shape["seq"] == 2 and mesh.shape["batch"] == 4 * LINE
    body = split_device if small_slice else general_device
    return jax.shard_map(body, mesh=mesh, in_specs=in_specs, out_specs=out_specs, check_vma=False)
```

```python
import functools

import jax
import jax.numpy as jnp
from jax import lax
from jax.experimental import pallas as pl
from jax.experimental.pallas import tpu as pltpu
from jax.sharding import PartitionSpec as P

HEAD_DIM = 64
MESH = pl.DeviceIdType.MESH


epsilon = 1e-05
highest = lax.Precision.HIGHEST
f32 = jnp.float32
bf16 = jnp.bfloat16

LINE = 4
GELU_C = 0.7978845608
GELU_K = 0.044715


def dot_nn(a, b):
    return lax.dot_general(a, b, (((1,), (0,)), ((), ())), preferred_element_type=f32)


def dot_nt(a, b):
    return lax.dot_general(a, b, (((1,), (1,)), ((), ())), preferred_element_type=f32)


def dot_tn(a, b):
    return lax.dot_general(a, b, (((0,), (0,)), ((), ())), preferred_element_type=f32)


def place():
    s = lax.axis_index("seq")
    b = lax.axis_index("batch")
    return s, b // 4, lax.rem(b // 2, 2), lax.rem(b, 2)


def device(s, z, y, c):
    return (s, z * 4 + y * 2 + c)


def remote(src, dst, send, recv, target):
    return pltpu.make_async_remote_copy(
        src_ref=src, dst_ref=dst, send_sem=send, recv_sem=recv, device_id=target, device_id_type=MESH
    )


def greet(targets):
    barrier = pltpu.get_barrier_semaphore()
    for target in targets:
        pl.semaphore_signal(barrier, inc=1, device_id=target, device_id_type=MESH)
    pl.semaphore_wait(barrier, len(targets))


def inverse_rms(values):
    return lax.rsqrt(jnp.mean(values * values, axis=-1, keepdims=True) + epsilon)


def head_mask(parity):
    lane = lax.broadcasted_iota(jnp.int32, (1, 128), 1)
    return jnp.where(lane // HEAD_DIM == parity, 1.0, 0.0).astype(f32)


def norm_apply(values_in, gain_vec):
    return (
        values_in
        * lax.rsqrt(jnp.mean(values_in * values_in, axis=-1, keepdims=True) + epsilon)
        * gain_vec
    )


def gelu_tanh(values_in):
    return jax.nn.gelu(values_in, approximate=True)


def general_device(
    tokens, cotangent, lengths, routed, w_qkv, w_out, w_up, w_down, gain_attn, gain_mlp, router
):
    slot_count, local_len, model_width = tokens.shape
    capacity = routed.shape[1]
    seq_devices = lax.axis_size("seq")
    own_count = capacity // seq_devices
    head_count = model_width // HEAD_DIM
    row_count = own_count * slot_count
    score_scale = HEAD_DIM ** (-0.5)
    gathered = (
        lax.all_gather(w_qkv, ("seq", "batch"), axis=0, tiled=True),
        lax.all_gather(w_out, ("seq", "batch"), axis=0, tiled=True),
        lax.all_gather(w_up, ("seq", "batch"), axis=0, tiled=True),
        lax.all_gather(w_down, ("seq", "batch"), axis=0, tiled=True),
        lax.all_gather(gain_attn, ("seq", "batch"), axis=0, tiled=True),
        lax.all_gather(gain_mlp, ("seq", "batch"), axis=0, tiled=True),
        lax.all_gather(router, ("seq", "batch"), axis=0, tiled=True),
    )
    full_qkv, full_out, full_up, full_down, full_ga, full_gm, full_router = gathered
    gain_one = full_ga.astype(f32)
    gain_two = full_gm.astype(f32)
    router_vec = full_router.astype(f32)
    counts = lengths // 8
    seq_place = lax.axis_index("seq")
    positions = seq_place * local_len + jnp.arange(local_len, dtype=jnp.int32)
    rank_all = jnp.arange(capacity, dtype=jnp.int32)
    live_all = rank_all[None, :] < counts[:, None]
    chooser = ((routed[:, :, None] == positions[None, None, :]) & live_all[:, :, None]).astype(bf16)
    pick_in = jnp.einsum("scp,spd->csd", chooser, tokens, preferred_element_type=f32)
    pick_cot = jnp.einsum("scp,spd->csd", chooser, cotangent, preferred_element_type=f32)
    picked, picked_cot = (
        lax.psum_scatter(
            pick_in.astype(jnp.bfloat16), "seq", scatter_dimension=0, tiled=True
        ).astype(jnp.float32),
        lax.psum_scatter(
            pick_cot.astype(jnp.bfloat16), "seq", scatter_dimension=0, tiled=True
        ).astype(jnp.float32),
    )
    own_rank = seq_place * own_count + jnp.arange(own_count, dtype=jnp.int32)
    live_own = own_rank[:, None] < counts[None, :]
    live_mask = live_own.reshape(row_count, 1).astype(f32)
    routed_in = picked.reshape(row_count, model_width)
    normed_one = norm_apply(routed_in, gain_one).astype(bf16)
    joined = jnp.dot(normed_one, full_qkv, preferred_element_type=f32).astype(bf16)
    query_rows = joined[:, :model_width].reshape(own_count, slot_count, head_count, HEAD_DIM)
    key_own = joined[:, model_width : 2 * model_width].reshape(own_count, slot_count, model_width)
    value_own = joined[:, 2 * model_width :].reshape(own_count, slot_count, model_width)
    key_every, value_every = (
        lax.all_gather(key_own, "seq", axis=0, tiled=True),
        lax.all_gather(value_own, "seq", axis=0, tiled=True),
    )
    key_rows = key_every.reshape(capacity, slot_count, head_count, HEAD_DIM)
    value_rows = value_every.reshape(capacity, slot_count, head_count, HEAD_DIM)
    scores = (
        jnp.einsum("qsha,ksha->shqk", query_rows, key_rows, preferred_element_type=f32)
        * score_scale
    )
    causal = rank_all[None, :] <= own_rank[:, None]
    allowed = causal[None, :, :] & (rank_all[None, None, :] < counts[:, None, None])
    scores = jnp.where(allowed[:, None], scores, -1000000000.0)
    row_max = jnp.max(scores, axis=-1, keepdims=True)
    weights_f = jnp.exp(scores - row_max)
    row_total = jnp.sum(weights_f, axis=-1, keepdims=True)
    weights_low = weights_f.astype(bf16)
    mixture = jnp.einsum("shqk,ksha->qsha", weights_low, value_rows, preferred_element_type=f32)
    mixture = mixture / jnp.transpose(row_total, (2, 0, 1, 3))
    attended = mixture.reshape(row_count, model_width).astype(bf16)
    branch_a = jnp.dot(attended, full_out, preferred_element_type=f32)
    hidden = routed_in + branch_a
    normed_two = norm_apply(hidden, gain_two).astype(bf16)
    up_proj = jnp.dot(normed_two, full_up, preferred_element_type=f32)
    activated = gelu_tanh(up_proj).astype(bf16)
    branch_m = jnp.dot(activated, full_down, preferred_element_type=f32)
    gate_prob = jax.nn.sigmoid(jnp.dot(routed_in, router_vec, precision=highest))
    branch = branch_a + branch_m
    update = (
        (gate_prob[:, None] * branch * live_mask)
        .astype(bf16)
        .reshape(own_count, slot_count, model_width)
    )
    update_every = lax.all_gather(update, "seq", axis=0, tiled=True)
    output = (
        tokens.astype(f32)
        + jnp.einsum("scp,csd->spd", chooser, update_every, preferred_element_type=f32)
    ).astype(bf16)
    cot_rows = picked_cot.reshape(row_count, model_width)
    grad_gate = jnp.sum(cot_rows * branch, axis=-1)
    grad_logit = grad_gate * gate_prob * (1.0 - gate_prob)
    grad_branch = gate_prob[:, None] * cot_rows
    grad_m = grad_branch.astype(bf16)
    grad_act = jnp.einsum("rd,fd->rf", grad_m, full_down, preferred_element_type=f32)
    unused_up, gelu_pull = jax.vjp(gelu_tanh, up_proj)
    grad_u = gelu_pull(grad_act)[0].astype(bf16)
    grad_n2 = jnp.einsum("rf,df->rd", grad_u, full_up, preferred_element_type=f32)
    unused_two, norm_pull_two = jax.vjp(norm_apply, hidden, gain_two)
    grad_hidden, grad_gm = norm_pull_two(grad_n2)
    grad_a = (grad_branch + grad_hidden).astype(bf16)
    grad_att = jnp.einsum("rd,ed->re", grad_a, full_out, preferred_element_type=f32).astype(bf16)
    grad_att4 = grad_att.reshape(own_count, slot_count, head_count, HEAD_DIM)
    delta_rows = jnp.sum(grad_att4.astype(f32) * mixture, axis=-1)
    delta = jnp.transpose(delta_rows, (1, 2, 0))[..., None]
    grad_p = jnp.einsum("qsha,ksha->shqk", grad_att4, value_rows, preferred_element_type=f32)
    probs = weights_f / row_total
    grad_s = (probs * (grad_p - delta)).astype(bf16)
    grad_q = (
        jnp.einsum("shqk,ksha->qsha", grad_s, key_rows, preferred_element_type=f32) * score_scale
    )
    grad_k = (
        jnp.einsum("shqk,qsha->ksha", grad_s, query_rows, preferred_element_type=f32) * score_scale
    )
    scaled_low = weights_low.astype(f32) / row_total
    grad_v = jnp.einsum("shqk,qsha->ksha", scaled_low, grad_att4.astype(f32), precision=highest)
    grad_k_own, grad_v_own = (
        lax.psum_scatter(
            grad_k.reshape(capacity, slot_count, model_width).astype(jnp.bfloat16),
            "seq",
            scatter_dimension=0,
            tiled=True,
        ).astype(jnp.float32),
        lax.psum_scatter(
            grad_v.reshape(capacity, slot_count, model_width).astype(jnp.bfloat16),
            "seq",
            scatter_dimension=0,
            tiled=True,
        ).astype(jnp.float32),
    )
    grad_joined = jnp.concatenate(
        [
            grad_q.reshape(row_count, model_width),
            grad_k_own.reshape(row_count, model_width),
            grad_v_own.reshape(row_count, model_width),
        ],
        axis=-1,
    ).astype(bf16)
    grad_n1 = jnp.einsum("re,de->rd", grad_joined, full_qkv, preferred_element_type=f32)
    unused_one, norm_pull_one = jax.vjp(norm_apply, routed_in, gain_one)
    grad_x1, grad_ga = norm_pull_one(grad_n1)
    grad_router = jnp.sum(routed_in * grad_logit[:, None], axis=0)
    grad_rows = (grad_hidden + grad_x1 + grad_logit[:, None] * router_vec[None, :]).astype(bf16)
    grad_rows = grad_rows.reshape(own_count, slot_count, model_width)
    grad_every = lax.all_gather(grad_rows, "seq", axis=0, tiled=True)
    input_grad = (
        cotangent.astype(f32)
        + jnp.einsum("scp,csd->spd", chooser, grad_every, preferred_element_type=f32)
    ).astype(bf16)
    part_qkv = jnp.einsum("rd,re->de", normed_one, grad_joined, preferred_element_type=f32)
    part_out = jnp.einsum("re,rd->ed", attended, grad_a, preferred_element_type=f32)
    part_up = jnp.einsum("rd,rf->df", normed_two, grad_u, preferred_element_type=f32)
    part_down = jnp.einsum("rf,rd->fd", activated, grad_m, preferred_element_type=f32)

    def sum_rows(part):
        return lax.psum_scatter(
            part.astype(bf16), ("seq", "batch"), scatter_dimension=0, tiled=True
        ).astype(f32)

    down_sum = sum_rows(part_down)
    grad_up = sum_rows(part_up)
    grad_out = sum_rows(part_out)
    grad_qkv = sum_rows(part_qkv)
    small_ga, small_gm, small_router = (
        lax.psum_scatter(grad_ga, ("seq", "batch"), scatter_dimension=0, tiled=True),
        lax.psum_scatter(grad_gm, ("seq", "batch"), scatter_dimension=0, tiled=True),
        lax.psum_scatter(grad_router, ("seq", "batch"), scatter_dimension=0, tiled=True),
    )
    return (
        output,
        input_grad,
        grad_qkv,
        grad_out,
        grad_up,
        down_sum,
        small_ga,
        small_gm,
        small_router,
    )


def block_kernel(
    tok_hbm, cot_hbm, wq_hbm, wo_hbm, wu_hbm, wd_hbm, small_ref, routed_ref, len_ref,
    upd_out, dx_out, fq_out, fo_out, fu_out, fd_out, vec_out,
    wq, wo, wu, wd, gv, stq, stu, stv, rcv,
    xs, xr, ds, dr, a_s, a_r, d2s, d2r, d1r, m_s, m_r, hid, dh, qkv, att, act, gp, logit, gains,
    gd, gu, rcd, rcu, ryd, ryu, rzd, rzu, rzb, ryb,
    fqk, fv, fo, fu, fd, sqk, sv, suu, rqk, rv, ruu, vs, vr, v_all,
    loc, out_sem, wz, vz, wy, vy, wc, vc, sx, rx, gc, hc, gy, hy, gz, hz, free,
):
    s, z, y, c = place()
    near, far = z + 1 - 2 * lax.rem(z, 2), LINE - 1 - z
    xdev, ydev, cdev = device(1 - s, z, y, c), device(s, z, 1 - y, c), device(s, z, y, 1 - c)
    ndev, fdev = device(s, near, y, c), device(s, far, y, c)
    model, half_q, half_u = xr.shape[2], att.shape[2], act.shape[2]
    ranks, half = xr.shape[1], xr.shape[2] // 2
    rows = xr.shape[0] * ranks
    part, half_d = stq.shape[0], wd.shape[3] // 2
    local, sent, outs = [], [], []

    def fetch(src, dst):
        copy = pltpu.make_async_copy(src, dst, loc.at[len(local)])
        copy.start()
        local.append(copy)
        return copy

    def send(src, dst, send_sem, recv_sem, target):
        copy = remote(src, dst, send_sem, recv_sem, target)
        copy.start()
        sent.append(copy)
        return copy

    def gone(copy):
        copy.wait_send()
        sent[:] = [other for other in sent if other is not copy]

    def arrive(ref, send_sem, recv_sem, target):
        remote(ref, ref, send_sem, recv_sem, target).wait_recv()

    def put(src, dst):
        copy = pltpu.make_async_copy(src, dst, out_sem.at[len(outs)])
        copy.start()
        outs.append(copy)

    stage, own_q = [], []
    for j in range(3):
        base, dst = 2 * j * half_q, pl.ds(j * half_q, half_q)
        stage.append(fetch(wq_hbm.at[:, pl.ds(base + (1 - s) * half_q, half_q)], stq.at[:, dst]))
        own_q.append(fetch(wq_hbm.at[:, pl.ds(base + s * half_q, half_q)], wq.at[s, z, y, c, :, dst]))
    get_tok = [fetch(tok_hbm.at[i], gd.at[pl.ds(2 * i, 2)]) for i in range(2)]
    own_o = fetch(wo_hbm, wo.at[z, y, c])
    stage_u = fetch(wu_hbm.at[:, pl.ds((1 - s) * half_u, half_u)], stu)
    own_u = fetch(wu_hbm.at[:, pl.ds(s * half_u, half_u)], wu.at[s, z, y, c])
    own_d = fetch(wd_hbm, wd.at[z, y, c])

    def down_half(i):
        return pl.ds(half_d * i, half_d)

    blocks = [
        lambda zz, yy, cc: wq.at[s, zz, yy, cc],
        lambda zz, yy, cc: wq.at[1 - s, zz, yy, cc],
        lambda zz, yy, cc: gv.at[zz, yy, cc],
        lambda zz, yy, cc: wo.at[zz, yy, cc],
        lambda zz, yy, cc: wu.at[s, zz, yy, cc],
        lambda zz, yy, cc: wu.at[1 - s, zz, yy, cc],
        lambda zz, yy, cc: wd.at[zz, yy, cc, down_half(0)],
        lambda zz, yy, cc: wd.at[zz, yy, cc, down_half(1)],
    ]
    lines = [
        lambda yy, cc: wq.at[s, :, yy, cc],
        lambda yy, cc: wq.at[1 - s, :, yy, cc],
        lambda yy, cc: gv.at[:, yy, cc],
        lambda yy, cc: wo.at[:, yy, cc],
        lambda yy, cc: wu.at[s, :, yy, cc],
        lambda yy, cc: wu.at[1 - s, :, yy, cc],
        lambda yy, cc: wd.at[:, yy, cc, down_half(0)],
        lambda yy, cc: wd.at[:, yy, cc, down_half(1)],
    ]
    Q_OWN, Q_SWAP, VEC, OUT, U_OWN, U_SWAP, D_0, D_1 = range(8)

    def spread(p):
        own = blocks[p](z, y, c)
        send(own, own, wz.at[p, 0], vz.at[p, 0], fdev)
        send(own, own, wz.at[p, 1], vz.at[p, 1], ndev)

    def spread_y(p):
        own = blocks[p](z, y, c)
        send(own, own, wy.at[p, 0], vy.at[p, 0], ydev)

    def after_far(p):
        ref = blocks[p](far, y, c)
        arrive(ref, wz.at[p, 0], vz.at[p, 0], fdev)
        send(ref, ref, wz.at[p, 2], vz.at[p, 2], ndev)
        send(ref, ref, wy.at[p, 1], vy.at[p, 1], ydev)

    def after_near(p):
        for i, zz in ((1, near), (2, LINE - 1 - near)):
            ref = blocks[p](zz, y, c)
            arrive(ref, wz.at[p, i], vz.at[p, i], ndev)
            send(ref, ref, wy.at[p, i + 1], vy.at[p, i + 1], ydev)
        line = lines[p](y, c)
        send(line, line, wc.at[p, 0], vc.at[p, 0], cdev)

    def after_y(p):
        for i, zz in enumerate((z, far, near, LINE - 1 - near)):
            arrive(blocks[p](zz, 1 - y, c), wy.at[p, i], vy.at[p, i], ydev)
        line = lines[p](1 - y, c)
        send(line, line, wc.at[p, 1], vc.at[p, 1], cdev)

    def after_c(p):
        for i, yy in enumerate((y, 1 - y)):
            arrive(lines[p](yy, 1 - c), wc.at[p, i], vc.at[p, i], cdev)

    def both(zz, cc):
        return wd.at[zz, :, cc, down_half(1)]

    def after_first_y():
        arrive(blocks[D_1](z, 1 - y, c), wy.at[D_1, 0], vy.at[D_1, 0], ydev)
        own = both(z, c)
        send(own, own, wz.at[D_1, 0], vz.at[D_1, 0], fdev)
        send(own, own, wz.at[D_1, 1], vz.at[D_1, 1], ndev)

    def after_first_far():
        ref = both(far, c)
        arrive(ref, wz.at[D_1, 0], vz.at[D_1, 0], fdev)
        send(ref, ref, wz.at[D_1, 2], vz.at[D_1, 2], ndev)

    def after_first_near():
        for i, zz in ((1, near), (2, LINE - 1 - near)):
            arrive(both(zz, c), wz.at[D_1, i], vz.at[D_1, i], ndev)
        ref = wd.at[:, :, c, down_half(1)]
        send(ref, ref, wc.at[D_1, 0], vc.at[D_1, 0], cdev)

    def after_first_c():
        arrive(wd.at[:, :, 1 - c, down_half(1)], wc.at[D_1, 0], vc.at[D_1, 0], cdev)

    spans = [pl.ds(0, 2 * part), pl.ds(2 * part, 2 * part), None, None]
    spans += [pl.ds(0, 2 * part), pl.ds(2 * part, part), pl.ds(3 * part, part)]
    parts = [
        (lambda cc, i=i: gu.at[i - 2, :, :, cc]) if q is None else (lambda cc, q=q: gd.at[:, :, cc, q])
        for i, q in enumerate(spans)
    ]
    land_c = [rcu.at[i - 2] if q is None else rcd.at[:, :, q] for i, q in enumerate(spans)]
    land_y = [ryu.at[i - 2] if q is None else ryd.at[:, q] for i, q in enumerate(spans)]
    land_z = [rzu.at[i - 2] if q is None else rzd.at[:, q] for i, q in enumerate(spans)]

    def c_start(k):
        return send(parts[k](1 - c), land_c[k], gc.at[k], hc.at[k], cdev)

    def c_end(k):
        ref, own = land_c[k], parts[k](c)
        arrive(ref, gc.at[k], hc.at[k], cdev)

        def add(i, carry):
            ref[i] = (ref[i].astype(f32) + own[i].astype(f32)).astype(bf16)
            return carry

        lax.fori_loop(0, LINE, add, 0)
        if k == 0:
            return [
                send(ref.at[LINE - 1 - near], rzb.at[1], gz.at[k, 1], hz.at[k, 1], ndev),
                send(ref.at[near], rzb.at[0], gz.at[k, 0], hz.at[k, 0], ndev),
            ]
        return [send(ref.at[:, 1 - y], land_y[k], gy.at[k], hy.at[k], ydev)]

    def y_end(k):
        ref, own = land_y[k], land_c[k]
        arrive(ref, gy.at[k], hy.at[k], ydev)

        def add(i, carry):
            ref[i] = (ref[i].astype(f32) + own[i, y].astype(f32)).astype(bf16)
            return carry

        lax.fori_loop(0, LINE, add, 0)
        return [
            send(ref.at[LINE - 1 - near], land_z[k].at[1], gz.at[k, 1], hz.at[k, 1], ndev),
            send(ref.at[near], land_z[k].at[0], gz.at[k, 0], hz.at[k, 0], ndev),
        ]

    def z_mid(k):
        ref = land_z[k].at[1]
        arrive(ref, gz.at[k, 1], hz.at[k, 1], ndev)
        ref[...] = (ref[...].astype(f32) + land_y[k][far].astype(f32)).astype(bf16)
        return send(ref, land_z[k].at[2], gz.at[k, 2], hz.at[k, 2], fdev)

    def z_end(k):
        arrive(land_z[k].at[0], gz.at[k, 0], hz.at[k, 0], ndev)
        arrive(land_z[k].at[2], gz.at[k, 2], hz.at[k, 2], fdev)
        return land_y[k][z].astype(f32) + land_z[k][0].astype(f32) + land_z[k][2].astype(f32)

    def first_mid():
        arrive(rzb.at[1], gz.at[0, 1], hz.at[0, 1], ndev)
        rzb[1] = (rzb[1].astype(f32) + land_c[0][far].astype(f32)).astype(bf16)
        return send(rzb.at[1], rzb.at[2], gz.at[0, 2], hz.at[0, 2], fdev)

    def first_end():
        arrive(rzb.at[0], gz.at[0, 0], hz.at[0, 0], ndev)
        arrive(rzb.at[2], gz.at[0, 2], hz.at[0, 2], fdev)
        rzb[0] = (land_c[0][z].astype(f32) + rzb[0].astype(f32) + rzb[2].astype(f32)).astype(bf16)
        return send(rzb.at[0, 1 - y], ryb, gy.at[0], hy.at[0], ydev)

    def first_sum():
        arrive(ryb, gy.at[0], hy.at[0], ydev)
        return rzb[0, y].astype(f32) + ryb[...].astype(f32)

    lane = lax.broadcasted_iota(jnp.int32, (part, model), 1)
    fits = (lax.rem(lane, part) == lax.broadcasted_iota(jnp.int32, (part, model), 0)) & (
        lane // part == s * 4 * LINE + z * 4 + y * 2 + c
    )
    stv[...] = dot_nn(small_ref[...], jnp.where(fits, 1.0, 0.0).astype(bf16)).astype(bf16)

    def chooser(i):
        count = len_ref[i] // 8
        rank = lax.broadcasted_iota(jnp.int32, (1, ranks), 1)
        row = jnp.where(rank < count, routed_ref[i : i + 1], -1).astype(f32)
        eye = lax.broadcasted_iota(jnp.int32, (ranks, ranks), 0) == lax.broadcasted_iota(
            jnp.int32, (ranks, ranks), 1
        )
        column = jnp.sum(jnp.where(eye, row, 0.0), axis=1, keepdims=True).astype(jnp.int32)
        count_here = tok_hbm.shape[1] * 512
        position = lax.broadcasted_iota(jnp.int32, (ranks, count_here), 1) + s * count_here
        return jnp.where(position == column, 1.0, 0.0).astype(bf16)

    def pick(i, dst):
        dst[i] = dot_nn(chooser(i), gd[2 * i : 2 * i + 2].reshape(tok_hbm.shape[1] * 512, model)).astype(bf16)

    def live_column(i):
        rank = lax.broadcasted_iota(jnp.int32, (ranks, 1), 0)
        return jnp.where(rank < len_ref[i] // 8, 1.0, 0.0).astype(f32)

    def allowed(i):
        query = lax.broadcasted_iota(jnp.int32, (ranks, ranks), 0)
        key = lax.broadcasted_iota(jnp.int32, (ranks, ranks), 1)
        return (key <= query) & (key < len_ref[i] // 8)

    greet([xdev, ydev, cdev, ndev, fdev])
    swap_v = send(stv, rcv, sx.at[0], rx.at[0], xdev)
    for copy in stage:
        copy.wait()
    send(stq, wq.at[s, z, y, c], sx.at[1], rx.at[1], xdev)
    for copy in own_q:
        copy.wait()
    spread(Q_OWN)
    spread_y(Q_OWN)
    x_swap = []
    get_tok[0].wait()
    pick(0, xs)
    x_swap.append(send(xs.at[0], xr.at[0], sx.at[3], rx.at[3], xdev))
    get_cot = [fetch(cot_hbm.at[0], gd.at[pl.ds(0, 2)])]
    stage_u.wait()
    send(stu, wu.at[s, z, y, c], sx.at[2], rx.at[2], xdev)
    get_tok[1].wait()
    pick(1, xs)
    x_swap.append(send(xs.at[1], xr.at[1], sx.at[4], rx.at[4], xdev))
    get_cot.append(fetch(cot_hbm.at[1], gd.at[pl.ds(2, 2)]))
    swap_v.wait_recv()
    gv[z, y, c] = stv[...] + rcv[...]
    after_far(Q_OWN)
    spread(VEC)
    spread_y(VEC)
    arrive(wq.at[1 - s, z, y, c], sx.at[1], rx.at[1], xdev)
    spread(Q_SWAP)
    spread_y(Q_SWAP)
    own_d.wait()
    get_cot[0].wait()
    pick(0, ds)
    d_swap = [send(ds.at[0], dr.at[0], sx.at[7], rx.at[7], xdev)]
    after_near(Q_OWN)
    after_far(VEC)
    spread_y(D_1)
    get_cot[1].wait()
    pick(1, ds)
    after_far(Q_SWAP)
    own_o.wait()
    spread(OUT)
    after_near(VEC)
    after_near(Q_SWAP)
    after_far(OUT)
    spread_y(OUT)
    own_u.wait()
    spread(U_OWN)
    spread_y(U_OWN)
    arrive(wu.at[1 - s, z, y, c], sx.at[2], rx.at[2], xdev)
    spread(U_SWAP)
    after_y(Q_OWN)
    after_y(VEC)
    after_c(Q_OWN)
    after_c(VEC)
    after_near(OUT)
    after_y(Q_SWAP)
    after_far(U_OWN)
    spread(D_0)
    spread_y(U_SWAP)
    spread_y(D_0)
    after_c(Q_SWAP)

    gains[...] = jnp.sum(gv[...].astype(f32).reshape(4 * LINE, 16, model), axis=0)
    gain_one, gain_two, router = gains[0:1], gains[1:2], gains[2:3]

    def enter(i):
        x_swap[i].wait()
        row = xr[i].astype(f32) + xs[i].astype(f32)
        xr[i] = row.astype(bf16)
        xs[i] = (row * inverse_rms(row) * gain_one).astype(bf16)
        for j in range(3):
            cols = pl.ds(j * half_q, half_q)
            qkv[i, :, cols] = dot_nn(xs[i], wq[:, :, :, :, :, cols].reshape(model, half_q)).astype(bf16)

    def attend(i):
        ok = allowed(i)

        def pair(j, carry):
            q2 = qkv[i, :, pl.ds(j * 128, 128)].astype(f32)
            k2 = qkv[i, :, pl.ds(half_q + j * 128, 128)]
            v2 = qkv[i, :, pl.ds(2 * half_q + j * 128, 128)]
            mixed = jnp.zeros(q2.shape, f32)
            for parity in range(2):
                mask = head_mask(parity)
                score = dot_nt((q2 * mask).astype(bf16), k2) * (HEAD_DIM**-0.5)
                score = jnp.where(ok, score, -1000000000.0)
                weight = jnp.exp(score - jnp.max(score, axis=-1, keepdims=True))
                total = jnp.sum(weight, axis=-1, keepdims=True)
                mixed += dot_nn(weight.astype(bf16), v2) / total * mask
            att[i, :, pl.ds(j * 128, 128)] = mixed.astype(bf16)
            return carry

        lax.fori_loop(0, half_q // 128, pair, 0)

    def leave(i):
        for j in range(2):
            cols = pl.ds(j * half, half)
            a_s[i, :, cols] = dot_nn(att[i], wo[:, :, :, :, cols].reshape(half_q, half)).astype(bf16)
        return send(a_s.at[i], a_r.at[i], sx.at[5 + i], rx.at[5 + i], xdev)

    enter(0)
    attend(0)
    after_y(OUT)
    after_c(OUT)
    a_swap = [leave(0)]
    after_far(U_SWAP)
    after_first_y()
    after_near(U_OWN)
    enter(1)
    attend(1)
    a_swap.append(leave(1))
    d_swap.append(send(ds.at[1], dr.at[1], sx.at[8], rx.at[8], xdev))
    after_far(D_0)
    after_near(U_SWAP)
    after_y(U_OWN)
    after_c(U_OWN)

    def mlp_up(i):
        a_swap[i].wait()
        row = xr[i].astype(f32) + (a_s[i].astype(f32) + a_r[i].astype(f32))
        hid[i] = row
        a_s[i] = (row * inverse_rms(row) * gain_two).astype(bf16)

        def tile(t, carry):
            cols = pl.ds(t * 512, 512)
            up = dot_nn(a_s[i], wu[:, :, :, :, :, cols].reshape(model, 512))
            curve = jnp.tanh(GELU_C * (up + GELU_K * up * up * up))
            act[i, :, cols] = (0.5 * up * (1.0 + curve)).astype(bf16)
            slope = 0.5 * (1.0 + curve) + 0.5 * up * (1.0 - curve * curve) * (
                GELU_C * (1.0 + 3.0 * GELU_K * up * up)
            )
            gp[i, :, cols] = slope.astype(bf16)
            return carry

        lax.fori_loop(0, half_u // 512, tile, 0)

    def gate_of(i):
        return jax.nn.sigmoid(jnp.sum(xr[i].astype(f32) * router, axis=-1, keepdims=True))

    def cotangent_rows(i):
        d_swap[i].wait()
        row = dr[i].astype(f32) + ds[i].astype(f32)
        dr[i] = row.astype(bf16)
        ds[i] = (gate_of(i) * row).astype(bf16)

    def mlp_back(i):
        def tile(t, carry):
            cols = pl.ds(t * 512, 512)
            back = dot_nt(ds[i], wd[t].reshape(512, model))
            gp[i, :, cols] = (back * gp[i, :, cols].astype(f32)).astype(bf16)
            return carry

        lax.fori_loop(0, half_u // 512, tile, 0)
        for j in range(2):
            cols = pl.ds(j * half, half)
            d2s[i, :, cols] = dot_nt(gp[i], wu[j].reshape(half, half_u)).astype(bf16)
        return send(d2s.at[i], d2r.at[i], sx.at[9 + i], rx.at[9 + i], xdev)

    def mlp_out(i):
        for j in range(2):
            cols = pl.ds(j * half, half)
            m_s[i, :, cols] = dot_nn(act[i], wd[:, :, :, :, cols].reshape(half_u, half)).astype(bf16)

    def mlp_send(i):
        return send(m_s.at[i], m_r.at[i], sx.at[11 + i], rx.at[11 + i], xdev)

    after_y(U_SWAP)
    after_first_far()
    after_c(U_SWAP)
    mlp_up(0)
    after_near(D_0)
    mlp_up(1)
    after_y(D_0)
    after_c(D_0)
    after_first_near()
    after_first_c()
    cotangent_rows(0)
    d2_swap = [mlp_back(0)]
    cotangent_rows(1)

    def down_tile(t, carry):
        grad = dot_tn(act[:, :, pl.ds(t * 512, 512)].reshape(rows, 512), ds[...].reshape(rows, model))
        gd[t] = grad.astype(bf16).reshape(gd.shape[1:])
        return carry

    lax.fori_loop(0, half_u // 512, down_tile, 0)
    c_down = [c_start(0), c_start(1)]
    d2_swap.append(mlp_back(1))
    z_first = c_end(0)
    y_down = c_end(1)
    mlp_out(0)
    m_swap = [mlp_send(0)]

    def up_tile(t, carry):
        cols = pl.ds(t * 512, 512)
        grad = dot_tn(a_s[...].reshape(rows, model), gp[:, :, cols].reshape(rows, 512))
        gu[:, :, :, :, :, cols] = grad.astype(bf16).reshape(gu.shape[:5] + (512,))
        return carry

    lax.fori_loop(0, half_u // 512, up_tile, 0)
    c_start(2)
    c_start(3)
    mlp_out(1)
    m_swap.append(mlp_send(1))

    def hidden_back(i):
        d2_swap[i].wait()
        back = d2s[i].astype(f32) + d2r[i].astype(f32)
        row = hid[i]
        r2 = inverse_rms(row)
        scaled = back * gain_two
        step = r2 * scaled - row * (r2 * r2 * r2 * jnp.mean(scaled * row, axis=-1, keepdims=True))
        dh[i] = step
        gp[i, :, 0:model] = (gate_of(i) * dr[i].astype(f32) + step).astype(bf16)
        gp[i, :, model : model + half_q] = dot_nt(gp[i, :, 0:model], wo[...].reshape(half_q, model)).astype(bf16)
        return jnp.sum(d2s[i].astype(f32) * row * r2, axis=0, keepdims=True)

    def attend_back(i):
        ok = allowed(i)
        scale = HEAD_DIM**-0.5

        def pair(j, carry):
            q2 = qkv[i, :, pl.ds(j * 128, 128)]
            k2 = qkv[i, :, pl.ds(half_q + j * 128, 128)]
            v2 = qkv[i, :, pl.ds(2 * half_q + j * 128, 128)]
            g2 = gp[i, :, pl.ds(model + j * 128, 128)].astype(f32)
            q2f = q2.astype(f32)
            dq2 = jnp.zeros(q2.shape, f32)
            dk2 = jnp.zeros(q2.shape, f32)
            dv2 = jnp.zeros(q2.shape, f32)
            for parity in range(2):
                mask = head_mask(parity)
                score = dot_nt((q2f * mask).astype(bf16), k2) * scale
                score = jnp.where(ok, score, -1000000000.0)
                weight = jnp.exp(score - jnp.max(score, axis=-1, keepdims=True))
                over = 1.0 / jnp.sum(weight, axis=-1, keepdims=True)
                gh = g2 * mask
                dp = dot_nt(gh.astype(bf16), v2)
                prob = weight * over
                delta = jnp.sum(prob * dp, axis=-1, keepdims=True)
                dscore = (prob * (dp - delta)).astype(bf16)
                dq2 += dot_nn(dscore, k2) * mask
                dk2 += dot_tn(dscore, q2) * mask
                dv2 += dot_tn(weight.astype(bf16), (gh * over).astype(bf16))
            act[i, :, pl.ds(j * 128, 128)] = (dq2 * scale).astype(bf16)
            act[i, :, pl.ds(half_q + j * 128, 128)] = (dk2 * scale).astype(bf16)
            act[i, :, pl.ds(2 * half_q + j * 128, 128)] = dv2.astype(bf16)
            return carry

        lax.fori_loop(0, half_q // 128, pair, 0)

    def inner_back(i):
        r1 = inverse_rms(xr[i].astype(f32))
        sums = []
        for j in range(2):
            cols = pl.ds(j * half, half)
            step = dot_nt(act[i, :, 0 : 3 * half_q], wq[j].reshape(half, 3 * half_q))
            d2s[i, :, cols] = step.astype(bf16)
            sums.append(jnp.sum(step * xr[i, :, cols].astype(f32) * r1, axis=0, keepdims=True))
        return send(d2s.at[i], d1r.at[i], sx.at[13 + i], rx.at[13 + i], xdev), sums

    grad_gm = hidden_back(0)
    c_end(2)
    attend_back(0)
    c_end(3)
    z_first.append(first_mid())
    swap_0, sums_0 = inner_back(0)
    z_down = y_end(1)
    grad_gm += hidden_back(1)
    attend_back(1)
    z_down.append(z_mid(1))
    for copy in c_down + z_first:
        gone(copy)
    first_end()
    pl.semaphore_signal(free.at[0], inc=1, device_id=cdev, device_id_type=MESH)
    y_end(2)

    def out_tile(t):
        cols = pl.ds(t * half, half)
        grad = dot_tn(att[...].reshape(rows, half_q), gp[:, :, cols].reshape(rows, half))
        gd[:, :, :, 3 * part :, cols] = grad.astype(bf16).reshape(wo.shape[:4] + (half,))

    def qkv_tile(t):
        grad = dot_tn(xs[...].reshape(rows, model), act[:, :, t * half_q : (t + 1) * half_q].reshape(rows, half_q))
        grad = grad.astype(bf16).reshape(wq.shape[:5] + (half_q,))
        if t < 2:
            gd[:, :, :, 0:part, t * half_q : (t + 1) * half_q] = grad[0]
            gd[:, :, :, part : 2 * part, t * half_q : (t + 1) * half_q] = grad[1]
        else:
            gd[:, :, :, 2 * part : 3 * part, 0:half_q] = grad[0]
            gd[:, :, :, 2 * part : 3 * part, half_q:] = grad[1]

    qkv_tile(0)
    qkv_tile(1)
    pl.semaphore_wait(free.at[0], 1)
    c_start(4)
    qkv_tile(2)
    fd[2 * part :] = z_end(1)
    for copy in y_down + z_down:
        gone(copy)
    for target in (ydev, cdev, ndev, fdev):
        pl.semaphore_signal(free.at[1], inc=1, device_id=target, device_id_type=MESH)
    out_tile(0)
    out_tile(1)
    c_end(4)
    swap_1, sums_1 = inner_back(1)
    d1_swap = [swap_0, swap_1]
    for j in range(2):
        vs[0:1, j * half : (j + 1) * half] = sums_0[j] + sums_1[j]
    vs[1:2] = grad_gm
    pl.semaphore_wait(free.at[1], 4)
    c_start(5)
    c_start(6)
    z_mid(2)
    c_end(5)
    y_end(3)
    fu[0] = z_end(2)

    grad_router = jnp.zeros((1, model), f32)
    for i in range(2):
        m_swap[i].wait()
        row = xr[i].astype(f32)
        gate = gate_of(i)
        branch = (hid[i] - row) + (m_s[i].astype(f32) + m_r[i].astype(f32))
        m_s[i] = (gate * branch * live_column(i)).astype(bf16)
        slope = jnp.sum(dr[i].astype(f32) * branch, axis=-1, keepdims=True) * gate * (1.0 - gate)
        logit[i] = slope
        grad_router += jnp.sum(row * slope, axis=0, keepdims=True)
    put(m_s, upd_out)
    vs[2:3] = 0.5 * grad_router
    vs[3:8] = jnp.zeros((5, model), f32)
    send(vs, vr.at[0], gc.at[7], hc.at[7], cdev)
    z_mid(3)
    arrive(vr.at[0], gc.at[7], hc.at[7], cdev)
    v_all[0] = vs[...] + vr[0]
    send(v_all.at[0], vr.at[1], gy.at[7], hy.at[7], ydev)
    c_end(6)
    fd[0 : 2 * part] = first_sum()
    put(fd, fd_out)
    fu[1] = z_end(3)
    suu[...] = fu[1 - s].astype(bf16)
    send(suu, ruu, sx.at[15], rx.at[15], xdev)
    put(fu.at[s], fu_out.at[:, pl.ds(s * half_u, half_u)])
    y_end(4)

    def rows_back(i):
        d1_swap[i].wait()
        row = xr[i].astype(f32)
        r1 = inverse_rms(row)
        scaled = (d2s[i].astype(f32) + d1r[i].astype(f32)) * gain_one
        step = r1 * scaled - row * (r1 * r1 * r1 * jnp.mean(scaled * row, axis=-1, keepdims=True))
        d2s[i] = (dh[i] + step + logit[i] * router).astype(bf16)
        put(d2s.at[i], dx_out.at[i])

    rows_back(0)
    y_end(5)
    arrive(vr.at[1], gy.at[7], hy.at[7], ydev)
    v_all[1] = v_all[0] + vr[1]
    send(v_all.at[1], vr.at[2], gz.at[7, 0], hz.at[7, 0], ndev)
    z_mid(4)
    rows_back(1)
    y_end(6)
    z_mid(5)
    fqk[...] = z_end(4).reshape(fqk.shape)
    sqk[...] = fqk[1 - s].astype(bf16)
    send(sqk, rqk, sx.at[16], rx.at[16], xdev)
    for j in range(2):
        put(fqk.at[s, :, pl.ds(j * half_q, half_q)], fq_out.at[:, pl.ds(2 * j * half_q + s * half_q, half_q)])
    arrive(vr.at[2], gz.at[7, 0], hz.at[7, 0], ndev)
    v_all[2] = v_all[1] + vr[2]
    send(v_all.at[2], vr.at[3], gz.at[7, 1], hz.at[7, 1], fdev)
    fv[...] = z_end(5)
    sv[...] = fv[:, pl.ds((1 - s) * half_q, half_q)].astype(bf16)
    send(sv, rv, sx.at[17], rx.at[17], xdev)
    put(fv.at[:, pl.ds(s * half_q, half_q)], fq_out.at[:, pl.ds(4 * half_q + s * half_q, half_q)])
    z_mid(6)
    arrive(vr.at[3], gz.at[7, 1], hz.at[7, 1], fdev)
    v_all[3] = v_all[2] + vr[3]
    send(v_all.at[3], vr.at[4], sx.at[18], rx.at[18], xdev)
    arrive(ruu, sx.at[15], rx.at[15], xdev)
    fu[1 - s] = ruu[...].astype(f32)
    put(fu.at[1 - s], fu_out.at[:, pl.ds((1 - s) * half_u, half_u)])
    arrive(rqk, sx.at[16], rx.at[16], xdev)
    fqk[1 - s] = rqk[...].astype(f32)
    for j in range(2):
        put(
            fqk.at[1 - s, :, pl.ds(j * half_q, half_q)],
            fq_out.at[:, pl.ds(2 * j * half_q + (1 - s) * half_q, half_q)],
        )
    fo[...] = z_end(6)
    put(fo, fo_out)
    arrive(rv, sx.at[17], rx.at[17], xdev)
    fv[:, pl.ds((1 - s) * half_q, half_q)] = rv[...].astype(f32)
    put(
        fv.at[:, pl.ds((1 - s) * half_q, half_q)],
        fq_out.at[:, pl.ds(4 * half_q + (1 - s) * half_q, half_q)],
    )
    arrive(vr.at[4], sx.at[18], rx.at[18], xdev)
    v_all[4] = v_all[3] + vr[4]
    put(v_all.at[4], vec_out)
    waited = x_swap + a_swap + d_swap + d2_swap + m_swap + d1_swap
    for copy in list(sent):
        if not any(copy is other for other in waited):
            copy.wait_send()
    for copy in outs:
        copy.wait()


def rows_kernel(
    len_ref, routed_ref, tok_ref, cot_ref, upd_ref, dx_ref, fq_ref, fo_ref, fu_ref, fd_ref, vec_ref,
    out_ref, grad_ref, fq_out, fo_out, fu_out, fd_out, one_out, two_out, three_out,
):
    slot, step = pl.program_id(0), pl.program_id(1)
    s = lax.axis_index("seq")
    tall, model = tok_ref.shape[1:]
    ranks = upd_ref.shape[1]
    rank = lax.broadcasted_iota(jnp.int32, (1, ranks), 1)
    routed = jnp.where(rank < len_ref[slot] // 8, routed_ref[pl.ds(slot, 1)], -1)
    first = (s * pl.num_programs(1) + step) * tall
    position = lax.broadcasted_iota(jnp.int32, (tall, ranks), 0) + first
    chooser = jnp.where(position == routed, 1.0, 0.0).astype(bf16)
    out_ref[0] = (tok_ref[0].astype(f32) + dot_nn(chooser, upd_ref[0])).astype(bf16)
    grad_ref[0] = (cot_ref[0].astype(f32) + dot_nn(chooser, dx_ref[0])).astype(bf16)

    @pl.when((slot == 0) & (step == 0))
    def _():
        fq_out[...] = fq_ref[...]
        fo_out[...] = fo_ref[...]
        fu_out[...] = fu_ref[...]
        fd_out[...] = fd_ref[...]
        part = one_out.shape[1]
        flat = s * lax.axis_size("batch") + lax.axis_index("batch")
        lane = lax.broadcasted_iota(jnp.int32, (part, model), 1)
        here = (lane // part == flat) & (
            lax.rem(lane, part) == lax.broadcasted_iota(jnp.int32, (part, model), 0)
        )
        eye = lax.broadcasted_iota(jnp.int32, (part, part), 0) == lax.broadcasted_iota(
            jnp.int32, (part, part), 1
        )
        for j, ref in enumerate((one_out, two_out, three_out)):
            column = jnp.sum(jnp.where(here, vec_ref[j : j + 1], 0.0), axis=1, keepdims=True)
            ref[...] = jnp.sum(jnp.where(eye, column, 0.0), axis=0, keepdims=True)


def split_device(
    tokens, cotangent, lengths, routed, w_qkv, w_out, w_up, w_down, gain_attn, gain_mlp, router
):
    slots, local_len, model = tokens.shape
    ranks = routed.shape[1]
    half_q, half_u = w_qkv.shape[1] // 6, w_up.shape[1] // 2
    part, down = w_qkv.shape[0], w_down.shape[0]
    small = jnp.concatenate(
        [gain_attn[None], gain_mlp[None], router[None], jnp.zeros((13, part), bf16)], axis=0
    )
    hbm = pl.BlockSpec(memory_space=pl.ANY)
    vmem = pl.BlockSpec(memory_space=pltpu.VMEM)
    smem = pl.BlockSpec(memory_space=pltpu.SMEM)
    sds, space, dma = jax.ShapeDtypeStruct, pltpu.VMEM, pltpu.SemaphoreType.DMA
    rows = (slots, ranks, model)
    grid = (LINE, 2, 2)
    wq_shape, wo_shape = (2,) + grid + (part, 3 * half_q), grid + (part, model)
    wu_shape, wd_shape = (2,) + grid + (part, half_u), grid + (down, model)
    blocked = (slots, local_len // 512, 2, 2, 128, model)
    row_bf16 = space(rows, bf16)

    def land(lead, tall, wide):
        return [space(lead + mid + (tall, wide), bf16) for mid in ((LINE, 2), (LINE,), (3,))]

    on_d, on_u = land((), down, model), land((2,), part, half_u)
    grad_shapes = (
        sds((part, 6 * half_q), f32), sds((part, model), f32), sds((part, 2 * half_u), f32), sds((down, model), f32),
    )
    upd, dxr, *sums, vec = pl.pallas_call(
        block_kernel,
        out_shape=(sds(rows, bf16), sds(rows, bf16)) + grad_shapes + (sds((8, model), f32),),
        in_specs=[hbm] * 6 + [vmem] * 2 + [smem],
        out_specs=[hbm] * 7,
        scratch_shapes=[
            space(wq_shape, bf16), space(wo_shape, bf16), space(wu_shape, bf16), space(wd_shape, bf16),
            space(grid + (16, model), bf16),
            space((part, 3 * half_q), bf16), space((part, half_u), bf16), space((16, model), bf16), space((16, model), bf16),
            *[row_bf16] * 11, space(rows, f32), space(rows, f32),
            space((slots, ranks, 3 * half_q), bf16), space((slots, ranks, half_q), bf16),
            space((slots, ranks, half_u), bf16), space((slots, ranks, half_u), bf16),
            space((slots, ranks, 1), f32), space((16, model), f32),
            space(wd_shape, bf16), space(wu_shape, bf16),
            on_d[0], on_u[0], on_d[1], on_u[1], on_d[2], on_u[2],
            space((3, 2, 2 * part, model), bf16), space((2 * part, model), bf16),
            space((2, part, model), f32), space((part, model), f32), space((part, model), f32),
            space((2, part, half_u), f32), space((down, model), f32),
            space((part, model), bf16), space((part, half_q), bf16), space((part, half_u), bf16),
            space((part, model), bf16), space((part, half_q), bf16), space((part, half_u), bf16),
            space((8, model), f32), space((5, 8, model), f32), space((5, 8, model), f32),
            dma((16,)), dma((16,)), dma((8, 3)), dma((8, 3)), dma((8, 4)), dma((8, 4)), dma((8, 2)), dma((8, 2)),
            dma((19,)), dma((19,)), dma((8,)), dma((8,)), dma((8,)), dma((8,)), dma((8, 3)), dma((8, 3)),
            pltpu.SemaphoreType.REGULAR((2,)),
        ],
        compiler_params=pltpu.CompilerParams(collective_id=1, has_side_effects=True, vmem_limit_bytes=60 << 20),
        name="block",
    )(tokens.reshape(blocked), cotangent.reshape(blocked), w_qkv, w_out, w_up, w_down, small, routed, lengths)

    tall = 512
    big = pl.BlockSpec((1, tall, model), lambda i, j: (i, j, 0))
    moved = pl.BlockSpec((1, ranks, model), lambda i, j: (i, 0, 0))

    def whole(shape):
        return pl.BlockSpec(shape, lambda i, j: (0, 0))

    whole_grads = [whole(g.shape) for g in grad_shapes]
    vectors = (sds((1, part), f32),) * 3
    output, input_grad, g_qkv, g_out, g_up, g_down, g_one, g_two, g_three = pl.pallas_call(
        rows_kernel,
        grid=(slots, local_len // tall),
        out_shape=(sds(tokens.shape, bf16), sds(tokens.shape, bf16)) + grad_shapes + vectors,
        in_specs=[smem, whole(routed.shape), big, big, moved, moved] + whole_grads + [whole((8, model))],
        out_specs=[big, big] + whole_grads + [whole((1, part))] * 3,
        compiler_params=pltpu.CompilerParams(vmem_limit_bytes=60 << 20),
        name="rows",
    )(lengths, routed, tokens, cotangent, upd, dxr, *sums, vec)
    return (
        output, input_grad, g_qkv, g_out, g_up, g_down,
        g_one.reshape(part), g_two.reshape(part), g_three.reshape(part),
    )


def solution(mesh):
    in_specs = (
        P("batch", "seq", None),
        P("batch", "seq", None),
        P("batch"),
        P("batch", None),
        P(("seq", "batch"), None),
        P(("seq", "batch"), None),
        P(("seq", "batch"), None),
        P(("seq", "batch"), None),
        P(("seq", "batch")),
        P(("seq", "batch")),
        P(("seq", "batch")),
    )
    out_specs = (
        P("batch", "seq", None),
        P("batch", "seq", None),
        P(("seq", "batch"), None),
        P(("seq", "batch"), None),
        P(("seq", "batch"), None),
        P(("seq", "batch"), None),
        P(("seq", "batch")),
        P(("seq", "batch")),
        P(("seq", "batch")),
    )
    small_slice = mesh.shape["seq"] == 2 and mesh.shape["batch"] == 4 * LINE
    body = split_device if small_slice else general_device
    return jax.shard_map(body, mesh=mesh, in_specs=in_specs, out_specs=out_specs, check_vma=False)
```

```python
import functools

import jax
import jax.numpy as jnp
from jax import lax
from jax.experimental import pallas as pl
from jax.experimental.pallas import tpu as pltpu
from jax.sharding import PartitionSpec as P

HEAD_DIM = 64
MESH = pl.DeviceIdType.MESH


epsilon = 1e-05
highest = lax.Precision.HIGHEST
f32 = jnp.float32
bf16 = jnp.bfloat16

LINE = 4
GELU_C = 0.7978845608
GELU_K = 0.044715


def dot_nn(a, b):
    return lax.dot_general(a, b, (((1,), (0,)), ((), ())), preferred_element_type=f32)


def dot_nt(a, b):
    return lax.dot_general(a, b, (((1,), (1,)), ((), ())), preferred_element_type=f32)


def dot_tn(a, b):
    return lax.dot_general(a, b, (((0,), (0,)), ((), ())), preferred_element_type=f32)


def place():
    s = lax.axis_index("seq")
    b = lax.axis_index("batch")
    return s, b // 4, lax.rem(b // 2, 2), lax.rem(b, 2)


def device(s, z, y, c):
    return (s, z * 4 + y * 2 + c)


def remote(src, dst, send, recv, target):
    return pltpu.make_async_remote_copy(
        src_ref=src, dst_ref=dst, send_sem=send, recv_sem=recv, device_id=target, device_id_type=MESH
    )


def greet(targets):
    barrier = pltpu.get_barrier_semaphore()
    for target in targets:
        pl.semaphore_signal(barrier, inc=1, device_id=target, device_id_type=MESH)
    pl.semaphore_wait(barrier, len(targets))


def inverse_rms(values):
    return lax.rsqrt(jnp.mean(values * values, axis=-1, keepdims=True) + epsilon)


def head_mask(parity):
    lane = lax.broadcasted_iota(jnp.int32, (1, 128), 1)
    return jnp.where(lane // HEAD_DIM == parity, 1.0, 0.0).astype(f32)


def norm_apply(values_in, gain_vec):
    return (
        values_in
        * lax.rsqrt(jnp.mean(values_in * values_in, axis=-1, keepdims=True) + epsilon)
        * gain_vec
    )


def gelu_tanh(values_in):
    return jax.nn.gelu(values_in, approximate=True)


def general_device(
    tokens, cotangent, lengths, routed, w_qkv, w_out, w_up, w_down, gain_attn, gain_mlp, router
):
    slot_count, local_len, model_width = tokens.shape
    capacity = routed.shape[1]
    seq_devices = lax.axis_size("seq")
    own_count = capacity // seq_devices
    head_count = model_width // HEAD_DIM
    row_count = own_count * slot_count
    score_scale = HEAD_DIM ** (-0.5)
    gathered = (
        lax.all_gather(w_qkv, ("seq", "batch"), axis=0, tiled=True),
        lax.all_gather(w_out, ("seq", "batch"), axis=0, tiled=True),
        lax.all_gather(w_up, ("seq", "batch"), axis=0, tiled=True),
        lax.all_gather(w_down, ("seq", "batch"), axis=0, tiled=True),
        lax.all_gather(gain_attn, ("seq", "batch"), axis=0, tiled=True),
        lax.all_gather(gain_mlp, ("seq", "batch"), axis=0, tiled=True),
        lax.all_gather(router, ("seq", "batch"), axis=0, tiled=True),
    )
    full_qkv, full_out, full_up, full_down, full_ga, full_gm, full_router = gathered
    gain_one = full_ga.astype(f32)
    gain_two = full_gm.astype(f32)
    router_vec = full_router.astype(f32)
    counts = lengths // 8
    seq_place = lax.axis_index("seq")
    positions = seq_place * local_len + jnp.arange(local_len, dtype=jnp.int32)
    rank_all = jnp.arange(capacity, dtype=jnp.int32)
    live_all = rank_all[None, :] < counts[:, None]
    chooser = ((routed[:, :, None] == positions[None, None, :]) & live_all[:, :, None]).astype(bf16)
    pick_in = jnp.einsum("scp,spd->csd", chooser, tokens, preferred_element_type=f32)
    pick_cot = jnp.einsum("scp,spd->csd", chooser, cotangent, preferred_element_type=f32)
    picked, picked_cot = (
        lax.psum_scatter(
            pick_in.astype(jnp.bfloat16), "seq", scatter_dimension=0, tiled=True
        ).astype(jnp.float32),
        lax.psum_scatter(
            pick_cot.astype(jnp.bfloat16), "seq", scatter_dimension=0, tiled=True
        ).astype(jnp.float32),
    )
    own_rank = seq_place * own_count + jnp.arange(own_count, dtype=jnp.int32)
    live_own = own_rank[:, None] < counts[None, :]
    live_mask = live_own.reshape(row_count, 1).astype(f32)
    routed_in = picked.reshape(row_count, model_width)
    normed_one = norm_apply(routed_in, gain_one).astype(bf16)
    joined = jnp.dot(normed_one, full_qkv, preferred_element_type=f32).astype(bf16)
    query_rows = joined[:, :model_width].reshape(own_count, slot_count, head_count, HEAD_DIM)
    key_own = joined[:, model_width : 2 * model_width].reshape(own_count, slot_count, model_width)
    value_own = joined[:, 2 * model_width :].reshape(own_count, slot_count, model_width)
    key_every, value_every = (
        lax.all_gather(key_own, "seq", axis=0, tiled=True),
        lax.all_gather(value_own, "seq", axis=0, tiled=True),
    )
    key_rows = key_every.reshape(capacity, slot_count, head_count, HEAD_DIM)
    value_rows = value_every.reshape(capacity, slot_count, head_count, HEAD_DIM)
    scores = (
        jnp.einsum("qsha,ksha->shqk", query_rows, key_rows, preferred_element_type=f32)
        * score_scale
    )
    causal = rank_all[None, :] <= own_rank[:, None]
    allowed = causal[None, :, :] & (rank_all[None, None, :] < counts[:, None, None])
    scores = jnp.where(allowed[:, None], scores, -1000000000.0)
    row_max = jnp.max(scores, axis=-1, keepdims=True)
    weights_f = jnp.exp(scores - row_max)
    row_total = jnp.sum(weights_f, axis=-1, keepdims=True)
    weights_low = weights_f.astype(bf16)
    mixture = jnp.einsum("shqk,ksha->qsha", weights_low, value_rows, preferred_element_type=f32)
    mixture = mixture / jnp.transpose(row_total, (2, 0, 1, 3))
    attended = mixture.reshape(row_count, model_width).astype(bf16)
    branch_a = jnp.dot(attended, full_out, preferred_element_type=f32)
    hidden = routed_in + branch_a
    normed_two = norm_apply(hidden, gain_two).astype(bf16)
    up_proj = jnp.dot(normed_two, full_up, preferred_element_type=f32)
    activated = gelu_tanh(up_proj).astype(bf16)
    branch_m = jnp.dot(activated, full_down, preferred_element_type=f32)
    gate_prob = jax.nn.sigmoid(jnp.dot(routed_in, router_vec, precision=highest))
    branch = branch_a + branch_m
    update = (
        (gate_prob[:, None] * branch * live_mask)
        .astype(bf16)
        .reshape(own_count, slot_count, model_width)
    )
    update_every = lax.all_gather(update, "seq", axis=0, tiled=True)
    output = (
        tokens.astype(f32)
        + jnp.einsum("scp,csd->spd", chooser, update_every, preferred_element_type=f32)
    ).astype(bf16)
    cot_rows = picked_cot.reshape(row_count, model_width)
    grad_gate = jnp.sum(cot_rows * branch, axis=-1)
    grad_logit = grad_gate * gate_prob * (1.0 - gate_prob)
    grad_branch = gate_prob[:, None] * cot_rows
    grad_m = grad_branch.astype(bf16)
    grad_act = jnp.einsum("rd,fd->rf", grad_m, full_down, preferred_element_type=f32)
    unused_up, gelu_pull = jax.vjp(gelu_tanh, up_proj)
    grad_u = gelu_pull(grad_act)[0].astype(bf16)
    grad_n2 = jnp.einsum("rf,df->rd", grad_u, full_up, preferred_element_type=f32)
    unused_two, norm_pull_two = jax.vjp(norm_apply, hidden, gain_two)
    grad_hidden, grad_gm = norm_pull_two(grad_n2)
    grad_a = (grad_branch + grad_hidden).astype(bf16)
    grad_att = jnp.einsum("rd,ed->re", grad_a, full_out, preferred_element_type=f32).astype(bf16)
    grad_att4 = grad_att.reshape(own_count, slot_count, head_count, HEAD_DIM)
    delta_rows = jnp.sum(grad_att4.astype(f32) * mixture, axis=-1)
    delta = jnp.transpose(delta_rows, (1, 2, 0))[..., None]
    grad_p = jnp.einsum("qsha,ksha->shqk", grad_att4, value_rows, preferred_element_type=f32)
    probs = weights_f / row_total
    grad_s = (probs * (grad_p - delta)).astype(bf16)
    grad_q = (
        jnp.einsum("shqk,ksha->qsha", grad_s, key_rows, preferred_element_type=f32) * score_scale
    )
    grad_k = (
        jnp.einsum("shqk,qsha->ksha", grad_s, query_rows, preferred_element_type=f32) * score_scale
    )
    scaled_low = weights_low.astype(f32) / row_total
    grad_v = jnp.einsum("shqk,qsha->ksha", scaled_low, grad_att4.astype(f32), precision=highest)
    grad_k_own, grad_v_own = (
        lax.psum_scatter(
            grad_k.reshape(capacity, slot_count, model_width).astype(jnp.bfloat16),
            "seq",
            scatter_dimension=0,
            tiled=True,
        ).astype(jnp.float32),
        lax.psum_scatter(
            grad_v.reshape(capacity, slot_count, model_width).astype(jnp.bfloat16),
            "seq",
            scatter_dimension=0,
            tiled=True,
        ).astype(jnp.float32),
    )
    grad_joined = jnp.concatenate(
        [
            grad_q.reshape(row_count, model_width),
            grad_k_own.reshape(row_count, model_width),
            grad_v_own.reshape(row_count, model_width),
        ],
        axis=-1,
    ).astype(bf16)
    grad_n1 = jnp.einsum("re,de->rd", grad_joined, full_qkv, preferred_element_type=f32)
    unused_one, norm_pull_one = jax.vjp(norm_apply, routed_in, gain_one)
    grad_x1, grad_ga = norm_pull_one(grad_n1)
    grad_router = jnp.sum(routed_in * grad_logit[:, None], axis=0)
    grad_rows = (grad_hidden + grad_x1 + grad_logit[:, None] * router_vec[None, :]).astype(bf16)
    grad_rows = grad_rows.reshape(own_count, slot_count, model_width)
    grad_every = lax.all_gather(grad_rows, "seq", axis=0, tiled=True)
    input_grad = (
        cotangent.astype(f32)
        + jnp.einsum("scp,csd->spd", chooser, grad_every, preferred_element_type=f32)
    ).astype(bf16)
    part_qkv = jnp.einsum("rd,re->de", normed_one, grad_joined, preferred_element_type=f32)
    part_out = jnp.einsum("re,rd->ed", attended, grad_a, preferred_element_type=f32)
    part_up = jnp.einsum("rd,rf->df", normed_two, grad_u, preferred_element_type=f32)
    part_down = jnp.einsum("rf,rd->fd", activated, grad_m, preferred_element_type=f32)

    def sum_rows(part):
        return lax.psum_scatter(
            part.astype(bf16), ("seq", "batch"), scatter_dimension=0, tiled=True
        ).astype(f32)

    down_sum = sum_rows(part_down)
    grad_up = sum_rows(part_up)
    grad_out = sum_rows(part_out)
    grad_qkv = sum_rows(part_qkv)
    small_ga, small_gm, small_router = (
        lax.psum_scatter(grad_ga, ("seq", "batch"), scatter_dimension=0, tiled=True),
        lax.psum_scatter(grad_gm, ("seq", "batch"), scatter_dimension=0, tiled=True),
        lax.psum_scatter(grad_router, ("seq", "batch"), scatter_dimension=0, tiled=True),
    )
    return (
        output,
        input_grad,
        grad_qkv,
        grad_out,
        grad_up,
        down_sum,
        small_ga,
        small_gm,
        small_router,
    )


def block_kernel(
    tok_hbm, cot_hbm, wq_hbm, wo_hbm, wu_hbm, wd_hbm, one_ref, two_ref, three_ref, routed_ref, len_ref,
    upd_out, dx_out, fq_out, fo_out, fu_out, fd_out, vec_out, live_out,
    wq, wo, wu, wd, gv, stq, stu, stv, rcv,
    xs, xr, ds, dr, a_s, a_r, d2s, d2r, d1r, m_s, m_r, hid, dh, qkv, att, act, gp, logit, gains,
    gd, gu, rcd, rcu, ryd, ryu, rzd, rzu, rzb, ryb,
    fqk, fv, fo, fu, fd, sqk, sv, suu, rqk, rv, ruu, vs, vr, v_all, live,
    loc, out_sem, wz, vz, wy, vy, wc, vc, sx, rx, gc, hc, gt, ht, gy, hy, gz, hz, free,
):
    s, z, y, c = place()
    near, far = z + 1 - 2 * lax.rem(z, 2), LINE - 1 - z
    xdev, ydev, cdev = device(1 - s, z, y, c), device(s, z, 1 - y, c), device(s, z, y, 1 - c)
    ndev, fdev = device(s, near, y, c), device(s, far, y, c)
    model, half_q, half_u = xr.shape[2], att.shape[2], act.shape[2]
    ranks, half = xr.shape[1], xr.shape[2] // 2
    rows = xr.shape[0] * ranks
    part, half_d = stq.shape[0], wd.shape[3] // 2
    local, sent, outs = [], [], []

    def fetch(src, dst):
        copy = pltpu.make_async_copy(src, dst, loc.at[len(local)])
        copy.start()
        local.append(copy)
        return copy

    def send(src, dst, send_sem, recv_sem, target):
        copy = remote(src, dst, send_sem, recv_sem, target)
        copy.start()
        sent.append(copy)
        return copy

    def gone(copy):
        copy.wait_send()
        sent[:] = [other for other in sent if other is not copy]

    def arrive(ref, send_sem, recv_sem, target):
        remote(ref, ref, send_sem, recv_sem, target).wait_recv()

    def put(src, dst):
        copy = pltpu.make_async_copy(src, dst, out_sem.at[len(outs)])
        copy.start()
        outs.append(copy)

    stage, own_q = [], []
    for j in range(3):
        base, dst = 2 * j * half_q, pl.ds(j * half_q, half_q)
        stage.append(fetch(wq_hbm.at[:, pl.ds(base + (1 - s) * half_q, half_q)], stq.at[:, dst]))
        own_q.append(fetch(wq_hbm.at[:, pl.ds(base + s * half_q, half_q)], wq.at[s, z, y, c, :, dst]))
    get_tok = [fetch(tok_hbm.at[i], gd.at[pl.ds(2 * i, 2)]) for i in range(2)]
    own_o = fetch(wo_hbm, wo.at[z, y, c])
    stage_u = fetch(wu_hbm.at[:, pl.ds((1 - s) * half_u, half_u)], stu)
    own_u = fetch(wu_hbm.at[:, pl.ds(s * half_u, half_u)], wu.at[s, z, y, c])
    own_d = fetch(wd_hbm, wd.at[z, y, c])

    def down_half(i):
        return pl.ds(half_d * i, half_d)

    blocks = [
        lambda zz, yy, cc: wq.at[s, zz, yy, cc],
        lambda zz, yy, cc: wq.at[1 - s, zz, yy, cc],
        lambda zz, yy, cc: gv.at[zz, yy, cc],
        lambda zz, yy, cc: wo.at[zz, yy, cc],
        lambda zz, yy, cc: wu.at[s, zz, yy, cc],
        lambda zz, yy, cc: wu.at[1 - s, zz, yy, cc],
        lambda zz, yy, cc: wd.at[zz, yy, cc, down_half(0)],
        lambda zz, yy, cc: wd.at[zz, yy, cc, down_half(1)],
    ]
    lines = [
        lambda yy, cc: wq.at[s, :, yy, cc],
        lambda yy, cc: wq.at[1 - s, :, yy, cc],
        lambda yy, cc: gv.at[:, yy, cc],
        lambda yy, cc: wo.at[:, yy, cc],
        lambda yy, cc: wu.at[s, :, yy, cc],
        lambda yy, cc: wu.at[1 - s, :, yy, cc],
        lambda yy, cc: wd.at[:, yy, cc, down_half(0)],
        lambda yy, cc: wd.at[:, yy, cc, down_half(1)],
    ]
    Q_OWN, Q_SWAP, VEC, OUT, U_OWN, U_SWAP, D_0, D_1 = range(8)

    def spread(p):
        own = blocks[p](z, y, c)
        send(own, own, wz.at[p, 0], vz.at[p, 0], fdev)
        send(own, own, wz.at[p, 1], vz.at[p, 1], ndev)

    def spread_y(p):
        own = blocks[p](z, y, c)
        send(own, own, wy.at[p, 0], vy.at[p, 0], ydev)

    def after_far(p):
        ref = blocks[p](far, y, c)
        arrive(ref, wz.at[p, 0], vz.at[p, 0], fdev)
        send(ref, ref, wz.at[p, 2], vz.at[p, 2], ndev)
        send(ref, ref, wy.at[p, 1], vy.at[p, 1], ydev)

    def after_near(p):
        for i, zz in ((1, near), (2, LINE - 1 - near)):
            ref = blocks[p](zz, y, c)
            arrive(ref, wz.at[p, i], vz.at[p, i], ndev)
            send(ref, ref, wy.at[p, i + 1], vy.at[p, i + 1], ydev)
        line = lines[p](y, c)
        send(line, line, wc.at[p, 0], vc.at[p, 0], cdev)

    def after_y(p):
        for i, zz in enumerate((z, far, near, LINE - 1 - near)):
            arrive(blocks[p](zz, 1 - y, c), wy.at[p, i], vy.at[p, i], ydev)
        line = lines[p](1 - y, c)
        send(line, line, wc.at[p, 1], vc.at[p, 1], cdev)

    def after_c(p):
        for i, yy in enumerate((y, 1 - y)):
            arrive(lines[p](yy, 1 - c), wc.at[p, i], vc.at[p, i], cdev)

    def both(zz, cc):
        return wd.at[zz, :, cc, down_half(1)]

    def after_first_y():
        arrive(blocks[D_1](z, 1 - y, c), wy.at[D_1, 0], vy.at[D_1, 0], ydev)
        own = both(z, c)
        send(own, own, wz.at[D_1, 0], vz.at[D_1, 0], fdev)
        send(own, own, wz.at[D_1, 1], vz.at[D_1, 1], ndev)

    def after_first_far():
        ref = both(far, c)
        arrive(ref, wz.at[D_1, 0], vz.at[D_1, 0], fdev)
        send(ref, ref, wz.at[D_1, 2], vz.at[D_1, 2], ndev)

    def after_first_near():
        for i, zz in ((1, near), (2, LINE - 1 - near)):
            arrive(both(zz, c), wz.at[D_1, i], vz.at[D_1, i], ndev)
        ref = wd.at[:, :, c, down_half(1)]
        send(ref, ref, wc.at[D_1, 0], vc.at[D_1, 0], cdev)

    def after_first_c():
        arrive(wd.at[:, :, 1 - c, down_half(1)], wc.at[D_1, 0], vc.at[D_1, 0], cdev)

    spans = [pl.ds(0, 2 * part), pl.ds(2 * part, 2 * part), None, None]
    spans += [pl.ds(i * part, part) for i in range(4)]
    parts = [
        (lambda cc, i=i: gu.at[i - 2, :, :, cc]) if q is None else (lambda cc, q=q: gd.at[:, :, cc, q])
        for i, q in enumerate(spans)
    ]
    land_c = [rcu.at[i - 2] if q is None else rcd.at[:, :, q] for i, q in enumerate(spans)]
    land_y = [ryu.at[i - 2] if q is None else ryd.at[:, q] for i, q in enumerate(spans)]
    land_z = [rzu.at[i - 2] if q is None else rzd.at[:, q] for i, q in enumerate(spans)]

    def c_start(k):
        return send(parts[k](1 - c), land_c[k], gc.at[k], hc.at[k], cdev)

    def c_end(k):
        ref, own = land_c[k], parts[k](c)
        if k < 2:
            for t in range(LINE):
                arrive(ref.at[t], gt.at[k, t], ht.at[k, t], cdev)
        else:
            arrive(ref, gc.at[k], hc.at[k], cdev)

        def add(i, carry):
            ref[i] = (ref[i].astype(f32) + own[i].astype(f32)).astype(bf16)
            return carry

        lax.fori_loop(0, LINE, add, 0)
        if k == 0:
            return [
                send(ref.at[LINE - 1 - near], rzb.at[1], gz.at[k, 1], hz.at[k, 1], ndev),
                send(ref.at[near], rzb.at[0], gz.at[k, 0], hz.at[k, 0], ndev),
            ]
        return [send(ref.at[:, 1 - y], land_y[k], gy.at[k], hy.at[k], ydev)]

    def y_end(k):
        ref, own = land_y[k], land_c[k]
        arrive(ref, gy.at[k], hy.at[k], ydev)

        def add(i, carry):
            ref[i] = (ref[i].astype(f32) + own[i, y].astype(f32)).astype(bf16)
            return carry

        lax.fori_loop(0, LINE, add, 0)
        return [
            send(ref.at[LINE - 1 - near], land_z[k].at[1], gz.at[k, 1], hz.at[k, 1], ndev),
            send(ref.at[near], land_z[k].at[0], gz.at[k, 0], hz.at[k, 0], ndev),
        ]

    def z_mid(k):
        ref = land_z[k].at[1]
        arrive(ref, gz.at[k, 1], hz.at[k, 1], ndev)
        ref[...] = (ref[...].astype(f32) + land_y[k][far].astype(f32)).astype(bf16)
        return send(ref, land_z[k].at[2], gz.at[k, 2], hz.at[k, 2], fdev)

    def z_end(k):
        arrive(land_z[k].at[0], gz.at[k, 0], hz.at[k, 0], ndev)
        arrive(land_z[k].at[2], gz.at[k, 2], hz.at[k, 2], fdev)
        return land_y[k][z].astype(f32) + land_z[k][0].astype(f32) + land_z[k][2].astype(f32)

    def first_mid():
        arrive(rzb.at[1], gz.at[0, 1], hz.at[0, 1], ndev)
        rzb[1] = (rzb[1].astype(f32) + land_c[0][far].astype(f32)).astype(bf16)
        return send(rzb.at[1], rzb.at[2], gz.at[0, 2], hz.at[0, 2], fdev)

    def first_end():
        arrive(rzb.at[0], gz.at[0, 0], hz.at[0, 0], ndev)
        arrive(rzb.at[2], gz.at[0, 2], hz.at[0, 2], fdev)
        rzb[0] = (land_c[0][z].astype(f32) + rzb[0].astype(f32) + rzb[2].astype(f32)).astype(bf16)
        return send(rzb.at[0, 1 - y], ryb, gy.at[0], hy.at[0], ydev)

    def first_sum():
        arrive(ryb, gy.at[0], hy.at[0], ydev)
        return rzb[0, y].astype(f32) + ryb[...].astype(f32)

    lane = lax.broadcasted_iota(jnp.int32, (part, model), 1)
    fits = (lax.rem(lane, part) == lax.broadcasted_iota(jnp.int32, (part, model), 0)) & (
        lane // part == s * 4 * LINE + z * 4 + y * 2 + c
    )
    line = lax.broadcasted_iota(jnp.int32, (16, part), 0)
    small = jnp.zeros((16, part), f32)
    for j, ref in enumerate((one_ref, two_ref, three_ref)):
        small = jnp.where(line == j, ref[...].astype(f32), small)
    stv[...] = dot_nn(small.astype(bf16), jnp.where(fits, 1.0, 0.0).astype(bf16)).astype(bf16)

    rank = lax.broadcasted_iota(jnp.int32, (1, ranks), 1)
    for i in range(2):
        live[i : i + 1] = jnp.where(rank < len_ref[i] // 8, routed_ref[i : i + 1], -1)

    def chooser(i):
        row = live[i : i + 1].astype(f32)
        eye = lax.broadcasted_iota(jnp.int32, (ranks, ranks), 0) == lax.broadcasted_iota(
            jnp.int32, (ranks, ranks), 1
        )
        column = jnp.sum(jnp.where(eye, row, 0.0), axis=1, keepdims=True).astype(jnp.int32)
        count_here = tok_hbm.shape[1] * 512
        position = lax.broadcasted_iota(jnp.int32, (ranks, count_here), 1) + s * count_here
        return jnp.where(position == column, 1.0, 0.0).astype(bf16)

    def pick(i, dst):
        dst[i] = dot_nn(chooser(i), gd[2 * i : 2 * i + 2].reshape(tok_hbm.shape[1] * 512, model)).astype(bf16)

    def live_column(i):
        rank = lax.broadcasted_iota(jnp.int32, (ranks, 1), 0)
        return jnp.where(rank < len_ref[i] // 8, 1.0, 0.0).astype(f32)

    def allowed(i):
        query = lax.broadcasted_iota(jnp.int32, (ranks, ranks), 0)
        key = lax.broadcasted_iota(jnp.int32, (ranks, ranks), 1)
        return (key <= query) & (key < len_ref[i] // 8)

    greet([xdev, ydev, cdev, ndev, fdev])
    swap_v = send(stv, rcv, sx.at[0], rx.at[0], xdev)
    for copy in stage:
        copy.wait()
    send(stq, wq.at[s, z, y, c], sx.at[1], rx.at[1], xdev)
    for copy in own_q:
        copy.wait()
    spread(Q_OWN)
    spread_y(Q_OWN)
    own_d.wait()
    spread_y(D_1)
    x_swap = []
    get_tok[0].wait()
    pick(0, xs)
    x_swap.append(send(xs.at[0], xr.at[0], sx.at[3], rx.at[3], xdev))
    get_cot = [fetch(cot_hbm.at[0], gd.at[pl.ds(0, 2)])]
    stage_u.wait()
    send(stu, wu.at[s, z, y, c], sx.at[2], rx.at[2], xdev)
    get_tok[1].wait()
    pick(1, xs)
    x_swap.append(send(xs.at[1], xr.at[1], sx.at[4], rx.at[4], xdev))
    get_cot.append(fetch(cot_hbm.at[1], gd.at[pl.ds(2, 2)]))
    put(live, live_out)
    swap_v.wait_recv()
    gv[z, y, c] = stv[...] + rcv[...]
    after_far(Q_OWN)
    spread(VEC)
    spread_y(VEC)
    arrive(wq.at[1 - s, z, y, c], sx.at[1], rx.at[1], xdev)
    spread(Q_SWAP)
    spread_y(Q_SWAP)
    get_cot[0].wait()
    pick(0, ds)
    d_swap = [send(ds.at[0], dr.at[0], sx.at[7], rx.at[7], xdev)]
    after_near(Q_OWN)
    after_far(VEC)
    get_cot[1].wait()
    pick(1, ds)
    after_far(Q_SWAP)
    own_o.wait()
    spread(OUT)
    after_near(VEC)
    after_near(Q_SWAP)
    after_far(OUT)
    spread_y(OUT)
    own_u.wait()
    spread(U_OWN)
    spread_y(U_OWN)
    arrive(wu.at[1 - s, z, y, c], sx.at[2], rx.at[2], xdev)
    spread(U_SWAP)
    after_y(Q_OWN)
    after_y(VEC)
    after_c(Q_OWN)
    after_c(VEC)
    after_near(OUT)
    after_y(Q_SWAP)
    after_far(U_OWN)
    spread(D_0)
    spread_y(U_SWAP)
    spread_y(D_0)
    after_c(Q_SWAP)

    gains[...] = jnp.sum(gv[...].astype(f32).reshape(4 * LINE, 16, model), axis=0)
    gain_one, gain_two, router = gains[0:1], gains[1:2], gains[2:3]

    def enter(i):
        x_swap[i].wait()
        row = xr[i].astype(f32) + xs[i].astype(f32)
        xr[i] = row.astype(bf16)
        xs[i] = (row * inverse_rms(row) * gain_one).astype(bf16)
        for j in range(3):
            cols = pl.ds(j * half_q, half_q)
            qkv[i, :, cols] = dot_nn(xs[i], wq[:, :, :, :, :, cols].reshape(model, half_q)).astype(bf16)

    def attend(i):
        ok = allowed(i)

        def pair(j, carry):
            q2 = qkv[i, :, pl.ds(j * 128, 128)].astype(f32)
            k2 = qkv[i, :, pl.ds(half_q + j * 128, 128)]
            v2 = qkv[i, :, pl.ds(2 * half_q + j * 128, 128)]
            mixed = jnp.zeros(q2.shape, f32)
            for parity in range(2):
                mask = head_mask(parity)
                score = dot_nt((q2 * mask).astype(bf16), k2) * (HEAD_DIM**-0.5)
                score = jnp.where(ok, score, -1000000000.0)
                weight = jnp.exp(score - jnp.max(score, axis=-1, keepdims=True))
                total = jnp.sum(weight, axis=-1, keepdims=True)
                mixed += dot_nn(weight.astype(bf16), v2) / total * mask
            att[i, :, pl.ds(j * 128, 128)] = mixed.astype(bf16)
            return carry

        lax.fori_loop(0, half_q // 128, pair, 0)

    def leave(i):
        for j in range(2):
            cols = pl.ds(j * half, half)
            a_s[i, :, cols] = dot_nn(att[i], wo[:, :, :, :, cols].reshape(half_q, half)).astype(bf16)
        return send(a_s.at[i], a_r.at[i], sx.at[5 + i], rx.at[5 + i], xdev)

    enter(0)
    attend(0)
    after_y(OUT)
    after_c(OUT)
    a_swap = [leave(0)]
    after_far(U_SWAP)
    after_first_y()
    after_near(U_OWN)
    enter(1)
    attend(1)
    a_swap.append(leave(1))
    d_swap.append(send(ds.at[1], dr.at[1], sx.at[8], rx.at[8], xdev))
    after_far(D_0)
    after_near(U_SWAP)
    after_y(U_OWN)
    after_c(U_OWN)

    def mlp_up(i):
        a_swap[i].wait()
        row = xr[i].astype(f32) + (a_s[i].astype(f32) + a_r[i].astype(f32))
        hid[i] = row
        a_s[i] = (row * inverse_rms(row) * gain_two).astype(bf16)

        def tile(t, carry):
            cols = pl.ds(t * 512, 512)
            up = dot_nn(a_s[i], wu[:, :, :, :, :, cols].reshape(model, 512))
            curve = jnp.tanh(GELU_C * (up + GELU_K * up * up * up))
            act[i, :, cols] = (0.5 * up * (1.0 + curve)).astype(bf16)
            slope = 0.5 * (1.0 + curve) + 0.5 * up * (1.0 - curve * curve) * (
                GELU_C * (1.0 + 3.0 * GELU_K * up * up)
            )
            gp[i, :, cols] = slope.astype(bf16)
            return carry

        lax.fori_loop(0, half_u // 512, tile, 0)

    def gate_of(i):
        return jax.nn.sigmoid(jnp.sum(xr[i].astype(f32) * router, axis=-1, keepdims=True))

    def cotangent_rows(i):
        d_swap[i].wait()
        row = dr[i].astype(f32) + ds[i].astype(f32)
        dr[i] = row.astype(bf16)
        ds[i] = (gate_of(i) * row).astype(bf16)

    def mlp_back(i):
        def tile(t, carry):
            cols = pl.ds(t * 512, 512)
            back = dot_nt(ds[i], wd[t].reshape(512, model))
            gp[i, :, cols] = (back * gp[i, :, cols].astype(f32)).astype(bf16)
            return carry

        lax.fori_loop(0, half_u // 512, tile, 0)
        for j in range(2):
            cols = pl.ds(j * half, half)
            d2s[i, :, cols] = dot_nt(gp[i], wu[j].reshape(half, half_u)).astype(bf16)
        return send(d2s.at[i], d2r.at[i], sx.at[9 + i], rx.at[9 + i], xdev)

    def mlp_out(i):
        for j in range(2):
            cols = pl.ds(j * half, half)
            m_s[i, :, cols] = dot_nn(act[i], wd[:, :, :, :, cols].reshape(half_u, half)).astype(bf16)

    def mlp_send(i):
        return send(m_s.at[i], m_r.at[i], sx.at[11 + i], rx.at[11 + i], xdev)

    after_y(U_SWAP)
    after_first_far()
    after_c(U_SWAP)
    mlp_up(0)
    after_near(D_0)
    mlp_up(1)
    after_y(D_0)
    after_c(D_0)
    after_first_near()
    after_first_c()
    cotangent_rows(0)
    d2_swap = [mlp_back(0)]
    cotangent_rows(1)

    c_down = []
    for t in range(LINE):
        grad = dot_tn(act[:, :, t * 512 : t * 512 + 512].reshape(rows, 512), ds[...].reshape(rows, model))
        gd[t] = grad.astype(bf16).reshape(gd.shape[1:])
        for k in (1, 0):
            c_down.append(send(gd.at[t, :, 1 - c, spans[k]], land_c[k].at[t], gt.at[k, t], ht.at[k, t], cdev))
    y_down = c_end(1)
    z_first = c_end(0)
    d2_swap.append(mlp_back(1))
    mlp_out(0)
    m_swap = [mlp_send(0)]

    def up_tile(t, carry):
        cols = pl.ds(t * 512, 512)
        grad = dot_tn(a_s[...].reshape(rows, model), gp[:, :, cols].reshape(rows, 512))
        gu[:, :, :, :, :, cols] = grad.astype(bf16).reshape(gu.shape[:5] + (512,))
        return carry

    lax.fori_loop(0, half_u // 512, up_tile, 0)
    c_start(2)
    c_start(3)
    mlp_out(1)
    m_swap.append(mlp_send(1))

    def hidden_back(i):
        d2_swap[i].wait()
        back = d2s[i].astype(f32) + d2r[i].astype(f32)
        row = hid[i]
        r2 = inverse_rms(row)
        scaled = back * gain_two
        step = r2 * scaled - row * (r2 * r2 * r2 * jnp.mean(scaled * row, axis=-1, keepdims=True))
        dh[i] = step
        gp[i, :, 0:model] = (gate_of(i) * dr[i].astype(f32) + step).astype(bf16)
        gp[i, :, model : model + half_q] = dot_nt(gp[i, :, 0:model], wo[...].reshape(half_q, model)).astype(bf16)
        return jnp.sum(d2s[i].astype(f32) * row * r2, axis=0, keepdims=True)

    def attend_back(i):
        ok = allowed(i)
        scale = HEAD_DIM**-0.5

        def pair(j, carry):
            q2 = qkv[i, :, pl.ds(j * 128, 128)]
            k2 = qkv[i, :, pl.ds(half_q + j * 128, 128)]
            v2 = qkv[i, :, pl.ds(2 * half_q + j * 128, 128)]
            g2 = gp[i, :, pl.ds(model + j * 128, 128)].astype(f32)
            q2f = q2.astype(f32)
            dq2 = jnp.zeros(q2.shape, f32)
            dk2 = jnp.zeros(q2.shape, f32)
            dv2 = jnp.zeros(q2.shape, f32)
            for parity in range(2):
                mask = head_mask(parity)
                score = dot_nt((q2f * mask).astype(bf16), k2) * scale
                score = jnp.where(ok, score, -1000000000.0)
                weight = jnp.exp(score - jnp.max(score, axis=-1, keepdims=True))
                over = 1.0 / jnp.sum(weight, axis=-1, keepdims=True)
                gh = g2 * mask
                dp = dot_nt(gh.astype(bf16), v2)
                prob = weight * over
                delta = jnp.sum(prob * dp, axis=-1, keepdims=True)
                dscore = (prob * (dp - delta)).astype(bf16)
                dq2 += dot_nn(dscore, k2) * mask
                dk2 += dot_tn(dscore, q2) * mask
                dv2 += dot_tn(weight.astype(bf16), (gh * over).astype(bf16))
            act[i, :, pl.ds(j * 128, 128)] = (dq2 * scale).astype(bf16)
            act[i, :, pl.ds(half_q + j * 128, 128)] = (dk2 * scale).astype(bf16)
            act[i, :, pl.ds(2 * half_q + j * 128, 128)] = dv2.astype(bf16)
            return carry

        lax.fori_loop(0, half_q // 128, pair, 0)

    def inner_back(i):
        r1 = inverse_rms(xr[i].astype(f32))
        sums = []
        for j in range(2):
            cols = pl.ds(j * half, half)
            step = dot_nt(act[i, :, 0 : 3 * half_q], wq[j].reshape(half, 3 * half_q))
            d2s[i, :, cols] = step.astype(bf16)
            sums.append(jnp.sum(step * xr[i, :, cols].astype(f32) * r1, axis=0, keepdims=True))
        return send(d2s.at[i], d1r.at[i], sx.at[13 + i], rx.at[13 + i], xdev), sums

    grad_gm = hidden_back(0)
    c_end(2)
    attend_back(0)
    c_end(3)
    z_first.append(first_mid())
    swap_0, sums_0 = inner_back(0)
    z_down = y_end(1)
    grad_gm += hidden_back(1)
    attend_back(1)
    z_down.append(z_mid(1))
    for copy in c_down + z_first:
        gone(copy)
    first_end()
    pl.semaphore_signal(free.at[0], inc=1, device_id=cdev, device_id_type=MESH)
    y_end(2)

    def out_tile(t):
        cols = pl.ds(t * half, half)
        grad = dot_tn(att[...].reshape(rows, half_q), gp[:, :, cols].reshape(rows, half))
        gd[:, :, :, 3 * part :, cols] = grad.astype(bf16).reshape(wo.shape[:4] + (half,))

    def qkv_tile(t):
        grad = dot_tn(xs[...].reshape(rows, model), act[:, :, t * half_q : (t + 1) * half_q].reshape(rows, half_q))
        grad = grad.astype(bf16).reshape(wq.shape[:5] + (half_q,))
        if t < 2:
            gd[:, :, :, 0:part, t * half_q : (t + 1) * half_q] = grad[0]
            gd[:, :, :, part : 2 * part, t * half_q : (t + 1) * half_q] = grad[1]
        else:
            gd[:, :, :, 2 * part : 3 * part, 0:half_q] = grad[0]
            gd[:, :, :, 2 * part : 3 * part, half_q:] = grad[1]

    qkv_tile(0)
    qkv_tile(1)
    pl.semaphore_wait(free.at[0], 1)
    c_start(4)
    c_start(5)
    qkv_tile(2)
    fd[2 * part :] = z_end(1)
    for copy in y_down + z_down:
        gone(copy)
    for target in (ydev, cdev, ndev, fdev):
        pl.semaphore_signal(free.at[1], inc=1, device_id=target, device_id_type=MESH)
    out_tile(0)
    out_tile(1)
    c_end(4)
    c_end(5)
    swap_1, sums_1 = inner_back(1)
    d1_swap = [swap_0, swap_1]
    for j in range(2):
        vs[0:1, j * half : (j + 1) * half] = sums_0[j] + sums_1[j]
    vs[1:2] = grad_gm
    pl.semaphore_wait(free.at[1], 4)
    c_start(6)
    c_start(7)
    z_mid(2)
    c_end(6)
    y_end(3)
    fu[0] = z_end(2)

    grad_router = jnp.zeros((1, model), f32)
    for i in range(2):
        m_swap[i].wait()
        row = xr[i].astype(f32)
        gate = gate_of(i)
        branch = (hid[i] - row) + (m_s[i].astype(f32) + m_r[i].astype(f32))
        m_s[i] = (gate * branch * live_column(i)).astype(bf16)
        slope = jnp.sum(dr[i].astype(f32) * branch, axis=-1, keepdims=True) * gate * (1.0 - gate)
        logit[i] = slope
        grad_router += jnp.sum(row * slope, axis=0, keepdims=True)
    put(m_s, upd_out)
    vs[2:3] = 0.5 * grad_router
    vs[3:8] = jnp.zeros((5, model), f32)
    send(vs, vr.at[0], gc.at[8], hc.at[8], cdev)
    z_mid(3)
    arrive(vr.at[0], gc.at[8], hc.at[8], cdev)
    v_all[0] = vs[...] + vr[0]
    send(v_all.at[0], vr.at[1], gy.at[8], hy.at[8], ydev)
    c_end(7)
    fd[0 : 2 * part] = first_sum()
    put(fd, fd_out)
    y_end(4)
    fu[1] = z_end(3)
    suu[...] = fu[1 - s].astype(bf16)
    send(suu, ruu, sx.at[15], rx.at[15], xdev)
    put(fu.at[s], fu_out.at[:, pl.ds(s * half_u, half_u)])
    z_mid(4)
    y_end(5)

    def rows_back(i):
        d1_swap[i].wait()
        row = xr[i].astype(f32)
        r1 = inverse_rms(row)
        scaled = (d2s[i].astype(f32) + d1r[i].astype(f32)) * gain_one
        step = r1 * scaled - row * (r1 * r1 * r1 * jnp.mean(scaled * row, axis=-1, keepdims=True))
        d2s[i] = (dh[i] + step + logit[i] * router).astype(bf16)
        put(d2s.at[i], dx_out.at[i])

    rows_back(0)
    z_mid(5)
    y_end(6)
    arrive(vr.at[1], gy.at[8], hy.at[8], ydev)
    v_all[1] = v_all[0] + vr[1]
    send(v_all.at[1], vr.at[2], gz.at[8, 0], hz.at[8, 0], ndev)
    z_mid(6)
    y_end(7)
    for i in range(2):
        fqk[i] = z_end(4 + i)
    sqk[...] = fqk[1 - s].astype(bf16)
    send(sqk, rqk, sx.at[16], rx.at[16], xdev)
    for j in range(2):
        put(fqk.at[s, :, pl.ds(j * half_q, half_q)], fq_out.at[:, pl.ds(2 * j * half_q + s * half_q, half_q)])
    arrive(vr.at[2], gz.at[8, 0], hz.at[8, 0], ndev)
    v_all[2] = v_all[1] + vr[2]
    send(v_all.at[2], vr.at[3], gz.at[8, 1], hz.at[8, 1], fdev)
    fv[...] = z_end(6)
    sv[...] = fv[:, pl.ds((1 - s) * half_q, half_q)].astype(bf16)
    send(sv, rv, sx.at[17], rx.at[17], xdev)
    put(fv.at[:, pl.ds(s * half_q, half_q)], fq_out.at[:, pl.ds(4 * half_q + s * half_q, half_q)])
    z_mid(7)
    rows_back(1)
    arrive(vr.at[3], gz.at[8, 1], hz.at[8, 1], fdev)
    v_all[3] = v_all[2] + vr[3]
    send(v_all.at[3], vr.at[4], sx.at[18], rx.at[18], xdev)
    arrive(ruu, sx.at[15], rx.at[15], xdev)
    fu[1 - s] = ruu[...].astype(f32)
    put(fu.at[1 - s], fu_out.at[:, pl.ds((1 - s) * half_u, half_u)])
    arrive(rqk, sx.at[16], rx.at[16], xdev)
    fqk[1 - s] = rqk[...].astype(f32)
    for j in range(2):
        put(
            fqk.at[1 - s, :, pl.ds(j * half_q, half_q)],
            fq_out.at[:, pl.ds(2 * j * half_q + (1 - s) * half_q, half_q)],
        )
    fo[...] = z_end(7)
    put(fo, fo_out)
    arrive(rv, sx.at[17], rx.at[17], xdev)
    fv[:, pl.ds((1 - s) * half_q, half_q)] = rv[...].astype(f32)
    put(
        fv.at[:, pl.ds((1 - s) * half_q, half_q)],
        fq_out.at[:, pl.ds(4 * half_q + (1 - s) * half_q, half_q)],
    )
    arrive(vr.at[4], sx.at[18], rx.at[18], xdev)
    v_all[4] = v_all[3] + vr[4]
    put(v_all.at[4], vec_out)
    waited = x_swap + a_swap + d_swap + d2_swap + m_swap + d1_swap
    for copy in list(sent):
        if not any(copy is other for other in waited):
            copy.wait_send()
    for copy in outs:
        copy.wait()


def rows_kernel(
    tok_hbm, cot_hbm, upd_hbm, dx_hbm, fq_hbm, fo_hbm, fu_hbm, fd_hbm, vec_hbm, live_hbm,
    out_hbm, grad_hbm, fq_out, fo_out, fu_out, fd_out, one_out, two_out, three_out,
    bases, moved, fq, fo, fu, fd, vec_ref, live_ref, one, two, three, get_sem, put_sem, rows_sem, pass_sem,
):
    s = lax.axis_index("seq")
    _, slots, chunks, tall, model = bases.shape
    ranks = moved.shape[2]
    whole = (tok_hbm, cot_hbm), (out_hbm, grad_hbm)
    tasks = [(i, t) for i in range(slots) for t in range(chunks)]

    def part_of(ref, i, t):
        return ref.at[i, pl.ds(t * tall, tall)]

    gets, puts = {}, []
    rows = [
        pltpu.make_async_copy(src.at[i], moved.at[a, i], rows_sem.at[a, i])
        for i in range(slots)
        for a, src in enumerate((upd_hbm, dx_hbm))
    ]
    get_live = pltpu.make_async_copy(live_hbm, live_ref, pass_sem.at[0, 4])
    get_vec = pltpu.make_async_copy(vec_hbm, vec_ref, pass_sem.at[0, 5])
    get_live.start()
    for i, t in tasks:
        for copy in rows[2 * i : 2 * i + 2] if t == 0 else []:
            copy.start()
        for a in range(2):
            gets[a, i, t] = pltpu.make_async_copy(part_of(whole[0][a], i, t), bases.at[a, i, t], get_sem.at[a, i, t])
            gets[a, i, t].start()
    through = ((fq_hbm, fq, fq_out), (fo_hbm, fo, fo_out), (fu_hbm, fu, fu_out), (fd_hbm, fd, fd_out))
    taken = [pltpu.make_async_copy(src, mid, pass_sem.at[0, j]) for j, (src, mid, _) in enumerate(through)]
    passed = [pltpu.make_async_copy(mid, dst, pass_sem.at[1, j]) for j, (_, mid, dst) in enumerate(through)]
    for copy in taken + [get_vec]:
        copy.start()
    get_live.wait()
    for n, (i, t) in enumerate(tasks):
        if n == len(tasks) - 2:
            for j in range(4):
                taken[j].wait()
                passed[j].start()
        position = lax.broadcasted_iota(jnp.int32, (tall, ranks), 0) + ((s * chunks + t) * tall)
        chooser = jnp.where(position == live_ref[i : i + 1], 1.0, 0.0).astype(bf16)
        for a in range(2):
            if t == 0:
                rows[2 * i + a].wait()
            gets[a, i, t].wait()
            bases[a, i, t] += dot_nn(chooser, moved[a, i]).astype(bf16)
            copy = pltpu.make_async_copy(bases.at[a, i, t], part_of(whole[1][a], i, t), put_sem.at[a, i, t])
            copy.start()
            puts.append(copy)
    part = one.shape[1]
    get_vec.wait()
    flat = s * lax.axis_size("batch") + lax.axis_index("batch")
    lane = lax.broadcasted_iota(jnp.int32, (part, model), 1)
    row = lax.broadcasted_iota(jnp.int32, (part, model), 0)
    here = (lane // part == flat) & (lax.rem(lane, part) == row)
    eye = lax.broadcasted_iota(jnp.int32, (part, part), 0) == lax.broadcasted_iota(jnp.int32, (part, part), 1)
    for j, (ref, dst) in enumerate(((one, one_out), (two, two_out), (three, three_out))):
        column = jnp.sum(jnp.where(here, vec_ref[j : j + 1], 0.0), axis=1, keepdims=True)
        ref[...] = jnp.sum(jnp.where(eye, column, 0.0), axis=0, keepdims=True)
        puts.append(pltpu.make_async_copy(ref, dst, pass_sem.at[1, 4 + j]))
        puts[-1].start()
    for copy in passed + puts:
        copy.wait()


def split_device(
    tokens, cotangent, lengths, routed, w_qkv, w_out, w_up, w_down, gain_attn, gain_mlp, router
):
    slots, local_len, model = tokens.shape
    ranks = routed.shape[1]
    half_q, half_u = w_qkv.shape[1] // 6, w_up.shape[1] // 2
    part, down = w_qkv.shape[0], w_down.shape[0]
    hbm = pl.BlockSpec(memory_space=pl.ANY)
    vmem = pl.BlockSpec(memory_space=pltpu.VMEM)
    smem = pl.BlockSpec(memory_space=pltpu.SMEM)
    sds, space, dma = jax.ShapeDtypeStruct, pltpu.VMEM, pltpu.SemaphoreType.DMA
    rows = (slots, ranks, model)
    grid = (LINE, 2, 2)
    wq_shape, wo_shape = (2,) + grid + (part, 3 * half_q), grid + (part, model)
    wu_shape, wd_shape = (2,) + grid + (part, half_u), grid + (down, model)
    blocked = (slots, local_len // 512, 2, 2, 128, model)
    row_bf16 = space(rows, bf16)

    def land(lead, tall, wide):
        return [space(lead + mid + (tall, wide), bf16) for mid in ((LINE, 2), (LINE,), (3,))]

    on_d, on_u = land((), down, model), land((2,), part, half_u)
    grad_shapes = (
        sds((part, 6 * half_q), f32), sds((part, model), f32), sds((part, 2 * half_u), f32), sds((down, model), f32),
    )
    upd, dxr, *sums, vec, live = pl.pallas_call(
        block_kernel,
        out_shape=(sds(rows, bf16), sds(rows, bf16)) + grad_shapes + (sds((8, model), f32), sds(routed.shape, jnp.int32)),
        in_specs=[hbm] * 6 + [vmem] * 4 + [smem],
        out_specs=[hbm] * 8,
        scratch_shapes=[
            space(wq_shape, bf16), space(wo_shape, bf16), space(wu_shape, bf16), space(wd_shape, bf16),
            space(grid + (16, model), bf16),
            space((part, 3 * half_q), bf16), space((part, half_u), bf16), space((16, model), bf16), space((16, model), bf16),
            *[row_bf16] * 11, space(rows, f32), space(rows, f32),
            space((slots, ranks, 3 * half_q), bf16), space((slots, ranks, half_q), bf16),
            space((slots, ranks, half_u), bf16), space((slots, ranks, half_u), bf16),
            space((slots, ranks, 1), f32), space((16, model), f32),
            space(wd_shape, bf16), space(wu_shape, bf16),
            on_d[0], on_u[0], on_d[1], on_u[1], on_d[2], on_u[2],
            space((3, 2, 2 * part, model), bf16), space((2 * part, model), bf16),
            space((2, part, model), f32), space((part, model), f32), space((part, model), f32),
            space((2, part, half_u), f32), space((down, model), f32),
            space((part, model), bf16), space((part, half_q), bf16), space((part, half_u), bf16),
            space((part, model), bf16), space((part, half_q), bf16), space((part, half_u), bf16),
            space((8, model), f32), space((5, 8, model), f32), space((5, 8, model), f32), space(routed.shape, jnp.int32),
            dma((16,)), dma((16,)), dma((8, 3)), dma((8, 3)), dma((8, 4)), dma((8, 4)), dma((8, 2)), dma((8, 2)),
            dma((19,)), dma((19,)), dma((9,)), dma((9,)), dma((2, LINE)), dma((2, LINE)), dma((9,)), dma((9,)), dma((9, 3)), dma((9, 3)),
            pltpu.SemaphoreType.REGULAR((2,)),
        ],
        compiler_params=pltpu.CompilerParams(collective_id=1, has_side_effects=True, vmem_limit_bytes=60 << 20),
        name="block",
    )(
        tokens.reshape(blocked), cotangent.reshape(blocked), w_qkv, w_out, w_up, w_down,
        gain_attn[None], gain_mlp[None], router[None], routed, lengths,
    )

    chunks = 2
    vectors = (sds((1, part), f32),) * 3
    output, input_grad, g_qkv, g_out, g_up, g_down, g_one, g_two, g_three = pl.pallas_call(
        rows_kernel,
        out_shape=(sds(tokens.shape, bf16), sds(tokens.shape, bf16)) + grad_shapes + vectors,
        in_specs=[hbm] * 10,
        out_specs=[hbm] * 9,
        scratch_shapes=[
            space((2, slots, chunks, local_len // chunks, model), bf16), space((2,) + rows, bf16),
            *[space(g.shape, f32) for g in grad_shapes],
            space((8, model), f32), space(routed.shape, jnp.int32), *[space((1, part), f32)] * 3,
            dma((2, slots, chunks)), dma((2, slots, chunks)), dma((2, slots)), dma((2, 7)),
        ],
        compiler_params=pltpu.CompilerParams(vmem_limit_bytes=60 << 20),
        name="rows",
    )(tokens, cotangent, upd, dxr, *sums, vec, live)
    return (
        output, input_grad, g_qkv, g_out, g_up, g_down,
        g_one.reshape(part), g_two.reshape(part), g_three.reshape(part),
    )


def solution(mesh):
    in_specs = (
        P("batch", "seq", None),
        P("batch", "seq", None),
        P("batch"),
        P("batch", None),
        P(("seq", "batch"), None),
        P(("seq", "batch"), None),
        P(("seq", "batch"), None),
        P(("seq", "batch"), None),
        P(("seq", "batch")),
        P(("seq", "batch")),
        P(("seq", "batch")),
    )
    out_specs = (
        P("batch", "seq", None),
        P("batch", "seq", None),
        P(("seq", "batch"), None),
        P(("seq", "batch"), None),
        P(("seq", "batch"), None),
        P(("seq", "batch"), None),
        P(("seq", "batch")),
        P(("seq", "batch")),
        P(("seq", "batch")),
    )
    small_slice = mesh.shape["seq"] == 2 and mesh.shape["batch"] == 4 * LINE
    body = split_device if small_slice else general_device
    return jax.shard_map(body, mesh=mesh, in_specs=in_specs, out_specs=out_specs, check_vma=False)
```

```python
import functools

import jax
import jax.numpy as jnp
from jax import lax
from jax.experimental import pallas as pl
from jax.experimental.pallas import tpu as pltpu
from jax.sharding import PartitionSpec as P

HEAD_DIM = 64
MESH = pl.DeviceIdType.MESH


epsilon = 1e-05
highest = lax.Precision.HIGHEST
f32 = jnp.float32
bf16 = jnp.bfloat16

LINE = 4
GELU_C = 0.7978845608
GELU_K = 0.044715


def dot_nn(a, b):
    return lax.dot_general(a, b, (((1,), (0,)), ((), ())), preferred_element_type=f32)


def dot_nt(a, b):
    return lax.dot_general(a, b, (((1,), (1,)), ((), ())), preferred_element_type=f32)


def dot_tn(a, b):
    return lax.dot_general(a, b, (((0,), (0,)), ((), ())), preferred_element_type=f32)


def place():
    s = lax.axis_index("seq")
    b = lax.axis_index("batch")
    return s, b // 4, lax.rem(b // 2, 2), lax.rem(b, 2)


def device(s, z, y, c):
    return (s, z * 4 + y * 2 + c)


def remote(src, dst, send, recv, target):
    return pltpu.make_async_remote_copy(
        src_ref=src, dst_ref=dst, send_sem=send, recv_sem=recv, device_id=target, device_id_type=MESH
    )


def greet(targets):
    barrier = pltpu.get_barrier_semaphore()
    for target in targets:
        pl.semaphore_signal(barrier, inc=1, device_id=target, device_id_type=MESH)
    pl.semaphore_wait(barrier, len(targets))


def inverse_rms(values):
    return lax.rsqrt(jnp.mean(values * values, axis=-1, keepdims=True) + epsilon)


def head_mask(parity):
    lane = lax.broadcasted_iota(jnp.int32, (1, 128), 1)
    return jnp.where(lane // HEAD_DIM == parity, 1.0, 0.0).astype(f32)


def norm_apply(values_in, gain_vec):
    return (
        values_in
        * lax.rsqrt(jnp.mean(values_in * values_in, axis=-1, keepdims=True) + epsilon)
        * gain_vec
    )


def gelu_tanh(values_in):
    return jax.nn.gelu(values_in, approximate=True)


def general_device(
    tokens, cotangent, lengths, routed, w_qkv, w_out, w_up, w_down, gain_attn, gain_mlp, router
):
    slot_count, local_len, model_width = tokens.shape
    capacity = routed.shape[1]
    seq_devices = lax.axis_size("seq")
    own_count = capacity // seq_devices
    head_count = model_width // HEAD_DIM
    row_count = own_count * slot_count
    score_scale = HEAD_DIM ** (-0.5)
    gathered = (
        lax.all_gather(w_qkv, ("seq", "batch"), axis=0, tiled=True),
        lax.all_gather(w_out, ("seq", "batch"), axis=0, tiled=True),
        lax.all_gather(w_up, ("seq", "batch"), axis=0, tiled=True),
        lax.all_gather(w_down, ("seq", "batch"), axis=0, tiled=True),
        lax.all_gather(gain_attn, ("seq", "batch"), axis=0, tiled=True),
        lax.all_gather(gain_mlp, ("seq", "batch"), axis=0, tiled=True),
        lax.all_gather(router, ("seq", "batch"), axis=0, tiled=True),
    )
    full_qkv, full_out, full_up, full_down, full_ga, full_gm, full_router = gathered
    gain_one = full_ga.astype(f32)
    gain_two = full_gm.astype(f32)
    router_vec = full_router.astype(f32)
    counts = lengths // 8
    seq_place = lax.axis_index("seq")
    positions = seq_place * local_len + jnp.arange(local_len, dtype=jnp.int32)
    rank_all = jnp.arange(capacity, dtype=jnp.int32)
    live_all = rank_all[None, :] < counts[:, None]
    chooser = ((routed[:, :, None] == positions[None, None, :]) & live_all[:, :, None]).astype(bf16)
    pick_in = jnp.einsum("scp,spd->csd", chooser, tokens, preferred_element_type=f32)
    pick_cot = jnp.einsum("scp,spd->csd", chooser, cotangent, preferred_element_type=f32)
    picked, picked_cot = (
        lax.psum_scatter(
            pick_in.astype(jnp.bfloat16), "seq", scatter_dimension=0, tiled=True
        ).astype(jnp.float32),
        lax.psum_scatter(
            pick_cot.astype(jnp.bfloat16), "seq", scatter_dimension=0, tiled=True
        ).astype(jnp.float32),
    )
    own_rank = seq_place * own_count + jnp.arange(own_count, dtype=jnp.int32)
    live_own = own_rank[:, None] < counts[None, :]
    live_mask = live_own.reshape(row_count, 1).astype(f32)
    routed_in = picked.reshape(row_count, model_width)
    normed_one = norm_apply(routed_in, gain_one).astype(bf16)
    joined = jnp.dot(normed_one, full_qkv, preferred_element_type=f32).astype(bf16)
    query_rows = joined[:, :model_width].reshape(own_count, slot_count, head_count, HEAD_DIM)
    key_own = joined[:, model_width : 2 * model_width].reshape(own_count, slot_count, model_width)
    value_own = joined[:, 2 * model_width :].reshape(own_count, slot_count, model_width)
    key_every, value_every = (
        lax.all_gather(key_own, "seq", axis=0, tiled=True),
        lax.all_gather(value_own, "seq", axis=0, tiled=True),
    )
    key_rows = key_every.reshape(capacity, slot_count, head_count, HEAD_DIM)
    value_rows = value_every.reshape(capacity, slot_count, head_count, HEAD_DIM)
    scores = (
        jnp.einsum("qsha,ksha->shqk", query_rows, key_rows, preferred_element_type=f32)
        * score_scale
    )
    causal = rank_all[None, :] <= own_rank[:, None]
    allowed = causal[None, :, :] & (rank_all[None, None, :] < counts[:, None, None])
    scores = jnp.where(allowed[:, None], scores, -1000000000.0)
    row_max = jnp.max(scores, axis=-1, keepdims=True)
    weights_f = jnp.exp(scores - row_max)
    row_total = jnp.sum(weights_f, axis=-1, keepdims=True)
    weights_low = weights_f.astype(bf16)
    mixture = jnp.einsum("shqk,ksha->qsha", weights_low, value_rows, preferred_element_type=f32)
    mixture = mixture / jnp.transpose(row_total, (2, 0, 1, 3))
    attended = mixture.reshape(row_count, model_width).astype(bf16)
    branch_a = jnp.dot(attended, full_out, preferred_element_type=f32)
    hidden = routed_in + branch_a
    normed_two = norm_apply(hidden, gain_two).astype(bf16)
    up_proj = jnp.dot(normed_two, full_up, preferred_element_type=f32)
    activated = gelu_tanh(up_proj).astype(bf16)
    branch_m = jnp.dot(activated, full_down, preferred_element_type=f32)
    gate_prob = jax.nn.sigmoid(jnp.dot(routed_in, router_vec, precision=highest))
    branch = branch_a + branch_m
    update = (
        (gate_prob[:, None] * branch * live_mask)
        .astype(bf16)
        .reshape(own_count, slot_count, model_width)
    )
    update_every = lax.all_gather(update, "seq", axis=0, tiled=True)
    output = (
        tokens.astype(f32)
        + jnp.einsum("scp,csd->spd", chooser, update_every, preferred_element_type=f32)
    ).astype(bf16)
    cot_rows = picked_cot.reshape(row_count, model_width)
    grad_gate = jnp.sum(cot_rows * branch, axis=-1)
    grad_logit = grad_gate * gate_prob * (1.0 - gate_prob)
    grad_branch = gate_prob[:, None] * cot_rows
    grad_m = grad_branch.astype(bf16)
    grad_act = jnp.einsum("rd,fd->rf", grad_m, full_down, preferred_element_type=f32)
    unused_up, gelu_pull = jax.vjp(gelu_tanh, up_proj)
    grad_u = gelu_pull(grad_act)[0].astype(bf16)
    grad_n2 = jnp.einsum("rf,df->rd", grad_u, full_up, preferred_element_type=f32)
    unused_two, norm_pull_two = jax.vjp(norm_apply, hidden, gain_two)
    grad_hidden, grad_gm = norm_pull_two(grad_n2)
    grad_a = (grad_branch + grad_hidden).astype(bf16)
    grad_att = jnp.einsum("rd,ed->re", grad_a, full_out, preferred_element_type=f32).astype(bf16)
    grad_att4 = grad_att.reshape(own_count, slot_count, head_count, HEAD_DIM)
    delta_rows = jnp.sum(grad_att4.astype(f32) * mixture, axis=-1)
    delta = jnp.transpose(delta_rows, (1, 2, 0))[..., None]
    grad_p = jnp.einsum("qsha,ksha->shqk", grad_att4, value_rows, preferred_element_type=f32)
    probs = weights_f / row_total
    grad_s = (probs * (grad_p - delta)).astype(bf16)
    grad_q = (
        jnp.einsum("shqk,ksha->qsha", grad_s, key_rows, preferred_element_type=f32) * score_scale
    )
    grad_k = (
        jnp.einsum("shqk,qsha->ksha", grad_s, query_rows, preferred_element_type=f32) * score_scale
    )
    scaled_low = weights_low.astype(f32) / row_total
    grad_v = jnp.einsum("shqk,qsha->ksha", scaled_low, grad_att4.astype(f32), precision=highest)
    grad_k_own, grad_v_own = (
        lax.psum_scatter(
            grad_k.reshape(capacity, slot_count, model_width).astype(jnp.bfloat16),
            "seq",
            scatter_dimension=0,
            tiled=True,
        ).astype(jnp.float32),
        lax.psum_scatter(
            grad_v.reshape(capacity, slot_count, model_width).astype(jnp.bfloat16),
            "seq",
            scatter_dimension=0,
            tiled=True,
        ).astype(jnp.float32),
    )
    grad_joined = jnp.concatenate(
        [
            grad_q.reshape(row_count, model_width),
            grad_k_own.reshape(row_count, model_width),
            grad_v_own.reshape(row_count, model_width),
        ],
        axis=-1,
    ).astype(bf16)
    grad_n1 = jnp.einsum("re,de->rd", grad_joined, full_qkv, preferred_element_type=f32)
    unused_one, norm_pull_one = jax.vjp(norm_apply, routed_in, gain_one)
    grad_x1, grad_ga = norm_pull_one(grad_n1)
    grad_router = jnp.sum(routed_in * grad_logit[:, None], axis=0)
    grad_rows = (grad_hidden + grad_x1 + grad_logit[:, None] * router_vec[None, :]).astype(bf16)
    grad_rows = grad_rows.reshape(own_count, slot_count, model_width)
    grad_every = lax.all_gather(grad_rows, "seq", axis=0, tiled=True)
    input_grad = (
        cotangent.astype(f32)
        + jnp.einsum("scp,csd->spd", chooser, grad_every, preferred_element_type=f32)
    ).astype(bf16)
    part_qkv = jnp.einsum("rd,re->de", normed_one, grad_joined, preferred_element_type=f32)
    part_out = jnp.einsum("re,rd->ed", attended, grad_a, preferred_element_type=f32)
    part_up = jnp.einsum("rd,rf->df", normed_two, grad_u, preferred_element_type=f32)
    part_down = jnp.einsum("rf,rd->fd", activated, grad_m, preferred_element_type=f32)

    def sum_rows(part):
        return lax.psum_scatter(
            part.astype(bf16), ("seq", "batch"), scatter_dimension=0, tiled=True
        ).astype(f32)

    down_sum = sum_rows(part_down)
    grad_up = sum_rows(part_up)
    grad_out = sum_rows(part_out)
    grad_qkv = sum_rows(part_qkv)
    small_ga, small_gm, small_router = (
        lax.psum_scatter(grad_ga, ("seq", "batch"), scatter_dimension=0, tiled=True),
        lax.psum_scatter(grad_gm, ("seq", "batch"), scatter_dimension=0, tiled=True),
        lax.psum_scatter(grad_router, ("seq", "batch"), scatter_dimension=0, tiled=True),
    )
    return (
        output,
        input_grad,
        grad_qkv,
        grad_out,
        grad_up,
        down_sum,
        small_ga,
        small_gm,
        small_router,
    )


def block_kernel(
    tok_hbm, cot_hbm, wq_hbm, wo_hbm, wu_hbm, wd_hbm, one_ref, two_ref, three_ref, routed_ref, len_ref,
    upd_out, dx_out, fq_out, fo_out, fu_out, fd_out, vec_out, live_out,
    wq, wo, wu, wd, gv, stq, stu, stv, rcv,
    xs, xr, ds, dr, a_s, a_r, d2s, d2r, d1r, m_s, m_r, hid, dh, qkv, att, act, gp, logit, gains,
    gd, gu, rcd, rcu, ryd, ryu, rzd, rzu, rzb, ryb,
    fqk, fv, fo, fu, fd, sqk, sv, suu, rqk, rv, ruu, vs, vr, v_all, live,
    loc, out_sem, wz, vz, wy, vy, wc, vc, sx, rx, gc, hc, gt, ht, gy, hy, gz, hz, free,
):
    s, z, y, c = place()
    near, far = z + 1 - 2 * lax.rem(z, 2), LINE - 1 - z
    xdev, ydev, cdev = device(1 - s, z, y, c), device(s, z, 1 - y, c), device(s, z, y, 1 - c)
    ndev, fdev = device(s, near, y, c), device(s, far, y, c)
    model, half_q, half_u = xr.shape[2], att.shape[2], act.shape[2]
    ranks, half = xr.shape[1], xr.shape[2] // 2
    rows = xr.shape[0] * ranks
    part, half_d = stq.shape[0], wd.shape[3] // 2
    local, sent, outs = [], [], []

    def fetch(src, dst):
        copy = pltpu.make_async_copy(src, dst, loc.at[len(local)])
        copy.start()
        local.append(copy)
        return copy

    def send(src, dst, send_sem, recv_sem, target):
        copy = remote(src, dst, send_sem, recv_sem, target)
        copy.start()
        sent.append(copy)
        return copy

    def gone(copy):
        copy.wait_send()
        sent[:] = [other for other in sent if other is not copy]

    def arrive(ref, send_sem, recv_sem, target):
        remote(ref, ref, send_sem, recv_sem, target).wait_recv()

    def put(src, dst):
        copy = pltpu.make_async_copy(src, dst, out_sem.at[len(outs)])
        copy.start()
        outs.append(copy)

    stage, own_q = [], []
    for j in range(3):
        base, dst = 2 * j * half_q, pl.ds(j * half_q, half_q)
        stage.append(fetch(wq_hbm.at[:, pl.ds(base + (1 - s) * half_q, half_q)], stq.at[:, dst]))
        own_q.append(fetch(wq_hbm.at[:, pl.ds(base + s * half_q, half_q)], wq.at[s, z, y, c, :, dst]))
    get_tok = [fetch(tok_hbm.at[i], gd.at[pl.ds(2 * i, 2)]) for i in range(2)]
    own_o = fetch(wo_hbm, wo.at[z, y, c])
    stage_u = fetch(wu_hbm.at[:, pl.ds((1 - s) * half_u, half_u)], stu)
    own_u = fetch(wu_hbm.at[:, pl.ds(s * half_u, half_u)], wu.at[s, z, y, c])
    own_d = fetch(wd_hbm, wd.at[z, y, c])

    def down_half(i):
        return pl.ds(half_d * i, half_d)

    blocks = [
        lambda zz, yy, cc: wq.at[s, zz, yy, cc],
        lambda zz, yy, cc: wq.at[1 - s, zz, yy, cc],
        lambda zz, yy, cc: gv.at[zz, yy, cc],
        lambda zz, yy, cc: wo.at[zz, yy, cc],
        lambda zz, yy, cc: wu.at[s, zz, yy, cc],
        lambda zz, yy, cc: wu.at[1 - s, zz, yy, cc],
        lambda zz, yy, cc: wd.at[zz, yy, cc, down_half(0)],
        lambda zz, yy, cc: wd.at[zz, yy, cc, down_half(1)],
    ]
    lines = [
        lambda yy, cc: wq.at[s, :, yy, cc],
        lambda yy, cc: wq.at[1 - s, :, yy, cc],
        lambda yy, cc: gv.at[:, yy, cc],
        lambda yy, cc: wo.at[:, yy, cc],
        lambda yy, cc: wu.at[s, :, yy, cc],
        lambda yy, cc: wu.at[1 - s, :, yy, cc],
        lambda yy, cc: wd.at[:, yy, cc, down_half(0)],
        lambda yy, cc: wd.at[:, yy, cc, down_half(1)],
    ]
    Q_OWN, Q_SWAP, VEC, OUT, U_OWN, U_SWAP, D_0, D_1 = range(8)

    def spread(p):
        own = blocks[p](z, y, c)
        send(own, own, wz.at[p, 0], vz.at[p, 0], fdev)
        send(own, own, wz.at[p, 1], vz.at[p, 1], ndev)

    def spread_y(p):
        own = blocks[p](z, y, c)
        send(own, own, wy.at[p, 0], vy.at[p, 0], ydev)

    def after_far(p):
        ref = blocks[p](far, y, c)
        arrive(ref, wz.at[p, 0], vz.at[p, 0], fdev)
        send(ref, ref, wz.at[p, 2], vz.at[p, 2], ndev)
        send(ref, ref, wy.at[p, 1], vy.at[p, 1], ydev)

    def after_near(p):
        for i, zz in ((1, near), (2, LINE - 1 - near)):
            ref = blocks[p](zz, y, c)
            arrive(ref, wz.at[p, i], vz.at[p, i], ndev)
            send(ref, ref, wy.at[p, i + 1], vy.at[p, i + 1], ydev)
        line = lines[p](y, c)
        send(line, line, wc.at[p, 0], vc.at[p, 0], cdev)

    def after_y(p):
        for i, zz in enumerate((z, far, near, LINE - 1 - near)):
            arrive(blocks[p](zz, 1 - y, c), wy.at[p, i], vy.at[p, i], ydev)
        line = lines[p](1 - y, c)
        send(line, line, wc.at[p, 1], vc.at[p, 1], cdev)

    def after_c(p):
        for i, yy in enumerate((y, 1 - y)):
            arrive(lines[p](yy, 1 - c), wc.at[p, i], vc.at[p, i], cdev)

    def both(zz, cc):
        return wd.at[zz, :, cc, down_half(1)]

    def after_first_y():
        arrive(blocks[D_1](z, 1 - y, c), wy.at[D_1, 0], vy.at[D_1, 0], ydev)
        own = both(z, c)
        send(own, own, wz.at[D_1, 0], vz.at[D_1, 0], fdev)
        send(own, own, wz.at[D_1, 1], vz.at[D_1, 1], ndev)

    def after_first_far():
        ref = both(far, c)
        arrive(ref, wz.at[D_1, 0], vz.at[D_1, 0], fdev)
        send(ref, ref, wz.at[D_1, 2], vz.at[D_1, 2], ndev)

    def after_first_near():
        for i, zz in ((1, near), (2, LINE - 1 - near)):
            arrive(both(zz, c), wz.at[D_1, i], vz.at[D_1, i], ndev)
        ref = wd.at[:, :, c, down_half(1)]
        send(ref, ref, wc.at[D_1, 0], vc.at[D_1, 0], cdev)

    def after_first_c():
        arrive(wd.at[:, :, 1 - c, down_half(1)], wc.at[D_1, 0], vc.at[D_1, 0], cdev)

    spans = [pl.ds(0, 2 * part), pl.ds(2 * part, 2 * part), None, None]
    spans += [pl.ds(i * part, part) for i in range(4)]
    parts = [
        (lambda cc, i=i: gu.at[i - 2, :, :, cc]) if q is None else (lambda cc, q=q: gd.at[:, :, cc, q])
        for i, q in enumerate(spans)
    ]
    land_c = [rcu.at[i - 2] if q is None else rcd.at[:, :, q] for i, q in enumerate(spans)]
    land_y = [ryu.at[i - 2] if q is None else ryd.at[:, q] for i, q in enumerate(spans)]
    land_z = [rzu.at[i - 2] if q is None else rzd.at[:, q] for i, q in enumerate(spans)]

    def c_start(k):
        return send(parts[k](1 - c), land_c[k], gc.at[k], hc.at[k], cdev)

    def c_end(k):
        ref, own = land_c[k], parts[k](c)
        if k < 2:
            for t in range(LINE):
                arrive(ref.at[t], gt.at[k, t], ht.at[k, t], cdev)
        else:
            arrive(ref, gc.at[k], hc.at[k], cdev)

        def add(i, carry):
            ref[i] = (ref[i].astype(f32) + own[i].astype(f32)).astype(bf16)
            return carry

        lax.fori_loop(0, LINE, add, 0)
        if k == 0:
            return [
                send(ref.at[LINE - 1 - near], rzb.at[1], gz.at[k, 1], hz.at[k, 1], ndev),
                send(ref.at[near], rzb.at[0], gz.at[k, 0], hz.at[k, 0], ndev),
            ]
        return [send(ref.at[:, 1 - y], land_y[k], gy.at[k], hy.at[k], ydev)]

    def y_end(k):
        ref, own = land_y[k], land_c[k]
        arrive(ref, gy.at[k], hy.at[k], ydev)

        def add(i, carry):
            ref[i] = (ref[i].astype(f32) + own[i, y].astype(f32)).astype(bf16)
            return carry

        lax.fori_loop(0, LINE, add, 0)
        return [
            send(ref.at[LINE - 1 - near], land_z[k].at[1], gz.at[k, 1], hz.at[k, 1], ndev),
            send(ref.at[near], land_z[k].at[0], gz.at[k, 0], hz.at[k, 0], ndev),
        ]

    def z_mid(k):
        ref = land_z[k].at[1]
        arrive(ref, gz.at[k, 1], hz.at[k, 1], ndev)
        ref[...] = (ref[...].astype(f32) + land_y[k][far].astype(f32)).astype(bf16)
        return send(ref, land_z[k].at[2], gz.at[k, 2], hz.at[k, 2], fdev)

    def z_end(k):
        arrive(land_z[k].at[0], gz.at[k, 0], hz.at[k, 0], ndev)
        arrive(land_z[k].at[2], gz.at[k, 2], hz.at[k, 2], fdev)
        return land_y[k][z].astype(f32) + land_z[k][0].astype(f32) + land_z[k][2].astype(f32)

    def first_mid():
        arrive(rzb.at[1], gz.at[0, 1], hz.at[0, 1], ndev)
        rzb[1] = (rzb[1].astype(f32) + land_c[0][far].astype(f32)).astype(bf16)
        return send(rzb.at[1], rzb.at[2], gz.at[0, 2], hz.at[0, 2], fdev)

    def first_end():
        arrive(rzb.at[0], gz.at[0, 0], hz.at[0, 0], ndev)
        arrive(rzb.at[2], gz.at[0, 2], hz.at[0, 2], fdev)
        rzb[0] = (land_c[0][z].astype(f32) + rzb[0].astype(f32) + rzb[2].astype(f32)).astype(bf16)
        return send(rzb.at[0, 1 - y], ryb, gy.at[0], hy.at[0], ydev)

    def first_sum():
        arrive(ryb, gy.at[0], hy.at[0], ydev)
        return rzb[0, y].astype(f32) + ryb[...].astype(f32)

    lane = lax.broadcasted_iota(jnp.int32, (part, model), 1)
    fits = (lax.rem(lane, part) == lax.broadcasted_iota(jnp.int32, (part, model), 0)) & (
        lane // part == s * 4 * LINE + z * 4 + y * 2 + c
    )
    line = lax.broadcasted_iota(jnp.int32, (16, part), 0)
    small = jnp.zeros((16, part), f32)
    for j, ref in enumerate((one_ref, two_ref, three_ref)):
        small = jnp.where(line == j, ref[...].astype(f32), small)
    stv[...] = dot_nn(small.astype(bf16), jnp.where(fits, 1.0, 0.0).astype(bf16)).astype(bf16)

    rank = lax.broadcasted_iota(jnp.int32, (1, ranks), 1)
    for i in range(2):
        live[i : i + 1] = jnp.where(rank < len_ref[i] // 8, routed_ref[i : i + 1], -1)

    def chooser(i):
        row = live[i : i + 1].astype(f32)
        eye = lax.broadcasted_iota(jnp.int32, (ranks, ranks), 0) == lax.broadcasted_iota(
            jnp.int32, (ranks, ranks), 1
        )
        column = jnp.sum(jnp.where(eye, row, 0.0), axis=1, keepdims=True).astype(jnp.int32)
        count_here = tok_hbm.shape[1] * 512
        position = lax.broadcasted_iota(jnp.int32, (ranks, count_here), 1) + s * count_here
        return jnp.where(position == column, 1.0, 0.0).astype(bf16)

    def pick(i, dst):
        dst[i] = dot_nn(chooser(i), gd[2 * i : 2 * i + 2].reshape(tok_hbm.shape[1] * 512, model)).astype(bf16)

    def live_column(i):
        rank = lax.broadcasted_iota(jnp.int32, (ranks, 1), 0)
        return jnp.where(rank < len_ref[i] // 8, 1.0, 0.0).astype(f32)

    def allowed(i):
        query = lax.broadcasted_iota(jnp.int32, (ranks, ranks), 0)
        key = lax.broadcasted_iota(jnp.int32, (ranks, ranks), 1)
        return (key <= query) & (key < len_ref[i] // 8)

    greet([xdev, ydev, cdev, ndev, fdev])
    swap_v = send(stv, rcv, sx.at[0], rx.at[0], xdev)
    for copy in stage:
        copy.wait()
    send(stq, wq.at[s, z, y, c], sx.at[1], rx.at[1], xdev)
    for copy in own_q:
        copy.wait()
    spread(Q_OWN)
    spread_y(Q_OWN)
    own_d.wait()
    spread_y(D_1)
    x_swap = []
    get_tok[0].wait()
    pick(0, xs)
    x_swap.append(send(xs.at[0], xr.at[0], sx.at[3], rx.at[3], xdev))
    get_cot = [fetch(cot_hbm.at[0], gd.at[pl.ds(0, 2)])]
    stage_u.wait()
    send(stu, wu.at[s, z, y, c], sx.at[2], rx.at[2], xdev)
    get_tok[1].wait()
    pick(1, xs)
    x_swap.append(send(xs.at[1], xr.at[1], sx.at[4], rx.at[4], xdev))
    get_cot.append(fetch(cot_hbm.at[1], gd.at[pl.ds(2, 2)]))
    put(live, live_out)
    swap_v.wait_recv()
    gv[z, y, c] = stv[...] + rcv[...]
    after_far(Q_OWN)
    spread(VEC)
    spread_y(VEC)
    arrive(wq.at[1 - s, z, y, c], sx.at[1], rx.at[1], xdev)
    spread(Q_SWAP)
    spread_y(Q_SWAP)
    get_cot[0].wait()
    pick(0, ds)
    d_swap = [send(ds.at[0], dr.at[0], sx.at[7], rx.at[7], xdev)]
    after_near(Q_OWN)
    after_far(VEC)
    get_cot[1].wait()
    pick(1, ds)
    after_far(Q_SWAP)
    own_o.wait()
    spread(OUT)
    after_near(VEC)
    after_near(Q_SWAP)
    after_far(OUT)
    spread_y(OUT)
    own_u.wait()
    spread(U_OWN)
    spread_y(U_OWN)
    arrive(wu.at[1 - s, z, y, c], sx.at[2], rx.at[2], xdev)
    spread(U_SWAP)
    after_y(Q_OWN)
    after_y(VEC)
    after_c(Q_OWN)
    after_c(VEC)
    after_near(OUT)
    after_y(Q_SWAP)
    after_far(U_OWN)
    spread(D_0)
    spread_y(U_SWAP)
    spread_y(D_0)
    after_c(Q_SWAP)

    gains[...] = jnp.sum(gv[...].astype(f32).reshape(4 * LINE, 16, model), axis=0)
    gain_one, gain_two, router = gains[0:1], gains[1:2], gains[2:3]

    def enter(i):
        x_swap[i].wait()
        row = xr[i].astype(f32) + xs[i].astype(f32)
        xr[i] = row.astype(bf16)
        xs[i] = (row * inverse_rms(row) * gain_one).astype(bf16)
        for j in range(3):
            cols = pl.ds(j * half_q, half_q)
            qkv[i, :, cols] = dot_nn(xs[i], wq[:, :, :, :, :, cols].reshape(model, half_q)).astype(bf16)

    def attend(i):
        ok = allowed(i)

        def pair(j, carry):
            q2 = qkv[i, :, pl.ds(j * 128, 128)].astype(f32)
            k2 = qkv[i, :, pl.ds(half_q + j * 128, 128)]
            v2 = qkv[i, :, pl.ds(2 * half_q + j * 128, 128)]
            mixed = jnp.zeros(q2.shape, f32)
            for parity in range(2):
                mask = head_mask(parity)
                score = dot_nt((q2 * mask).astype(bf16), k2) * (HEAD_DIM**-0.5)
                score = jnp.where(ok, score, -1000000000.0)
                weight = jnp.exp(score - jnp.max(score, axis=-1, keepdims=True))
                total = jnp.sum(weight, axis=-1, keepdims=True)
                mixed += dot_nn(weight.astype(bf16), v2) / total * mask
            att[i, :, pl.ds(j * 128, 128)] = mixed.astype(bf16)
            return carry

        lax.fori_loop(0, half_q // 128, pair, 0)

    def leave(i):
        for j in range(2):
            cols = pl.ds(j * half, half)
            a_s[i, :, cols] = dot_nn(att[i], wo[:, :, :, :, cols].reshape(half_q, half)).astype(bf16)
        return send(a_s.at[i], a_r.at[i], sx.at[5 + i], rx.at[5 + i], xdev)

    enter(0)
    attend(0)
    after_y(OUT)
    after_c(OUT)
    a_swap = [leave(0)]
    after_far(U_SWAP)
    after_first_y()
    after_near(U_OWN)
    enter(1)
    attend(1)
    a_swap.append(leave(1))
    d_swap.append(send(ds.at[1], dr.at[1], sx.at[8], rx.at[8], xdev))
    after_far(D_0)
    after_near(U_SWAP)
    after_y(U_OWN)
    after_c(U_OWN)

    def mlp_up(i):
        a_swap[i].wait()
        row = xr[i].astype(f32) + (a_s[i].astype(f32) + a_r[i].astype(f32))
        hid[i] = row
        a_s[i] = (row * inverse_rms(row) * gain_two).astype(bf16)

        def tile(t, carry):
            cols = pl.ds(t * 512, 512)
            up = dot_nn(a_s[i], wu[:, :, :, :, :, cols].reshape(model, 512))
            curve = jnp.tanh(GELU_C * (up + GELU_K * up * up * up))
            act[i, :, cols] = (0.5 * up * (1.0 + curve)).astype(bf16)
            slope = 0.5 * (1.0 + curve) + 0.5 * up * (1.0 - curve * curve) * (
                GELU_C * (1.0 + 3.0 * GELU_K * up * up)
            )
            gp[i, :, cols] = slope.astype(bf16)
            return carry

        lax.fori_loop(0, half_u // 512, tile, 0)

    def gate_of(i):
        return jax.nn.sigmoid(jnp.sum(xr[i].astype(f32) * router, axis=-1, keepdims=True))

    def cotangent_rows(i):
        d_swap[i].wait()
        row = dr[i].astype(f32) + ds[i].astype(f32)
        dr[i] = row.astype(bf16)
        ds[i] = (gate_of(i) * row).astype(bf16)

    def mlp_back(i):
        def tile(t, carry):
            cols = pl.ds(t * 512, 512)
            back = dot_nt(ds[i], wd[t].reshape(512, model))
            gp[i, :, cols] = (back * gp[i, :, cols].astype(f32)).astype(bf16)
            return carry

        lax.fori_loop(0, half_u // 512, tile, 0)
        for j in range(2):
            cols = pl.ds(j * half, half)
            d2s[i, :, cols] = dot_nt(gp[i], wu[j].reshape(half, half_u)).astype(bf16)
        return send(d2s.at[i], d2r.at[i], sx.at[9 + i], rx.at[9 + i], xdev)

    def mlp_out(i):
        for j in range(2):
            cols = pl.ds(j * half, half)
            m_s[i, :, cols] = dot_nn(act[i], wd[:, :, :, :, cols].reshape(half_u, half)).astype(bf16)

    def mlp_send(i):
        return send(m_s.at[i], m_r.at[i], sx.at[11 + i], rx.at[11 + i], xdev)

    after_y(U_SWAP)
    after_first_far()
    after_c(U_SWAP)
    mlp_up(0)
    after_near(D_0)
    cotangent_rows(0)

    def down_tile(t, carry):
        gd[t] = dot_tn(act[0, :, pl.ds(t * 512, 512)], ds[0]).astype(bf16).reshape(gd.shape[1:])
        return carry

    lax.fori_loop(0, LINE, down_tile, 0)
    mlp_up(1)
    after_y(D_0)
    after_c(D_0)
    after_first_near()
    after_first_c()
    d2_swap = [mlp_back(0)]
    cotangent_rows(1)

    c_down = []

    def c_tile(t, k):
        c_down.append(send(gd.at[t, :, 1 - c, spans[k]], land_c[k].at[t], gt.at[k, t], ht.at[k, t], cdev))

    for t in range(LINE):
        grad = dot_tn(act[1, :, t * 512 : t * 512 + 512], ds[1])
        gd[t] = (gd[t].astype(f32) + grad.reshape(gd.shape[1:])).astype(bf16)
        c_tile(t, 1)
    for t in range(LINE):
        c_tile(t, 0)
    y_down = c_end(1)
    z_first = c_end(0)
    d2_swap.append(mlp_back(1))
    mlp_out(0)
    m_swap = [mlp_send(0)]

    def up_tile(t, carry):
        cols = pl.ds(t * 512, 512)
        grad = dot_tn(a_s[...].reshape(rows, model), gp[:, :, cols].reshape(rows, 512))
        gu[:, :, :, :, :, cols] = grad.astype(bf16).reshape(gu.shape[:5] + (512,))
        return carry

    lax.fori_loop(0, half_u // 512, up_tile, 0)
    c_start(2)
    c_start(3)
    mlp_out(1)
    m_swap.append(mlp_send(1))

    def hidden_back(i):
        d2_swap[i].wait()
        back = d2s[i].astype(f32) + d2r[i].astype(f32)
        row = hid[i]
        r2 = inverse_rms(row)
        scaled = back * gain_two
        step = r2 * scaled - row * (r2 * r2 * r2 * jnp.mean(scaled * row, axis=-1, keepdims=True))
        dh[i] = step
        gp[i, :, 0:model] = (gate_of(i) * dr[i].astype(f32) + step).astype(bf16)
        gp[i, :, model : model + half_q] = dot_nt(gp[i, :, 0:model], wo[...].reshape(half_q, model)).astype(bf16)
        return jnp.sum(d2s[i].astype(f32) * row * r2, axis=0, keepdims=True)

    def attend_back(i):
        ok = allowed(i)
        scale = HEAD_DIM**-0.5

        def pair(j, carry):
            q2 = qkv[i, :, pl.ds(j * 128, 128)]
            k2 = qkv[i, :, pl.ds(half_q + j * 128, 128)]
            v2 = qkv[i, :, pl.ds(2 * half_q + j * 128, 128)]
            g2 = gp[i, :, pl.ds(model + j * 128, 128)].astype(f32)
            q2f = q2.astype(f32)
            dq2 = jnp.zeros(q2.shape, f32)
            dk2 = jnp.zeros(q2.shape, f32)
            dv2 = jnp.zeros(q2.shape, f32)
            for parity in range(2):
                mask = head_mask(parity)
                score = dot_nt((q2f * mask).astype(bf16), k2) * scale
                score = jnp.where(ok, score, -1000000000.0)
                weight = jnp.exp(score - jnp.max(score, axis=-1, keepdims=True))
                over = 1.0 / jnp.sum(weight, axis=-1, keepdims=True)
                gh = g2 * mask
                dp = dot_nt(gh.astype(bf16), v2)
                prob = weight * over
                delta = jnp.sum(prob * dp, axis=-1, keepdims=True)
                dscore = (prob * (dp - delta)).astype(bf16)
                dq2 += dot_nn(dscore, k2) * mask
                dk2 += dot_tn(dscore, q2) * mask
                dv2 += dot_tn(weight.astype(bf16), (gh * over).astype(bf16))
            act[i, :, pl.ds(j * 128, 128)] = (dq2 * scale).astype(bf16)
            act[i, :, pl.ds(half_q + j * 128, 128)] = (dk2 * scale).astype(bf16)
            act[i, :, pl.ds(2 * half_q + j * 128, 128)] = dv2.astype(bf16)
            return carry

        lax.fori_loop(0, half_q // 128, pair, 0)

    def inner_back(i):
        r1 = inverse_rms(xr[i].astype(f32))
        sums = []
        for j in range(2):
            cols = pl.ds(j * half, half)
            step = dot_nt(act[i, :, 0 : 3 * half_q], wq[j].reshape(half, 3 * half_q))
            d2s[i, :, cols] = step.astype(bf16)
            sums.append(jnp.sum(step * xr[i, :, cols].astype(f32) * r1, axis=0, keepdims=True))
        return send(d2s.at[i], d1r.at[i], sx.at[13 + i], rx.at[13 + i], xdev), sums

    grad_gm = hidden_back(0)
    c_end(2)
    attend_back(0)
    c_end(3)
    z_first.append(first_mid())
    swap_0, sums_0 = inner_back(0)
    z_down = y_end(1)
    grad_gm += hidden_back(1)
    attend_back(1)
    z_down.append(z_mid(1))
    for copy in c_down + z_first:
        gone(copy)
    first_end()
    pl.semaphore_signal(free.at[0], inc=1, device_id=cdev, device_id_type=MESH)
    y_end(2)

    def out_tile(t):
        cols = pl.ds(t * half, half)
        grad = dot_tn(att[...].reshape(rows, half_q), gp[:, :, cols].reshape(rows, half))
        gd[:, :, :, 3 * part :, cols] = grad.astype(bf16).reshape(wo.shape[:4] + (half,))

    def qkv_tile(t):
        grad = dot_tn(xs[...].reshape(rows, model), act[:, :, t * half_q : (t + 1) * half_q].reshape(rows, half_q))
        grad = grad.astype(bf16).reshape(wq.shape[:5] + (half_q,))
        if t < 2:
            gd[:, :, :, 0:part, t * half_q : (t + 1) * half_q] = grad[0]
            gd[:, :, :, part : 2 * part, t * half_q : (t + 1) * half_q] = grad[1]
        else:
            gd[:, :, :, 2 * part : 3 * part, 0:half_q] = grad[0]
            gd[:, :, :, 2 * part : 3 * part, half_q:] = grad[1]

    qkv_tile(0)
    qkv_tile(1)
    pl.semaphore_wait(free.at[0], 1)
    c_start(4)
    c_start(5)
    qkv_tile(2)
    fd[2 * part :] = z_end(1)
    for copy in y_down + z_down:
        gone(copy)
    for target in (ydev, cdev, ndev, fdev):
        pl.semaphore_signal(free.at[1], inc=1, device_id=target, device_id_type=MESH)
    out_tile(0)
    out_tile(1)
    c_end(4)
    c_end(5)
    swap_1, sums_1 = inner_back(1)
    d1_swap = [swap_0, swap_1]
    for j in range(2):
        vs[0:1, j * half : (j + 1) * half] = sums_0[j] + sums_1[j]
    vs[1:2] = grad_gm
    pl.semaphore_wait(free.at[1], 4)
    c_start(6)
    c_start(7)
    z_mid(2)
    c_end(6)
    y_end(3)
    fu[0] = z_end(2)

    grad_router = jnp.zeros((1, model), f32)
    for i in range(2):
        m_swap[i].wait()
        row = xr[i].astype(f32)
        gate = gate_of(i)
        branch = (hid[i] - row) + (m_s[i].astype(f32) + m_r[i].astype(f32))
        m_s[i] = (gate * branch * live_column(i)).astype(bf16)
        slope = jnp.sum(dr[i].astype(f32) * branch, axis=-1, keepdims=True) * gate * (1.0 - gate)
        logit[i] = slope
        grad_router += jnp.sum(row * slope, axis=0, keepdims=True)
    put(m_s, upd_out)
    vs[2:3] = 0.5 * grad_router
    vs[3:8] = jnp.zeros((5, model), f32)
    send(vs, vr.at[0], gc.at[8], hc.at[8], cdev)
    z_mid(3)
    arrive(vr.at[0], gc.at[8], hc.at[8], cdev)
    v_all[0] = vs[...] + vr[0]
    send(v_all.at[0], vr.at[1], gz.at[8, 0], hz.at[8, 0], ndev)
    c_end(7)
    fd[0 : 2 * part] = first_sum()
    put(fd, fd_out)
    y_end(4)
    fu[1] = z_end(3)
    suu[...] = fu[1 - s].astype(bf16)
    send(suu, ruu, sx.at[15], rx.at[15], xdev)
    put(fu.at[s], fu_out.at[:, pl.ds(s * half_u, half_u)])
    arrive(vr.at[1], gz.at[8, 0], hz.at[8, 0], ndev)
    v_all[1] = v_all[0] + vr[1]
    send(v_all.at[1], vr.at[2], gz.at[8, 1], hz.at[8, 1], fdev)
    z_mid(4)
    y_end(5)

    def rows_back(i):
        d1_swap[i].wait()
        row = xr[i].astype(f32)
        r1 = inverse_rms(row)
        scaled = (d2s[i].astype(f32) + d1r[i].astype(f32)) * gain_one
        step = r1 * scaled - row * (r1 * r1 * r1 * jnp.mean(scaled * row, axis=-1, keepdims=True))
        d2s[i] = (dh[i] + step + logit[i] * router).astype(bf16)
        put(d2s.at[i], dx_out.at[i])

    rows_back(0)
    arrive(vr.at[2], gz.at[8, 1], hz.at[8, 1], fdev)
    v_all[2] = v_all[1] + vr[2]
    send(v_all.at[2], vr.at[3], gy.at[8], hy.at[8], ydev)
    z_mid(5)
    y_end(6)
    z_mid(6)
    y_end(7)
    arrive(vr.at[3], gy.at[8], hy.at[8], ydev)
    v_all[3] = v_all[2] + vr[3]
    send(v_all.at[3], vr.at[4], sx.at[18], rx.at[18], xdev)
    for i in range(2):
        fqk[i] = z_end(4 + i)
    sqk[...] = fqk[1 - s].astype(bf16)
    send(sqk, rqk, sx.at[16], rx.at[16], xdev)
    for j in range(2):
        put(fqk.at[s, :, pl.ds(j * half_q, half_q)], fq_out.at[:, pl.ds(2 * j * half_q + s * half_q, half_q)])
    fv[...] = z_end(6)
    sv[...] = fv[:, pl.ds((1 - s) * half_q, half_q)].astype(bf16)
    send(sv, rv, sx.at[17], rx.at[17], xdev)
    put(fv.at[:, pl.ds(s * half_q, half_q)], fq_out.at[:, pl.ds(4 * half_q + s * half_q, half_q)])
    z_mid(7)
    rows_back(1)
    arrive(ruu, sx.at[15], rx.at[15], xdev)
    fu[1 - s] = ruu[...].astype(f32)
    put(fu.at[1 - s], fu_out.at[:, pl.ds((1 - s) * half_u, half_u)])
    arrive(rqk, sx.at[16], rx.at[16], xdev)
    fqk[1 - s] = rqk[...].astype(f32)
    for j in range(2):
        put(
            fqk.at[1 - s, :, pl.ds(j * half_q, half_q)],
            fq_out.at[:, pl.ds(2 * j * half_q + (1 - s) * half_q, half_q)],
        )
    fo[...] = z_end(7)
    put(fo, fo_out)
    arrive(rv, sx.at[17], rx.at[17], xdev)
    fv[:, pl.ds((1 - s) * half_q, half_q)] = rv[...].astype(f32)
    put(
        fv.at[:, pl.ds((1 - s) * half_q, half_q)],
        fq_out.at[:, pl.ds(4 * half_q + (1 - s) * half_q, half_q)],
    )
    arrive(vr.at[4], sx.at[18], rx.at[18], xdev)
    v_all[4] = v_all[3] + vr[4]
    put(v_all.at[4], vec_out)
    waited = x_swap + a_swap + d_swap + d2_swap + m_swap + d1_swap
    for copy in list(sent):
        if not any(copy is other for other in waited):
            copy.wait_send()
    for copy in outs:
        copy.wait()


def rows_kernel(
    tok_hbm, cot_hbm, upd_hbm, dx_hbm, fq_hbm, fo_hbm, fu_hbm, fd_hbm, vec_hbm, live_hbm,
    out_hbm, grad_hbm, fq_out, fo_out, fu_out, fd_out, one_out, two_out, three_out,
    bases, moved, fq, fo, fu, fd, vec_ref, live_ref, one, two, three, get_sem, put_sem, rows_sem, pass_sem,
):
    s = lax.axis_index("seq")
    _, slots, chunks, tall, model = bases.shape
    ranks = moved.shape[2]
    whole = (tok_hbm, cot_hbm), (out_hbm, grad_hbm)
    tasks = [(i, t) for i in range(slots) for t in range(chunks)]

    def part_of(ref, i, t):
        return ref.at[i, pl.ds(t * tall, tall)]

    gets, puts = {}, []
    rows = [
        pltpu.make_async_copy(src.at[i], moved.at[a, i], rows_sem.at[a, i])
        for i in range(slots)
        for a, src in enumerate((upd_hbm, dx_hbm))
    ]
    get_live = pltpu.make_async_copy(live_hbm, live_ref, pass_sem.at[0, 4])
    get_vec = pltpu.make_async_copy(vec_hbm, vec_ref, pass_sem.at[0, 5])
    get_live.start()
    for i, t in tasks:
        for copy in rows[2 * i : 2 * i + 2] if t == 0 else []:
            copy.start()
        for a in range(2):
            gets[a, i, t] = pltpu.make_async_copy(part_of(whole[0][a], i, t), bases.at[a, i, t], get_sem.at[a, i, t])
            gets[a, i, t].start()
    through = ((fq_hbm, fq, fq_out), (fo_hbm, fo, fo_out), (fu_hbm, fu, fu_out), (fd_hbm, fd, fd_out))
    taken = [pltpu.make_async_copy(src, mid, pass_sem.at[0, j]) for j, (src, mid, _) in enumerate(through)]
    passed = [pltpu.make_async_copy(mid, dst, pass_sem.at[1, j]) for j, (_, mid, dst) in enumerate(through)]
    for copy in taken + [get_vec]:
        copy.start()
    get_live.wait()
    for n, (i, t) in enumerate(tasks):
        if n == len(tasks) - 2:
            for j in range(4):
                taken[j].wait()
                passed[j].start()
        position = lax.broadcasted_iota(jnp.int32, (tall, ranks), 0) + ((s * chunks + t) * tall)
        chooser = jnp.where(position == live_ref[i : i + 1], 1.0, 0.0).astype(bf16)
        for a in range(2):
            if t == 0:
                rows[2 * i + a].wait()
            gets[a, i, t].wait()
            bases[a, i, t] += dot_nn(chooser, moved[a, i]).astype(bf16)
            copy = pltpu.make_async_copy(bases.at[a, i, t], part_of(whole[1][a], i, t), put_sem.at[a, i, t])
            copy.start()
            puts.append(copy)
    part = one.shape[1]
    get_vec.wait()
    flat = s * lax.axis_size("batch") + lax.axis_index("batch")
    lane = lax.broadcasted_iota(jnp.int32, (part, model), 1)
    row = lax.broadcasted_iota(jnp.int32, (part, model), 0)
    here = (lane // part == flat) & (lax.rem(lane, part) == row)
    eye = lax.broadcasted_iota(jnp.int32, (part, part), 0) == lax.broadcasted_iota(jnp.int32, (part, part), 1)
    for j, (ref, dst) in enumerate(((one, one_out), (two, two_out), (three, three_out))):
        column = jnp.sum(jnp.where(here, vec_ref[j : j + 1], 0.0), axis=1, keepdims=True)
        ref[...] = jnp.sum(jnp.where(eye, column, 0.0), axis=0, keepdims=True)
        puts.append(pltpu.make_async_copy(ref, dst, pass_sem.at[1, 4 + j]))
        puts[-1].start()
    for copy in passed + puts:
        copy.wait()


def split_device(
    tokens, cotangent, lengths, routed, w_qkv, w_out, w_up, w_down, gain_attn, gain_mlp, router
):
    slots, local_len, model = tokens.shape
    ranks = routed.shape[1]
    half_q, half_u = w_qkv.shape[1] // 6, w_up.shape[1] // 2
    part, down = w_qkv.shape[0], w_down.shape[0]
    hbm = pl.BlockSpec(memory_space=pl.ANY)
    vmem = pl.BlockSpec(memory_space=pltpu.VMEM)
    smem = pl.BlockSpec(memory_space=pltpu.SMEM)
    sds, space, dma = jax.ShapeDtypeStruct, pltpu.VMEM, pltpu.SemaphoreType.DMA
    rows = (slots, ranks, model)
    grid = (LINE, 2, 2)
    wq_shape, wo_shape = (2,) + grid + (part, 3 * half_q), grid + (part, model)
    wu_shape, wd_shape = (2,) + grid + (part, half_u), grid + (down, model)
    blocked = (slots, local_len // 512, 2, 2, 128, model)
    row_bf16 = space(rows, bf16)

    def land(lead, tall, wide):
        return [space(lead + mid + (tall, wide), bf16) for mid in ((LINE, 2), (LINE,), (3,))]

    on_d, on_u = land((), down, model), land((2,), part, half_u)
    grad_shapes = (
        sds((part, 6 * half_q), f32), sds((part, model), f32), sds((part, 2 * half_u), f32), sds((down, model), f32),
    )
    upd, dxr, *sums, vec, live = pl.pallas_call(
        block_kernel,
        out_shape=(sds(rows, bf16), sds(rows, bf16)) + grad_shapes + (sds((8, model), f32), sds(routed.shape, jnp.int32)),
        in_specs=[hbm] * 6 + [vmem] * 4 + [smem],
        out_specs=[hbm] * 8,
        scratch_shapes=[
            space(wq_shape, bf16), space(wo_shape, bf16), space(wu_shape, bf16), space(wd_shape, bf16),
            space(grid + (16, model), bf16),
            space((part, 3 * half_q), bf16), space((part, half_u), bf16), space((16, model), bf16), space((16, model), bf16),
            *[row_bf16] * 11, space(rows, f32), space(rows, f32),
            space((slots, ranks, 3 * half_q), bf16), space((slots, ranks, half_q), bf16),
            space((slots, ranks, half_u), bf16), space((slots, ranks, half_u), bf16),
            space((slots, ranks, 1), f32), space((16, model), f32),
            space(wd_shape, bf16), space(wu_shape, bf16),
            on_d[0], on_u[0], on_d[1], on_u[1], on_d[2], on_u[2],
            space((3, 2, 2 * part, model), bf16), space((2 * part, model), bf16),
            space((2, part, model), f32), space((part, model), f32), space((part, model), f32),
            space((2, part, half_u), f32), space((down, model), f32),
            space((part, model), bf16), space((part, half_q), bf16), space((part, half_u), bf16),
            space((part, model), bf16), space((part, half_q), bf16), space((part, half_u), bf16),
            space((8, model), f32), space((5, 8, model), f32), space((5, 8, model), f32), space(routed.shape, jnp.int32),
            dma((16,)), dma((16,)), dma((8, 3)), dma((8, 3)), dma((8, 4)), dma((8, 4)), dma((8, 2)), dma((8, 2)),
            dma((19,)), dma((19,)), dma((9,)), dma((9,)), dma((2, LINE)), dma((2, LINE)), dma((9,)), dma((9,)), dma((9, 3)), dma((9, 3)),
            pltpu.SemaphoreType.REGULAR((2,)),
        ],
        compiler_params=pltpu.CompilerParams(collective_id=1, has_side_effects=True, vmem_limit_bytes=60 << 20),
        name="block",
    )(
        tokens.reshape(blocked), cotangent.reshape(blocked), w_qkv, w_out, w_up, w_down,
        gain_attn[None], gain_mlp[None], router[None], routed, lengths,
    )

    chunks = 2
    vectors = (sds((1, part), f32),) * 3
    output, input_grad, g_qkv, g_out, g_up, g_down, g_one, g_two, g_three = pl.pallas_call(
        rows_kernel,
        out_shape=(sds(tokens.shape, bf16), sds(tokens.shape, bf16)) + grad_shapes + vectors,
        in_specs=[hbm] * 10,
        out_specs=[hbm] * 9,
        scratch_shapes=[
            space((2, slots, chunks, local_len // chunks, model), bf16), space((2,) + rows, bf16),
            *[space(g.shape, f32) for g in grad_shapes],
            space((8, model), f32), space(routed.shape, jnp.int32), *[space((1, part), f32)] * 3,
            dma((2, slots, chunks)), dma((2, slots, chunks)), dma((2, slots)), dma((2, 7)),
        ],
        compiler_params=pltpu.CompilerParams(vmem_limit_bytes=60 << 20),
        name="rows",
    )(tokens, cotangent, upd, dxr, *sums, vec, live)
    return (
        output, input_grad, g_qkv, g_out, g_up, g_down,
        g_one.reshape(part), g_two.reshape(part), g_three.reshape(part),
    )


def solution(mesh):
    in_specs = (
        P("batch", "seq", None),
        P("batch", "seq", None),
        P("batch"),
        P("batch", None),
        P(("seq", "batch"), None),
        P(("seq", "batch"), None),
        P(("seq", "batch"), None),
        P(("seq", "batch"), None),
        P(("seq", "batch")),
        P(("seq", "batch")),
        P(("seq", "batch")),
    )
    out_specs = (
        P("batch", "seq", None),
        P("batch", "seq", None),
        P(("seq", "batch"), None),
        P(("seq", "batch"), None),
        P(("seq", "batch"), None),
        P(("seq", "batch"), None),
        P(("seq", "batch")),
        P(("seq", "batch")),
        P(("seq", "batch")),
    )
    small_slice = mesh.shape["seq"] == 2 and mesh.shape["batch"] == 4 * LINE
    body = split_device if small_slice else general_device
    return jax.shard_map(body, mesh=mesh, in_specs=in_specs, out_specs=out_specs, check_vma=False)
```

```python
import functools

import jax
import jax.numpy as jnp
from jax import lax
from jax.experimental import pallas as pl
from jax.experimental.pallas import tpu as pltpu
from jax.sharding import PartitionSpec as P

HEAD_DIM = 64
MESH = pl.DeviceIdType.MESH


epsilon = 1e-05
highest = lax.Precision.HIGHEST
f32 = jnp.float32
bf16 = jnp.bfloat16

LINE = 4
GELU_C = 0.7978845608
GELU_K = 0.044715


def dot_nn(a, b):
    return lax.dot_general(a, b, (((1,), (0,)), ((), ())), preferred_element_type=f32)


def dot_nt(a, b):
    return lax.dot_general(a, b, (((1,), (1,)), ((), ())), preferred_element_type=f32)


def dot_tn(a, b):
    return lax.dot_general(a, b, (((0,), (0,)), ((), ())), preferred_element_type=f32)


def place():
    s = lax.axis_index("seq")
    b = lax.axis_index("batch")
    return s, b // 4, lax.rem(b // 2, 2), lax.rem(b, 2)


def device(s, z, y, c):
    return (s, z * 4 + y * 2 + c)


def remote(src, dst, send, recv, target):
    return pltpu.make_async_remote_copy(
        src_ref=src, dst_ref=dst, send_sem=send, recv_sem=recv, device_id=target, device_id_type=MESH
    )


def greet(targets):
    barrier = pltpu.get_barrier_semaphore()
    for target in targets:
        pl.semaphore_signal(barrier, inc=1, device_id=target, device_id_type=MESH)
    pl.semaphore_wait(barrier, len(targets))


def inverse_rms(values):
    return lax.rsqrt(jnp.mean(values * values, axis=-1, keepdims=True) + epsilon)


def head_mask(parity):
    lane = lax.broadcasted_iota(jnp.int32, (1, 128), 1)
    return jnp.where(lane // HEAD_DIM == parity, 1.0, 0.0).astype(f32)


def norm_apply(values_in, gain_vec):
    return (
        values_in
        * lax.rsqrt(jnp.mean(values_in * values_in, axis=-1, keepdims=True) + epsilon)
        * gain_vec
    )


def gelu_tanh(values_in):
    return jax.nn.gelu(values_in, approximate=True)


def general_device(
    tokens, cotangent, lengths, routed, w_qkv, w_out, w_up, w_down, gain_attn, gain_mlp, router
):
    slot_count, local_len, model_width = tokens.shape
    capacity = routed.shape[1]
    seq_devices = lax.axis_size("seq")
    own_count = capacity // seq_devices
    head_count = model_width // HEAD_DIM
    row_count = own_count * slot_count
    score_scale = HEAD_DIM ** (-0.5)
    gathered = (
        lax.all_gather(w_qkv, ("seq", "batch"), axis=0, tiled=True),
        lax.all_gather(w_out, ("seq", "batch"), axis=0, tiled=True),
        lax.all_gather(w_up, ("seq", "batch"), axis=0, tiled=True),
        lax.all_gather(w_down, ("seq", "batch"), axis=0, tiled=True),
        lax.all_gather(gain_attn, ("seq", "batch"), axis=0, tiled=True),
        lax.all_gather(gain_mlp, ("seq", "batch"), axis=0, tiled=True),
        lax.all_gather(router, ("seq", "batch"), axis=0, tiled=True),
    )
    full_qkv, full_out, full_up, full_down, full_ga, full_gm, full_router = gathered
    gain_one = full_ga.astype(f32)
    gain_two = full_gm.astype(f32)
    router_vec = full_router.astype(f32)
    counts = lengths // 8
    seq_place = lax.axis_index("seq")
    positions = seq_place * local_len + jnp.arange(local_len, dtype=jnp.int32)
    rank_all = jnp.arange(capacity, dtype=jnp.int32)
    live_all = rank_all[None, :] < counts[:, None]
    chooser = ((routed[:, :, None] == positions[None, None, :]) & live_all[:, :, None]).astype(bf16)
    pick_in = jnp.einsum("scp,spd->csd", chooser, tokens, preferred_element_type=f32)
    pick_cot = jnp.einsum("scp,spd->csd", chooser, cotangent, preferred_element_type=f32)
    picked, picked_cot = (
        lax.psum_scatter(
            pick_in.astype(jnp.bfloat16), "seq", scatter_dimension=0, tiled=True
        ).astype(jnp.float32),
        lax.psum_scatter(
            pick_cot.astype(jnp.bfloat16), "seq", scatter_dimension=0, tiled=True
        ).astype(jnp.float32),
    )
    own_rank = seq_place * own_count + jnp.arange(own_count, dtype=jnp.int32)
    live_own = own_rank[:, None] < counts[None, :]
    live_mask = live_own.reshape(row_count, 1).astype(f32)
    routed_in = picked.reshape(row_count, model_width)
    normed_one = norm_apply(routed_in, gain_one).astype(bf16)
    joined = jnp.dot(normed_one, full_qkv, preferred_element_type=f32).astype(bf16)
    query_rows = joined[:, :model_width].reshape(own_count, slot_count, head_count, HEAD_DIM)
    key_own = joined[:, model_width : 2 * model_width].reshape(own_count, slot_count, model_width)
    value_own = joined[:, 2 * model_width :].reshape(own_count, slot_count, model_width)
    key_every, value_every = (
        lax.all_gather(key_own, "seq", axis=0, tiled=True),
        lax.all_gather(value_own, "seq", axis=0, tiled=True),
    )
    key_rows = key_every.reshape(capacity, slot_count, head_count, HEAD_DIM)
    value_rows = value_every.reshape(capacity, slot_count, head_count, HEAD_DIM)
    scores = (
        jnp.einsum("qsha,ksha->shqk", query_rows, key_rows, preferred_element_type=f32)
        * score_scale
    )
    causal = rank_all[None, :] <= own_rank[:, None]
    allowed = causal[None, :, :] & (rank_all[None, None, :] < counts[:, None, None])
    scores = jnp.where(allowed[:, None], scores, -1000000000.0)
    row_max = jnp.max(scores, axis=-1, keepdims=True)
    weights_f = jnp.exp(scores - row_max)
    row_total = jnp.sum(weights_f, axis=-1, keepdims=True)
    weights_low = weights_f.astype(bf16)
    mixture = jnp.einsum("shqk,ksha->qsha", weights_low, value_rows, preferred_element_type=f32)
    mixture = mixture / jnp.transpose(row_total, (2, 0, 1, 3))
    attended = mixture.reshape(row_count, model_width).astype(bf16)
    branch_a = jnp.dot(attended, full_out, preferred_element_type=f32)
    hidden = routed_in + branch_a
    normed_two = norm_apply(hidden, gain_two).astype(bf16)
    up_proj = jnp.dot(normed_two, full_up, preferred_element_type=f32)
    activated = gelu_tanh(up_proj).astype(bf16)
    branch_m = jnp.dot(activated, full_down, preferred_element_type=f32)
    gate_prob = jax.nn.sigmoid(jnp.dot(routed_in, router_vec, precision=highest))
    branch = branch_a + branch_m
    update = (
        (gate_prob[:, None] * branch * live_mask)
        .astype(bf16)
        .reshape(own_count, slot_count, model_width)
    )
    update_every = lax.all_gather(update, "seq", axis=0, tiled=True)
    output = (
        tokens.astype(f32)
        + jnp.einsum("scp,csd->spd", chooser, update_every, preferred_element_type=f32)
    ).astype(bf16)
    cot_rows = picked_cot.reshape(row_count, model_width)
    grad_gate = jnp.sum(cot_rows * branch, axis=-1)
    grad_logit = grad_gate * gate_prob * (1.0 - gate_prob)
    grad_branch = gate_prob[:, None] * cot_rows
    grad_m = grad_branch.astype(bf16)
    grad_act = jnp.einsum("rd,fd->rf", grad_m, full_down, preferred_element_type=f32)
    unused_up, gelu_pull = jax.vjp(gelu_tanh, up_proj)
    grad_u = gelu_pull(grad_act)[0].astype(bf16)
    grad_n2 = jnp.einsum("rf,df->rd", grad_u, full_up, preferred_element_type=f32)
    unused_two, norm_pull_two = jax.vjp(norm_apply, hidden, gain_two)
    grad_hidden, grad_gm = norm_pull_two(grad_n2)
    grad_a = (grad_branch + grad_hidden).astype(bf16)
    grad_att = jnp.einsum("rd,ed->re", grad_a, full_out, preferred_element_type=f32).astype(bf16)
    grad_att4 = grad_att.reshape(own_count, slot_count, head_count, HEAD_DIM)
    delta_rows = jnp.sum(grad_att4.astype(f32) * mixture, axis=-1)
    delta = jnp.transpose(delta_rows, (1, 2, 0))[..., None]
    grad_p = jnp.einsum("qsha,ksha->shqk", grad_att4, value_rows, preferred_element_type=f32)
    probs = weights_f / row_total
    grad_s = (probs * (grad_p - delta)).astype(bf16)
    grad_q = (
        jnp.einsum("shqk,ksha->qsha", grad_s, key_rows, preferred_element_type=f32) * score_scale
    )
    grad_k = (
        jnp.einsum("shqk,qsha->ksha", grad_s, query_rows, preferred_element_type=f32) * score_scale
    )
    scaled_low = weights_low.astype(f32) / row_total
    grad_v = jnp.einsum("shqk,qsha->ksha", scaled_low, grad_att4.astype(f32), precision=highest)
    grad_k_own, grad_v_own = (
        lax.psum_scatter(
            grad_k.reshape(capacity, slot_count, model_width).astype(jnp.bfloat16),
            "seq",
            scatter_dimension=0,
            tiled=True,
        ).astype(jnp.float32),
        lax.psum_scatter(
            grad_v.reshape(capacity, slot_count, model_width).astype(jnp.bfloat16),
            "seq",
            scatter_dimension=0,
            tiled=True,
        ).astype(jnp.float32),
    )
    grad_joined = jnp.concatenate(
        [
            grad_q.reshape(row_count, model_width),
            grad_k_own.reshape(row_count, model_width),
            grad_v_own.reshape(row_count, model_width),
        ],
        axis=-1,
    ).astype(bf16)
    grad_n1 = jnp.einsum("re,de->rd", grad_joined, full_qkv, preferred_element_type=f32)
    unused_one, norm_pull_one = jax.vjp(norm_apply, routed_in, gain_one)
    grad_x1, grad_ga = norm_pull_one(grad_n1)
    grad_router = jnp.sum(routed_in * grad_logit[:, None], axis=0)
    grad_rows = (grad_hidden + grad_x1 + grad_logit[:, None] * router_vec[None, :]).astype(bf16)
    grad_rows = grad_rows.reshape(own_count, slot_count, model_width)
    grad_every = lax.all_gather(grad_rows, "seq", axis=0, tiled=True)
    input_grad = (
        cotangent.astype(f32)
        + jnp.einsum("scp,csd->spd", chooser, grad_every, preferred_element_type=f32)
    ).astype(bf16)
    part_qkv = jnp.einsum("rd,re->de", normed_one, grad_joined, preferred_element_type=f32)
    part_out = jnp.einsum("re,rd->ed", attended, grad_a, preferred_element_type=f32)
    part_up = jnp.einsum("rd,rf->df", normed_two, grad_u, preferred_element_type=f32)
    part_down = jnp.einsum("rf,rd->fd", activated, grad_m, preferred_element_type=f32)

    def sum_rows(part):
        return lax.psum_scatter(
            part.astype(bf16), ("seq", "batch"), scatter_dimension=0, tiled=True
        ).astype(f32)

    down_sum = sum_rows(part_down)
    grad_up = sum_rows(part_up)
    grad_out = sum_rows(part_out)
    grad_qkv = sum_rows(part_qkv)
    small_ga, small_gm, small_router = (
        lax.psum_scatter(grad_ga, ("seq", "batch"), scatter_dimension=0, tiled=True),
        lax.psum_scatter(grad_gm, ("seq", "batch"), scatter_dimension=0, tiled=True),
        lax.psum_scatter(grad_router, ("seq", "batch"), scatter_dimension=0, tiled=True),
    )
    return (
        output,
        input_grad,
        grad_qkv,
        grad_out,
        grad_up,
        down_sum,
        small_ga,
        small_gm,
        small_router,
    )


def block_kernel(
    tok_hbm, cot_hbm, wq_hbm, wo_hbm, wu_hbm, wd_hbm, one_hbm, two_hbm, three_hbm, routed_hbm, len_hbm,
    upd_out, dx_out, fq_out, fo_out, fu_out, fd_out, vec_out, live_out,
    wq, wo, wu, wd, gv, stq, stu, stv, rcv,
    xs, xr, ds, dr, a_s, a_r, d2s, d2r, d1r, m_s, m_r, hid, dh, qkv, att, act, gp, logit, gains,
    gd, gu, rcd, rcu, ryd, ryu, rzd, rzu, rzb, ryb,
    fqk, fv, fo, fu, fd, sqk, sv, suu, rqk, rv, ruu, vs, vr, v_all, live,
    one_ref, two_ref, three_ref, routed_ref, len_ref,
    loc, out_sem, wz, vz, wy, vy, wc, vc, sx, rx, gc, hc, gt, ht, gy, hy, gz, hz, free,
):
    s, z, y, c = place()
    near, far = z + 1 - 2 * lax.rem(z, 2), LINE - 1 - z
    xdev, ydev, cdev = device(1 - s, z, y, c), device(s, z, 1 - y, c), device(s, z, y, 1 - c)
    ndev, fdev = device(s, near, y, c), device(s, far, y, c)
    model, half_q, half_u = xr.shape[2], att.shape[2], act.shape[2]
    ranks, half = xr.shape[1], xr.shape[2] // 2
    rows = xr.shape[0] * ranks
    part, half_d = stq.shape[0], wd.shape[3] // 2
    local, sent, outs = [], [], []

    def fetch(src, dst):
        copy = pltpu.make_async_copy(src, dst, loc.at[len(local)])
        copy.start()
        local.append(copy)
        return copy

    def send(src, dst, send_sem, recv_sem, target):
        copy = remote(src, dst, send_sem, recv_sem, target)
        copy.start()
        sent.append(copy)
        return copy

    def gone(copy):
        copy.wait_send()
        sent[:] = [other for other in sent if other is not copy]

    def arrive(ref, send_sem, recv_sem, target):
        remote(ref, ref, send_sem, recv_sem, target).wait_recv()

    def put(src, dst):
        copy = pltpu.make_async_copy(src, dst, out_sem.at[len(outs)])
        copy.start()
        outs.append(copy)

    barrier = pltpu.get_barrier_semaphore()
    for target in (xdev, ydev, cdev, ndev, fdev):
        pl.semaphore_signal(barrier, inc=1, device_id=target, device_id_type=MESH)

    stage, own_q = [], []
    small_in = [
        fetch(src, dst)
        for src, dst in (
            (one_hbm, one_ref), (two_hbm, two_ref), (three_hbm, three_ref), (routed_hbm, routed_ref), (len_hbm, len_ref),
        )
    ]
    for j in range(3):
        base, dst = 2 * j * half_q, pl.ds(j * half_q, half_q)
        stage.append(fetch(wq_hbm.at[:, pl.ds(base + (1 - s) * half_q, half_q)], stq.at[:, dst]))
        own_q.append(fetch(wq_hbm.at[:, pl.ds(base + s * half_q, half_q)], wq.at[s, z, y, c, :, dst]))
    get_tok = [fetch(tok_hbm.at[i], gd.at[pl.ds(2 * i, 2)]) for i in range(2)]
    own_o = fetch(wo_hbm, wo.at[z, y, c])
    stage_u = fetch(wu_hbm.at[:, pl.ds((1 - s) * half_u, half_u)], stu)
    own_u = fetch(wu_hbm.at[:, pl.ds(s * half_u, half_u)], wu.at[s, z, y, c])
    own_d = fetch(wd_hbm, wd.at[z, y, c])

    def down_half(i):
        return pl.ds(half_d * i, half_d)

    blocks = [
        lambda zz, yy, cc: wq.at[s, zz, yy, cc],
        lambda zz, yy, cc: wq.at[1 - s, zz, yy, cc],
        lambda zz, yy, cc: gv.at[zz, yy, cc],
        lambda zz, yy, cc: wo.at[zz, yy, cc],
        lambda zz, yy, cc: wu.at[s, zz, yy, cc],
        lambda zz, yy, cc: wu.at[1 - s, zz, yy, cc],
        lambda zz, yy, cc: wd.at[zz, yy, cc, down_half(0)],
        lambda zz, yy, cc: wd.at[zz, yy, cc, down_half(1)],
    ]
    lines = [
        lambda yy, cc: wq.at[s, :, yy, cc],
        lambda yy, cc: wq.at[1 - s, :, yy, cc],
        lambda yy, cc: gv.at[:, yy, cc],
        lambda yy, cc: wo.at[:, yy, cc],
        lambda yy, cc: wu.at[s, :, yy, cc],
        lambda yy, cc: wu.at[1 - s, :, yy, cc],
        lambda yy, cc: wd.at[:, yy, cc, down_half(0)],
        lambda yy, cc: wd.at[:, yy, cc, down_half(1)],
    ]
    Q_OWN, Q_SWAP, VEC, OUT, U_OWN, U_SWAP, D_0, D_1 = range(8)

    planes = [
        lambda cc: wq.at[s, :, :, cc],
        lambda cc: wq.at[1 - s, :, :, cc],
        lambda cc: gv.at[:, :, cc],
        lambda cc: wo.at[:, :, cc],
        lambda cc: wu.at[s, :, :, cc],
        lambda cc: wu.at[1 - s, :, :, cc],
        lambda cc: wd.at[:, :, cc, down_half(0)],
        lambda cc: wd.at[:, :, cc, down_half(1)],
    ]

    def pass_on(ref, send_sem, recv_sem, target):
        remote(ref, ref, send_sem, recv_sem, target).start()

    def spread(p):
        own = blocks[p](z, y, c)
        pass_on(own, wz.at[p], vz.at[p, 0], fdev)
        pass_on(own, wz.at[p], vz.at[p, 1], ndev)

    def spread_y(p):
        pass_on(blocks[p](z, y, c), wy.at[p], vy.at[p], ydev)

    def after_far(p):
        ref = blocks[p](far, y, c)
        arrive(ref, wz.at[p], vz.at[p, 0], fdev)
        pass_on(ref, wz.at[p], vz.at[p, 2], ndev)
        pass_on(ref, wy.at[p], vy.at[p], ydev)

    def after_near(p):
        for i, zz in ((1, near), (2, LINE - 1 - near)):
            ref = blocks[p](zz, y, c)
            arrive(ref, wz.at[p], vz.at[p, i], ndev)
            pass_on(ref, wy.at[p], vy.at[p], ydev)
        pass_on(lines[p](y, c), wc.at[p], vc.at[p], cdev)

    def after_y(p):
        line = lines[p](1 - y, c)
        arrive(line, wy.at[p], vy.at[p], ydev)
        pass_on(line, wc.at[p], vc.at[p], cdev)

    def after_c(p):
        arrive(planes[p](1 - c), wc.at[p], vc.at[p], cdev)

    def both(zz, cc):
        return wd.at[zz, :, cc, down_half(1)]

    def after_first_y():
        arrive(blocks[D_1](z, 1 - y, c), wy.at[D_1], vy.at[D_1], ydev)
        own = both(z, c)
        pass_on(own, wz.at[D_1], vz.at[D_1, 0], fdev)
        pass_on(own, wz.at[D_1], vz.at[D_1, 1], ndev)

    def after_first_far():
        ref = both(far, c)
        arrive(ref, wz.at[D_1], vz.at[D_1, 0], fdev)
        pass_on(ref, wz.at[D_1], vz.at[D_1, 2], ndev)

    def after_first_near():
        for i, zz in ((1, near), (2, LINE - 1 - near)):
            arrive(both(zz, c), wz.at[D_1], vz.at[D_1, i], ndev)
        pass_on(planes[D_1](c), wc.at[D_1], vc.at[D_1], cdev)

    def after_first_c():
        arrive(planes[D_1](1 - c), wc.at[D_1], vc.at[D_1], cdev)

    def left(ref, send_sem, recv_sem, target):
        remote(ref, ref, send_sem, recv_sem, target).wait_send()

    def gathered():
        three = pl.ds(0, LINE - 1)
        passed = [
            wq.at[s, three, y, c], wq.at[1 - s, three, y, c], gv.at[three, y, c], wo.at[three, y, c],
            wu.at[s, three, y, c], wu.at[1 - s, three, y, c], wd.at[three, y, c, down_half(0)],
            wd.at[three, :, c, down_half(1)],
        ]
        for p in range(8):
            left(passed[p], wz.at[p], vz.at[p, 0], ndev)
            left(blocks[p](z, y, c) if p == D_1 else lines[p](y, c), wy.at[p], vy.at[p], ydev)
            left(planes[p](c), wc.at[p], vc.at[p], cdev)

    spans = [pl.ds(0, 2 * part), pl.ds(2 * part, 2 * part), None, None]
    spans += [pl.ds(i * part, part) for i in range(4)]
    parts = [
        (lambda cc, i=i: gu.at[i - 2, :, :, cc]) if q is None else (lambda cc, q=q: gd.at[:, :, cc, q])
        for i, q in enumerate(spans)
    ]
    land_c = [rcu.at[i - 2] if q is None else rcd.at[:, :, q] for i, q in enumerate(spans)]
    land_y = [ryu.at[i - 2] if q is None else ryd.at[:, q] for i, q in enumerate(spans)]
    land_z = [rzu.at[i - 2] if q is None else rzd.at[:, q] for i, q in enumerate(spans)]

    def c_start(k):
        return send(parts[k](1 - c), land_c[k], gc.at[k], hc.at[k], cdev)

    def c_end(k):
        ref, own = land_c[k], parts[k](c)
        if k < 2:
            arrive(ref, gt.at[k], ht.at[k], cdev)
        else:
            arrive(ref, gc.at[k], hc.at[k], cdev)

        def add(i, carry):
            ref[i] = (ref[i].astype(f32) + own[i].astype(f32)).astype(bf16)
            return carry

        lax.fori_loop(0, LINE, add, 0)
        if k == 0:
            return [
                send(ref.at[LINE - 1 - near], rzb.at[1], gz.at[k, 1], hz.at[k, 1], ndev),
                send(ref.at[near], rzb.at[0], gz.at[k, 0], hz.at[k, 0], ndev),
            ]
        return [send(ref.at[:, 1 - y], land_y[k], gy.at[k], hy.at[k], ydev)]

    def y_end(k):
        ref, own = land_y[k], land_c[k]
        arrive(ref, gy.at[k], hy.at[k], ydev)

        def add(i, carry):
            ref[i] = (ref[i].astype(f32) + own[i, y].astype(f32)).astype(bf16)
            return carry

        lax.fori_loop(0, LINE, add, 0)
        return [
            send(ref.at[LINE - 1 - near], land_z[k].at[1], gz.at[k, 1], hz.at[k, 1], ndev),
            send(ref.at[near], land_z[k].at[0], gz.at[k, 0], hz.at[k, 0], ndev),
        ]

    def z_mid(k):
        ref = land_z[k].at[1]
        arrive(ref, gz.at[k, 1], hz.at[k, 1], ndev)
        ref[...] = (ref[...].astype(f32) + land_y[k][far].astype(f32)).astype(bf16)
        return send(ref, land_z[k].at[2], gz.at[k, 2], hz.at[k, 2], fdev)

    def z_end(k):
        arrive(land_z[k].at[0], gz.at[k, 0], hz.at[k, 0], ndev)
        arrive(land_z[k].at[2], gz.at[k, 2], hz.at[k, 2], fdev)
        return land_y[k][z].astype(f32) + land_z[k][0].astype(f32) + land_z[k][2].astype(f32)

    def first_mid():
        arrive(rzb.at[1], gz.at[0, 1], hz.at[0, 1], ndev)
        rzb[1] = (rzb[1].astype(f32) + land_c[0][far].astype(f32)).astype(bf16)
        return send(rzb.at[1], rzb.at[2], gz.at[0, 2], hz.at[0, 2], fdev)

    def first_end():
        arrive(rzb.at[0], gz.at[0, 0], hz.at[0, 0], ndev)
        arrive(rzb.at[2], gz.at[0, 2], hz.at[0, 2], fdev)
        rzb[0] = (land_c[0][z].astype(f32) + rzb[0].astype(f32) + rzb[2].astype(f32)).astype(bf16)
        return send(rzb.at[0, 1 - y], ryb, gy.at[0], hy.at[0], ydev)

    def first_sum():
        arrive(ryb, gy.at[0], hy.at[0], ydev)
        return rzb[0, y].astype(f32) + ryb[...].astype(f32)

    for copy in small_in:
        copy.wait()
    lane = lax.broadcasted_iota(jnp.int32, (part, model), 1)
    fits = (lax.rem(lane, part) == lax.broadcasted_iota(jnp.int32, (part, model), 0)) & (
        lane // part == s * 4 * LINE + z * 4 + y * 2 + c
    )
    line = lax.broadcasted_iota(jnp.int32, (16, part), 0)
    small = jnp.zeros((16, part), f32)
    for j, ref in enumerate((one_ref, two_ref, three_ref)):
        small = jnp.where(line == j, ref[...].astype(f32), small)
    stv[...] = dot_nn(small.astype(bf16), jnp.where(fits, 1.0, 0.0).astype(bf16)).astype(bf16)

    rank = lax.broadcasted_iota(jnp.int32, (1, ranks), 1)

    def count(i):
        return lax.shift_right_arithmetic(len_ref[:, i : i + 1], 3)

    for i in range(2):
        live[i : i + 1] = jnp.where(rank < count(i), routed_ref[i : i + 1], -1)

    def chooser(i):
        row = live[i : i + 1].astype(f32)
        eye = lax.broadcasted_iota(jnp.int32, (ranks, ranks), 0) == lax.broadcasted_iota(
            jnp.int32, (ranks, ranks), 1
        )
        column = jnp.sum(jnp.where(eye, row, 0.0), axis=1, keepdims=True).astype(jnp.int32)
        count_here = tok_hbm.shape[1] * 512
        position = lax.broadcasted_iota(jnp.int32, (ranks, count_here), 1) + s * count_here
        return jnp.where(position == column, 1.0, 0.0).astype(bf16)

    def pick(i, dst):
        dst[i] = dot_nn(chooser(i), gd[2 * i : 2 * i + 2].reshape(tok_hbm.shape[1] * 512, model)).astype(bf16)

    def live_column(i):
        rank = lax.broadcasted_iota(jnp.int32, (ranks, 1), 0)
        return jnp.where(rank < count(i), 1.0, 0.0).astype(f32)

    def allowed(i):
        query = lax.broadcasted_iota(jnp.int32, (ranks, ranks), 0)
        key = lax.broadcasted_iota(jnp.int32, (ranks, ranks), 1)
        return (key <= query) & (key < count(i))

    for copy in stage:
        copy.wait()
    pl.semaphore_wait(barrier, 5)
    send(stq, wq.at[s, z, y, c], sx.at[1], rx.at[1], xdev)
    swap_v = send(stv, rcv, sx.at[0], rx.at[0], xdev)
    for copy in own_q:
        copy.wait()
    spread(Q_OWN)
    spread_y(Q_OWN)
    own_d.wait()
    spread_y(D_1)
    x_swap = []
    get_tok[0].wait()
    pick(0, xs)
    x_swap.append(send(xs.at[0], xr.at[0], sx.at[3], rx.at[3], xdev))
    get_cot = [fetch(cot_hbm.at[0], gd.at[pl.ds(0, 2)])]
    stage_u.wait()
    send(stu, wu.at[s, z, y, c], sx.at[2], rx.at[2], xdev)
    get_tok[1].wait()
    pick(1, xs)
    x_swap.append(send(xs.at[1], xr.at[1], sx.at[4], rx.at[4], xdev))
    get_cot.append(fetch(cot_hbm.at[1], gd.at[pl.ds(2, 2)]))
    put(live, live_out)
    swap_v.wait_recv()
    gv[z, y, c] = stv[...] + rcv[...]
    after_far(Q_OWN)
    spread(VEC)
    spread_y(VEC)
    arrive(wq.at[1 - s, z, y, c], sx.at[1], rx.at[1], xdev)
    spread(Q_SWAP)
    spread_y(Q_SWAP)
    get_cot[0].wait()
    pick(0, ds)
    d_swap = [send(ds.at[0], dr.at[0], sx.at[7], rx.at[7], xdev)]
    after_near(Q_OWN)
    after_far(VEC)
    get_cot[1].wait()
    pick(1, ds)
    after_far(Q_SWAP)
    own_o.wait()
    spread(OUT)
    after_near(VEC)
    after_near(Q_SWAP)
    after_far(OUT)
    spread_y(OUT)
    own_u.wait()
    spread(U_OWN)
    spread_y(U_OWN)
    arrive(wu.at[1 - s, z, y, c], sx.at[2], rx.at[2], xdev)
    spread(U_SWAP)
    after_y(Q_OWN)
    after_y(VEC)
    after_c(Q_OWN)
    after_c(VEC)
    after_near(OUT)
    after_y(Q_SWAP)
    after_far(U_OWN)
    spread(D_0)
    spread_y(U_SWAP)
    spread_y(D_0)
    after_c(Q_SWAP)

    gains[...] = jnp.sum(gv[...].astype(f32).reshape(4 * LINE, 16, model), axis=0)
    gain_one, gain_two, router = gains[0:1], gains[1:2], gains[2:3]

    def enter(i):
        x_swap[i].wait()
        row = xr[i].astype(f32) + xs[i].astype(f32)
        xr[i] = row.astype(bf16)
        xs[i] = (row * inverse_rms(row) * gain_one).astype(bf16)
        for j in range(3):
            cols = pl.ds(j * half_q, half_q)
            qkv[i, :, cols] = dot_nn(xs[i], wq[:, :, :, :, :, cols].reshape(model, half_q)).astype(bf16)

    def attend(i):
        ok = allowed(i)

        def pair(j, carry):
            q2 = qkv[i, :, pl.ds(j * 128, 128)].astype(f32)
            k2 = qkv[i, :, pl.ds(half_q + j * 128, 128)]
            v2 = qkv[i, :, pl.ds(2 * half_q + j * 128, 128)]
            mixed = jnp.zeros(q2.shape, f32)
            for parity in range(2):
                mask = head_mask(parity)
                score = dot_nt((q2 * mask).astype(bf16), k2) * (HEAD_DIM**-0.5)
                score = jnp.where(ok, score, -1000000000.0)
                weight = jnp.exp(score - jnp.max(score, axis=-1, keepdims=True))
                total = jnp.sum(weight, axis=-1, keepdims=True)
                mixed += dot_nn(weight.astype(bf16), v2) / total * mask
            att[i, :, pl.ds(j * 128, 128)] = mixed.astype(bf16)
            return carry

        lax.fori_loop(0, half_q // 128, pair, 0)

    def leave(i):
        for j in range(2):
            cols = pl.ds(j * half, half)
            a_s[i, :, cols] = dot_nn(att[i], wo[:, :, :, :, cols].reshape(half_q, half)).astype(bf16)
        return send(a_s.at[i], a_r.at[i], sx.at[5 + i], rx.at[5 + i], xdev)

    enter(0)
    attend(0)
    after_y(OUT)
    after_c(OUT)
    a_swap = [leave(0)]
    after_far(U_SWAP)
    after_first_y()
    after_near(U_OWN)
    enter(1)
    attend(1)
    a_swap.append(leave(1))
    d_swap.append(send(ds.at[1], dr.at[1], sx.at[8], rx.at[8], xdev))
    after_far(D_0)
    after_near(U_SWAP)
    after_y(U_OWN)
    after_c(U_OWN)

    def mlp_up(i):
        a_swap[i].wait()
        row = xr[i].astype(f32) + (a_s[i].astype(f32) + a_r[i].astype(f32))
        hid[i] = row
        a_s[i] = (row * inverse_rms(row) * gain_two).astype(bf16)

        def tile(t, carry):
            cols = pl.ds(t * 512, 512)
            up = dot_nn(a_s[i], wu[:, :, :, :, :, cols].reshape(model, 512))
            curve = jnp.tanh(GELU_C * (up + GELU_K * up * up * up))
            act[i, :, cols] = (0.5 * up * (1.0 + curve)).astype(bf16)
            slope = 0.5 * (1.0 + curve) + 0.5 * up * (1.0 - curve * curve) * (
                GELU_C * (1.0 + 3.0 * GELU_K * up * up)
            )
            gp[i, :, cols] = slope.astype(bf16)
            return carry

        lax.fori_loop(0, half_u // 512, tile, 0)

    def gate_of(i):
        return jax.nn.sigmoid(jnp.sum(xr[i].astype(f32) * router, axis=-1, keepdims=True))

    def cotangent_rows(i):
        d_swap[i].wait()
        row = dr[i].astype(f32) + ds[i].astype(f32)
        dr[i] = row.astype(bf16)
        ds[i] = (gate_of(i) * row).astype(bf16)

    def mlp_back(i):
        def tile(t, carry):
            cols = pl.ds(t * 512, 512)
            back = dot_nt(ds[i], wd[t].reshape(512, model))
            gp[i, :, cols] = (back * gp[i, :, cols].astype(f32)).astype(bf16)
            return carry

        lax.fori_loop(0, half_u // 512, tile, 0)
        for j in range(2):
            cols = pl.ds(j * half, half)
            d2s[i, :, cols] = dot_nt(gp[i], wu[j].reshape(half, half_u)).astype(bf16)
        return send(d2s.at[i], d2r.at[i], sx.at[9 + i], rx.at[9 + i], xdev)

    def mlp_out(i):
        for j in range(2):
            cols = pl.ds(j * half, half)
            m_s[i, :, cols] = dot_nn(act[i], wd[:, :, :, :, cols].reshape(half_u, half)).astype(bf16)

    def mlp_send(i):
        return send(m_s.at[i], m_r.at[i], sx.at[11 + i], rx.at[11 + i], xdev)

    after_y(U_SWAP)
    after_first_far()
    after_c(U_SWAP)
    mlp_up(0)
    after_near(D_0)
    cotangent_rows(0)

    def down_tile(t, carry):
        gd[t] = dot_tn(act[0, :, pl.ds(t * 512, 512)], ds[0]).astype(bf16).reshape(gd.shape[1:])
        return carry

    lax.fori_loop(0, LINE, down_tile, 0)
    mlp_up(1)
    after_y(D_0)
    after_c(D_0)
    after_first_near()
    after_first_c()
    d2_swap = [mlp_back(0)]
    cotangent_rows(1)

    def c_tile(t, k):
        remote(gd.at[t, :, 1 - c, spans[k]], land_c[k].at[t], gt.at[k], ht.at[k], cdev).start()

    for t in range(LINE):
        grad = dot_tn(act[1, :, t * 512 : t * 512 + 512], ds[1])
        gd[t] = (gd[t].astype(f32) + grad.reshape(gd.shape[1:])).astype(bf16)
        c_tile(t, 1)
    for t in range(LINE):
        c_tile(t, 0)
    y_down = c_end(1)
    z_first = c_end(0)
    d2_swap.append(mlp_back(1))
    mlp_out(0)
    m_swap = [mlp_send(0)]

    def up_tile(t, carry):
        cols = pl.ds(t * 512, 512)
        grad = dot_tn(a_s[...].reshape(rows, model), gp[:, :, cols].reshape(rows, 512))
        gu[:, :, :, :, :, cols] = grad.astype(bf16).reshape(gu.shape[:5] + (512,))
        return carry

    lax.fori_loop(0, half_u // 512, up_tile, 0)
    c_start(2)
    c_start(3)
    mlp_out(1)
    m_swap.append(mlp_send(1))

    def hidden_back(i):
        d2_swap[i].wait()
        back = d2s[i].astype(f32) + d2r[i].astype(f32)
        row = hid[i]
        r2 = inverse_rms(row)
        scaled = back * gain_two
        step = r2 * scaled - row * (r2 * r2 * r2 * jnp.mean(scaled * row, axis=-1, keepdims=True))
        dh[i] = step
        gp[i, :, 0:model] = (gate_of(i) * dr[i].astype(f32) + step).astype(bf16)
        gp[i, :, model : model + half_q] = dot_nt(gp[i, :, 0:model], wo[...].reshape(half_q, model)).astype(bf16)
        return jnp.sum(d2s[i].astype(f32) * row * r2, axis=0, keepdims=True)

    def attend_back(i):
        ok = allowed(i)
        scale = HEAD_DIM**-0.5

        def pair(j, carry):
            q2 = qkv[i, :, pl.ds(j * 128, 128)]
            k2 = qkv[i, :, pl.ds(half_q + j * 128, 128)]
            v2 = qkv[i, :, pl.ds(2 * half_q + j * 128, 128)]
            g2 = gp[i, :, pl.ds(model + j * 128, 128)].astype(f32)
            q2f = q2.astype(f32)
            dq2 = jnp.zeros(q2.shape, f32)
            dk2 = jnp.zeros(q2.shape, f32)
            dv2 = jnp.zeros(q2.shape, f32)
            for parity in range(2):
                mask = head_mask(parity)
                score = dot_nt((q2f * mask).astype(bf16), k2) * scale
                score = jnp.where(ok, score, -1000000000.0)
                weight = jnp.exp(score - jnp.max(score, axis=-1, keepdims=True))
                over = 1.0 / jnp.sum(weight, axis=-1, keepdims=True)
                gh = g2 * mask
                dp = dot_nt(gh.astype(bf16), v2)
                prob = weight * over
                delta = jnp.sum(prob * dp, axis=-1, keepdims=True)
                dscore = (prob * (dp - delta)).astype(bf16)
                dq2 += dot_nn(dscore, k2) * mask
                dk2 += dot_tn(dscore, q2) * mask
                dv2 += dot_tn(weight.astype(bf16), (gh * over).astype(bf16))
            act[i, :, pl.ds(j * 128, 128)] = (dq2 * scale).astype(bf16)
            act[i, :, pl.ds(half_q + j * 128, 128)] = (dk2 * scale).astype(bf16)
            act[i, :, pl.ds(2 * half_q + j * 128, 128)] = dv2.astype(bf16)
            return carry

        lax.fori_loop(0, half_q // 128, pair, 0)

    def inner_back(i):
        r1 = inverse_rms(xr[i].astype(f32))
        sums = []
        for j in range(2):
            cols = pl.ds(j * half, half)
            step = dot_nt(act[i, :, 0 : 3 * half_q], wq[j].reshape(half, 3 * half_q))
            d2s[i, :, cols] = step.astype(bf16)
            sums.append(jnp.sum(step * xr[i, :, cols].astype(f32) * r1, axis=0, keepdims=True))
        return send(d2s.at[i], d1r.at[i], sx.at[13 + i], rx.at[13 + i], xdev), sums

    grad_gm = hidden_back(0)
    c_end(2)
    attend_back(0)
    c_end(3)
    z_first.append(first_mid())
    swap_0, sums_0 = inner_back(0)
    z_down = y_end(1)
    grad_gm += hidden_back(1)
    attend_back(1)
    z_down.append(z_mid(1))
    for k in range(2):
        left(parts[k](1 - c), gt.at[k], ht.at[k], cdev)
    for copy in z_first:
        gone(copy)
    first_end()
    pl.semaphore_signal(free.at[0], inc=1, device_id=cdev, device_id_type=MESH)
    y_end(2)

    def out_tile(t):
        cols = pl.ds(t * half, half)
        grad = dot_tn(att[...].reshape(rows, half_q), gp[:, :, cols].reshape(rows, half))
        gd[:, :, :, 3 * part :, cols] = grad.astype(bf16).reshape(wo.shape[:4] + (half,))

    def qkv_tile(t):
        grad = dot_tn(xs[...].reshape(rows, model), act[:, :, t * half_q : (t + 1) * half_q].reshape(rows, half_q))
        grad = grad.astype(bf16).reshape(wq.shape[:5] + (half_q,))
        if t < 2:
            gd[:, :, :, 0:part, t * half_q : (t + 1) * half_q] = grad[0]
            gd[:, :, :, part : 2 * part, t * half_q : (t + 1) * half_q] = grad[1]
        else:
            gd[:, :, :, 2 * part : 3 * part, 0:half_q] = grad[0]
            gd[:, :, :, 2 * part : 3 * part, half_q:] = grad[1]

    qkv_tile(0)
    qkv_tile(1)
    pl.semaphore_wait(free.at[0], 1)
    c_start(4)
    c_start(5)
    qkv_tile(2)
    fd[2 * part :] = z_end(1)
    for copy in y_down + z_down:
        gone(copy)
    for target in (ydev, cdev, ndev, fdev):
        pl.semaphore_signal(free.at[1], inc=1, device_id=target, device_id_type=MESH)
    out_tile(0)
    out_tile(1)
    c_end(4)
    c_end(5)
    swap_1, sums_1 = inner_back(1)
    d1_swap = [swap_0, swap_1]
    for j in range(2):
        vs[0:1, j * half : (j + 1) * half] = sums_0[j] + sums_1[j]
    vs[1:2] = grad_gm
    pl.semaphore_wait(free.at[1], 4)
    c_start(6)
    c_start(7)
    z_mid(2)
    c_end(6)
    y_end(3)
    fu[0] = z_end(2)

    grad_router = jnp.zeros((1, model), f32)
    for i in range(2):
        m_swap[i].wait()
        row = xr[i].astype(f32)
        gate = gate_of(i)
        branch = (hid[i] - row) + (m_s[i].astype(f32) + m_r[i].astype(f32))
        m_s[i] = (gate * branch * live_column(i)).astype(bf16)
        slope = jnp.sum(dr[i].astype(f32) * branch, axis=-1, keepdims=True) * gate * (1.0 - gate)
        logit[i] = slope
        grad_router += jnp.sum(row * slope, axis=0, keepdims=True)
    put(m_s, upd_out)
    vs[2:3] = 0.5 * grad_router
    vs[3:8] = jnp.zeros((5, model), f32)
    send(vs, vr.at[0], gc.at[8], hc.at[8], cdev)
    z_mid(3)
    arrive(vr.at[0], gc.at[8], hc.at[8], cdev)
    v_all[0] = vs[...] + vr[0]
    send(v_all.at[0], vr.at[1], gz.at[8, 0], hz.at[8, 0], ndev)
    c_end(7)
    fd[0 : 2 * part] = first_sum()
    put(fd, fd_out)
    y_end(4)
    fu[1] = z_end(3)
    suu[...] = fu[1 - s].astype(bf16)
    send(suu, ruu, sx.at[15], rx.at[15], xdev)
    put(fu.at[s], fu_out.at[:, pl.ds(s * half_u, half_u)])
    arrive(vr.at[1], gz.at[8, 0], hz.at[8, 0], ndev)
    v_all[1] = v_all[0] + vr[1]
    send(v_all.at[1], vr.at[2], gz.at[8, 1], hz.at[8, 1], fdev)
    z_mid(4)
    y_end(5)

    def rows_back(i):
        d1_swap[i].wait()
        row = xr[i].astype(f32)
        r1 = inverse_rms(row)
        scaled = (d2s[i].astype(f32) + d1r[i].astype(f32)) * gain_one
        step = r1 * scaled - row * (r1 * r1 * r1 * jnp.mean(scaled * row, axis=-1, keepdims=True))
        d2s[i] = (dh[i] + step + logit[i] * router).astype(bf16)
        put(d2s.at[i], dx_out.at[i])

    rows_back(0)
    arrive(vr.at[2], gz.at[8, 1], hz.at[8, 1], fdev)
    v_all[2] = v_all[1] + vr[2]
    send(v_all.at[2], vr.at[3], gy.at[8], hy.at[8], ydev)
    z_mid(5)
    y_end(6)
    z_mid(6)
    y_end(7)
    arrive(vr.at[3], gy.at[8], hy.at[8], ydev)
    v_all[3] = v_all[2] + vr[3]
    send(v_all.at[3], vr.at[4], sx.at[18], rx.at[18], xdev)
    for i in range(2):
        fqk[i] = z_end(4 + i)
    sqk[...] = fqk[1 - s].astype(bf16)
    send(sqk, rqk, sx.at[16], rx.at[16], xdev)
    for j in range(2):
        put(fqk.at[s, :, pl.ds(j * half_q, half_q)], fq_out.at[:, pl.ds(2 * j * half_q + s * half_q, half_q)])
    fv[...] = z_end(6)
    sv[...] = fv[:, pl.ds((1 - s) * half_q, half_q)].astype(bf16)
    send(sv, rv, sx.at[17], rx.at[17], xdev)
    put(fv.at[:, pl.ds(s * half_q, half_q)], fq_out.at[:, pl.ds(4 * half_q + s * half_q, half_q)])
    z_mid(7)
    rows_back(1)
    arrive(ruu, sx.at[15], rx.at[15], xdev)
    fu[1 - s] = ruu[...].astype(f32)
    put(fu.at[1 - s], fu_out.at[:, pl.ds((1 - s) * half_u, half_u)])
    arrive(rqk, sx.at[16], rx.at[16], xdev)
    fqk[1 - s] = rqk[...].astype(f32)
    for j in range(2):
        put(
            fqk.at[1 - s, :, pl.ds(j * half_q, half_q)],
            fq_out.at[:, pl.ds(2 * j * half_q + (1 - s) * half_q, half_q)],
        )
    fo[...] = z_end(7)
    put(fo, fo_out)
    arrive(rv, sx.at[17], rx.at[17], xdev)
    fv[:, pl.ds((1 - s) * half_q, half_q)] = rv[...].astype(f32)
    put(
        fv.at[:, pl.ds((1 - s) * half_q, half_q)],
        fq_out.at[:, pl.ds(4 * half_q + (1 - s) * half_q, half_q)],
    )
    arrive(vr.at[4], sx.at[18], rx.at[18], xdev)
    v_all[4] = v_all[3] + vr[4]
    put(v_all.at[4], vec_out)
    gathered()
    waited = x_swap + a_swap + d_swap + d2_swap + m_swap + d1_swap
    for copy in list(sent):
        if not any(copy is other for other in waited):
            copy.wait_send()
    for copy in outs:
        copy.wait()


def rows_kernel(
    tok_hbm, cot_hbm, upd_hbm, dx_hbm, fq_hbm, fo_hbm, fu_hbm, fd_hbm, vec_hbm, live_hbm,
    out_hbm, grad_hbm, fq_out, fo_out, fu_out, fd_out, one_out, two_out, three_out,
    bases, moved, fq, fo, fu, fd, vec_ref, live_ref, one, two, three, get_sem, put_sem, rows_sem, pass_sem,
):
    s = lax.axis_index("seq")
    _, slots, chunks, tall, model = bases.shape
    ranks = moved.shape[2]
    whole = (tok_hbm, cot_hbm), (out_hbm, grad_hbm)
    tasks = [(i, t) for i in range(slots) for t in range(chunks)]

    def part_of(ref, i, t):
        return ref.at[i, pl.ds(t * tall, tall)]

    gets, puts = {}, []
    rows = [
        pltpu.make_async_copy(src.at[i], moved.at[a, i], rows_sem.at[a, i])
        for i in range(slots)
        for a, src in enumerate((upd_hbm, dx_hbm))
    ]
    get_live = pltpu.make_async_copy(live_hbm, live_ref, pass_sem.at[0, 4])
    get_vec = pltpu.make_async_copy(vec_hbm, vec_ref, pass_sem.at[0, 5])
    get_live.start()
    for i, t in tasks:
        for a in range(2):
            if t == 0:
                rows[2 * i + a].start()
            gets[a, i, t] = pltpu.make_async_copy(part_of(whole[0][a], i, t), bases.at[a, i, t], get_sem.at[a, i, t])
            gets[a, i, t].start()
    through = ((fq_hbm, fq, fq_out), (fo_hbm, fo, fo_out), (fu_hbm, fu, fu_out), (fd_hbm, fd, fd_out))
    taken = [pltpu.make_async_copy(src, mid, pass_sem.at[0, j]) for j, (src, mid, _) in enumerate(through)]
    passed = [pltpu.make_async_copy(mid, dst, pass_sem.at[1, j]) for j, (_, mid, dst) in enumerate(through)]
    for copy in taken + [get_vec]:
        copy.start()
    get_live.wait()
    for n, (i, t) in enumerate(tasks):
        if n == len(tasks) - 2:
            for j in range(4):
                taken[j].wait()
                passed[j].start()
        position = lax.broadcasted_iota(jnp.int32, (tall, ranks), 0) + ((s * chunks + t) * tall)
        chooser = jnp.where(position == live_ref[i : i + 1], 1.0, 0.0).astype(bf16)
        for a in range(2):
            if t == 0:
                rows[2 * i + a].wait()
            gets[a, i, t].wait()
            bases[a, i, t] += dot_nn(chooser, moved[a, i]).astype(bf16)
            copy = pltpu.make_async_copy(bases.at[a, i, t], part_of(whole[1][a], i, t), put_sem.at[a, i, t])
            copy.start()
            puts.append(copy)
    part = one.shape[1]
    get_vec.wait()
    flat = s * lax.axis_size("batch") + lax.axis_index("batch")
    lane = lax.broadcasted_iota(jnp.int32, (part, model), 1)
    row = lax.broadcasted_iota(jnp.int32, (part, model), 0)
    here = (lane // part == flat) & (lax.rem(lane, part) == row)
    eye = lax.broadcasted_iota(jnp.int32, (part, part), 0) == lax.broadcasted_iota(jnp.int32, (part, part), 1)
    for j, (ref, dst) in enumerate(((one, one_out), (two, two_out), (three, three_out))):
        column = jnp.sum(jnp.where(here, vec_ref[j : j + 1], 0.0), axis=1, keepdims=True)
        ref[...] = jnp.sum(jnp.where(eye, column, 0.0), axis=0, keepdims=True)
        puts.append(pltpu.make_async_copy(ref, dst, pass_sem.at[1, 4 + j]))
        puts[-1].start()
    for copy in passed + puts:
        copy.wait()


def split_device(
    tokens, cotangent, lengths, routed, w_qkv, w_out, w_up, w_down, gain_attn, gain_mlp, router
):
    slots, local_len, model = tokens.shape
    ranks = routed.shape[1]
    half_q, half_u = w_qkv.shape[1] // 6, w_up.shape[1] // 2
    part, down = w_qkv.shape[0], w_down.shape[0]
    hbm = pl.BlockSpec(memory_space=pl.ANY)
    sds, space, dma = jax.ShapeDtypeStruct, pltpu.VMEM, pltpu.SemaphoreType.DMA
    rows = (slots, ranks, model)
    grid = (LINE, 2, 2)
    wq_shape, wo_shape = (2,) + grid + (part, 3 * half_q), grid + (part, model)
    wu_shape, wd_shape = (2,) + grid + (part, half_u), grid + (down, model)
    blocked = (slots, local_len // 512, 2, 2, 128, model)
    row_bf16 = space(rows, bf16)

    def land(lead, tall, wide):
        return [space(lead + mid + (tall, wide), bf16) for mid in ((LINE, 2), (LINE,), (3,))]

    on_d, on_u = land((), down, model), land((2,), part, half_u)
    grad_shapes = (
        sds((part, 6 * half_q), f32), sds((part, model), f32), sds((part, 2 * half_u), f32), sds((down, model), f32),
    )
    upd, dxr, *sums, vec, live = pl.pallas_call(
        block_kernel,
        out_shape=(sds(rows, bf16), sds(rows, bf16)) + grad_shapes + (sds((8, model), f32), sds(routed.shape, jnp.int32)),
        in_specs=[hbm] * 11,
        out_specs=[hbm] * 8,
        scratch_shapes=[
            space(wq_shape, bf16), space(wo_shape, bf16), space(wu_shape, bf16), space(wd_shape, bf16),
            space(grid + (16, model), bf16),
            space((part, 3 * half_q), bf16), space((part, half_u), bf16), space((16, model), bf16), space((16, model), bf16),
            *[row_bf16] * 11, space(rows, f32), space(rows, f32),
            space((slots, ranks, 3 * half_q), bf16), space((slots, ranks, half_q), bf16),
            space((slots, ranks, half_u), bf16), space((slots, ranks, half_u), bf16),
            space((slots, ranks, 1), f32), space((16, model), f32),
            space(wd_shape, bf16), space(wu_shape, bf16),
            on_d[0], on_u[0], on_d[1], on_u[1], on_d[2], on_u[2],
            space((3, 2, 2 * part, model), bf16), space((2 * part, model), bf16),
            space((2, part, model), f32), space((part, model), f32), space((part, model), f32),
            space((2, part, half_u), f32), space((down, model), f32),
            space((part, model), bf16), space((part, half_q), bf16), space((part, half_u), bf16),
            space((part, model), bf16), space((part, half_q), bf16), space((part, half_u), bf16),
            space((8, model), f32), space((5, 8, model), f32), space((5, 8, model), f32), space(routed.shape, jnp.int32),
            *[space((1, part), bf16)] * 3, space(routed.shape, jnp.int32), space((1, slots), jnp.int32),
            dma((19,)), dma((15,)), dma((8,)), dma((8, 3)), dma((8,)), dma((8,)), dma((8,)), dma((8,)),
            dma((19,)), dma((19,)), dma((9,)), dma((9,)), dma((2,)), dma((2,)), dma((9,)), dma((9,)), dma((9, 3)), dma((9, 3)),
            pltpu.SemaphoreType.REGULAR((2,)),
        ],
        compiler_params=pltpu.CompilerParams(collective_id=1, has_side_effects=True, vmem_limit_bytes=60 << 20),
        name="block",
    )(
        tokens.reshape(blocked), cotangent.reshape(blocked), w_qkv, w_out, w_up, w_down,
        gain_attn[None], gain_mlp[None], router[None], routed, lengths[None],
    )

    chunks = 2
    vectors = (sds((1, part), f32),) * 3
    output, input_grad, g_qkv, g_out, g_up, g_down, g_one, g_two, g_three = pl.pallas_call(
        rows_kernel,
        out_shape=(sds(tokens.shape, bf16), sds(tokens.shape, bf16)) + grad_shapes + vectors,
        in_specs=[hbm] * 10,
        out_specs=[hbm] * 9,
        scratch_shapes=[
            space((2, slots, chunks, local_len // chunks, model), bf16), space((2,) + rows, bf16),
            *[space(g.shape, f32) for g in grad_shapes],
            space((8, model), f32), space(routed.shape, jnp.int32), *[space((1, part), f32)] * 3,
            dma((2, slots, chunks)), dma((2, slots, chunks)), dma((2, slots)), dma((2, 7)),
        ],
        compiler_params=pltpu.CompilerParams(vmem_limit_bytes=60 << 20),
        name="rows",
    )(tokens, cotangent, upd, dxr, *sums, vec, live)
    return (
        output, input_grad, g_qkv, g_out, g_up, g_down,
        g_one.reshape(part), g_two.reshape(part), g_three.reshape(part),
    )


def solution(mesh):
    in_specs = (
        P("batch", "seq", None),
        P("batch", "seq", None),
        P("batch"),
        P("batch", None),
        P(("seq", "batch"), None),
        P(("seq", "batch"), None),
        P(("seq", "batch"), None),
        P(("seq", "batch"), None),
        P(("seq", "batch")),
        P(("seq", "batch")),
        P(("seq", "batch")),
    )
    out_specs = (
        P("batch", "seq", None),
        P("batch", "seq", None),
        P(("seq", "batch"), None),
        P(("seq", "batch"), None),
        P(("seq", "batch"), None),
        P(("seq", "batch"), None),
        P(("seq", "batch")),
        P(("seq", "batch")),
        P(("seq", "batch")),
    )
    small_slice = mesh.shape["seq"] == 2 and mesh.shape["batch"] == 4 * LINE
    body = split_device if small_slice else general_device
    return jax.shard_map(body, mesh=mesh, in_specs=in_specs, out_specs=out_specs, check_vma=False)
```

```python
import functools

import jax
import jax.numpy as jnp
from jax import lax
from jax.experimental import pallas as pl
from jax.experimental.pallas import tpu as pltpu
from jax.sharding import PartitionSpec as P

HEAD_DIM = 64
MESH = pl.DeviceIdType.MESH


epsilon = 1e-05
highest = lax.Precision.HIGHEST
f32 = jnp.float32
bf16 = jnp.bfloat16

LINE = 4
GELU_C = 0.7978845608
GELU_K = 0.044715


def dot_nn(a, b):
    return lax.dot_general(a, b, (((1,), (0,)), ((), ())), preferred_element_type=f32)


def dot_nt(a, b):
    return lax.dot_general(a, b, (((1,), (1,)), ((), ())), preferred_element_type=f32)


def dot_tn(a, b):
    return lax.dot_general(a, b, (((0,), (0,)), ((), ())), preferred_element_type=f32)


def place():
    s = lax.axis_index("seq")
    b = lax.axis_index("batch")
    return s, b // 4, lax.rem(b // 2, 2), lax.rem(b, 2)


def device(s, z, y, c):
    return (s, z * 4 + y * 2 + c)


def remote(src, dst, send, recv, target):
    return pltpu.make_async_remote_copy(
        src_ref=src, dst_ref=dst, send_sem=send, recv_sem=recv, device_id=target, device_id_type=MESH
    )


def greet(targets):
    barrier = pltpu.get_barrier_semaphore()
    for target in targets:
        pl.semaphore_signal(barrier, inc=1, device_id=target, device_id_type=MESH)
    pl.semaphore_wait(barrier, len(targets))


def inverse_rms(values):
    return lax.rsqrt(jnp.mean(values * values, axis=-1, keepdims=True) + epsilon)


def head_mask(parity):
    lane = lax.broadcasted_iota(jnp.int32, (1, 128), 1)
    return jnp.where(lane // HEAD_DIM == parity, 1.0, 0.0).astype(f32)


def norm_apply(values_in, gain_vec):
    return (
        values_in
        * lax.rsqrt(jnp.mean(values_in * values_in, axis=-1, keepdims=True) + epsilon)
        * gain_vec
    )


def gelu_tanh(values_in):
    return jax.nn.gelu(values_in, approximate=True)


def general_device(
    tokens, cotangent, lengths, routed, w_qkv, w_out, w_up, w_down, gain_attn, gain_mlp, router
):
    slot_count, local_len, model_width = tokens.shape
    capacity = routed.shape[1]
    seq_devices = lax.axis_size("seq")
    own_count = capacity // seq_devices
    head_count = model_width // HEAD_DIM
    row_count = own_count * slot_count
    score_scale = HEAD_DIM ** (-0.5)
    gathered = (
        lax.all_gather(w_qkv, ("seq", "batch"), axis=0, tiled=True),
        lax.all_gather(w_out, ("seq", "batch"), axis=0, tiled=True),
        lax.all_gather(w_up, ("seq", "batch"), axis=0, tiled=True),
        lax.all_gather(w_down, ("seq", "batch"), axis=0, tiled=True),
        lax.all_gather(gain_attn, ("seq", "batch"), axis=0, tiled=True),
        lax.all_gather(gain_mlp, ("seq", "batch"), axis=0, tiled=True),
        lax.all_gather(router, ("seq", "batch"), axis=0, tiled=True),
    )
    full_qkv, full_out, full_up, full_down, full_ga, full_gm, full_router = gathered
    gain_one = full_ga.astype(f32)
    gain_two = full_gm.astype(f32)
    router_vec = full_router.astype(f32)
    counts = lengths // 8
    seq_place = lax.axis_index("seq")
    positions = seq_place * local_len + jnp.arange(local_len, dtype=jnp.int32)
    rank_all = jnp.arange(capacity, dtype=jnp.int32)
    live_all = rank_all[None, :] < counts[:, None]
    chooser = ((routed[:, :, None] == positions[None, None, :]) & live_all[:, :, None]).astype(bf16)
    pick_in = jnp.einsum("scp,spd->csd", chooser, tokens, preferred_element_type=f32)
    pick_cot = jnp.einsum("scp,spd->csd", chooser, cotangent, preferred_element_type=f32)
    picked, picked_cot = (
        lax.psum_scatter(
            pick_in.astype(jnp.bfloat16), "seq", scatter_dimension=0, tiled=True
        ).astype(jnp.float32),
        lax.psum_scatter(
            pick_cot.astype(jnp.bfloat16), "seq", scatter_dimension=0, tiled=True
        ).astype(jnp.float32),
    )
    own_rank = seq_place * own_count + jnp.arange(own_count, dtype=jnp.int32)
    live_own = own_rank[:, None] < counts[None, :]
    live_mask = live_own.reshape(row_count, 1).astype(f32)
    routed_in = picked.reshape(row_count, model_width)
    normed_one = norm_apply(routed_in, gain_one).astype(bf16)
    joined = jnp.dot(normed_one, full_qkv, preferred_element_type=f32).astype(bf16)
    query_rows = joined[:, :model_width].reshape(own_count, slot_count, head_count, HEAD_DIM)
    key_own = joined[:, model_width : 2 * model_width].reshape(own_count, slot_count, model_width)
    value_own = joined[:, 2 * model_width :].reshape(own_count, slot_count, model_width)
    key_every, value_every = (
        lax.all_gather(key_own, "seq", axis=0, tiled=True),
        lax.all_gather(value_own, "seq", axis=0, tiled=True),
    )
    key_rows = key_every.reshape(capacity, slot_count, head_count, HEAD_DIM)
    value_rows = value_every.reshape(capacity, slot_count, head_count, HEAD_DIM)
    scores = (
        jnp.einsum("qsha,ksha->shqk", query_rows, key_rows, preferred_element_type=f32)
        * score_scale
    )
    causal = rank_all[None, :] <= own_rank[:, None]
    allowed = causal[None, :, :] & (rank_all[None, None, :] < counts[:, None, None])
    scores = jnp.where(allowed[:, None], scores, -1000000000.0)
    row_max = jnp.max(scores, axis=-1, keepdims=True)
    weights_f = jnp.exp(scores - row_max)
    row_total = jnp.sum(weights_f, axis=-1, keepdims=True)
    weights_low = weights_f.astype(bf16)
    mixture = jnp.einsum("shqk,ksha->qsha", weights_low, value_rows, preferred_element_type=f32)
    mixture = mixture / jnp.transpose(row_total, (2, 0, 1, 3))
    attended = mixture.reshape(row_count, model_width).astype(bf16)
    branch_a = jnp.dot(attended, full_out, preferred_element_type=f32)
    hidden = routed_in + branch_a
    normed_two = norm_apply(hidden, gain_two).astype(bf16)
    up_proj = jnp.dot(normed_two, full_up, preferred_element_type=f32)
    activated = gelu_tanh(up_proj).astype(bf16)
    branch_m = jnp.dot(activated, full_down, preferred_element_type=f32)
    gate_prob = jax.nn.sigmoid(jnp.dot(routed_in, router_vec, precision=highest))
    branch = branch_a + branch_m
    update = (
        (gate_prob[:, None] * branch * live_mask)
        .astype(bf16)
        .reshape(own_count, slot_count, model_width)
    )
    update_every = lax.all_gather(update, "seq", axis=0, tiled=True)
    output = (
        tokens.astype(f32)
        + jnp.einsum("scp,csd->spd", chooser, update_every, preferred_element_type=f32)
    ).astype(bf16)
    cot_rows = picked_cot.reshape(row_count, model_width)
    grad_gate = jnp.sum(cot_rows * branch, axis=-1)
    grad_logit = grad_gate * gate_prob * (1.0 - gate_prob)
    grad_branch = gate_prob[:, None] * cot_rows
    grad_m = grad_branch.astype(bf16)
    grad_act = jnp.einsum("rd,fd->rf", grad_m, full_down, preferred_element_type=f32)
    unused_up, gelu_pull = jax.vjp(gelu_tanh, up_proj)
    grad_u = gelu_pull(grad_act)[0].astype(bf16)
    grad_n2 = jnp.einsum("rf,df->rd", grad_u, full_up, preferred_element_type=f32)
    unused_two, norm_pull_two = jax.vjp(norm_apply, hidden, gain_two)
    grad_hidden, grad_gm = norm_pull_two(grad_n2)
    grad_a = (grad_branch + grad_hidden).astype(bf16)
    grad_att = jnp.einsum("rd,ed->re", grad_a, full_out, preferred_element_type=f32).astype(bf16)
    grad_att4 = grad_att.reshape(own_count, slot_count, head_count, HEAD_DIM)
    delta_rows = jnp.sum(grad_att4.astype(f32) * mixture, axis=-1)
    delta = jnp.transpose(delta_rows, (1, 2, 0))[..., None]
    grad_p = jnp.einsum("qsha,ksha->shqk", grad_att4, value_rows, preferred_element_type=f32)
    probs = weights_f / row_total
    grad_s = (probs * (grad_p - delta)).astype(bf16)
    grad_q = (
        jnp.einsum("shqk,ksha->qsha", grad_s, key_rows, preferred_element_type=f32) * score_scale
    )
    grad_k = (
        jnp.einsum("shqk,qsha->ksha", grad_s, query_rows, preferred_element_type=f32) * score_scale
    )
    scaled_low = weights_low.astype(f32) / row_total
    grad_v = jnp.einsum("shqk,qsha->ksha", scaled_low, grad_att4.astype(f32), precision=highest)
    grad_k_own, grad_v_own = (
        lax.psum_scatter(
            grad_k.reshape(capacity, slot_count, model_width).astype(jnp.bfloat16),
            "seq",
            scatter_dimension=0,
            tiled=True,
        ).astype(jnp.float32),
        lax.psum_scatter(
            grad_v.reshape(capacity, slot_count, model_width).astype(jnp.bfloat16),
            "seq",
            scatter_dimension=0,
            tiled=True,
        ).astype(jnp.float32),
    )
    grad_joined = jnp.concatenate(
        [
            grad_q.reshape(row_count, model_width),
            grad_k_own.reshape(row_count, model_width),
            grad_v_own.reshape(row_count, model_width),
        ],
        axis=-1,
    ).astype(bf16)
    grad_n1 = jnp.einsum("re,de->rd", grad_joined, full_qkv, preferred_element_type=f32)
    unused_one, norm_pull_one = jax.vjp(norm_apply, routed_in, gain_one)
    grad_x1, grad_ga = norm_pull_one(grad_n1)
    grad_router = jnp.sum(routed_in * grad_logit[:, None], axis=0)
    grad_rows = (grad_hidden + grad_x1 + grad_logit[:, None] * router_vec[None, :]).astype(bf16)
    grad_rows = grad_rows.reshape(own_count, slot_count, model_width)
    grad_every = lax.all_gather(grad_rows, "seq", axis=0, tiled=True)
    input_grad = (
        cotangent.astype(f32)
        + jnp.einsum("scp,csd->spd", chooser, grad_every, preferred_element_type=f32)
    ).astype(bf16)
    part_qkv = jnp.einsum("rd,re->de", normed_one, grad_joined, preferred_element_type=f32)
    part_out = jnp.einsum("re,rd->ed", attended, grad_a, preferred_element_type=f32)
    part_up = jnp.einsum("rd,rf->df", normed_two, grad_u, preferred_element_type=f32)
    part_down = jnp.einsum("rf,rd->fd", activated, grad_m, preferred_element_type=f32)

    def sum_rows(part):
        return lax.psum_scatter(
            part.astype(bf16), ("seq", "batch"), scatter_dimension=0, tiled=True
        ).astype(f32)

    down_sum = sum_rows(part_down)
    grad_up = sum_rows(part_up)
    grad_out = sum_rows(part_out)
    grad_qkv = sum_rows(part_qkv)
    small_ga, small_gm, small_router = (
        lax.psum_scatter(grad_ga, ("seq", "batch"), scatter_dimension=0, tiled=True),
        lax.psum_scatter(grad_gm, ("seq", "batch"), scatter_dimension=0, tiled=True),
        lax.psum_scatter(grad_router, ("seq", "batch"), scatter_dimension=0, tiled=True),
    )
    return (
        output,
        input_grad,
        grad_qkv,
        grad_out,
        grad_up,
        down_sum,
        small_ga,
        small_gm,
        small_router,
    )


def block_kernel(
    tok_hbm, cot_hbm, wq_hbm, wo_hbm, wu_hbm, wd_hbm, one_hbm, two_hbm, three_hbm, routed_hbm, len_hbm,
    upd_out, dx_out, fq_out, fo_out, fu_out, fd_out, vec_out, live_out,
    wq, wo, wu, wd, gv, stq, stu, stv, rcv,
    xs, xr, ds, dr, a_s, a_r, d2s, d2r, d1r, m_s, m_r, hid, dh, qkv, att, act, gp, logit, gains,
    gd, gu, rcd, rcu, ryd, ryu, rzd, rzu, rzb, ryb,
    fqk, fv, fo, fu, fd, sqk, sv, suu, rqk, rv, ruu, vs, vr, v_all, live,
    one_ref, two_ref, three_ref, routed_ref, len_ref,
    loc, out_sem, wz, vz, wy, vy, wc, vc, sx, rx, gc, hc, gt, ht, gy, hy, gz, hz, free,
):
    s, z, y, c = place()
    near, far = z + 1 - 2 * lax.rem(z, 2), LINE - 1 - z
    xdev, ydev, cdev = device(1 - s, z, y, c), device(s, z, 1 - y, c), device(s, z, y, 1 - c)
    ndev, fdev = device(s, near, y, c), device(s, far, y, c)
    model, half_q, half_u = xr.shape[2], att.shape[2], act.shape[2]
    ranks, half = xr.shape[1], xr.shape[2] // 2
    rows = xr.shape[0] * ranks
    part, half_d = stq.shape[0], wd.shape[3] // 2
    local, sent, outs = [], [], []

    def fetch(src, dst):
        copy = pltpu.make_async_copy(src, dst, loc.at[len(local)])
        copy.start()
        local.append(copy)
        return copy

    def send(src, dst, send_sem, recv_sem, target):
        copy = remote(src, dst, send_sem, recv_sem, target)
        copy.start()
        sent.append(copy)
        return copy

    def gone(copy):
        copy.wait_send()
        sent[:] = [other for other in sent if other is not copy]

    def arrive(ref, send_sem, recv_sem, target):
        remote(ref, ref, send_sem, recv_sem, target).wait_recv()

    def put(src, dst):
        copy = pltpu.make_async_copy(src, dst, out_sem.at[len(outs)])
        copy.start()
        outs.append(copy)

    barrier = pltpu.get_barrier_semaphore()
    for target in (xdev, ydev, cdev, ndev, fdev):
        pl.semaphore_signal(barrier, inc=1, device_id=target, device_id_type=MESH)

    stage, own_q = [], []
    small_in = [
        fetch(src, dst)
        for src, dst in (
            (one_hbm, one_ref), (two_hbm, two_ref), (three_hbm, three_ref), (routed_hbm, routed_ref), (len_hbm, len_ref),
        )
    ]
    for j in range(3):
        base, dst = 2 * j * half_q, pl.ds(j * half_q, half_q)
        stage.append(fetch(wq_hbm.at[:, pl.ds(base + (1 - s) * half_q, half_q)], stq.at[:, dst]))
        own_q.append(fetch(wq_hbm.at[:, pl.ds(base + s * half_q, half_q)], wq.at[s, z, y, c, :, dst]))
    get_tok = [fetch(tok_hbm.at[i], gd.at[pl.ds(2 * i, 2)]) for i in range(2)]
    own_o = fetch(wo_hbm, wo.at[z, y, c])
    stage_u = fetch(wu_hbm.at[:, pl.ds((1 - s) * half_u, half_u)], stu)
    own_u = fetch(wu_hbm.at[:, pl.ds(s * half_u, half_u)], wu.at[s, z, y, c])
    own_d = fetch(wd_hbm, wd.at[z, y, c])

    def down_half(i):
        return pl.ds(half_d * i, half_d)

    blocks = [
        lambda zz, yy, cc: wq.at[s, zz, yy, cc],
        lambda zz, yy, cc: wq.at[1 - s, zz, yy, cc],
        lambda zz, yy, cc: gv.at[zz, yy, cc],
        lambda zz, yy, cc: wo.at[zz, yy, cc],
        lambda zz, yy, cc: wu.at[s, zz, yy, cc],
        lambda zz, yy, cc: wu.at[1 - s, zz, yy, cc],
        lambda zz, yy, cc: wd.at[zz, yy, cc, down_half(0)],
        lambda zz, yy, cc: wd.at[zz, yy, cc, down_half(1)],
    ]
    lines = [
        lambda yy, cc: wq.at[s, :, yy, cc],
        lambda yy, cc: wq.at[1 - s, :, yy, cc],
        lambda yy, cc: gv.at[:, yy, cc],
        lambda yy, cc: wo.at[:, yy, cc],
        lambda yy, cc: wu.at[s, :, yy, cc],
        lambda yy, cc: wu.at[1 - s, :, yy, cc],
        lambda yy, cc: wd.at[:, yy, cc, down_half(0)],
        lambda yy, cc: wd.at[:, yy, cc, down_half(1)],
    ]
    Q_OWN, Q_SWAP, VEC, OUT, U_OWN, U_SWAP, D_0, D_1 = range(8)

    planes = [
        lambda cc: wq.at[s, :, :, cc],
        lambda cc: wq.at[1 - s, :, :, cc],
        lambda cc: gv.at[:, :, cc],
        lambda cc: wo.at[:, :, cc],
        lambda cc: wu.at[s, :, :, cc],
        lambda cc: wu.at[1 - s, :, :, cc],
        lambda cc: wd.at[:, :, cc, down_half(0)],
        lambda cc: wd.at[:, :, cc, down_half(1)],
    ]

    def pass_on(ref, send_sem, recv_sem, target):
        remote(ref, ref, send_sem, recv_sem, target).start()

    def spread(p):
        own = blocks[p](z, y, c)
        pass_on(own, wz.at[p], vz.at[p, 0], fdev)
        pass_on(own, wz.at[p], vz.at[p, 1], ndev)

    def spread_y(p):
        pass_on(blocks[p](z, y, c), wy.at[p], vy.at[p], ydev)

    def after_far(p):
        ref = blocks[p](far, y, c)
        arrive(ref, wz.at[p], vz.at[p, 0], fdev)
        pass_on(ref, wz.at[p], vz.at[p, 2], ndev)
        pass_on(ref, wy.at[p], vy.at[p], ydev)

    def after_near(p):
        for i, zz in ((1, near), (2, LINE - 1 - near)):
            ref = blocks[p](zz, y, c)
            arrive(ref, wz.at[p], vz.at[p, i], ndev)
            pass_on(ref, wy.at[p], vy.at[p], ydev)
        pass_on(lines[p](y, c), wc.at[p], vc.at[p], cdev)

    def after_y(p):
        line = lines[p](1 - y, c)
        arrive(line, wy.at[p], vy.at[p], ydev)
        pass_on(line, wc.at[p], vc.at[p], cdev)

    def after_c(p):
        arrive(planes[p](1 - c), wc.at[p], vc.at[p], cdev)

    def both(zz, cc):
        return wd.at[zz, :, cc, down_half(1)]

    def after_first_y():
        arrive(blocks[D_1](z, 1 - y, c), wy.at[D_1], vy.at[D_1], ydev)
        own = both(z, c)
        pass_on(own, wz.at[D_1], vz.at[D_1, 0], fdev)
        pass_on(own, wz.at[D_1], vz.at[D_1, 1], ndev)

    def after_first_far():
        ref = both(far, c)
        arrive(ref, wz.at[D_1], vz.at[D_1, 0], fdev)
        pass_on(ref, wz.at[D_1], vz.at[D_1, 2], ndev)

    def after_first_near():
        for i, zz in ((1, near), (2, LINE - 1 - near)):
            arrive(both(zz, c), wz.at[D_1], vz.at[D_1, i], ndev)
        pass_on(planes[D_1](c), wc.at[D_1], vc.at[D_1], cdev)

    def after_first_c():
        arrive(planes[D_1](1 - c), wc.at[D_1], vc.at[D_1], cdev)

    def left(ref, send_sem, recv_sem, target):
        remote(ref, ref, send_sem, recv_sem, target).wait_send()

    def gathered():
        three = pl.ds(0, LINE - 1)
        passed = [
            wq.at[s, three, y, c], wq.at[1 - s, three, y, c], gv.at[three, y, c], wo.at[three, y, c],
            wu.at[s, three, y, c], wu.at[1 - s, three, y, c], wd.at[three, y, c, down_half(0)],
            wd.at[three, :, c, down_half(1)],
        ]
        for p in range(8):
            left(passed[p], wz.at[p], vz.at[p, 0], ndev)
            left(blocks[p](z, y, c) if p == D_1 else lines[p](y, c), wy.at[p], vy.at[p], ydev)
            left(planes[p](c), wc.at[p], vc.at[p], cdev)

    spans = [pl.ds(0, 2 * part), pl.ds(2 * part, 2 * part), None, None]
    spans += [pl.ds(i * part, part) for i in range(4)]
    parts = [
        (lambda cc, i=i: gu.at[i - 2, :, :, cc]) if q is None else (lambda cc, q=q: gd.at[:, :, cc, q])
        for i, q in enumerate(spans)
    ]
    land_c = [rcu.at[i - 2] if q is None else rcd.at[:, :, q] for i, q in enumerate(spans)]
    land_y = [ryu.at[i - 2] if q is None else ryd.at[:, q] for i, q in enumerate(spans)]
    land_z = [rzu.at[i - 2] if q is None else rzd.at[:, q] for i, q in enumerate(spans)]

    def c_start(k):
        return send(parts[k](1 - c), land_c[k], gc.at[k], hc.at[k], cdev)

    def c_end(k):
        ref, own = land_c[k], parts[k](c)
        if k < 2:
            arrive(ref, gt.at[k], ht.at[k], cdev)
        else:
            arrive(ref, gc.at[k], hc.at[k], cdev)

        def add(i, carry):
            ref[i] = (ref[i].astype(f32) + own[i].astype(f32)).astype(bf16)
            return carry

        lax.fori_loop(0, LINE, add, 0)
        if k == 0:
            return [
                send(ref.at[LINE - 1 - near], rzb.at[1], gz.at[k, 1], hz.at[k, 1], ndev),
                send(ref.at[near], rzb.at[0], gz.at[k, 0], hz.at[k, 0], ndev),
            ]
        return [send(ref.at[:, 1 - y], land_y[k], gy.at[k], hy.at[k], ydev)]

    def y_end(k):
        ref, own = land_y[k], land_c[k]
        arrive(ref, gy.at[k], hy.at[k], ydev)

        def add(i, carry):
            ref[i] = (ref[i].astype(f32) + own[i, y].astype(f32)).astype(bf16)
            return carry

        lax.fori_loop(0, LINE, add, 0)
        return [
            send(ref.at[LINE - 1 - near], land_z[k].at[1], gz.at[k, 1], hz.at[k, 1], ndev),
            send(ref.at[near], land_z[k].at[0], gz.at[k, 0], hz.at[k, 0], ndev),
        ]

    def z_mid(k):
        ref = land_z[k].at[1]
        arrive(ref, gz.at[k, 1], hz.at[k, 1], ndev)
        ref[...] = (ref[...].astype(f32) + land_y[k][far].astype(f32)).astype(bf16)
        return send(ref, land_z[k].at[2], gz.at[k, 2], hz.at[k, 2], fdev)

    def z_end(k):
        arrive(land_z[k].at[0], gz.at[k, 0], hz.at[k, 0], ndev)
        arrive(land_z[k].at[2], gz.at[k, 2], hz.at[k, 2], fdev)
        return land_y[k][z].astype(f32) + land_z[k][0].astype(f32) + land_z[k][2].astype(f32)

    def first_mid():
        arrive(rzb.at[1], gz.at[0, 1], hz.at[0, 1], ndev)
        rzb[1] = (rzb[1].astype(f32) + land_c[0][far].astype(f32)).astype(bf16)
        return send(rzb.at[1], rzb.at[2], gz.at[0, 2], hz.at[0, 2], fdev)

    def first_end():
        arrive(rzb.at[0], gz.at[0, 0], hz.at[0, 0], ndev)
        arrive(rzb.at[2], gz.at[0, 2], hz.at[0, 2], fdev)
        rzb[0] = (land_c[0][z].astype(f32) + rzb[0].astype(f32) + rzb[2].astype(f32)).astype(bf16)
        return send(rzb.at[0, 1 - y], ryb, gy.at[0], hy.at[0], ydev)

    def first_sum():
        arrive(ryb, gy.at[0], hy.at[0], ydev)
        return rzb[0, y].astype(f32) + ryb[...].astype(f32)

    for copy in small_in:
        copy.wait()
    fits = lax.broadcasted_iota(jnp.int32, (part, model), 1) == s * part + lax.broadcasted_iota(
        jnp.int32, (part, model), 0
    )
    line = lax.broadcasted_iota(jnp.int32, (16, part), 0)
    small = jnp.zeros((16, part), f32)
    for j, ref in enumerate((one_ref, two_ref, three_ref)):
        small = jnp.where(line == j, ref[...].astype(f32), small)
    gains[...] = dot_nn(small.astype(bf16), jnp.where(fits, 1.0, 0.0).astype(bf16))
    stv[...] = gains[:, 0:128].astype(bf16)

    rank = lax.broadcasted_iota(jnp.int32, (1, ranks), 1)

    def count(i):
        return lax.shift_right_arithmetic(len_ref[:, i : i + 1], 3)

    for i in range(2):
        live[i : i + 1] = jnp.where(rank < count(i), routed_ref[i : i + 1], -1)

    def chooser(i):
        row = live[i : i + 1].astype(f32)
        eye = lax.broadcasted_iota(jnp.int32, (ranks, ranks), 0) == lax.broadcasted_iota(
            jnp.int32, (ranks, ranks), 1
        )
        column = jnp.sum(jnp.where(eye, row, 0.0), axis=1, keepdims=True).astype(jnp.int32)
        count_here = tok_hbm.shape[1] * 512
        position = lax.broadcasted_iota(jnp.int32, (ranks, count_here), 1) + s * count_here
        return jnp.where(position == column, 1.0, 0.0).astype(bf16)

    def pick(i, dst):
        dst[i] = dot_nn(chooser(i), gd[2 * i : 2 * i + 2].reshape(tok_hbm.shape[1] * 512, model)).astype(bf16)

    def live_column(i):
        rank = lax.broadcasted_iota(jnp.int32, (ranks, 1), 0)
        return jnp.where(rank < count(i), 1.0, 0.0).astype(f32)

    def allowed(i):
        query = lax.broadcasted_iota(jnp.int32, (ranks, ranks), 0)
        key = lax.broadcasted_iota(jnp.int32, (ranks, ranks), 1)
        return (key <= query) & (key < count(i))

    for copy in stage:
        copy.wait()
    pl.semaphore_wait(barrier, 5)
    send(stq, wq.at[s, z, y, c], sx.at[1], rx.at[1], xdev)
    swap_v = send(stv, rcv, sx.at[0], rx.at[0], xdev)
    for copy in own_q:
        copy.wait()
    spread(Q_OWN)
    spread_y(Q_OWN)
    own_d.wait()
    spread_y(D_1)
    x_swap = []
    get_tok[0].wait()
    pick(0, xs)
    x_swap.append(send(xs.at[0], xr.at[0], sx.at[3], rx.at[3], xdev))
    get_cot = [fetch(cot_hbm.at[0], gd.at[pl.ds(0, 2)])]
    stage_u.wait()
    send(stu, wu.at[s, z, y, c], sx.at[2], rx.at[2], xdev)
    get_tok[1].wait()
    pick(1, xs)
    x_swap.append(send(xs.at[1], xr.at[1], sx.at[4], rx.at[4], xdev))
    get_cot.append(fetch(cot_hbm.at[1], gd.at[pl.ds(2, 2)]))
    put(live, live_out)
    swap_v.wait_recv()
    gv[z, y, c] = stv[...] + rcv[...]
    after_far(Q_OWN)
    spread(VEC)
    spread_y(VEC)
    arrive(wq.at[1 - s, z, y, c], sx.at[1], rx.at[1], xdev)
    spread(Q_SWAP)
    spread_y(Q_SWAP)
    get_cot[0].wait()
    pick(0, ds)
    d_swap = [send(ds.at[0], dr.at[0], sx.at[7], rx.at[7], xdev)]
    after_near(Q_OWN)
    after_far(VEC)
    get_cot[1].wait()
    pick(1, ds)
    after_far(Q_SWAP)
    own_o.wait()
    spread(OUT)
    after_near(VEC)
    after_near(Q_SWAP)
    after_far(OUT)
    spread_y(OUT)
    own_u.wait()
    spread(U_OWN)
    spread_y(U_OWN)
    arrive(wu.at[1 - s, z, y, c], sx.at[2], rx.at[2], xdev)
    spread(U_SWAP)
    after_y(Q_OWN)
    after_y(VEC)
    after_c(Q_OWN)
    after_c(VEC)
    after_near(OUT)
    after_y(Q_SWAP)
    after_far(U_OWN)
    spread(D_0)
    spread_y(U_SWAP)
    spread_y(D_0)
    after_c(Q_SWAP)

    group = lax.broadcasted_iota(jnp.int32, (16, 128), 1) // part
    for q in range(LINE):
        for i in range(2):
            tile = jnp.zeros((16, 128), f32)
            for j in range(4):
                moved = pltpu.roll(gv[q, j // 2, j % 2].astype(f32), (j - i) * part % 128, 1)
                tile = jnp.where(group == j, moved, tile)
            gains[:, i * half + q * 128 : i * half + (q + 1) * 128] = tile
    gain_one, gain_two, router = gains[0:1], gains[1:2], gains[2:3]

    def enter(i):
        x_swap[i].wait()
        row = xr[i].astype(f32) + xs[i].astype(f32)
        xr[i] = row.astype(bf16)
        xs[i] = (row * inverse_rms(row) * gain_one).astype(bf16)
        for j in range(3):
            cols = pl.ds(j * half_q, half_q)
            qkv[i, :, cols] = dot_nn(xs[i], wq[:, :, :, :, :, cols].reshape(model, half_q)).astype(bf16)

    def attend(i):
        ok = allowed(i)

        def pair(j, carry):
            q2 = qkv[i, :, pl.ds(j * 128, 128)].astype(f32)
            k2 = qkv[i, :, pl.ds(half_q + j * 128, 128)]
            v2 = qkv[i, :, pl.ds(2 * half_q + j * 128, 128)]
            mixed = jnp.zeros(q2.shape, f32)
            for parity in range(2):
                mask = head_mask(parity)
                score = dot_nt((q2 * mask).astype(bf16), k2) * (HEAD_DIM**-0.5)
                score = jnp.where(ok, score, -1000000000.0)
                weight = jnp.exp(score - jnp.max(score, axis=-1, keepdims=True))
                total = jnp.sum(weight, axis=-1, keepdims=True)
                mixed += dot_nn(weight.astype(bf16), v2) / total * mask
            att[i, :, pl.ds(j * 128, 128)] = mixed.astype(bf16)
            return carry

        lax.fori_loop(0, half_q // 128, pair, 0)

    def leave(i):
        for j in range(2):
            cols = pl.ds(j * half, half)
            a_s[i, :, cols] = dot_nn(att[i], wo[:, :, :, :, cols].reshape(half_q, half)).astype(bf16)
        return send(a_s.at[i], a_r.at[i], sx.at[5 + i], rx.at[5 + i], xdev)

    enter(0)
    attend(0)
    after_y(OUT)
    after_c(OUT)
    a_swap = [leave(0)]
    after_far(U_SWAP)
    after_first_y()
    after_near(U_OWN)
    enter(1)
    attend(1)
    a_swap.append(leave(1))
    d_swap.append(send(ds.at[1], dr.at[1], sx.at[8], rx.at[8], xdev))
    after_far(D_0)
    after_near(U_SWAP)
    after_y(U_OWN)
    after_c(U_OWN)

    def mlp_up(i):
        a_swap[i].wait()
        row = xr[i].astype(f32) + (a_s[i].astype(f32) + a_r[i].astype(f32))
        hid[i] = row
        a_s[i] = (row * inverse_rms(row) * gain_two).astype(bf16)

        def tile(t, carry):
            cols = pl.ds(t * 512, 512)
            up = dot_nn(a_s[i], wu[:, :, :, :, :, cols].reshape(model, 512))
            curve = jnp.tanh(GELU_C * (up + GELU_K * up * up * up))
            act[i, :, cols] = (0.5 * up * (1.0 + curve)).astype(bf16)
            slope = 0.5 * (1.0 + curve) + 0.5 * up * (1.0 - curve * curve) * (
                GELU_C * (1.0 + 3.0 * GELU_K * up * up)
            )
            gp[i, :, cols] = slope.astype(bf16)
            return carry

        lax.fori_loop(0, half_u // 512, tile, 0)

    def gate_of(i):
        return jax.nn.sigmoid(jnp.sum(xr[i].astype(f32) * router, axis=-1, keepdims=True))

    def cotangent_rows(i):
        d_swap[i].wait()
        row = dr[i].astype(f32) + ds[i].astype(f32)
        dr[i] = row.astype(bf16)
        ds[i] = (gate_of(i) * row).astype(bf16)

    def mlp_back(i):
        def tile(t, carry):
            cols = pl.ds(t * 512, 512)
            back = dot_nt(ds[i], wd[t].reshape(512, model))
            gp[i, :, cols] = (back * gp[i, :, cols].astype(f32)).astype(bf16)
            return carry

        lax.fori_loop(0, half_u // 512, tile, 0)
        for j in range(2):
            cols = pl.ds(j * half, half)
            d2s[i, :, cols] = dot_nt(gp[i], wu[j].reshape(half, half_u)).astype(bf16)
        return send(d2s.at[i], d2r.at[i], sx.at[9 + i], rx.at[9 + i], xdev)

    def mlp_out(i):
        for j in range(2):
            cols = pl.ds(j * half, half)
            m_s[i, :, cols] = dot_nn(act[i], wd[:, :, :, :, cols].reshape(half_u, half)).astype(bf16)

    def mlp_send(i):
        return send(m_s.at[i], m_r.at[i], sx.at[11 + i], rx.at[11 + i], xdev)

    after_y(U_SWAP)
    after_first_far()
    after_c(U_SWAP)
    mlp_up(0)
    after_near(D_0)
    cotangent_rows(0)

    def down_tile(t, carry):
        gd[t] = dot_tn(act[0, :, pl.ds(t * 512, 512)], ds[0]).astype(bf16).reshape(gd.shape[1:])
        return carry

    lax.fori_loop(0, LINE, down_tile, 0)
    mlp_up(1)
    after_y(D_0)
    after_c(D_0)
    after_first_near()
    after_first_c()
    d2_swap = [mlp_back(0)]
    cotangent_rows(1)

    def c_tile(t, k):
        remote(gd.at[t, :, 1 - c, spans[k]], land_c[k].at[t], gt.at[k], ht.at[k], cdev).start()

    for t in range(LINE):
        grad = dot_tn(act[1, :, t * 512 : t * 512 + 512], ds[1])
        gd[t] = (gd[t].astype(f32) + grad.reshape(gd.shape[1:])).astype(bf16)
        c_tile(t, 1)
    for t in range(LINE):
        c_tile(t, 0)
    y_down = c_end(1)
    z_first = c_end(0)
    d2_swap.append(mlp_back(1))
    mlp_out(0)
    m_swap = [mlp_send(0)]

    def up_tile(t, carry):
        cols = pl.ds(t * 512, 512)
        grad = dot_tn(a_s[...].reshape(rows, model), gp[:, :, cols].reshape(rows, 512))
        gu[:, :, :, :, :, cols] = grad.astype(bf16).reshape(gu.shape[:5] + (512,))
        return carry

    lax.fori_loop(0, half_u // 512, up_tile, 0)
    c_start(2)
    c_start(3)
    mlp_out(1)
    m_swap.append(mlp_send(1))

    def hidden_back(i):
        d2_swap[i].wait()
        back = d2s[i].astype(f32) + d2r[i].astype(f32)
        row = hid[i]
        r2 = inverse_rms(row)
        scaled = back * gain_two
        step = r2 * scaled - row * (r2 * r2 * r2 * jnp.mean(scaled * row, axis=-1, keepdims=True))
        dh[i] = step
        gp[i, :, 0:model] = (gate_of(i) * dr[i].astype(f32) + step).astype(bf16)
        gp[i, :, model : model + half_q] = dot_nt(gp[i, :, 0:model], wo[...].reshape(half_q, model)).astype(bf16)
        return jnp.sum(d2s[i].astype(f32) * row * r2, axis=0, keepdims=True)

    def attend_back(i):
        ok = allowed(i)
        scale = HEAD_DIM**-0.5

        def pair(j, carry):
            q2 = qkv[i, :, pl.ds(j * 128, 128)]
            k2 = qkv[i, :, pl.ds(half_q + j * 128, 128)]
            v2 = qkv[i, :, pl.ds(2 * half_q + j * 128, 128)]
            g2 = gp[i, :, pl.ds(model + j * 128, 128)].astype(f32)
            q2f = q2.astype(f32)
            dq2 = jnp.zeros(q2.shape, f32)
            dk2 = jnp.zeros(q2.shape, f32)
            dv2 = jnp.zeros(q2.shape, f32)
            for parity in range(2):
                mask = head_mask(parity)
                score = dot_nt((q2f * mask).astype(bf16), k2) * scale
                score = jnp.where(ok, score, -1000000000.0)
                weight = jnp.exp(score - jnp.max(score, axis=-1, keepdims=True))
                over = 1.0 / jnp.sum(weight, axis=-1, keepdims=True)
                gh = g2 * mask
                dp = dot_nt(gh.astype(bf16), v2)
                prob = weight * over
                delta = jnp.sum(prob * dp, axis=-1, keepdims=True)
                dscore = (prob * (dp - delta)).astype(bf16)
                dq2 += dot_nn(dscore, k2) * mask
                dk2 += dot_tn(dscore, q2) * mask
                dv2 += dot_tn(weight.astype(bf16), (gh * over).astype(bf16))
            act[i, :, pl.ds(j * 128, 128)] = (dq2 * scale).astype(bf16)
            act[i, :, pl.ds(half_q + j * 128, 128)] = (dk2 * scale).astype(bf16)
            act[i, :, pl.ds(2 * half_q + j * 128, 128)] = dv2.astype(bf16)
            return carry

        lax.fori_loop(0, half_q // 128, pair, 0)

    def inner_back(i):
        r1 = inverse_rms(xr[i].astype(f32))
        sums = []
        for j in range(2):
            cols = pl.ds(j * half, half)
            step = dot_nt(act[i, :, 0 : 3 * half_q], wq[j].reshape(half, 3 * half_q))
            d2s[i, :, cols] = step.astype(bf16)
            sums.append(jnp.sum(step * xr[i, :, cols].astype(f32) * r1, axis=0, keepdims=True))
        return send(d2s.at[i], d1r.at[i], sx.at[13 + i], rx.at[13 + i], xdev), sums

    grad_gm = hidden_back(0)
    c_end(2)
    attend_back(0)
    c_end(3)
    z_first.append(first_mid())
    swap_0, sums_0 = inner_back(0)
    z_down = y_end(1)
    grad_gm += hidden_back(1)
    attend_back(1)
    z_down.append(z_mid(1))
    for k in range(2):
        left(parts[k](1 - c), gt.at[k], ht.at[k], cdev)
    for copy in z_first:
        gone(copy)
    first_end()
    pl.semaphore_signal(free.at[0], inc=1, device_id=cdev, device_id_type=MESH)
    y_end(2)

    def out_tile(t):
        cols = pl.ds(t * half, half)
        grad = dot_tn(att[...].reshape(rows, half_q), gp[:, :, cols].reshape(rows, half))
        gd[:, :, :, 3 * part :, cols] = grad.astype(bf16).reshape(wo.shape[:4] + (half,))

    def qkv_tile(t):
        grad = dot_tn(xs[...].reshape(rows, model), act[:, :, t * half_q : (t + 1) * half_q].reshape(rows, half_q))
        grad = grad.astype(bf16).reshape(wq.shape[:5] + (half_q,))
        if t < 2:
            gd[:, :, :, 0:part, t * half_q : (t + 1) * half_q] = grad[0]
            gd[:, :, :, part : 2 * part, t * half_q : (t + 1) * half_q] = grad[1]
        else:
            gd[:, :, :, 2 * part : 3 * part, 0:half_q] = grad[0]
            gd[:, :, :, 2 * part : 3 * part, half_q:] = grad[1]

    qkv_tile(0)
    qkv_tile(1)
    pl.semaphore_wait(free.at[0], 1)
    c_start(4)
    c_start(5)
    qkv_tile(2)
    fd[2 * part :] = z_end(1)
    for copy in y_down + z_down:
        gone(copy)
    for target in (ydev, cdev, ndev, fdev):
        pl.semaphore_signal(free.at[1], inc=1, device_id=target, device_id_type=MESH)
    out_tile(0)
    out_tile(1)
    c_end(4)
    c_end(5)
    swap_1, sums_1 = inner_back(1)
    d1_swap = [swap_0, swap_1]
    for j in range(2):
        gains[8:9, j * half : (j + 1) * half] = sums_0[j] + sums_1[j]
    gains[9:10] = grad_gm
    pl.semaphore_wait(free.at[1], 4)
    c_start(6)
    c_start(7)
    z_mid(2)
    c_end(6)
    y_end(3)
    fu[0] = z_end(2)

    grad_router = jnp.zeros((1, model), f32)
    for i in range(2):
        m_swap[i].wait()
        row = xr[i].astype(f32)
        gate = gate_of(i)
        branch = (hid[i] - row) + (m_s[i].astype(f32) + m_r[i].astype(f32))
        m_s[i] = (gate * branch * live_column(i)).astype(bf16)
        slope = jnp.sum(dr[i].astype(f32) * branch, axis=-1, keepdims=True) * gate * (1.0 - gate)
        logit[i] = slope
        grad_router += jnp.sum(row * slope, axis=0, keepdims=True)
    put(m_s, upd_out)
    gains[10:11] = 0.5 * grad_router
    for j in range(3):
        for t in range(model // 128):
            vs[8 * j + t : 8 * j + t + 1] = gains[8 + j : 9 + j, t * 128 : (t + 1) * 128]
    send(vs, vr.at[0], gc.at[8], hc.at[8], cdev)
    z_mid(3)
    arrive(vr.at[0], gc.at[8], hc.at[8], cdev)
    v_all[0] = vs[...] + vr[0]
    send(v_all.at[0], vr.at[1], gz.at[8, 0], hz.at[8, 0], ndev)
    c_end(7)
    fd[0 : 2 * part] = first_sum()
    put(fd, fd_out)
    y_end(4)
    fu[1] = z_end(3)
    suu[...] = fu[1 - s].astype(bf16)
    send(suu, ruu, sx.at[15], rx.at[15], xdev)
    put(fu.at[s], fu_out.at[:, pl.ds(s * half_u, half_u)])
    arrive(vr.at[1], gz.at[8, 0], hz.at[8, 0], ndev)
    v_all[1] = v_all[0] + vr[1]
    send(v_all.at[1], vr.at[2], gz.at[8, 1], hz.at[8, 1], fdev)
    z_mid(4)
    y_end(5)

    def rows_back(i):
        d1_swap[i].wait()
        row = xr[i].astype(f32)
        r1 = inverse_rms(row)
        scaled = (d2s[i].astype(f32) + d1r[i].astype(f32)) * gain_one
        step = r1 * scaled - row * (r1 * r1 * r1 * jnp.mean(scaled * row, axis=-1, keepdims=True))
        d2s[i] = (dh[i] + step + logit[i] * router).astype(bf16)
        put(d2s.at[i], dx_out.at[i])

    rows_back(0)
    arrive(vr.at[2], gz.at[8, 1], hz.at[8, 1], fdev)
    v_all[2] = v_all[1] + vr[2]
    send(v_all.at[2], vr.at[3], gy.at[8], hy.at[8], ydev)
    z_mid(5)
    y_end(6)
    z_mid(6)
    y_end(7)
    arrive(vr.at[3], gy.at[8], hy.at[8], ydev)
    v_all[3] = v_all[2] + vr[3]
    send(v_all.at[3], vr.at[4], sx.at[18], rx.at[18], xdev)
    for i in range(2):
        fqk[i] = z_end(4 + i)
    sqk[...] = fqk[1 - s].astype(bf16)
    send(sqk, rqk, sx.at[16], rx.at[16], xdev)
    for j in range(2):
        put(fqk.at[s, :, pl.ds(j * half_q, half_q)], fq_out.at[:, pl.ds(2 * j * half_q + s * half_q, half_q)])
    fv[...] = z_end(6)
    sv[...] = fv[:, pl.ds((1 - s) * half_q, half_q)].astype(bf16)
    send(sv, rv, sx.at[17], rx.at[17], xdev)
    put(fv.at[:, pl.ds(s * half_q, half_q)], fq_out.at[:, pl.ds(4 * half_q + s * half_q, half_q)])
    z_mid(7)
    rows_back(1)
    arrive(ruu, sx.at[15], rx.at[15], xdev)
    fu[1 - s] = ruu[...].astype(f32)
    put(fu.at[1 - s], fu_out.at[:, pl.ds((1 - s) * half_u, half_u)])
    arrive(rqk, sx.at[16], rx.at[16], xdev)
    fqk[1 - s] = rqk[...].astype(f32)
    for j in range(2):
        put(
            fqk.at[1 - s, :, pl.ds(j * half_q, half_q)],
            fq_out.at[:, pl.ds(2 * j * half_q + (1 - s) * half_q, half_q)],
        )
    fo[...] = z_end(7)
    put(fo, fo_out)
    arrive(rv, sx.at[17], rx.at[17], xdev)
    fv[:, pl.ds((1 - s) * half_q, half_q)] = rv[...].astype(f32)
    put(
        fv.at[:, pl.ds((1 - s) * half_q, half_q)],
        fq_out.at[:, pl.ds(4 * half_q + (1 - s) * half_q, half_q)],
    )
    arrive(vr.at[4], sx.at[18], rx.at[18], xdev)
    v_all[4] = v_all[3] + vr[4]
    put(v_all.at[4], vec_out)
    gathered()
    waited = x_swap + a_swap + d_swap + d2_swap + m_swap + d1_swap
    for copy in list(sent):
        if not any(copy is other for other in waited):
            copy.wait_send()
    for copy in outs:
        copy.wait()


def rows_kernel(
    tok_hbm, cot_hbm, upd_hbm, dx_hbm, fq_hbm, fo_hbm, fu_hbm, fd_hbm, vec_hbm, live_hbm,
    out_hbm, grad_hbm, fq_out, fo_out, fu_out, fd_out, one_out, two_out, three_out,
    bases, moved, fq, fo, fu, fd, vec_ref, live_ref, one, two, three, get_sem, put_sem, rows_sem, pass_sem,
):
    s = lax.axis_index("seq")
    _, slots, chunks, tall, model = bases.shape
    ranks = moved.shape[2]
    whole = (tok_hbm, cot_hbm), (out_hbm, grad_hbm)
    tasks = [(i, t) for i in range(slots) for t in range(chunks)]

    def part_of(ref, i, t):
        return ref.at[i, pl.ds(t * tall, tall)]

    gets, puts = {}, []
    rows = [
        pltpu.make_async_copy(src.at[i], moved.at[a, i], rows_sem.at[a, i])
        for i in range(slots)
        for a, src in enumerate((upd_hbm, dx_hbm))
    ]
    get_live = pltpu.make_async_copy(live_hbm, live_ref, pass_sem.at[0, 4])
    get_vec = pltpu.make_async_copy(vec_hbm, vec_ref, pass_sem.at[0, 5])
    get_live.start()
    for i, t in tasks:
        for a in range(2):
            if t == 0:
                rows[2 * i + a].start()
            gets[a, i, t] = pltpu.make_async_copy(part_of(whole[0][a], i, t), bases.at[a, i, t], get_sem.at[a, i, t])
            gets[a, i, t].start()
    through = ((fq_hbm, fq, fq_out), (fo_hbm, fo, fo_out), (fu_hbm, fu, fu_out), (fd_hbm, fd, fd_out))
    taken = [pltpu.make_async_copy(src, mid, pass_sem.at[0, j]) for j, (src, mid, _) in enumerate(through)]
    passed = [pltpu.make_async_copy(mid, dst, pass_sem.at[1, j]) for j, (_, mid, dst) in enumerate(through)]
    for copy in taken + [get_vec]:
        copy.start()
    get_live.wait()
    for n, (i, t) in enumerate(tasks):
        if n == len(tasks) - 2:
            for j in range(4):
                taken[j].wait()
                passed[j].start()
        position = lax.broadcasted_iota(jnp.int32, (tall, ranks), 0) + ((s * chunks + t) * tall)
        chooser = jnp.where(position == live_ref[i : i + 1], 1.0, 0.0).astype(bf16)
        for a in range(2):
            if t == 0:
                rows[2 * i + a].wait()
            gets[a, i, t].wait()
            bases[a, i, t] += dot_nn(chooser, moved[a, i]).astype(bf16)
            copy = pltpu.make_async_copy(bases.at[a, i, t], part_of(whole[1][a], i, t), put_sem.at[a, i, t])
            copy.start()
            puts.append(copy)
    part = one.shape[1]
    get_vec.wait()
    flat = s * lax.axis_size("batch") + lax.axis_index("batch")
    each = 128 // part
    lane = lax.broadcasted_iota(jnp.int32, (part, 128), 1)
    here = lane == lax.rem(flat, each) * part + lax.broadcasted_iota(jnp.int32, (part, 128), 0)
    eye = lax.broadcasted_iota(jnp.int32, (part, part), 0) == lax.broadcasted_iota(jnp.int32, (part, part), 1)
    for j, (ref, dst) in enumerate(((one, one_out), (two, two_out), (three, three_out))):
        line = vec_ref[pl.ds(8 * j + flat // each, 1)]
        column = jnp.sum(jnp.where(here, line, 0.0), axis=1, keepdims=True)
        ref[...] = jnp.sum(jnp.where(eye, column, 0.0), axis=0, keepdims=True)
        puts.append(pltpu.make_async_copy(ref, dst, pass_sem.at[1, 4 + j]))
        puts[-1].start()
    for copy in passed + puts:
        copy.wait()


def split_device(
    tokens, cotangent, lengths, routed, w_qkv, w_out, w_up, w_down, gain_attn, gain_mlp, router
):
    slots, local_len, model = tokens.shape
    ranks = routed.shape[1]
    half_q, half_u = w_qkv.shape[1] // 6, w_up.shape[1] // 2
    part, down = w_qkv.shape[0], w_down.shape[0]
    hbm = pl.BlockSpec(memory_space=pl.ANY)
    sds, space, dma = jax.ShapeDtypeStruct, pltpu.VMEM, pltpu.SemaphoreType.DMA
    rows = (slots, ranks, model)
    grid = (LINE, 2, 2)
    wq_shape, wo_shape = (2,) + grid + (part, 3 * half_q), grid + (part, model)
    wu_shape, wd_shape = (2,) + grid + (part, half_u), grid + (down, model)
    blocked = (slots, local_len // 512, 2, 2, 128, model)
    row_bf16 = space(rows, bf16)

    def land(lead, tall, wide):
        return [space(lead + mid + (tall, wide), bf16) for mid in ((LINE, 2), (LINE,), (3,))]

    on_d, on_u = land((), down, model), land((2,), part, half_u)
    grad_shapes = (
        sds((part, 6 * half_q), f32), sds((part, model), f32), sds((part, 2 * half_u), f32), sds((down, model), f32),
    )
    upd, dxr, *sums, vec, live = pl.pallas_call(
        block_kernel,
        out_shape=(sds(rows, bf16), sds(rows, bf16)) + grad_shapes + (sds((24, 128), f32), sds(routed.shape, jnp.int32)),
        in_specs=[hbm] * 11,
        out_specs=[hbm] * 8,
        scratch_shapes=[
            space(wq_shape, bf16), space(wo_shape, bf16), space(wu_shape, bf16), space(wd_shape, bf16),
            space(grid + (16, 128), bf16),
            space((part, 3 * half_q), bf16), space((part, half_u), bf16), space((16, 128), bf16), space((16, 128), bf16),
            *[row_bf16] * 11, space(rows, f32), space(rows, f32),
            space((slots, ranks, 3 * half_q), bf16), space((slots, ranks, half_q), bf16),
            space((slots, ranks, half_u), bf16), space((slots, ranks, half_u), bf16),
            space((slots, ranks, 1), f32), space((16, model), f32),
            space(wd_shape, bf16), space(wu_shape, bf16),
            on_d[0], on_u[0], on_d[1], on_u[1], on_d[2], on_u[2],
            space((3, 2, 2 * part, model), bf16), space((2 * part, model), bf16),
            space((2, part, model), f32), space((part, model), f32), space((part, model), f32),
            space((2, part, half_u), f32), space((down, model), f32),
            space((part, model), bf16), space((part, half_q), bf16), space((part, half_u), bf16),
            space((part, model), bf16), space((part, half_q), bf16), space((part, half_u), bf16),
            space((24, 128), f32), space((5, 24, 128), f32), space((5, 24, 128), f32), space(routed.shape, jnp.int32),
            *[space((1, part), bf16)] * 3, space(routed.shape, jnp.int32), space((1, slots), jnp.int32),
            dma((19,)), dma((15,)), dma((8,)), dma((8, 3)), dma((8,)), dma((8,)), dma((8,)), dma((8,)),
            dma((19,)), dma((19,)), dma((9,)), dma((9,)), dma((2,)), dma((2,)), dma((9,)), dma((9,)), dma((9, 3)), dma((9, 3)),
            pltpu.SemaphoreType.REGULAR((2,)),
        ],
        compiler_params=pltpu.CompilerParams(collective_id=1, has_side_effects=True, vmem_limit_bytes=60 << 20),
        name="block",
    )(
        tokens.reshape(blocked), cotangent.reshape(blocked), w_qkv, w_out, w_up, w_down,
        gain_attn[None], gain_mlp[None], router[None], routed, lengths[None],
    )

    chunks = 2
    vectors = (sds((1, part), f32),) * 3
    output, input_grad, g_qkv, g_out, g_up, g_down, g_one, g_two, g_three = pl.pallas_call(
        rows_kernel,
        out_shape=(sds(tokens.shape, bf16), sds(tokens.shape, bf16)) + grad_shapes + vectors,
        in_specs=[hbm] * 10,
        out_specs=[hbm] * 9,
        scratch_shapes=[
            space((2, slots, chunks, local_len // chunks, model), bf16), space((2,) + rows, bf16),
            *[space(g.shape, f32) for g in grad_shapes],
            space((24, 128), f32), space(routed.shape, jnp.int32), *[space((1, part), f32)] * 3,
            dma((2, slots, chunks)), dma((2, slots, chunks)), dma((2, slots)), dma((2, 7)),
        ],
        compiler_params=pltpu.CompilerParams(vmem_limit_bytes=60 << 20),
        name="rows",
    )(tokens, cotangent, upd, dxr, *sums, vec, live)
    return (
        output, input_grad, g_qkv, g_out, g_up, g_down,
        g_one.reshape(part), g_two.reshape(part), g_three.reshape(part),
    )


def solution(mesh):
    in_specs = (
        P("batch", "seq", None),
        P("batch", "seq", None),
        P("batch"),
        P("batch", None),
        P(("seq", "batch"), None),
        P(("seq", "batch"), None),
        P(("seq", "batch"), None),
        P(("seq", "batch"), None),
        P(("seq", "batch")),
        P(("seq", "batch")),
        P(("seq", "batch")),
    )
    out_specs = (
        P("batch", "seq", None),
        P("batch", "seq", None),
        P(("seq", "batch"), None),
        P(("seq", "batch"), None),
        P(("seq", "batch"), None),
        P(("seq", "batch"), None),
        P(("seq", "batch")),
        P(("seq", "batch")),
        P(("seq", "batch")),
    )
    small_slice = mesh.shape["seq"] == 2 and mesh.shape["batch"] == 4 * LINE
    body = split_device if small_slice else general_device
    return jax.shard_map(body, mesh=mesh, in_specs=in_specs, out_specs=out_specs, check_vma=False)
```

```python
import functools

import jax
import jax.numpy as jnp
from jax import lax
from jax.experimental import pallas as pl
from jax.experimental.pallas import tpu as pltpu
from jax.sharding import PartitionSpec as P

HEAD_DIM = 64
MESH = pl.DeviceIdType.MESH


epsilon = 1e-05
highest = lax.Precision.HIGHEST
f32 = jnp.float32
bf16 = jnp.bfloat16

LINE = 4
GELU_C = 0.7978845608
GELU_K = 0.044715


def dot_nn(a, b):
    return lax.dot_general(a, b, (((1,), (0,)), ((), ())), preferred_element_type=f32)


def dot_nt(a, b):
    return lax.dot_general(a, b, (((1,), (1,)), ((), ())), preferred_element_type=f32)


def dot_tn(a, b):
    return lax.dot_general(a, b, (((0,), (0,)), ((), ())), preferred_element_type=f32)


def place():
    s = lax.axis_index("seq")
    b = lax.axis_index("batch")
    return s, b // 4, lax.rem(b // 2, 2), lax.rem(b, 2)


def device(s, z, y, c):
    return (s, z * 4 + y * 2 + c)


def remote(src, dst, send, recv, target):
    return pltpu.make_async_remote_copy(
        src_ref=src, dst_ref=dst, send_sem=send, recv_sem=recv, device_id=target, device_id_type=MESH
    )


def greet(targets):
    barrier = pltpu.get_barrier_semaphore()
    for target in targets:
        pl.semaphore_signal(barrier, inc=1, device_id=target, device_id_type=MESH)
    pl.semaphore_wait(barrier, len(targets))


def inverse_rms(values):
    return lax.rsqrt(jnp.mean(values * values, axis=-1, keepdims=True) + epsilon)


def head_mask(parity):
    lane = lax.broadcasted_iota(jnp.int32, (1, 128), 1)
    return jnp.where(lane // HEAD_DIM == parity, 1.0, 0.0).astype(f32)


def norm_apply(values_in, gain_vec):
    return (
        values_in
        * lax.rsqrt(jnp.mean(values_in * values_in, axis=-1, keepdims=True) + epsilon)
        * gain_vec
    )


def gelu_tanh(values_in):
    return jax.nn.gelu(values_in, approximate=True)


def general_device(
    tokens, cotangent, lengths, routed, w_qkv, w_out, w_up, w_down, gain_attn, gain_mlp, router
):
    slot_count, local_len, model_width = tokens.shape
    capacity = routed.shape[1]
    seq_devices = lax.axis_size("seq")
    own_count = capacity // seq_devices
    head_count = model_width // HEAD_DIM
    row_count = own_count * slot_count
    score_scale = HEAD_DIM ** (-0.5)
    gathered = (
        lax.all_gather(w_qkv, ("seq", "batch"), axis=0, tiled=True),
        lax.all_gather(w_out, ("seq", "batch"), axis=0, tiled=True),
        lax.all_gather(w_up, ("seq", "batch"), axis=0, tiled=True),
        lax.all_gather(w_down, ("seq", "batch"), axis=0, tiled=True),
        lax.all_gather(gain_attn, ("seq", "batch"), axis=0, tiled=True),
        lax.all_gather(gain_mlp, ("seq", "batch"), axis=0, tiled=True),
        lax.all_gather(router, ("seq", "batch"), axis=0, tiled=True),
    )
    full_qkv, full_out, full_up, full_down, full_ga, full_gm, full_router = gathered
    gain_one = full_ga.astype(f32)
    gain_two = full_gm.astype(f32)
    router_vec = full_router.astype(f32)
    counts = lengths // 8
    seq_place = lax.axis_index("seq")
    positions = seq_place * local_len + jnp.arange(local_len, dtype=jnp.int32)
    rank_all = jnp.arange(capacity, dtype=jnp.int32)
    live_all = rank_all[None, :] < counts[:, None]
    chooser = ((routed[:, :, None] == positions[None, None, :]) & live_all[:, :, None]).astype(bf16)
    pick_in = jnp.einsum("scp,spd->csd", chooser, tokens, preferred_element_type=f32)
    pick_cot = jnp.einsum("scp,spd->csd", chooser, cotangent, preferred_element_type=f32)
    picked, picked_cot = (
        lax.psum_scatter(
            pick_in.astype(jnp.bfloat16), "seq", scatter_dimension=0, tiled=True
        ).astype(jnp.float32),
        lax.psum_scatter(
            pick_cot.astype(jnp.bfloat16), "seq", scatter_dimension=0, tiled=True
        ).astype(jnp.float32),
    )
    own_rank = seq_place * own_count + jnp.arange(own_count, dtype=jnp.int32)
    live_own = own_rank[:, None] < counts[None, :]
    live_mask = live_own.reshape(row_count, 1).astype(f32)
    routed_in = picked.reshape(row_count, model_width)
    normed_one = norm_apply(routed_in, gain_one).astype(bf16)
    joined = jnp.dot(normed_one, full_qkv, preferred_element_type=f32).astype(bf16)
    query_rows = joined[:, :model_width].reshape(own_count, slot_count, head_count, HEAD_DIM)
    key_own = joined[:, model_width : 2 * model_width].reshape(own_count, slot_count, model_width)
    value_own = joined[:, 2 * model_width :].reshape(own_count, slot_count, model_width)
    key_every, value_every = (
        lax.all_gather(key_own, "seq", axis=0, tiled=True),
        lax.all_gather(value_own, "seq", axis=0, tiled=True),
    )
    key_rows = key_every.reshape(capacity, slot_count, head_count, HEAD_DIM)
    value_rows = value_every.reshape(capacity, slot_count, head_count, HEAD_DIM)
    scores = (
        jnp.einsum("qsha,ksha->shqk", query_rows, key_rows, preferred_element_type=f32)
        * score_scale
    )
    causal = rank_all[None, :] <= own_rank[:, None]
    allowed = causal[None, :, :] & (rank_all[None, None, :] < counts[:, None, None])
    scores = jnp.where(allowed[:, None], scores, -1000000000.0)
    row_max = jnp.max(scores, axis=-1, keepdims=True)
    weights_f = jnp.exp(scores - row_max)
    row_total = jnp.sum(weights_f, axis=-1, keepdims=True)
    weights_low = weights_f.astype(bf16)
    mixture = jnp.einsum("shqk,ksha->qsha", weights_low, value_rows, preferred_element_type=f32)
    mixture = mixture / jnp.transpose(row_total, (2, 0, 1, 3))
    attended = mixture.reshape(row_count, model_width).astype(bf16)
    branch_a = jnp.dot(attended, full_out, preferred_element_type=f32)
    hidden = routed_in + branch_a
    normed_two = norm_apply(hidden, gain_two).astype(bf16)
    up_proj = jnp.dot(normed_two, full_up, preferred_element_type=f32)
    activated = gelu_tanh(up_proj).astype(bf16)
    branch_m = jnp.dot(activated, full_down, preferred_element_type=f32)
    gate_prob = jax.nn.sigmoid(jnp.dot(routed_in, router_vec, precision=highest))
    branch = branch_a + branch_m
    update = (
        (gate_prob[:, None] * branch * live_mask)
        .astype(bf16)
        .reshape(own_count, slot_count, model_width)
    )
    update_every = lax.all_gather(update, "seq", axis=0, tiled=True)
    output = (
        tokens.astype(f32)
        + jnp.einsum("scp,csd->spd", chooser, update_every, preferred_element_type=f32)
    ).astype(bf16)
    cot_rows = picked_cot.reshape(row_count, model_width)
    grad_gate = jnp.sum(cot_rows * branch, axis=-1)
    grad_logit = grad_gate * gate_prob * (1.0 - gate_prob)
    grad_branch = gate_prob[:, None] * cot_rows
    grad_m = grad_branch.astype(bf16)
    grad_act = jnp.einsum("rd,fd->rf", grad_m, full_down, preferred_element_type=f32)
    unused_up, gelu_pull = jax.vjp(gelu_tanh, up_proj)
    grad_u = gelu_pull(grad_act)[0].astype(bf16)
    grad_n2 = jnp.einsum("rf,df->rd", grad_u, full_up, preferred_element_type=f32)
    unused_two, norm_pull_two = jax.vjp(norm_apply, hidden, gain_two)
    grad_hidden, grad_gm = norm_pull_two(grad_n2)
    grad_a = (grad_branch + grad_hidden).astype(bf16)
    grad_att = jnp.einsum("rd,ed->re", grad_a, full_out, preferred_element_type=f32).astype(bf16)
    grad_att4 = grad_att.reshape(own_count, slot_count, head_count, HEAD_DIM)
    delta_rows = jnp.sum(grad_att4.astype(f32) * mixture, axis=-1)
    delta = jnp.transpose(delta_rows, (1, 2, 0))[..., None]
    grad_p = jnp.einsum("qsha,ksha->shqk", grad_att4, value_rows, preferred_element_type=f32)
    probs = weights_f / row_total
    grad_s = (probs * (grad_p - delta)).astype(bf16)
    grad_q = (
        jnp.einsum("shqk,ksha->qsha", grad_s, key_rows, preferred_element_type=f32) * score_scale
    )
    grad_k = (
        jnp.einsum("shqk,qsha->ksha", grad_s, query_rows, preferred_element_type=f32) * score_scale
    )
    scaled_low = weights_low.astype(f32) / row_total
    grad_v = jnp.einsum("shqk,qsha->ksha", scaled_low, grad_att4.astype(f32), precision=highest)
    grad_k_own, grad_v_own = (
        lax.psum_scatter(
            grad_k.reshape(capacity, slot_count, model_width).astype(jnp.bfloat16),
            "seq",
            scatter_dimension=0,
            tiled=True,
        ).astype(jnp.float32),
        lax.psum_scatter(
            grad_v.reshape(capacity, slot_count, model_width).astype(jnp.bfloat16),
            "seq",
            scatter_dimension=0,
            tiled=True,
        ).astype(jnp.float32),
    )
    grad_joined = jnp.concatenate(
        [
            grad_q.reshape(row_count, model_width),
            grad_k_own.reshape(row_count, model_width),
            grad_v_own.reshape(row_count, model_width),
        ],
        axis=-1,
    ).astype(bf16)
    grad_n1 = jnp.einsum("re,de->rd", grad_joined, full_qkv, preferred_element_type=f32)
    unused_one, norm_pull_one = jax.vjp(norm_apply, routed_in, gain_one)
    grad_x1, grad_ga = norm_pull_one(grad_n1)
    grad_router = jnp.sum(routed_in * grad_logit[:, None], axis=0)
    grad_rows = (grad_hidden + grad_x1 + grad_logit[:, None] * router_vec[None, :]).astype(bf16)
    grad_rows = grad_rows.reshape(own_count, slot_count, model_width)
    grad_every = lax.all_gather(grad_rows, "seq", axis=0, tiled=True)
    input_grad = (
        cotangent.astype(f32)
        + jnp.einsum("scp,csd->spd", chooser, grad_every, preferred_element_type=f32)
    ).astype(bf16)
    part_qkv = jnp.einsum("rd,re->de", normed_one, grad_joined, preferred_element_type=f32)
    part_out = jnp.einsum("re,rd->ed", attended, grad_a, preferred_element_type=f32)
    part_up = jnp.einsum("rd,rf->df", normed_two, grad_u, preferred_element_type=f32)
    part_down = jnp.einsum("rf,rd->fd", activated, grad_m, preferred_element_type=f32)

    def sum_rows(part):
        return lax.psum_scatter(
            part.astype(bf16), ("seq", "batch"), scatter_dimension=0, tiled=True
        ).astype(f32)

    down_sum = sum_rows(part_down)
    grad_up = sum_rows(part_up)
    grad_out = sum_rows(part_out)
    grad_qkv = sum_rows(part_qkv)
    small_ga, small_gm, small_router = (
        lax.psum_scatter(grad_ga, ("seq", "batch"), scatter_dimension=0, tiled=True),
        lax.psum_scatter(grad_gm, ("seq", "batch"), scatter_dimension=0, tiled=True),
        lax.psum_scatter(grad_router, ("seq", "batch"), scatter_dimension=0, tiled=True),
    )
    return (
        output,
        input_grad,
        grad_qkv,
        grad_out,
        grad_up,
        down_sum,
        small_ga,
        small_gm,
        small_router,
    )


def block_kernel(
    tok_hbm, cot_hbm, wq_hbm, wo_hbm, wu_hbm, wd_hbm, one_hbm, two_hbm, three_hbm, routed_hbm, len_hbm,
    upd_out, dx_out, fq_out, fo_out, fu_out, fd_out, vec_out, live_out,
    wq, wo, wu, wd, gv, stq, stu, stv, rcv,
    xs, xr, ds, dr, a_s, a_r, d2s, d2r, d1r, m_s, m_r, hid, dh, qkv, att, act, gp, logit, gains,
    gd, gu, rcd, rcu, ryd, ryu, rzd, rzu, rzb, ryb,
    fqk, fv, fo, fu, fd, sqk, sv, suu, rqk, rv, ruu, vs, vr, v_all, live,
    one_ref, two_ref, three_ref, routed_ref, len_ref,
    loc, out_sem, wz, vz, wy, vy, wc, vc, sx, rx, gc, hc, gt, ht, gy, hy, gz, hz, free,
):
    s, z, y, c = place()
    near, far = z + 1 - 2 * lax.rem(z, 2), LINE - 1 - z
    xdev, ydev, cdev = device(1 - s, z, y, c), device(s, z, 1 - y, c), device(s, z, y, 1 - c)
    ndev, fdev = device(s, near, y, c), device(s, far, y, c)
    model, half_q, half_u = xr.shape[2], att.shape[2], act.shape[2]
    ranks, half = xr.shape[1], xr.shape[2] // 2
    rows = xr.shape[0] * ranks
    part, half_d = stq.shape[0], wd.shape[3] // 2
    local, sent, outs = [], [], []

    def fetch(src, dst):
        copy = pltpu.make_async_copy(src, dst, loc.at[len(local)])
        copy.start()
        local.append(copy)
        return copy

    def send(src, dst, send_sem, recv_sem, target):
        copy = remote(src, dst, send_sem, recv_sem, target)
        copy.start()
        sent.append(copy)
        return copy

    def gone(copy):
        copy.wait_send()
        sent[:] = [other for other in sent if other is not copy]

    def arrive(ref, send_sem, recv_sem, target):
        remote(ref, ref, send_sem, recv_sem, target).wait_recv()

    def put(src, dst):
        copy = pltpu.make_async_copy(src, dst, out_sem.at[len(outs)])
        copy.start()
        outs.append(copy)

    barrier = pltpu.get_barrier_semaphore()
    for target in (xdev, ydev, cdev, ndev, fdev):
        pl.semaphore_signal(barrier, inc=1, device_id=target, device_id_type=MESH)

    stage, own_q = [], []
    small_in = [
        fetch(src, dst)
        for src, dst in (
            (one_hbm, one_ref), (two_hbm, two_ref), (three_hbm, three_ref), (routed_hbm, routed_ref), (len_hbm, len_ref),
        )
    ]
    for j in range(3):
        base, dst = 2 * j * half_q, pl.ds(j * half_q, half_q)
        stage.append(fetch(wq_hbm.at[:, pl.ds(base + (1 - s) * half_q, half_q)], stq.at[:, dst]))
        own_q.append(fetch(wq_hbm.at[:, pl.ds(base + s * half_q, half_q)], wq.at[s, z, y, c, :, dst]))
    get_tok = [fetch(tok_hbm.at[i], gd.at[pl.ds(2 * i, 2)]) for i in range(2)]
    own_o = fetch(wo_hbm, wo.at[z, y, c])
    stage_u = fetch(wu_hbm.at[:, pl.ds((1 - s) * half_u, half_u)], stu)
    own_u = fetch(wu_hbm.at[:, pl.ds(s * half_u, half_u)], wu.at[s, z, y, c])
    own_d = fetch(wd_hbm, wd.at[z, y, c])

    def down_half(i):
        return pl.ds(half_d * i, half_d)

    blocks = [
        lambda zz, yy, cc: wq.at[s, zz, yy, cc],
        lambda zz, yy, cc: wq.at[1 - s, zz, yy, cc],
        lambda zz, yy, cc: gv.at[zz, yy, cc],
        lambda zz, yy, cc: wo.at[zz, yy, cc],
        lambda zz, yy, cc: wu.at[s, zz, yy, cc],
        lambda zz, yy, cc: wu.at[1 - s, zz, yy, cc],
        lambda zz, yy, cc: wd.at[zz, yy, cc, down_half(0)],
        lambda zz, yy, cc: wd.at[zz, yy, cc, down_half(1)],
    ]
    lines = [
        lambda yy, cc: wq.at[s, :, yy, cc],
        lambda yy, cc: wq.at[1 - s, :, yy, cc],
        lambda yy, cc: gv.at[:, yy, cc],
        lambda yy, cc: wo.at[:, yy, cc],
        lambda yy, cc: wu.at[s, :, yy, cc],
        lambda yy, cc: wu.at[1 - s, :, yy, cc],
        lambda yy, cc: wd.at[:, yy, cc, down_half(0)],
        lambda yy, cc: wd.at[:, yy, cc, down_half(1)],
    ]
    Q_OWN, Q_SWAP, VEC, OUT, U_OWN, U_SWAP, D_0, D_1 = range(8)

    planes = [
        lambda cc: wq.at[s, :, :, cc],
        lambda cc: wq.at[1 - s, :, :, cc],
        lambda cc: gv.at[:, :, cc],
        lambda cc: wo.at[:, :, cc],
        lambda cc: wu.at[s, :, :, cc],
        lambda cc: wu.at[1 - s, :, :, cc],
        lambda cc: wd.at[:, :, cc, down_half(0)],
        lambda cc: wd.at[:, :, cc, down_half(1)],
    ]

    def pass_on(ref, send_sem, recv_sem, target):
        remote(ref, ref, send_sem, recv_sem, target).start()

    def spread(p):
        own = blocks[p](z, y, c)
        pass_on(own, wz.at[p], vz.at[p, 0], fdev)
        pass_on(own, wz.at[p], vz.at[p, 1], ndev)

    def spread_y(p):
        pass_on(blocks[p](z, y, c), wy.at[p], vy.at[p], ydev)

    def after_far(p):
        ref = blocks[p](far, y, c)
        arrive(ref, wz.at[p], vz.at[p, 0], fdev)
        pass_on(ref, wz.at[p], vz.at[p, 2], ndev)
        pass_on(ref, wy.at[p], vy.at[p], ydev)

    def after_near(p):
        for i, zz in ((1, near), (2, LINE - 1 - near)):
            ref = blocks[p](zz, y, c)
            arrive(ref, wz.at[p], vz.at[p, i], ndev)
            pass_on(ref, wy.at[p], vy.at[p], ydev)
        pass_on(lines[p](y, c), wc.at[p], vc.at[p], cdev)

    def after_y(p):
        line = lines[p](1 - y, c)
        arrive(line, wy.at[p], vy.at[p], ydev)
        pass_on(line, wc.at[p], vc.at[p], cdev)

    def after_c(p):
        arrive(planes[p](1 - c), wc.at[p], vc.at[p], cdev)

    def both(zz, cc):
        return wd.at[zz, :, cc, down_half(1)]

    def after_first_y():
        arrive(blocks[D_1](z, 1 - y, c), wy.at[D_1], vy.at[D_1], ydev)
        own = both(z, c)
        pass_on(own, wz.at[D_1], vz.at[D_1, 0], fdev)
        pass_on(own, wz.at[D_1], vz.at[D_1, 1], ndev)

    def after_first_far():
        ref = both(far, c)
        arrive(ref, wz.at[D_1], vz.at[D_1, 0], fdev)
        pass_on(ref, wz.at[D_1], vz.at[D_1, 2], ndev)

    def after_first_near():
        for i, zz in ((1, near), (2, LINE - 1 - near)):
            arrive(both(zz, c), wz.at[D_1], vz.at[D_1, i], ndev)
        pass_on(planes[D_1](c), wc.at[D_1], vc.at[D_1], cdev)

    def after_first_c():
        arrive(planes[D_1](1 - c), wc.at[D_1], vc.at[D_1], cdev)

    def left(ref, send_sem, recv_sem, target):
        remote(ref, ref, send_sem, recv_sem, target).wait_send()

    def gathered():
        three = pl.ds(0, LINE - 1)
        passed = [
            wq.at[s, three, y, c], wq.at[1 - s, three, y, c], gv.at[three, y, c], wo.at[three, y, c],
            wu.at[s, three, y, c], wu.at[1 - s, three, y, c], wd.at[three, y, c, down_half(0)],
            wd.at[three, :, c, down_half(1)],
        ]
        for p in range(8):
            left(passed[p], wz.at[p], vz.at[p, 0], ndev)
            left(blocks[p](z, y, c) if p == D_1 else lines[p](y, c), wy.at[p], vy.at[p], ydev)
            left(planes[p](c), wc.at[p], vc.at[p], cdev)

    spans = [pl.ds(0, 2 * part), pl.ds(2 * part, 2 * part), None, None]
    spans += [pl.ds(i * part, part) for i in range(4)]
    parts = [
        (lambda cc, i=i: gu.at[i - 2, :, :, cc]) if q is None else (lambda cc, q=q: gd.at[:, :, cc, q])
        for i, q in enumerate(spans)
    ]
    land_c = [rcu.at[i - 2] if q is None else rcd.at[:, :, q] for i, q in enumerate(spans)]
    land_y = [ryu.at[i - 2] if q is None else ryd.at[:, q] for i, q in enumerate(spans)]
    land_z = [rzu.at[i - 2] if q is None else rzd.at[:, q] for i, q in enumerate(spans)]

    def c_start(k):
        return send(parts[k](1 - c), land_c[k], gc.at[k], hc.at[k], cdev)

    def c_end(k):
        ref, own = land_c[k], parts[k](c)
        if k < 2:
            arrive(ref, gt.at[k], ht.at[k], cdev)
        else:
            arrive(ref, gc.at[k], hc.at[k], cdev)

        def add(i, carry):
            ref[i] = (ref[i].astype(f32) + own[i].astype(f32)).astype(bf16)
            return carry

        lax.fori_loop(0, LINE, add, 0)
        if k == 0:
            remote(ref.at[LINE - 1 - near], rzb.at[1], gz.at[k], hz.at[k, 1], ndev).start()
            remote(ref.at[near], rzb.at[0], gz.at[k], hz.at[k, 0], ndev).start()
            return []
        return [send(ref.at[:, 1 - y], land_y[k], gy.at[k], hy.at[k], ydev)]

    def y_end(k):
        ref, own = land_y[k], land_c[k]
        arrive(ref, gy.at[k], hy.at[k], ydev)

        def add(i, carry):
            ref[i] = (ref[i].astype(f32) + own[i, y].astype(f32)).astype(bf16)
            return carry

        lax.fori_loop(0, LINE, add, 0)
        remote(ref.at[LINE - 1 - near], land_z[k].at[1], gz.at[k], hz.at[k, 1], ndev).start()
        remote(ref.at[near], land_z[k].at[0], gz.at[k], hz.at[k, 0], ndev).start()

    def z_mid(k):
        ref = land_z[k].at[1]
        arrive(ref, gz.at[k], hz.at[k, 1], ndev)
        ref[...] = (ref[...].astype(f32) + land_y[k][far].astype(f32)).astype(bf16)
        remote(ref, land_z[k].at[2], gz.at[k], hz.at[k, 2], fdev).start()

    def z_end(k):
        arrive(land_z[k].at[0], gz.at[k], hz.at[k, 0], ndev)
        arrive(land_z[k].at[2], gz.at[k], hz.at[k, 2], fdev)
        return land_y[k][z].astype(f32) + land_z[k][0].astype(f32) + land_z[k][2].astype(f32)

    def first_mid():
        arrive(rzb.at[1], gz.at[0], hz.at[0, 1], ndev)
        rzb[1] = (rzb[1].astype(f32) + land_c[0][far].astype(f32)).astype(bf16)
        remote(rzb.at[1], rzb.at[2], gz.at[0], hz.at[0, 2], fdev).start()

    def first_end():
        arrive(rzb.at[0], gz.at[0], hz.at[0, 0], ndev)
        arrive(rzb.at[2], gz.at[0], hz.at[0, 2], fdev)
        rzb[0] = (land_c[0][z].astype(f32) + rzb[0].astype(f32) + rzb[2].astype(f32)).astype(bf16)
        return send(rzb.at[0, 1 - y], ryb, gy.at[0], hy.at[0], ydev)

    def first_sum():
        arrive(ryb, gy.at[0], hy.at[0], ydev)
        return rzb[0, y].astype(f32) + ryb[...].astype(f32)

    for copy in small_in:
        copy.wait()
    fits = lax.broadcasted_iota(jnp.int32, (part, model), 1) == s * part + lax.broadcasted_iota(
        jnp.int32, (part, model), 0
    )
    line = lax.broadcasted_iota(jnp.int32, (16, part), 0)
    small = jnp.zeros((16, part), f32)
    for j, ref in enumerate((one_ref, two_ref, three_ref)):
        small = jnp.where(line == j, ref[...].astype(f32), small)
    gains[...] = dot_nn(small.astype(bf16), jnp.where(fits, 1.0, 0.0).astype(bf16))
    stv[...] = gains[:, 0:128].astype(bf16)

    rank = lax.broadcasted_iota(jnp.int32, (1, ranks), 1)

    def count(i):
        return lax.shift_right_arithmetic(len_ref[:, i : i + 1], 3)

    for i in range(2):
        live[i : i + 1] = jnp.where(rank < count(i), routed_ref[i : i + 1], -1)

    def chooser(i):
        row = live[i : i + 1].astype(f32)
        eye = lax.broadcasted_iota(jnp.int32, (ranks, ranks), 0) == lax.broadcasted_iota(
            jnp.int32, (ranks, ranks), 1
        )
        column = jnp.sum(jnp.where(eye, row, 0.0), axis=1, keepdims=True).astype(jnp.int32)
        count_here = tok_hbm.shape[1] * 512
        position = lax.broadcasted_iota(jnp.int32, (ranks, count_here), 1) + s * count_here
        return jnp.where(position == column, 1.0, 0.0).astype(bf16)

    def pick(i, dst):
        dst[i] = dot_nn(chooser(i), gd[2 * i : 2 * i + 2].reshape(tok_hbm.shape[1] * 512, model)).astype(bf16)

    def live_column(i):
        rank = lax.broadcasted_iota(jnp.int32, (ranks, 1), 0)
        return jnp.where(rank < count(i), 1.0, 0.0).astype(f32)

    def allowed(i):
        query = lax.broadcasted_iota(jnp.int32, (ranks, ranks), 0)
        key = lax.broadcasted_iota(jnp.int32, (ranks, ranks), 1)
        return (key <= query) & (key < count(i))

    for copy in stage:
        copy.wait()
    pl.semaphore_wait(barrier, 5)
    send(stq, wq.at[s, z, y, c], sx.at[1], rx.at[1], xdev)
    swap_v = send(stv, rcv, sx.at[0], rx.at[0], xdev)
    for copy in own_q:
        copy.wait()
    spread(Q_OWN)
    spread_y(Q_OWN)
    own_d.wait()
    spread_y(D_1)
    x_swap = []
    get_tok[0].wait()
    pick(0, xs)
    x_swap.append(send(xs.at[0], xr.at[0], sx.at[3], rx.at[3], xdev))
    get_cot = [fetch(cot_hbm.at[0], gd.at[pl.ds(0, 2)])]
    stage_u.wait()
    send(stu, wu.at[s, z, y, c], sx.at[2], rx.at[2], xdev)
    get_tok[1].wait()
    pick(1, xs)
    x_swap.append(send(xs.at[1], xr.at[1], sx.at[4], rx.at[4], xdev))
    get_cot.append(fetch(cot_hbm.at[1], gd.at[pl.ds(2, 2)]))
    put(live, live_out)
    swap_v.wait_recv()
    gv[z, y, c] = stv[...] + rcv[...]
    after_far(Q_OWN)
    spread(VEC)
    spread_y(VEC)
    arrive(wq.at[1 - s, z, y, c], sx.at[1], rx.at[1], xdev)
    spread(Q_SWAP)
    spread_y(Q_SWAP)
    get_cot[0].wait()
    pick(0, ds)
    d_swap = [send(ds.at[0], dr.at[0], sx.at[7], rx.at[7], xdev)]
    after_near(Q_OWN)
    after_far(VEC)
    get_cot[1].wait()
    pick(1, ds)
    after_far(Q_SWAP)
    own_o.wait()
    spread(OUT)
    after_near(VEC)
    after_near(Q_SWAP)
    after_far(OUT)
    spread_y(OUT)
    own_u.wait()
    spread(U_OWN)
    spread_y(U_OWN)
    arrive(wu.at[1 - s, z, y, c], sx.at[2], rx.at[2], xdev)
    spread(U_SWAP)
    after_y(Q_OWN)
    after_y(VEC)
    after_c(Q_OWN)
    after_c(VEC)
    after_near(OUT)
    after_y(Q_SWAP)
    after_far(U_OWN)
    spread(D_0)
    spread_y(U_SWAP)
    spread_y(D_0)
    after_c(Q_SWAP)

    group = lax.broadcasted_iota(jnp.int32, (16, 128), 1) // part
    for q in range(LINE):
        for i in range(2):
            tile = jnp.zeros((16, 128), f32)
            for j in range(4):
                moved = pltpu.roll(gv[q, j // 2, j % 2].astype(f32), (j - i) * part % 128, 1)
                tile = jnp.where(group == j, moved, tile)
            gains[:, i * half + q * 128 : i * half + (q + 1) * 128] = tile
    gain_one, gain_two, router = gains[0:1], gains[1:2], gains[2:3]

    def enter(i):
        x_swap[i].wait()
        row = xr[i].astype(f32) + xs[i].astype(f32)
        xr[i] = row.astype(bf16)
        xs[i] = (row * inverse_rms(row) * gain_one).astype(bf16)
        for j in range(3):
            cols = pl.ds(j * half_q, half_q)
            qkv[i, :, cols] = dot_nn(xs[i], wq[:, :, :, :, :, cols].reshape(model, half_q)).astype(bf16)

    def attend(i):
        ok = allowed(i)

        def pair(j, carry):
            q2 = qkv[i, :, pl.ds(j * 128, 128)].astype(f32)
            k2 = qkv[i, :, pl.ds(half_q + j * 128, 128)]
            v2 = qkv[i, :, pl.ds(2 * half_q + j * 128, 128)]
            mixed = jnp.zeros(q2.shape, f32)
            for parity in range(2):
                mask = head_mask(parity)
                score = dot_nt((q2 * mask).astype(bf16), k2) * (HEAD_DIM**-0.5)
                score = jnp.where(ok, score, -1000000000.0)
                weight = jnp.exp(score - jnp.max(score, axis=-1, keepdims=True))
                total = jnp.sum(weight, axis=-1, keepdims=True)
                mixed += dot_nn(weight.astype(bf16), v2) / total * mask
            att[i, :, pl.ds(j * 128, 128)] = mixed.astype(bf16)
            return carry

        lax.fori_loop(0, half_q // 128, pair, 0)

    def leave(i):
        for j in range(2):
            cols = pl.ds(j * half, half)
            a_s[i, :, cols] = dot_nn(att[i], wo[:, :, :, :, cols].reshape(half_q, half)).astype(bf16)
        return send(a_s.at[i], a_r.at[i], sx.at[5 + i], rx.at[5 + i], xdev)

    enter(0)
    attend(0)
    after_y(OUT)
    after_c(OUT)
    a_swap = [leave(0)]
    after_far(U_SWAP)
    after_first_y()
    after_near(U_OWN)
    enter(1)
    attend(1)
    a_swap.append(leave(1))
    d_swap.append(send(ds.at[1], dr.at[1], sx.at[8], rx.at[8], xdev))
    after_far(D_0)
    after_near(U_SWAP)
    after_y(U_OWN)
    after_c(U_OWN)

    def mlp_up(i):
        a_swap[i].wait()
        row = xr[i].astype(f32) + (a_s[i].astype(f32) + a_r[i].astype(f32))
        hid[i] = row
        a_s[i] = (row * inverse_rms(row) * gain_two).astype(bf16)

        def tile(t, carry):
            cols = pl.ds(t * 512, 512)
            up = dot_nn(a_s[i], wu[:, :, :, :, :, cols].reshape(model, 512))
            curve = jnp.tanh(GELU_C * (up + GELU_K * up * up * up))
            act[i, :, cols] = (0.5 * up * (1.0 + curve)).astype(bf16)
            slope = 0.5 * (1.0 + curve) + 0.5 * up * (1.0 - curve * curve) * (
                GELU_C * (1.0 + 3.0 * GELU_K * up * up)
            )
            gp[i, :, cols] = slope.astype(bf16)
            return carry

        lax.fori_loop(0, half_u // 512, tile, 0)

    def gate_of(i):
        return jax.nn.sigmoid(jnp.sum(xr[i].astype(f32) * router, axis=-1, keepdims=True))

    def cotangent_rows(i):
        d_swap[i].wait()
        row = dr[i].astype(f32) + ds[i].astype(f32)
        dr[i] = row.astype(bf16)
        ds[i] = (gate_of(i) * row).astype(bf16)

    def mlp_back(i):
        def tile(t, carry):
            cols = pl.ds(t * 512, 512)
            back = dot_nt(ds[i], wd[t].reshape(512, model))
            gp[i, :, cols] = (back * gp[i, :, cols].astype(f32)).astype(bf16)
            return carry

        lax.fori_loop(0, half_u // 512, tile, 0)
        for j in range(2):
            cols = pl.ds(j * half, half)
            d2s[i, :, cols] = dot_nt(gp[i], wu[j].reshape(half, half_u)).astype(bf16)
        return send(d2s.at[i], d2r.at[i], sx.at[9 + i], rx.at[9 + i], xdev)

    def mlp_out(i):
        for j in range(2):
            cols = pl.ds(j * half, half)
            m_s[i, :, cols] = dot_nn(act[i], wd[:, :, :, :, cols].reshape(half_u, half)).astype(bf16)

    def mlp_send(i):
        return send(m_s.at[i], m_r.at[i], sx.at[11 + i], rx.at[11 + i], xdev)

    after_y(U_SWAP)
    after_first_far()
    after_c(U_SWAP)
    mlp_up(0)
    after_near(D_0)
    cotangent_rows(0)

    def down_tile(t, carry):
        gd[t] = dot_tn(act[0, :, pl.ds(t * 512, 512)], ds[0]).astype(bf16).reshape(gd.shape[1:])
        return carry

    lax.fori_loop(0, LINE, down_tile, 0)
    mlp_up(1)
    after_y(D_0)
    after_c(D_0)
    after_first_near()
    after_first_c()
    d2_swap = [mlp_back(0)]
    cotangent_rows(1)

    def c_tile(t, k):
        remote(gd.at[t, :, 1 - c, spans[k]], land_c[k].at[t], gt.at[k], ht.at[k], cdev).start()

    for t in range(LINE):
        grad = dot_tn(act[1, :, t * 512 : t * 512 + 512], ds[1])
        gd[t] = (gd[t].astype(f32) + grad.reshape(gd.shape[1:])).astype(bf16)
        c_tile(t, 1)
    for t in range(LINE):
        c_tile(t, 0)
    y_down = c_end(1)
    c_end(0)
    d2_swap.append(mlp_back(1))
    mlp_out(0)
    m_swap = [mlp_send(0)]

    def up_tile(t, carry):
        cols = pl.ds(t * 512, 512)
        grad = dot_tn(a_s[...].reshape(rows, model), gp[:, :, cols].reshape(rows, 512))
        gu[:, :, :, :, :, cols] = grad.astype(bf16).reshape(gu.shape[:5] + (512,))
        return carry

    lax.fori_loop(0, half_u // 512, up_tile, 0)
    c_start(2)
    c_start(3)
    mlp_out(1)
    m_swap.append(mlp_send(1))

    def hidden_back(i):
        d2_swap[i].wait()
        back = d2s[i].astype(f32) + d2r[i].astype(f32)
        row = hid[i]
        r2 = inverse_rms(row)
        scaled = back * gain_two
        step = r2 * scaled - row * (r2 * r2 * r2 * jnp.mean(scaled * row, axis=-1, keepdims=True))
        dh[i] = step
        gp[i, :, 0:model] = (gate_of(i) * dr[i].astype(f32) + step).astype(bf16)
        gp[i, :, model : model + half_q] = dot_nt(gp[i, :, 0:model], wo[...].reshape(half_q, model)).astype(bf16)
        return jnp.sum(d2s[i].astype(f32) * row * r2, axis=0, keepdims=True)

    def attend_back(i):
        ok = allowed(i)
        scale = HEAD_DIM**-0.5

        def pair(j, carry):
            q2 = qkv[i, :, pl.ds(j * 128, 128)]
            k2 = qkv[i, :, pl.ds(half_q + j * 128, 128)]
            v2 = qkv[i, :, pl.ds(2 * half_q + j * 128, 128)]
            g2 = gp[i, :, pl.ds(model + j * 128, 128)].astype(f32)
            q2f = q2.astype(f32)
            dq2 = jnp.zeros(q2.shape, f32)
            dk2 = jnp.zeros(q2.shape, f32)
            dv2 = jnp.zeros(q2.shape, f32)
            for parity in range(2):
                mask = head_mask(parity)
                score = dot_nt((q2f * mask).astype(bf16), k2) * scale
                score = jnp.where(ok, score, -1000000000.0)
                weight = jnp.exp(score - jnp.max(score, axis=-1, keepdims=True))
                over = 1.0 / jnp.sum(weight, axis=-1, keepdims=True)
                gh = g2 * mask
                dp = dot_nt(gh.astype(bf16), v2)
                prob = weight * over
                delta = jnp.sum(prob * dp, axis=-1, keepdims=True)
                dscore = (prob * (dp - delta)).astype(bf16)
                dq2 += dot_nn(dscore, k2) * mask
                dk2 += dot_tn(dscore, q2) * mask
                dv2 += dot_tn(weight.astype(bf16), (gh * over).astype(bf16))
            act[i, :, pl.ds(j * 128, 128)] = (dq2 * scale).astype(bf16)
            act[i, :, pl.ds(half_q + j * 128, 128)] = (dk2 * scale).astype(bf16)
            act[i, :, pl.ds(2 * half_q + j * 128, 128)] = dv2.astype(bf16)
            return carry

        lax.fori_loop(0, half_q // 128, pair, 0)

    def inner_back(i):
        r1 = inverse_rms(xr[i].astype(f32))
        sums = []
        for j in range(2):
            cols = pl.ds(j * half, half)
            step = dot_nt(act[i, :, 0 : 3 * half_q], wq[j].reshape(half, 3 * half_q))
            d2s[i, :, cols] = step.astype(bf16)
            sums.append(jnp.sum(step * xr[i, :, cols].astype(f32) * r1, axis=0, keepdims=True))
        return send(d2s.at[i], d1r.at[i], sx.at[13 + i], rx.at[13 + i], xdev), sums

    grad_gm = hidden_back(0)
    c_end(2)
    attend_back(0)
    c_end(3)
    first_mid()
    swap_0, sums_0 = inner_back(0)
    y_end(1)
    grad_gm += hidden_back(1)
    attend_back(1)
    z_mid(1)
    for k in range(2):
        left(parts[k](1 - c), gt.at[k], ht.at[k], cdev)
    left(rzb, gz.at[0], hz.at[0, 0], ndev)
    first_end()
    pl.semaphore_signal(free.at[0], inc=1, device_id=cdev, device_id_type=MESH)
    y_end(2)

    def out_tile(t):
        cols = pl.ds(t * half, half)
        grad = dot_tn(att[...].reshape(rows, half_q), gp[:, :, cols].reshape(rows, half))
        gd[:, :, :, 3 * part :, cols] = grad.astype(bf16).reshape(wo.shape[:4] + (half,))

    def qkv_tile(t):
        grad = dot_tn(xs[...].reshape(rows, model), act[:, :, t * half_q : (t + 1) * half_q].reshape(rows, half_q))
        grad = grad.astype(bf16).reshape(wq.shape[:5] + (half_q,))
        if t < 2:
            gd[:, :, :, 0:part, t * half_q : (t + 1) * half_q] = grad[0]
            gd[:, :, :, part : 2 * part, t * half_q : (t + 1) * half_q] = grad[1]
        else:
            gd[:, :, :, 2 * part : 3 * part, 0:half_q] = grad[0]
            gd[:, :, :, 2 * part : 3 * part, half_q:] = grad[1]

    qkv_tile(0)
    qkv_tile(1)
    pl.semaphore_wait(free.at[0], 1)
    c_start(4)
    c_start(5)
    qkv_tile(2)
    fd[2 * part :] = z_end(1)
    for copy in y_down:
        gone(copy)
    left(land_z[1], gz.at[1], hz.at[1, 0], ndev)
    for target in (ydev, cdev, ndev, fdev):
        pl.semaphore_signal(free.at[1], inc=1, device_id=target, device_id_type=MESH)
    out_tile(0)
    out_tile(1)
    c_end(4)
    c_end(5)
    swap_1, sums_1 = inner_back(1)
    d1_swap = [swap_0, swap_1]
    for j in range(2):
        gains[8:9, j * half : (j + 1) * half] = sums_0[j] + sums_1[j]
    gains[9:10] = grad_gm
    pl.semaphore_wait(free.at[1], 4)
    c_start(6)
    c_start(7)
    z_mid(2)
    c_end(6)
    y_end(3)
    fu[0] = z_end(2)

    grad_router = jnp.zeros((1, model), f32)
    for i in range(2):
        m_swap[i].wait()
        row = xr[i].astype(f32)
        gate = gate_of(i)
        branch = (hid[i] - row) + (m_s[i].astype(f32) + m_r[i].astype(f32))
        m_s[i] = (gate * branch * live_column(i)).astype(bf16)
        slope = jnp.sum(dr[i].astype(f32) * branch, axis=-1, keepdims=True) * gate * (1.0 - gate)
        logit[i] = slope
        grad_router += jnp.sum(row * slope, axis=0, keepdims=True)
    put(m_s, upd_out)
    gains[10:11] = 0.5 * grad_router
    for j in range(3):
        for t in range(model // 128):
            vs[8 * j + t : 8 * j + t + 1] = gains[8 + j : 9 + j, t * 128 : (t + 1) * 128]
    send(vs, vr.at[0], gc.at[8], hc.at[8], cdev)
    z_mid(3)
    arrive(vr.at[0], gc.at[8], hc.at[8], cdev)
    v_all[0] = vs[...] + vr[0]
    send(v_all.at[0], vr.at[1], gz.at[8], hz.at[8, 0], ndev)
    c_end(7)
    fd[0 : 2 * part] = first_sum()
    put(fd, fd_out)
    y_end(4)
    fu[1] = z_end(3)
    suu[...] = fu[1 - s].astype(bf16)
    send(suu, ruu, sx.at[15], rx.at[15], xdev)
    put(fu.at[s], fu_out.at[:, pl.ds(s * half_u, half_u)])
    arrive(vr.at[1], gz.at[8], hz.at[8, 0], ndev)
    v_all[1] = v_all[0] + vr[1]
    send(v_all.at[1], vr.at[2], gz.at[9], hz.at[8, 1], fdev)
    z_mid(4)
    y_end(5)

    def rows_back(i):
        d1_swap[i].wait()
        row = xr[i].astype(f32)
        r1 = inverse_rms(row)
        scaled = (d2s[i].astype(f32) + d1r[i].astype(f32)) * gain_one
        step = r1 * scaled - row * (r1 * r1 * r1 * jnp.mean(scaled * row, axis=-1, keepdims=True))
        d2s[i] = (dh[i] + step + logit[i] * router).astype(bf16)
        put(d2s.at[i], dx_out.at[i])

    rows_back(0)
    arrive(vr.at[2], gz.at[9], hz.at[8, 1], fdev)
    v_all[2] = v_all[1] + vr[2]
    send(v_all.at[2], vr.at[3], gy.at[8], hy.at[8], ydev)
    z_mid(5)
    y_end(6)
    z_mid(6)
    y_end(7)
    arrive(vr.at[3], gy.at[8], hy.at[8], ydev)
    v_all[3] = v_all[2] + vr[3]
    send(v_all.at[3], vr.at[4], sx.at[18], rx.at[18], xdev)
    for i in range(2):
        fqk[i] = z_end(4 + i)
    sqk[...] = fqk[1 - s].astype(bf16)
    send(sqk, rqk, sx.at[16], rx.at[16], xdev)
    for j in range(2):
        put(fqk.at[s, :, pl.ds(j * half_q, half_q)], fq_out.at[:, pl.ds(2 * j * half_q + s * half_q, half_q)])
    fv[...] = z_end(6)
    sv[...] = fv[:, pl.ds((1 - s) * half_q, half_q)].astype(bf16)
    send(sv, rv, sx.at[17], rx.at[17], xdev)
    put(fv.at[:, pl.ds(s * half_q, half_q)], fq_out.at[:, pl.ds(4 * half_q + s * half_q, half_q)])
    z_mid(7)
    rows_back(1)
    arrive(ruu, sx.at[15], rx.at[15], xdev)
    fu[1 - s] = ruu[...].astype(f32)
    put(fu.at[1 - s], fu_out.at[:, pl.ds((1 - s) * half_u, half_u)])
    arrive(rqk, sx.at[16], rx.at[16], xdev)
    fqk[1 - s] = rqk[...].astype(f32)
    for j in range(2):
        put(
            fqk.at[1 - s, :, pl.ds(j * half_q, half_q)],
            fq_out.at[:, pl.ds(2 * j * half_q + (1 - s) * half_q, half_q)],
        )
    fo[...] = z_end(7)
    put(fo, fo_out)
    arrive(rv, sx.at[17], rx.at[17], xdev)
    fv[:, pl.ds((1 - s) * half_q, half_q)] = rv[...].astype(f32)
    put(
        fv.at[:, pl.ds((1 - s) * half_q, half_q)],
        fq_out.at[:, pl.ds(4 * half_q + (1 - s) * half_q, half_q)],
    )
    arrive(vr.at[4], sx.at[18], rx.at[18], xdev)
    v_all[4] = v_all[3] + vr[4]
    put(v_all.at[4], vec_out)
    gathered()
    for k in range(2, 8):
        left(land_z[k], gz.at[k], hz.at[k, 0], ndev)
    waited = x_swap + a_swap + d_swap + d2_swap + m_swap + d1_swap
    for copy in list(sent):
        if not any(copy is other for other in waited):
            copy.wait_send()
    for copy in outs:
        copy.wait()


def rows_kernel(
    tok_hbm, cot_hbm, upd_hbm, dx_hbm, fq_hbm, fo_hbm, fu_hbm, fd_hbm, vec_hbm, live_hbm,
    out_hbm, grad_hbm, fq_out, fo_out, fu_out, fd_out, one_out, two_out, three_out,
    bases, moved, fq, fo, fu, fd, vec_ref, live_ref, one, two, three, get_sem, put_sem, rows_sem, pass_sem,
):
    s = lax.axis_index("seq")
    _, slots, chunks, tall, model = bases.shape
    ranks = moved.shape[2]
    whole = (tok_hbm, cot_hbm), (out_hbm, grad_hbm)
    tasks = [(i, t) for i in range(slots) for t in range(chunks)]

    def part_of(ref, i, t):
        return ref.at[i, pl.ds(t * tall, tall)]

    gets, puts = {}, []
    rows = [
        pltpu.make_async_copy(src.at[i], moved.at[a, i], rows_sem.at[a, i])
        for i in range(slots)
        for a, src in enumerate((upd_hbm, dx_hbm))
    ]
    get_live = pltpu.make_async_copy(live_hbm, live_ref, pass_sem.at[0, 4])
    get_vec = pltpu.make_async_copy(vec_hbm, vec_ref, pass_sem.at[0, 5])
    get_live.start()
    for i, t in tasks:
        for a in range(2):
            if t == 0:
                rows[2 * i + a].start()
            gets[a, i, t] = pltpu.make_async_copy(part_of(whole[0][a], i, t), bases.at[a, i, t], get_sem.at[a, i, t])
            gets[a, i, t].start()
    through = ((fq_hbm, fq, fq_out), (fo_hbm, fo, fo_out), (fu_hbm, fu, fu_out), (fd_hbm, fd, fd_out))
    taken = [pltpu.make_async_copy(src, mid, pass_sem.at[0, j]) for j, (src, mid, _) in enumerate(through)]
    passed = [pltpu.make_async_copy(mid, dst, pass_sem.at[1, j]) for j, (_, mid, dst) in enumerate(through)]
    for copy in taken + [get_vec]:
        copy.start()
    get_live.wait()
    for n, (i, t) in enumerate(tasks):
        if n == len(tasks) - 1:
            for j in range(4):
                taken[j].wait()
                passed[j].start()
        position = lax.broadcasted_iota(jnp.int32, (tall, ranks), 0) + ((s * chunks + t) * tall)
        chooser = jnp.where(position == live_ref[i : i + 1], 1.0, 0.0).astype(bf16)
        for a in range(2):
            if t == 0:
                rows[2 * i + a].wait()
            gets[a, i, t].wait()
            bases[a, i, t] += dot_nn(chooser, moved[a, i]).astype(bf16)
            copy = pltpu.make_async_copy(bases.at[a, i, t], part_of(whole[1][a], i, t), put_sem.at[a, i, t])
            copy.start()
            puts.append(copy)
    part = one.shape[1]
    get_vec.wait()
    flat = s * lax.axis_size("batch") + lax.axis_index("batch")
    each = 128 // part
    lane = lax.broadcasted_iota(jnp.int32, (part, 128), 1)
    here = lane == lax.rem(flat, each) * part + lax.broadcasted_iota(jnp.int32, (part, 128), 0)
    eye = lax.broadcasted_iota(jnp.int32, (part, part), 0) == lax.broadcasted_iota(jnp.int32, (part, part), 1)
    for j, (ref, dst) in enumerate(((one, one_out), (two, two_out), (three, three_out))):
        line = vec_ref[pl.ds(8 * j + flat // each, 1)]
        column = jnp.sum(jnp.where(here, line, 0.0), axis=1, keepdims=True)
        ref[...] = jnp.sum(jnp.where(eye, column, 0.0), axis=0, keepdims=True)
        puts.append(pltpu.make_async_copy(ref, dst, pass_sem.at[1, 4 + j]))
        puts[-1].start()
    for copy in passed + puts:
        copy.wait()


def split_device(
    tokens, cotangent, lengths, routed, w_qkv, w_out, w_up, w_down, gain_attn, gain_mlp, router
):
    slots, local_len, model = tokens.shape
    ranks = routed.shape[1]
    half_q, half_u = w_qkv.shape[1] // 6, w_up.shape[1] // 2
    part, down = w_qkv.shape[0], w_down.shape[0]
    hbm = pl.BlockSpec(memory_space=pl.ANY)
    sds, space, dma = jax.ShapeDtypeStruct, pltpu.VMEM, pltpu.SemaphoreType.DMA
    rows = (slots, ranks, model)
    grid = (LINE, 2, 2)
    wq_shape, wo_shape = (2,) + grid + (part, 3 * half_q), grid + (part, model)
    wu_shape, wd_shape = (2,) + grid + (part, half_u), grid + (down, model)
    blocked = (slots, local_len // 512, 2, 2, 128, model)
    row_bf16 = space(rows, bf16)

    def land(lead, tall, wide):
        return [space(lead + mid + (tall, wide), bf16) for mid in ((LINE, 2), (LINE,), (3,))]

    on_d, on_u = land((), down, model), land((2,), part, half_u)
    grad_shapes = (
        sds((part, 6 * half_q), f32), sds((part, model), f32), sds((part, 2 * half_u), f32), sds((down, model), f32),
    )
    upd, dxr, *sums, vec, live = pl.pallas_call(
        block_kernel,
        out_shape=(sds(rows, bf16), sds(rows, bf16)) + grad_shapes + (sds((24, 128), f32), sds(routed.shape, jnp.int32)),
        in_specs=[hbm] * 11,
        out_specs=[hbm] * 8,
        scratch_shapes=[
            space(wq_shape, bf16), space(wo_shape, bf16), space(wu_shape, bf16), space(wd_shape, bf16),
            space(grid + (16, 128), bf16),
            space((part, 3 * half_q), bf16), space((part, half_u), bf16), space((16, 128), bf16), space((16, 128), bf16),
            *[row_bf16] * 11, space(rows, f32), space(rows, f32),
            space((slots, ranks, 3 * half_q), bf16), space((slots, ranks, half_q), bf16),
            space((slots, ranks, half_u), bf16), space((slots, ranks, half_u), bf16),
            space((slots, ranks, 1), f32), space((16, model), f32),
            space(wd_shape, bf16), space(wu_shape, bf16),
            on_d[0], on_u[0], on_d[1], on_u[1], on_d[2], on_u[2],
            space((3, 2, 2 * part, model), bf16), space((2 * part, model), bf16),
            space((2, part, model), f32), space((part, model), f32), space((part, model), f32),
            space((2, part, half_u), f32), space((down, model), f32),
            space((part, model), bf16), space((part, half_q), bf16), space((part, half_u), bf16),
            space((part, model), bf16), space((part, half_q), bf16), space((part, half_u), bf16),
            space((24, 128), f32), space((5, 24, 128), f32), space((5, 24, 128), f32), space(routed.shape, jnp.int32),
            *[space((1, part), bf16)] * 3, space(routed.shape, jnp.int32), space((1, slots), jnp.int32),
            dma((19,)), dma((15,)), dma((8,)), dma((8, 3)), dma((8,)), dma((8,)), dma((8,)), dma((8,)),
            dma((19,)), dma((19,)), dma((9,)), dma((9,)), dma((2,)), dma((2,)), dma((9,)), dma((9,)), dma((10,)), dma((9, 3)),
            pltpu.SemaphoreType.REGULAR((2,)),
        ],
        compiler_params=pltpu.CompilerParams(collective_id=1, has_side_effects=True, vmem_limit_bytes=60 << 20),
        name="block",
    )(
        tokens.reshape(blocked), cotangent.reshape(blocked), w_qkv, w_out, w_up, w_down,
        gain_attn[None], gain_mlp[None], router[None], routed, lengths[None],
    )

    chunks = 2
    vectors = (sds((1, part), f32),) * 3
    output, input_grad, g_qkv, g_out, g_up, g_down, g_one, g_two, g_three = pl.pallas_call(
        rows_kernel,
        out_shape=(sds(tokens.shape, bf16), sds(tokens.shape, bf16)) + grad_shapes + vectors,
        in_specs=[hbm] * 10,
        out_specs=[hbm] * 9,
        scratch_shapes=[
            space((2, slots, chunks, local_len // chunks, model), bf16), space((2,) + rows, bf16),
            *[space(g.shape, f32) for g in grad_shapes],
            space((24, 128), f32), space(routed.shape, jnp.int32), *[space((1, part), f32)] * 3,
            dma((2, slots, chunks)), dma((2, slots, chunks)), dma((2, slots)), dma((2, 7)),
        ],
        compiler_params=pltpu.CompilerParams(vmem_limit_bytes=60 << 20),
        name="rows",
    )(tokens, cotangent, upd, dxr, *sums, vec, live)
    return (
        output, input_grad, g_qkv, g_out, g_up, g_down,
        g_one.reshape(part), g_two.reshape(part), g_three.reshape(part),
    )


def solution(mesh):
    in_specs = (
        P("batch", "seq", None),
        P("batch", "seq", None),
        P("batch"),
        P("batch", None),
        P(("seq", "batch"), None),
        P(("seq", "batch"), None),
        P(("seq", "batch"), None),
        P(("seq", "batch"), None),
        P(("seq", "batch")),
        P(("seq", "batch")),
        P(("seq", "batch")),
    )
    out_specs = (
        P("batch", "seq", None),
        P("batch", "seq", None),
        P(("seq", "batch"), None),
        P(("seq", "batch"), None),
        P(("seq", "batch"), None),
        P(("seq", "batch"), None),
        P(("seq", "batch")),
        P(("seq", "batch")),
        P(("seq", "batch")),
    )
    small_slice = mesh.shape["seq"] == 2 and mesh.shape["batch"] == 4 * LINE
    body = split_device if small_slice else general_device
    return jax.shard_map(body, mesh=mesh, in_specs=in_specs, out_specs=out_specs, check_vma=False)
```

```python
import functools

import jax
import jax.numpy as jnp
from jax import lax
from jax.experimental import pallas as pl
from jax.experimental.pallas import tpu as pltpu
from jax.sharding import PartitionSpec as P

HEAD_DIM = 64
MESH = pl.DeviceIdType.MESH


epsilon = 1e-05
highest = lax.Precision.HIGHEST
f32 = jnp.float32
bf16 = jnp.bfloat16

LINE = 4
GELU_C = 0.7978845608
GELU_K = 0.044715


def dot_nn(a, b):
    return lax.dot_general(a, b, (((1,), (0,)), ((), ())), preferred_element_type=f32)


def dot_nt(a, b):
    return lax.dot_general(a, b, (((1,), (1,)), ((), ())), preferred_element_type=f32)


def dot_tn(a, b):
    return lax.dot_general(a, b, (((0,), (0,)), ((), ())), preferred_element_type=f32)


def place():
    s = lax.axis_index("seq")
    b = lax.axis_index("batch")
    return s, b // 4, lax.rem(b // 2, 2), lax.rem(b, 2)


def device(s, z, y, c):
    return (s, z * 4 + y * 2 + c)


def remote(src, dst, send, recv, target):
    return pltpu.make_async_remote_copy(
        src_ref=src, dst_ref=dst, send_sem=send, recv_sem=recv, device_id=target, device_id_type=MESH
    )


def greet(targets):
    barrier = pltpu.get_barrier_semaphore()
    for target in targets:
        pl.semaphore_signal(barrier, inc=1, device_id=target, device_id_type=MESH)
    pl.semaphore_wait(barrier, len(targets))


def inverse_rms(values):
    return lax.rsqrt(jnp.mean(values * values, axis=-1, keepdims=True) + epsilon)


def head_mask(parity):
    lane = lax.broadcasted_iota(jnp.int32, (1, 128), 1)
    return jnp.where(lane // HEAD_DIM == parity, 1.0, 0.0).astype(f32)


def norm_apply(values_in, gain_vec):
    return (
        values_in
        * lax.rsqrt(jnp.mean(values_in * values_in, axis=-1, keepdims=True) + epsilon)
        * gain_vec
    )


def gelu_tanh(values_in):
    return jax.nn.gelu(values_in, approximate=True)


def general_device(
    tokens, cotangent, lengths, routed, w_qkv, w_out, w_up, w_down, gain_attn, gain_mlp, router
):
    slot_count, local_len, model_width = tokens.shape
    capacity = routed.shape[1]
    seq_devices = lax.axis_size("seq")
    own_count = capacity // seq_devices
    head_count = model_width // HEAD_DIM
    row_count = own_count * slot_count
    score_scale = HEAD_DIM ** (-0.5)
    gathered = (
        lax.all_gather(w_qkv, ("seq", "batch"), axis=0, tiled=True),
        lax.all_gather(w_out, ("seq", "batch"), axis=0, tiled=True),
        lax.all_gather(w_up, ("seq", "batch"), axis=0, tiled=True),
        lax.all_gather(w_down, ("seq", "batch"), axis=0, tiled=True),
        lax.all_gather(gain_attn, ("seq", "batch"), axis=0, tiled=True),
        lax.all_gather(gain_mlp, ("seq", "batch"), axis=0, tiled=True),
        lax.all_gather(router, ("seq", "batch"), axis=0, tiled=True),
    )
    full_qkv, full_out, full_up, full_down, full_ga, full_gm, full_router = gathered
    gain_one = full_ga.astype(f32)
    gain_two = full_gm.astype(f32)
    router_vec = full_router.astype(f32)
    counts = lengths // 8
    seq_place = lax.axis_index("seq")
    positions = seq_place * local_len + jnp.arange(local_len, dtype=jnp.int32)
    rank_all = jnp.arange(capacity, dtype=jnp.int32)
    live_all = rank_all[None, :] < counts[:, None]
    chooser = ((routed[:, :, None] == positions[None, None, :]) & live_all[:, :, None]).astype(bf16)
    pick_in = jnp.einsum("scp,spd->csd", chooser, tokens, preferred_element_type=f32)
    pick_cot = jnp.einsum("scp,spd->csd", chooser, cotangent, preferred_element_type=f32)
    picked, picked_cot = (
        lax.psum_scatter(
            pick_in.astype(jnp.bfloat16), "seq", scatter_dimension=0, tiled=True
        ).astype(jnp.float32),
        lax.psum_scatter(
            pick_cot.astype(jnp.bfloat16), "seq", scatter_dimension=0, tiled=True
        ).astype(jnp.float32),
    )
    own_rank = seq_place * own_count + jnp.arange(own_count, dtype=jnp.int32)
    live_own = own_rank[:, None] < counts[None, :]
    live_mask = live_own.reshape(row_count, 1).astype(f32)
    routed_in = picked.reshape(row_count, model_width)
    normed_one = norm_apply(routed_in, gain_one).astype(bf16)
    joined = jnp.dot(normed_one, full_qkv, preferred_element_type=f32).astype(bf16)
    query_rows = joined[:, :model_width].reshape(own_count, slot_count, head_count, HEAD_DIM)
    key_own = joined[:, model_width : 2 * model_width].reshape(own_count, slot_count, model_width)
    value_own = joined[:, 2 * model_width :].reshape(own_count, slot_count, model_width)
    key_every, value_every = (
        lax.all_gather(key_own, "seq", axis=0, tiled=True),
        lax.all_gather(value_own, "seq", axis=0, tiled=True),
    )
    key_rows = key_every.reshape(capacity, slot_count, head_count, HEAD_DIM)
    value_rows = value_every.reshape(capacity, slot_count, head_count, HEAD_DIM)
    scores = (
        jnp.einsum("qsha,ksha->shqk", query_rows, key_rows, preferred_element_type=f32)
        * score_scale
    )
    causal = rank_all[None, :] <= own_rank[:, None]
    allowed = causal[None, :, :] & (rank_all[None, None, :] < counts[:, None, None])
    scores = jnp.where(allowed[:, None], scores, -1000000000.0)
    row_max = jnp.max(scores, axis=-1, keepdims=True)
    weights_f = jnp.exp(scores - row_max)
    row_total = jnp.sum(weights_f, axis=-1, keepdims=True)
    weights_low = weights_f.astype(bf16)
    mixture = jnp.einsum("shqk,ksha->qsha", weights_low, value_rows, preferred_element_type=f32)
    mixture = mixture / jnp.transpose(row_total, (2, 0, 1, 3))
    attended = mixture.reshape(row_count, model_width).astype(bf16)
    branch_a = jnp.dot(attended, full_out, preferred_element_type=f32)
    hidden = routed_in + branch_a
    normed_two = norm_apply(hidden, gain_two).astype(bf16)
    up_proj = jnp.dot(normed_two, full_up, preferred_element_type=f32)
    activated = gelu_tanh(up_proj).astype(bf16)
    branch_m = jnp.dot(activated, full_down, preferred_element_type=f32)
    gate_prob = jax.nn.sigmoid(jnp.dot(routed_in, router_vec, precision=highest))
    branch = branch_a + branch_m
    update = (
        (gate_prob[:, None] * branch * live_mask)
        .astype(bf16)
        .reshape(own_count, slot_count, model_width)
    )
    update_every = lax.all_gather(update, "seq", axis=0, tiled=True)
    output = (
        tokens.astype(f32)
        + jnp.einsum("scp,csd->spd", chooser, update_every, preferred_element_type=f32)
    ).astype(bf16)
    cot_rows = picked_cot.reshape(row_count, model_width)
    grad_gate = jnp.sum(cot_rows * branch, axis=-1)
    grad_logit = grad_gate * gate_prob * (1.0 - gate_prob)
    grad_branch = gate_prob[:, None] * cot_rows
    grad_m = grad_branch.astype(bf16)
    grad_act = jnp.einsum("rd,fd->rf", grad_m, full_down, preferred_element_type=f32)
    unused_up, gelu_pull = jax.vjp(gelu_tanh, up_proj)
    grad_u = gelu_pull(grad_act)[0].astype(bf16)
    grad_n2 = jnp.einsum("rf,df->rd", grad_u, full_up, preferred_element_type=f32)
    unused_two, norm_pull_two = jax.vjp(norm_apply, hidden, gain_two)
    grad_hidden, grad_gm = norm_pull_two(grad_n2)
    grad_a = (grad_branch + grad_hidden).astype(bf16)
    grad_att = jnp.einsum("rd,ed->re", grad_a, full_out, preferred_element_type=f32).astype(bf16)
    grad_att4 = grad_att.reshape(own_count, slot_count, head_count, HEAD_DIM)
    delta_rows = jnp.sum(grad_att4.astype(f32) * mixture, axis=-1)
    delta = jnp.transpose(delta_rows, (1, 2, 0))[..., None]
    grad_p = jnp.einsum("qsha,ksha->shqk", grad_att4, value_rows, preferred_element_type=f32)
    probs = weights_f / row_total
    grad_s = (probs * (grad_p - delta)).astype(bf16)
    grad_q = (
        jnp.einsum("shqk,ksha->qsha", grad_s, key_rows, preferred_element_type=f32) * score_scale
    )
    grad_k = (
        jnp.einsum("shqk,qsha->ksha", grad_s, query_rows, preferred_element_type=f32) * score_scale
    )
    scaled_low = weights_low.astype(f32) / row_total
    grad_v = jnp.einsum("shqk,qsha->ksha", scaled_low, grad_att4.astype(f32), precision=highest)
    grad_k_own, grad_v_own = (
        lax.psum_scatter(
            grad_k.reshape(capacity, slot_count, model_width).astype(jnp.bfloat16),
            "seq",
            scatter_dimension=0,
            tiled=True,
        ).astype(jnp.float32),
        lax.psum_scatter(
            grad_v.reshape(capacity, slot_count, model_width).astype(jnp.bfloat16),
            "seq",
            scatter_dimension=0,
            tiled=True,
        ).astype(jnp.float32),
    )
    grad_joined = jnp.concatenate(
        [
            grad_q.reshape(row_count, model_width),
            grad_k_own.reshape(row_count, model_width),
            grad_v_own.reshape(row_count, model_width),
        ],
        axis=-1,
    ).astype(bf16)
    grad_n1 = jnp.einsum("re,de->rd", grad_joined, full_qkv, preferred_element_type=f32)
    unused_one, norm_pull_one = jax.vjp(norm_apply, routed_in, gain_one)
    grad_x1, grad_ga = norm_pull_one(grad_n1)
    grad_router = jnp.sum(routed_in * grad_logit[:, None], axis=0)
    grad_rows = (grad_hidden + grad_x1 + grad_logit[:, None] * router_vec[None, :]).astype(bf16)
    grad_rows = grad_rows.reshape(own_count, slot_count, model_width)
    grad_every = lax.all_gather(grad_rows, "seq", axis=0, tiled=True)
    input_grad = (
        cotangent.astype(f32)
        + jnp.einsum("scp,csd->spd", chooser, grad_every, preferred_element_type=f32)
    ).astype(bf16)
    part_qkv = jnp.einsum("rd,re->de", normed_one, grad_joined, preferred_element_type=f32)
    part_out = jnp.einsum("re,rd->ed", attended, grad_a, preferred_element_type=f32)
    part_up = jnp.einsum("rd,rf->df", normed_two, grad_u, preferred_element_type=f32)
    part_down = jnp.einsum("rf,rd->fd", activated, grad_m, preferred_element_type=f32)

    def sum_rows(part):
        return lax.psum_scatter(
            part.astype(bf16), ("seq", "batch"), scatter_dimension=0, tiled=True
        ).astype(f32)

    down_sum = sum_rows(part_down)
    grad_up = sum_rows(part_up)
    grad_out = sum_rows(part_out)
    grad_qkv = sum_rows(part_qkv)
    small_ga, small_gm, small_router = (
        lax.psum_scatter(grad_ga, ("seq", "batch"), scatter_dimension=0, tiled=True),
        lax.psum_scatter(grad_gm, ("seq", "batch"), scatter_dimension=0, tiled=True),
        lax.psum_scatter(grad_router, ("seq", "batch"), scatter_dimension=0, tiled=True),
    )
    return (
        output,
        input_grad,
        grad_qkv,
        grad_out,
        grad_up,
        down_sum,
        small_ga,
        small_gm,
        small_router,
    )


def block_kernel(
    tok_hbm, cot_hbm, wq_hbm, wo_hbm, wu_hbm, wd_hbm, one_hbm, two_hbm, three_hbm, routed_hbm, len_hbm,
    upd_out, dx_out, fq_out, fo_out, fu_out, fd_out, vec_out, live_out,
    wq, wo, wu, wd, gv, stq, stu, stv, rcv,
    xs, xr, ds, dr, a_s, a_r, d2s, d2r, d1r, m_s, m_r, hid, dh, qkv, att, act, gp, logit, gains,
    gd, gu, rcd, rcu, ryd, ryu, rzd, rzu, rzb, ryb,
    fqk, fv, fo, fu, fd, sqk, sv, suu, rqk, rv, ruu, vs, vr, v_all, live,
    one_ref, two_ref, three_ref, routed_ref, len_ref,
    loc, out_sem, wz, vz, wy, vy, wc, vc, sx, rx, gc, hc, gt, ht, gy, hy, gz, hz, free,
):
    s, z, y, c = place()
    near, far = z + 1 - 2 * lax.rem(z, 2), LINE - 1 - z
    xdev, ydev, cdev = device(1 - s, z, y, c), device(s, z, 1 - y, c), device(s, z, y, 1 - c)
    ndev, fdev = device(s, near, y, c), device(s, far, y, c)
    model, half_q, half_u = xr.shape[2], att.shape[2], act.shape[2]
    ranks, half = xr.shape[1], xr.shape[2] // 2
    rows = xr.shape[0] * ranks
    part, half_d = stq.shape[0], wd.shape[3] // 2
    local, sent, outs = [], [], []

    def fetch(src, dst):
        copy = pltpu.make_async_copy(src, dst, loc.at[len(local)])
        copy.start()
        local.append(copy)
        return copy

    def send(src, dst, send_sem, recv_sem, target):
        copy = remote(src, dst, send_sem, recv_sem, target)
        copy.start()
        sent.append(copy)
        return copy

    def gone(copy):
        copy.wait_send()
        sent[:] = [other for other in sent if other is not copy]

    def arrive(ref, send_sem, recv_sem, target):
        remote(ref, ref, send_sem, recv_sem, target).wait_recv()

    def put(src, dst):
        copy = pltpu.make_async_copy(src, dst, out_sem.at[len(outs)])
        copy.start()
        outs.append(copy)

    barrier = pltpu.get_barrier_semaphore()
    for target in (xdev, ydev, cdev, ndev, fdev):
        pl.semaphore_signal(barrier, inc=1, device_id=target, device_id_type=MESH)

    stage, own_q = [], []
    small_in = [
        fetch(src, dst)
        for src, dst in (
            (one_hbm, one_ref), (two_hbm, two_ref), (three_hbm, three_ref), (routed_hbm, routed_ref), (len_hbm, len_ref),
        )
    ]
    for j in range(3):
        base, dst = 2 * j * half_q, pl.ds(j * half_q, half_q)
        stage.append(fetch(wq_hbm.at[:, pl.ds(base + (1 - s) * half_q, half_q)], stq.at[:, dst]))
        own_q.append(fetch(wq_hbm.at[:, pl.ds(base + s * half_q, half_q)], wq.at[s, z, y, c, :, dst]))
    get_tok = [fetch(tok_hbm.at[i], gd.at[pl.ds(2 * i, 2)]) for i in range(2)]
    own_o = fetch(wo_hbm, wo.at[z, y, c])
    stage_u = fetch(wu_hbm.at[:, pl.ds((1 - s) * half_u, half_u)], stu)
    own_u = fetch(wu_hbm.at[:, pl.ds(s * half_u, half_u)], wu.at[s, z, y, c])
    own_d = fetch(wd_hbm, wd.at[z, y, c])

    def down_half(i):
        return pl.ds(half_d * i, half_d)

    blocks = [
        lambda zz, yy, cc: wq.at[s, zz, yy, cc],
        lambda zz, yy, cc: wq.at[1 - s, zz, yy, cc],
        lambda zz, yy, cc: gv.at[zz, yy, cc],
        lambda zz, yy, cc: wo.at[zz, yy, cc],
        lambda zz, yy, cc: wu.at[s, zz, yy, cc],
        lambda zz, yy, cc: wu.at[1 - s, zz, yy, cc],
        lambda zz, yy, cc: wd.at[zz, yy, cc, down_half(0)],
        lambda zz, yy, cc: wd.at[zz, yy, cc, down_half(1)],
    ]
    lines = [
        lambda yy, cc: wq.at[s, :, yy, cc],
        lambda yy, cc: wq.at[1 - s, :, yy, cc],
        lambda yy, cc: gv.at[:, yy, cc],
        lambda yy, cc: wo.at[:, yy, cc],
        lambda yy, cc: wu.at[s, :, yy, cc],
        lambda yy, cc: wu.at[1 - s, :, yy, cc],
        lambda yy, cc: wd.at[:, yy, cc, down_half(0)],
        lambda yy, cc: wd.at[:, yy, cc, down_half(1)],
    ]
    Q_OWN, Q_SWAP, VEC, OUT, U_OWN, U_SWAP, D_0, D_1 = range(8)

    planes = [
        lambda cc: wq.at[s, :, :, cc],
        lambda cc: wq.at[1 - s, :, :, cc],
        lambda cc: gv.at[:, :, cc],
        lambda cc: wo.at[:, :, cc],
        lambda cc: wu.at[s, :, :, cc],
        lambda cc: wu.at[1 - s, :, :, cc],
        lambda cc: wd.at[:, :, cc, down_half(0)],
        lambda cc: wd.at[:, :, cc, down_half(1)],
    ]

    def pass_on(ref, send_sem, recv_sem, target):
        remote(ref, ref, send_sem, recv_sem, target).start()

    def spread(p):
        own = blocks[p](z, y, c)
        pass_on(own, wz.at[p], vz.at[p, 0], fdev)
        pass_on(own, wz.at[p], vz.at[p, 1], ndev)

    def spread_y(p):
        pass_on(blocks[p](z, y, c), wy.at[p], vy.at[p], ydev)

    def after_far(p):
        ref = blocks[p](far, y, c)
        arrive(ref, wz.at[p], vz.at[p, 0], fdev)
        pass_on(ref, wz.at[p], vz.at[p, 2], ndev)
        pass_on(ref, wy.at[p], vy.at[p], ydev)

    def after_near(p):
        for i, zz in ((1, near), (2, LINE - 1 - near)):
            ref = blocks[p](zz, y, c)
            arrive(ref, wz.at[p], vz.at[p, i], ndev)
            pass_on(ref, wy.at[p], vy.at[p], ydev)
        pass_on(lines[p](y, c), wc.at[p], vc.at[p], cdev)

    def after_y(p):
        line = lines[p](1 - y, c)
        arrive(line, wy.at[p], vy.at[p], ydev)
        pass_on(line, wc.at[p], vc.at[p], cdev)

    def after_c(p):
        arrive(planes[p](1 - c), wc.at[p], vc.at[p], cdev)

    def both(zz, cc):
        return wd.at[zz, :, cc, down_half(1)]

    def after_first_y():
        arrive(blocks[D_1](z, 1 - y, c), wy.at[D_1], vy.at[D_1], ydev)
        own = both(z, c)
        pass_on(own, wz.at[D_1], vz.at[D_1, 0], fdev)
        pass_on(own, wz.at[D_1], vz.at[D_1, 1], ndev)

    def after_first_far():
        ref = both(far, c)
        arrive(ref, wz.at[D_1], vz.at[D_1, 0], fdev)
        pass_on(ref, wz.at[D_1], vz.at[D_1, 2], ndev)

    def after_first_near():
        for i, zz in ((1, near), (2, LINE - 1 - near)):
            arrive(both(zz, c), wz.at[D_1], vz.at[D_1, i], ndev)
        pass_on(planes[D_1](c), wc.at[D_1], vc.at[D_1], cdev)

    def after_first_c():
        arrive(planes[D_1](1 - c), wc.at[D_1], vc.at[D_1], cdev)

    def left(ref, send_sem, recv_sem, target):
        remote(ref, ref, send_sem, recv_sem, target).wait_send()

    def gathered():
        three = pl.ds(0, LINE - 1)
        passed = [
            wq.at[s, three, y, c], wq.at[1 - s, three, y, c], gv.at[three, y, c], wo.at[three, y, c],
            wu.at[s, three, y, c], wu.at[1 - s, three, y, c], wd.at[three, y, c, down_half(0)],
            wd.at[three, :, c, down_half(1)],
        ]
        for p in range(8):
            left(passed[p], wz.at[p], vz.at[p, 0], ndev)
            left(blocks[p](z, y, c) if p == D_1 else lines[p](y, c), wy.at[p], vy.at[p], ydev)
            left(planes[p](c), wc.at[p], vc.at[p], cdev)

    spans = [pl.ds(0, 2 * part), pl.ds(2 * part, 2 * part), None, None]
    spans += [pl.ds(i * part, part) for i in range(4)]
    parts = [
        (lambda cc, i=i: gu.at[i - 2, :, :, cc]) if q is None else (lambda cc, q=q: gd.at[:, :, cc, q])
        for i, q in enumerate(spans)
    ]
    land_c = [rcu.at[i - 2] if q is None else rcd.at[:, :, q] for i, q in enumerate(spans)]
    land_y = [ryu.at[i - 2] if q is None else ryd.at[:, q] for i, q in enumerate(spans)]
    land_z = [rzu.at[i - 2] if q is None else rzd.at[:, q] for i, q in enumerate(spans)]

    def c_start(k):
        return send(parts[k](1 - c), land_c[k], gc.at[k], hc.at[k], cdev)

    def c_end(k):
        ref, own = land_c[k], parts[k](c)
        if k < 2:
            arrive(ref, gt.at[k], ht.at[k], cdev)
        else:
            arrive(ref, gc.at[k], hc.at[k], cdev)

        def add(i, carry):
            ref[i] = (ref[i].astype(f32) + own[i].astype(f32)).astype(bf16)
            return carry

        lax.fori_loop(0, LINE, add, 0)
        if k == 0:
            remote(ref.at[LINE - 1 - near], rzb.at[1], gz.at[k], hz.at[k, 1], ndev).start()
            remote(ref.at[near], rzb.at[0], gz.at[k], hz.at[k, 0], ndev).start()
            return []
        return [send(ref.at[:, 1 - y], land_y[k], gy.at[k], hy.at[k], ydev)]

    def y_end(k):
        ref, own = land_y[k], land_c[k]
        arrive(ref, gy.at[k], hy.at[k], ydev)

        def add(i, carry):
            ref[i] = (ref[i].astype(f32) + own[i, y].astype(f32)).astype(bf16)
            return carry

        lax.fori_loop(0, LINE, add, 0)
        remote(ref.at[LINE - 1 - near], land_z[k].at[1], gz.at[k], hz.at[k, 1], ndev).start()
        remote(ref.at[near], land_z[k].at[0], gz.at[k], hz.at[k, 0], ndev).start()

    def z_mid(k):
        ref = land_z[k].at[1]
        arrive(ref, gz.at[k], hz.at[k, 1], ndev)
        ref[...] = (ref[...].astype(f32) + land_y[k][far].astype(f32)).astype(bf16)
        remote(ref, land_z[k].at[2], gz.at[k], hz.at[k, 2], fdev).start()

    def z_end(k):
        arrive(land_z[k].at[0], gz.at[k], hz.at[k, 0], ndev)
        arrive(land_z[k].at[2], gz.at[k], hz.at[k, 2], fdev)
        return land_y[k][z].astype(f32) + land_z[k][0].astype(f32) + land_z[k][2].astype(f32)

    def first_mid():
        arrive(rzb.at[1], gz.at[0], hz.at[0, 1], ndev)
        rzb[1] = (rzb[1].astype(f32) + land_c[0][far].astype(f32)).astype(bf16)
        remote(rzb.at[1], rzb.at[2], gz.at[0], hz.at[0, 2], fdev).start()

    def first_end():
        arrive(rzb.at[0], gz.at[0], hz.at[0, 0], ndev)
        arrive(rzb.at[2], gz.at[0], hz.at[0, 2], fdev)
        rzb[0] = (land_c[0][z].astype(f32) + rzb[0].astype(f32) + rzb[2].astype(f32)).astype(bf16)
        return send(rzb.at[0, 1 - y], ryb, gy.at[0], hy.at[0], ydev)

    def first_sum():
        arrive(ryb, gy.at[0], hy.at[0], ydev)
        return rzb[0, y].astype(f32) + ryb[...].astype(f32)

    for copy in small_in:
        copy.wait()
    fits = lax.broadcasted_iota(jnp.int32, (part, model), 1) == s * part + lax.broadcasted_iota(
        jnp.int32, (part, model), 0
    )
    line = lax.broadcasted_iota(jnp.int32, (16, part), 0)
    small = jnp.zeros((16, part), f32)
    for j, ref in enumerate((one_ref, two_ref, three_ref)):
        small = jnp.where(line == j, ref[...].astype(f32), small)
    gains[...] = dot_nn(small.astype(bf16), jnp.where(fits, 1.0, 0.0).astype(bf16))
    stv[...] = gains[:, 0:128].astype(bf16)

    rank = lax.broadcasted_iota(jnp.int32, (1, ranks), 1)

    def count(i):
        return lax.shift_right_arithmetic(len_ref[:, i : i + 1], 3)

    for i in range(2):
        live[i : i + 1] = jnp.where(rank < count(i), routed_ref[i : i + 1], -1)

    def chooser(i):
        row = live[i : i + 1].astype(f32)
        eye = lax.broadcasted_iota(jnp.int32, (ranks, ranks), 0) == lax.broadcasted_iota(
            jnp.int32, (ranks, ranks), 1
        )
        column = jnp.sum(jnp.where(eye, row, 0.0), axis=1, keepdims=True).astype(jnp.int32)
        count_here = tok_hbm.shape[1] * 512
        position = lax.broadcasted_iota(jnp.int32, (ranks, count_here), 1) + s * count_here
        return jnp.where(position == column, 1.0, 0.0).astype(bf16)

    def pick(i, dst):
        dst[i] = dot_nn(chooser(i), gd[2 * i : 2 * i + 2].reshape(tok_hbm.shape[1] * 512, model)).astype(bf16)

    def live_column(i):
        rank = lax.broadcasted_iota(jnp.int32, (ranks, 1), 0)
        return jnp.where(rank < count(i), 1.0, 0.0).astype(f32)

    def allowed(i):
        query = lax.broadcasted_iota(jnp.int32, (ranks, ranks), 0)
        key = lax.broadcasted_iota(jnp.int32, (ranks, ranks), 1)
        return (key <= query) & (key < count(i))

    for copy in stage:
        copy.wait()
    pl.semaphore_wait(barrier, 5)
    send(stq, wq.at[s, z, y, c], sx.at[1], rx.at[1], xdev)
    swap_v = send(stv, rcv, sx.at[0], rx.at[0], xdev)
    for copy in own_q:
        copy.wait()
    spread(Q_OWN)
    spread_y(Q_OWN)
    own_d.wait()
    spread_y(D_1)
    x_swap = []
    get_tok[0].wait()
    pick(0, xs)
    x_swap.append(send(xs.at[0], xr.at[0], sx.at[3], rx.at[3], xdev))
    get_cot = [fetch(cot_hbm.at[0], gd.at[pl.ds(0, 2)])]
    stage_u.wait()
    send(stu, wu.at[s, z, y, c], sx.at[2], rx.at[2], xdev)
    get_tok[1].wait()
    pick(1, xs)
    x_swap.append(send(xs.at[1], xr.at[1], sx.at[4], rx.at[4], xdev))
    get_cot.append(fetch(cot_hbm.at[1], gd.at[pl.ds(2, 2)]))
    put(live, live_out)
    swap_v.wait_recv()
    gv[z, y, c] = stv[...] + rcv[...]
    after_far(Q_OWN)
    spread(VEC)
    spread_y(VEC)
    arrive(wq.at[1 - s, z, y, c], sx.at[1], rx.at[1], xdev)
    spread(Q_SWAP)
    spread_y(Q_SWAP)
    get_cot[0].wait()
    pick(0, ds)
    d_swap = [send(ds.at[0], dr.at[0], sx.at[7], rx.at[7], xdev)]
    after_near(Q_OWN)
    after_far(VEC)
    get_cot[1].wait()
    pick(1, ds)
    after_far(Q_SWAP)
    own_o.wait()
    spread(OUT)
    after_near(VEC)
    after_near(Q_SWAP)
    after_far(OUT)
    spread_y(OUT)
    own_u.wait()
    spread(U_OWN)
    spread_y(U_OWN)
    arrive(wu.at[1 - s, z, y, c], sx.at[2], rx.at[2], xdev)
    spread(U_SWAP)
    after_y(Q_OWN)
    after_y(VEC)
    after_c(Q_OWN)
    after_c(VEC)
    after_near(OUT)
    after_y(Q_SWAP)
    after_far(U_OWN)
    spread(D_0)
    spread_y(U_SWAP)
    spread_y(D_0)
    after_c(Q_SWAP)

    group = lax.broadcasted_iota(jnp.int32, (16, 128), 1) // part
    for q in range(LINE):
        for i in range(2):
            tile = jnp.zeros((16, 128), f32)
            for j in range(4):
                moved = pltpu.roll(gv[q, j // 2, j % 2].astype(f32), (j - i) * part % 128, 1)
                tile = jnp.where(group == j, moved, tile)
            gains[:, i * half + q * 128 : i * half + (q + 1) * 128] = tile
    gain_one, gain_two, router = gains[0:1], gains[1:2], gains[2:3]

    def enter(i):
        x_swap[i].wait()
        row = xr[i].astype(f32) + xs[i].astype(f32)
        xr[i] = row.astype(bf16)
        xs[i] = (row * inverse_rms(row) * gain_one).astype(bf16)
        for j in range(3):
            cols = pl.ds(j * half_q, half_q)
            qkv[i, :, cols] = dot_nn(xs[i], wq[:, :, :, :, :, cols].reshape(model, half_q)).astype(bf16)

    def attend(i):
        ok = allowed(i)

        def pair(j, carry):
            q2 = qkv[i, :, pl.ds(j * 128, 128)].astype(f32)
            k2 = qkv[i, :, pl.ds(half_q + j * 128, 128)]
            v2 = qkv[i, :, pl.ds(2 * half_q + j * 128, 128)]
            mixed = jnp.zeros(q2.shape, f32)
            for parity in range(2):
                mask = head_mask(parity)
                score = dot_nt((q2 * mask).astype(bf16), k2) * (HEAD_DIM**-0.5)
                score = jnp.where(ok, score, -1000000000.0)
                weight = jnp.exp(score - jnp.max(score, axis=-1, keepdims=True))
                total = jnp.sum(weight, axis=-1, keepdims=True)
                mixed += dot_nn(weight.astype(bf16), v2) / total * mask
            att[i, :, pl.ds(j * 128, 128)] = mixed.astype(bf16)
            return carry

        lax.fori_loop(0, half_q // 128, pair, 0)

    def leave(i):
        for j in range(2):
            cols = pl.ds(j * half, half)
            a_s[i, :, cols] = dot_nn(att[i], wo[:, :, :, :, cols].reshape(half_q, half)).astype(bf16)
        return send(a_s.at[i], a_r.at[i], sx.at[5 + i], rx.at[5 + i], xdev)

    enter(0)
    attend(0)
    after_y(OUT)
    after_c(OUT)
    a_swap = [leave(0)]
    after_far(U_SWAP)
    after_first_y()
    after_near(U_OWN)
    enter(1)
    attend(1)
    a_swap.append(leave(1))
    d_swap.append(send(ds.at[1], dr.at[1], sx.at[8], rx.at[8], xdev))
    after_far(D_0)
    after_near(U_SWAP)
    after_y(U_OWN)
    after_c(U_OWN)

    def mlp_up(i):
        a_swap[i].wait()
        row = xr[i].astype(f32) + (a_s[i].astype(f32) + a_r[i].astype(f32))
        hid[i] = row
        a_s[i] = (row * inverse_rms(row) * gain_two).astype(bf16)

        def tile(t, carry):
            cols = pl.ds(t * 512, 512)
            up = dot_nn(a_s[i], wu[:, :, :, :, :, cols].reshape(model, 512))
            curve = jnp.tanh(GELU_C * (up + GELU_K * up * up * up))
            act[i, :, cols] = (0.5 * up * (1.0 + curve)).astype(bf16)
            slope = 0.5 * (1.0 + curve) + 0.5 * up * (1.0 - curve * curve) * (
                GELU_C * (1.0 + 3.0 * GELU_K * up * up)
            )
            gp[i, :, cols] = slope.astype(bf16)
            return carry

        lax.fori_loop(0, half_u // 512, tile, 0)

    def gate_of(i):
        return jax.nn.sigmoid(jnp.sum(xr[i].astype(f32) * router, axis=-1, keepdims=True))

    def cotangent_rows(i):
        d_swap[i].wait()
        row = dr[i].astype(f32) + ds[i].astype(f32)
        dr[i] = row.astype(bf16)
        ds[i] = (gate_of(i) * row).astype(bf16)

    def mlp_back(i):
        def tile(t, carry):
            cols = pl.ds(t * 512, 512)
            back = dot_nt(ds[i], wd[t].reshape(512, model))
            gp[i, :, cols] = (back * gp[i, :, cols].astype(f32)).astype(bf16)
            return carry

        lax.fori_loop(0, half_u // 512, tile, 0)
        for j in range(2):
            cols = pl.ds(j * half, half)
            d2s[i, :, cols] = dot_nt(gp[i], wu[j].reshape(half, half_u)).astype(bf16)
        return send(d2s.at[i], d2r.at[i], sx.at[9 + i], rx.at[9 + i], xdev)

    def mlp_out(i):
        for j in range(2):
            cols = pl.ds(j * half, half)
            m_s[i, :, cols] = dot_nn(act[i], wd[:, :, :, :, cols].reshape(half_u, half)).astype(bf16)

    def mlp_send(i):
        return send(m_s.at[i], m_r.at[i], sx.at[11 + i], rx.at[11 + i], xdev)

    after_y(U_SWAP)
    after_first_far()
    after_c(U_SWAP)
    mlp_up(0)
    after_near(D_0)
    cotangent_rows(0)

    def down_tile(t, carry):
        gd[t] = dot_tn(act[0, :, pl.ds(t * 512, 512)], ds[0]).astype(bf16).reshape(gd.shape[1:])
        return carry

    lax.fori_loop(0, LINE, down_tile, 0)
    mlp_up(1)
    after_y(D_0)
    after_c(D_0)
    after_first_near()
    after_first_c()
    d2_swap = [mlp_back(0)]
    cotangent_rows(1)

    def c_tile(t, k):
        remote(gd.at[t, :, 1 - c, spans[k]], land_c[k].at[t], gt.at[k], ht.at[k], cdev).start()

    for t in range(LINE):
        grad = dot_tn(act[1, :, t * 512 : t * 512 + 512], ds[1])
        gd[t] = (gd[t].astype(f32) + grad.reshape(gd.shape[1:])).astype(bf16)
        c_tile(t, 1)
    for t in range(LINE):
        c_tile(t, 0)
    y_down = c_end(1)
    c_end(0)
    d2_swap.append(mlp_back(1))
    mlp_out(0)
    m_swap = [mlp_send(0)]

    def up_tile(t, carry):
        cols = pl.ds(t * 512, 512)
        grad = dot_tn(a_s[...].reshape(rows, model), gp[:, :, cols].reshape(rows, 512))
        gu[:, :, :, :, :, cols] = grad.astype(bf16).reshape(gu.shape[:5] + (512,))
        return carry

    lax.fori_loop(0, half_u // 512, up_tile, 0)
    c_start(2)
    c_start(3)
    mlp_out(1)
    m_swap.append(mlp_send(1))

    def hidden_back(i):
        d2_swap[i].wait()
        back = d2s[i].astype(f32) + d2r[i].astype(f32)
        row = hid[i]
        r2 = inverse_rms(row)
        scaled = back * gain_two
        step = r2 * scaled - row * (r2 * r2 * r2 * jnp.mean(scaled * row, axis=-1, keepdims=True))
        dh[i] = step
        gp[i, :, 0:model] = (gate_of(i) * dr[i].astype(f32) + step).astype(bf16)
        gp[i, :, model : model + half_q] = dot_nt(gp[i, :, 0:model], wo[...].reshape(half_q, model)).astype(bf16)
        return jnp.sum(d2s[i].astype(f32) * row * r2, axis=0, keepdims=True)

    def attend_back(i):
        ok = allowed(i)
        scale = HEAD_DIM**-0.5

        def pair(j, carry):
            q2 = qkv[i, :, pl.ds(j * 128, 128)]
            k2 = qkv[i, :, pl.ds(half_q + j * 128, 128)]
            v2 = qkv[i, :, pl.ds(2 * half_q + j * 128, 128)]
            g2 = gp[i, :, pl.ds(model + j * 128, 128)].astype(f32)
            q2f = q2.astype(f32)
            dq2 = jnp.zeros(q2.shape, f32)
            dk2 = jnp.zeros(q2.shape, f32)
            dv2 = jnp.zeros(q2.shape, f32)
            for parity in range(2):
                mask = head_mask(parity)
                score = dot_nt((q2f * mask).astype(bf16), k2) * scale
                score = jnp.where(ok, score, -1000000000.0)
                weight = jnp.exp(score - jnp.max(score, axis=-1, keepdims=True))
                over = 1.0 / jnp.sum(weight, axis=-1, keepdims=True)
                gh = g2 * mask
                dp = dot_nt(gh.astype(bf16), v2)
                prob = weight * over
                delta = jnp.sum(prob * dp, axis=-1, keepdims=True)
                dscore = (prob * (dp - delta)).astype(bf16)
                dq2 += dot_nn(dscore, k2) * mask
                dk2 += dot_tn(dscore, q2) * mask
                dv2 += dot_tn(weight.astype(bf16), (gh * over).astype(bf16))
            act[i, :, pl.ds(j * 128, 128)] = (dq2 * scale).astype(bf16)
            act[i, :, pl.ds(half_q + j * 128, 128)] = (dk2 * scale).astype(bf16)
            act[i, :, pl.ds(2 * half_q + j * 128, 128)] = dv2.astype(bf16)
            return carry

        lax.fori_loop(0, half_q // 128, pair, 0)

    def inner_back(i):
        r1 = inverse_rms(xr[i].astype(f32))
        sums = []
        for j in range(2):
            cols = pl.ds(j * half, half)
            step = dot_nt(act[i, :, 0 : 3 * half_q], wq[j].reshape(half, 3 * half_q))
            d2s[i, :, cols] = step.astype(bf16)
            sums.append(jnp.sum(step * xr[i, :, cols].astype(f32) * r1, axis=0, keepdims=True))
        return send(d2s.at[i], d1r.at[i], sx.at[13 + i], rx.at[13 + i], xdev), sums

    grad_gm = hidden_back(0)
    c_end(2)
    attend_back(0)
    c_end(3)
    first_mid()
    swap_0, sums_0 = inner_back(0)
    y_end(1)
    grad_gm += hidden_back(1)
    attend_back(1)
    z_mid(1)
    for k in range(2):
        left(parts[k](1 - c), gt.at[k], ht.at[k], cdev)
    left(rzb, gz.at[0], hz.at[0, 0], ndev)
    first_end()
    pl.semaphore_signal(free.at[0], inc=1, device_id=cdev, device_id_type=MESH)
    y_end(2)

    def out_tile(t):
        cols = pl.ds(t * half, half)
        grad = dot_tn(att[...].reshape(rows, half_q), gp[:, :, cols].reshape(rows, half))
        gd[:, :, :, 3 * part :, cols] = grad.astype(bf16).reshape(wo.shape[:4] + (half,))

    def qkv_tile(t):
        grad = dot_tn(xs[...].reshape(rows, model), act[:, :, t * half_q : (t + 1) * half_q].reshape(rows, half_q))
        grad = grad.astype(bf16).reshape(wq.shape[:5] + (half_q,))
        if t < 2:
            gd[:, :, :, 0:part, t * half_q : (t + 1) * half_q] = grad[0]
            gd[:, :, :, part : 2 * part, t * half_q : (t + 1) * half_q] = grad[1]
        else:
            gd[:, :, :, 2 * part : 3 * part, 0:half_q] = grad[0]
            gd[:, :, :, 2 * part : 3 * part, half_q:] = grad[1]

    qkv_tile(0)
    qkv_tile(1)
    pl.semaphore_wait(free.at[0], 1)
    c_start(4)
    c_start(5)
    qkv_tile(2)
    fd[2 * part :] = z_end(1)
    for copy in y_down:
        gone(copy)
    left(land_z[1], gz.at[1], hz.at[1, 0], ndev)
    for target in (ydev, cdev, ndev, fdev):
        pl.semaphore_signal(free.at[1], inc=1, device_id=target, device_id_type=MESH)
    out_tile(0)
    out_tile(1)
    c_end(4)
    c_end(5)
    swap_1, sums_1 = inner_back(1)
    d1_swap = [swap_0, swap_1]
    for j in range(2):
        gains[8:9, j * half : (j + 1) * half] = sums_0[j] + sums_1[j]
    gains[9:10] = grad_gm
    pl.semaphore_wait(free.at[1], 4)
    c_start(6)
    c_start(7)
    z_mid(2)
    c_end(6)
    y_end(3)
    fu[0] = z_end(2)

    grad_router = jnp.zeros((1, model), f32)
    for i in range(2):
        m_swap[i].wait()
        row = xr[i].astype(f32)
        gate = gate_of(i)
        branch = (hid[i] - row) + (m_s[i].astype(f32) + m_r[i].astype(f32))
        m_s[i] = (gate * branch * live_column(i)).astype(bf16)
        slope = jnp.sum(dr[i].astype(f32) * branch, axis=-1, keepdims=True) * gate * (1.0 - gate)
        logit[i] = slope
        grad_router += jnp.sum(row * slope, axis=0, keepdims=True)
    put(m_s, upd_out)
    gains[10:11] = 0.5 * grad_router
    for j in range(3):
        for t in range(model // 128):
            vs[8 * j + t : 8 * j + t + 1] = gains[8 + j : 9 + j, t * 128 : (t + 1) * 128]
    send(vs, vr.at[0], gc.at[8], hc.at[8], cdev)
    z_mid(3)
    arrive(vr.at[0], gc.at[8], hc.at[8], cdev)
    v_all[0] = vs[...] + vr[0]
    send(v_all.at[0], vr.at[1], gz.at[8], hz.at[8, 0], ndev)
    c_end(7)
    fd[0 : 2 * part] = first_sum()
    put(fd, fd_out)
    y_end(4)
    fu[1] = z_end(3)
    suu[...] = fu[1 - s].astype(bf16)
    send(suu, ruu, sx.at[15], rx.at[15], xdev)
    put(fu.at[s], fu_out.at[:, pl.ds(s * half_u, half_u)])
    arrive(vr.at[1], gz.at[8], hz.at[8, 0], ndev)
    v_all[1] = v_all[0] + vr[1]
    send(v_all.at[1], vr.at[2], gz.at[9], hz.at[8, 1], fdev)
    z_mid(4)
    y_end(5)

    def rows_back(i):
        d1_swap[i].wait()
        row = xr[i].astype(f32)
        r1 = inverse_rms(row)
        scaled = (d2s[i].astype(f32) + d1r[i].astype(f32)) * gain_one
        step = r1 * scaled - row * (r1 * r1 * r1 * jnp.mean(scaled * row, axis=-1, keepdims=True))
        d2s[i] = (dh[i] + step + logit[i] * router).astype(bf16)
        put(d2s.at[i], dx_out.at[i])

    rows_back(0)
    arrive(vr.at[2], gz.at[9], hz.at[8, 1], fdev)
    v_all[2] = v_all[1] + vr[2]
    send(v_all.at[2], vr.at[3], gy.at[8], hy.at[8], ydev)
    z_mid(5)
    y_end(6)
    z_mid(6)
    y_end(7)
    arrive(vr.at[3], gy.at[8], hy.at[8], ydev)
    v_all[3] = v_all[2] + vr[3]
    send(v_all.at[3], vr.at[4], sx.at[18], rx.at[18], xdev)
    for i in range(2):
        fqk[i] = z_end(4 + i)
    sqk[...] = fqk[1 - s].astype(bf16)
    send(sqk, rqk, sx.at[16], rx.at[16], xdev)
    for j in range(2):
        put(fqk.at[s, :, pl.ds(j * half_q, half_q)], fq_out.at[:, pl.ds(2 * j * half_q + s * half_q, half_q)])
    z_mid(7)
    fv[...] = z_end(6)
    sv[...] = fv[:, pl.ds((1 - s) * half_q, half_q)].astype(bf16)
    send(sv, rv, sx.at[17], rx.at[17], xdev)
    put(fv.at[:, pl.ds(s * half_q, half_q)], fq_out.at[:, pl.ds(4 * half_q + s * half_q, half_q)])
    rows_back(1)
    arrive(ruu, sx.at[15], rx.at[15], xdev)
    fu[1 - s] = ruu[...].astype(f32)
    put(fu.at[1 - s], fu_out.at[:, pl.ds((1 - s) * half_u, half_u)])
    arrive(rqk, sx.at[16], rx.at[16], xdev)
    fqk[1 - s] = rqk[...].astype(f32)
    for j in range(2):
        put(
            fqk.at[1 - s, :, pl.ds(j * half_q, half_q)],
            fq_out.at[:, pl.ds(2 * j * half_q + (1 - s) * half_q, half_q)],
        )
    fo[...] = z_end(7)
    put(fo, fo_out)
    arrive(rv, sx.at[17], rx.at[17], xdev)
    fv[:, pl.ds((1 - s) * half_q, half_q)] = rv[...].astype(f32)
    put(
        fv.at[:, pl.ds((1 - s) * half_q, half_q)],
        fq_out.at[:, pl.ds(4 * half_q + (1 - s) * half_q, half_q)],
    )
    arrive(vr.at[4], sx.at[18], rx.at[18], xdev)
    v_all[4] = v_all[3] + vr[4]
    put(v_all.at[4], vec_out)
    gathered()
    for k in range(2, 8):
        left(land_z[k], gz.at[k], hz.at[k, 0], ndev)
    waited = x_swap + a_swap + d_swap + d2_swap + m_swap + d1_swap
    for copy in list(sent):
        if not any(copy is other for other in waited):
            copy.wait_send()
    for copy in outs:
        copy.wait()


def rows_kernel(
    tok_hbm, cot_hbm, upd_hbm, dx_hbm, fq_hbm, fo_hbm, fu_hbm, fd_hbm, vec_hbm, live_hbm,
    out_hbm, grad_hbm, fq_out, fo_out, fu_out, fd_out, one_out, two_out, three_out,
    bases, moved, fq, fo, fu, fd, vec_ref, live_ref, one, two, three, get_sem, put_sem, rows_sem, pass_sem,
):
    s = lax.axis_index("seq")
    _, slots, chunks, tall, model = bases.shape
    ranks = moved.shape[2]
    whole = (tok_hbm, cot_hbm), (out_hbm, grad_hbm)
    tasks = [(i, t) for i in range(slots) for t in range(chunks)]

    def part_of(ref, i, t):
        return ref.at[i, pl.ds(t * tall, tall)]

    gets, puts = {}, []
    rows = [
        pltpu.make_async_copy(src.at[i], moved.at[a, i], rows_sem.at[a, i])
        for i in range(slots)
        for a, src in enumerate((upd_hbm, dx_hbm))
    ]
    get_live = pltpu.make_async_copy(live_hbm, live_ref, pass_sem.at[0, 4])
    get_vec = pltpu.make_async_copy(vec_hbm, vec_ref, pass_sem.at[0, 5])
    get_live.start()
    for i, t in tasks:
        for a in range(2):
            if t == 0:
                rows[2 * i + a].start()
            gets[a, i, t] = pltpu.make_async_copy(part_of(whole[0][a], i, t), bases.at[a, i, t], get_sem.at[a, i, t])
            gets[a, i, t].start()
    through = ((fq_hbm, fq, fq_out), (fo_hbm, fo, fo_out), (fu_hbm, fu, fu_out), (fd_hbm, fd, fd_out))
    taken = [pltpu.make_async_copy(src, mid, pass_sem.at[0, j]) for j, (src, mid, _) in enumerate(through)]
    passed = [pltpu.make_async_copy(mid, dst, pass_sem.at[1, j]) for j, (_, mid, dst) in enumerate(through)]
    for copy in taken + [get_vec]:
        copy.start()
    get_live.wait()
    for n, (i, t) in enumerate(tasks):
        if n == len(tasks) - 1:
            for j in range(4):
                taken[j].wait()
                passed[j].start()
        position = lax.broadcasted_iota(jnp.int32, (tall, ranks), 0) + ((s * chunks + t) * tall)
        chooser = jnp.where(position == live_ref[i : i + 1], 1.0, 0.0).astype(bf16)
        for a in range(2):
            if t == 0:
                rows[2 * i + a].wait()
            gets[a, i, t].wait()
            bases[a, i, t] += dot_nn(chooser, moved[a, i]).astype(bf16)
            copy = pltpu.make_async_copy(bases.at[a, i, t], part_of(whole[1][a], i, t), put_sem.at[a, i, t])
            copy.start()
            puts.append(copy)
    part = one.shape[1]
    get_vec.wait()
    flat = s * lax.axis_size("batch") + lax.axis_index("batch")
    each = 128 // part
    lane = lax.broadcasted_iota(jnp.int32, (part, 128), 1)
    here = lane == lax.rem(flat, each) * part + lax.broadcasted_iota(jnp.int32, (part, 128), 0)
    eye = lax.broadcasted_iota(jnp.int32, (part, part), 0) == lax.broadcasted_iota(jnp.int32, (part, part), 1)
    for j, (ref, dst) in enumerate(((one, one_out), (two, two_out), (three, three_out))):
        line = vec_ref[pl.ds(8 * j + flat // each, 1)]
        column = jnp.sum(jnp.where(here, line, 0.0), axis=1, keepdims=True)
        ref[...] = jnp.sum(jnp.where(eye, column, 0.0), axis=0, keepdims=True)
        puts.append(pltpu.make_async_copy(ref, dst, pass_sem.at[1, 4 + j]))
        puts[-1].start()
    for copy in passed + puts:
        copy.wait()


def split_device(
    tokens, cotangent, lengths, routed, w_qkv, w_out, w_up, w_down, gain_attn, gain_mlp, router
):
    slots, local_len, model = tokens.shape
    ranks = routed.shape[1]
    half_q, half_u = w_qkv.shape[1] // 6, w_up.shape[1] // 2
    part, down = w_qkv.shape[0], w_down.shape[0]
    hbm = pl.BlockSpec(memory_space=pl.ANY)
    sds, space, dma = jax.ShapeDtypeStruct, pltpu.VMEM, pltpu.SemaphoreType.DMA
    rows = (slots, ranks, model)
    grid = (LINE, 2, 2)
    wq_shape, wo_shape = (2,) + grid + (part, 3 * half_q), grid + (part, model)
    wu_shape, wd_shape = (2,) + grid + (part, half_u), grid + (down, model)
    blocked = (slots, local_len // 512, 2, 2, 128, model)
    row_bf16 = space(rows, bf16)

    def land(lead, tall, wide):
        return [space(lead + mid + (tall, wide), bf16) for mid in ((LINE, 2), (LINE,), (3,))]

    on_d, on_u = land((), down, model), land((2,), part, half_u)
    grad_shapes = (
        sds((part, 6 * half_q), f32), sds((part, model), f32), sds((part, 2 * half_u), f32), sds((down, model), f32),
    )
    upd, dxr, *sums, vec, live = pl.pallas_call(
        block_kernel,
        out_shape=(sds(rows, bf16), sds(rows, bf16)) + grad_shapes + (sds((24, 128), f32), sds(routed.shape, jnp.int32)),
        in_specs=[hbm] * 11,
        out_specs=[hbm] * 8,
        scratch_shapes=[
            space(wq_shape, bf16), space(wo_shape, bf16), space(wu_shape, bf16), space(wd_shape, bf16),
            space(grid + (16, 128), bf16),
            space((part, 3 * half_q), bf16), space((part, half_u), bf16), space((16, 128), bf16), space((16, 128), bf16),
            *[row_bf16] * 11, space(rows, f32), space(rows, f32),
            space((slots, ranks, 3 * half_q), bf16), space((slots, ranks, half_q), bf16),
            space((slots, ranks, half_u), bf16), space((slots, ranks, half_u), bf16),
            space((slots, ranks, 1), f32), space((16, model), f32),
            space(wd_shape, bf16), space(wu_shape, bf16),
            on_d[0], on_u[0], on_d[1], on_u[1], on_d[2], on_u[2],
            space((3, 2, 2 * part, model), bf16), space((2 * part, model), bf16),
            space((2, part, model), f32), space((part, model), f32), space((part, model), f32),
            space((2, part, half_u), f32), space((down, model), f32),
            space((part, model), bf16), space((part, half_q), bf16), space((part, half_u), bf16),
            space((part, model), bf16), space((part, half_q), bf16), space((part, half_u), bf16),
            space((24, 128), f32), space((5, 24, 128), f32), space((5, 24, 128), f32), space(routed.shape, jnp.int32),
            *[space((1, part), bf16)] * 3, space(routed.shape, jnp.int32), space((1, slots), jnp.int32),
            dma((19,)), dma((15,)), dma((8,)), dma((8, 3)), dma((8,)), dma((8,)), dma((8,)), dma((8,)),
            dma((19,)), dma((19,)), dma((9,)), dma((9,)), dma((2,)), dma((2,)), dma((9,)), dma((9,)), dma((10,)), dma((9, 3)),
            pltpu.SemaphoreType.REGULAR((2,)),
        ],
        compiler_params=pltpu.CompilerParams(collective_id=1, has_side_effects=True, vmem_limit_bytes=60 << 20),
        name="block",
    )(
        tokens.reshape(blocked), cotangent.reshape(blocked), w_qkv, w_out, w_up, w_down,
        gain_attn[None], gain_mlp[None], router[None], routed, lengths[None],
    )

    chunks = 2
    vectors = (sds((1, part), f32),) * 3
    output, input_grad, g_qkv, g_out, g_up, g_down, g_one, g_two, g_three = pl.pallas_call(
        rows_kernel,
        out_shape=(sds(tokens.shape, bf16), sds(tokens.shape, bf16)) + grad_shapes + vectors,
        in_specs=[hbm] * 10,
        out_specs=[hbm] * 9,
        scratch_shapes=[
            space((2, slots, chunks, local_len // chunks, model), bf16), space((2,) + rows, bf16),
            *[space(g.shape, f32) for g in grad_shapes],
            space((24, 128), f32), space(routed.shape, jnp.int32), *[space((1, part), f32)] * 3,
            dma((2, slots, chunks)), dma((2, slots, chunks)), dma((2, slots)), dma((2, 7)),
        ],
        compiler_params=pltpu.CompilerParams(vmem_limit_bytes=60 << 20),
        name="rows",
    )(tokens, cotangent, upd, dxr, *sums, vec, live)
    return (
        output, input_grad, g_qkv, g_out, g_up, g_down,
        g_one.reshape(part), g_two.reshape(part), g_three.reshape(part),
    )


def solution(mesh):
    in_specs = (
        P("batch", "seq", None),
        P("batch", "seq", None),
        P("batch"),
        P("batch", None),
        P(("seq", "batch"), None),
        P(("seq", "batch"), None),
        P(("seq", "batch"), None),
        P(("seq", "batch"), None),
        P(("seq", "batch")),
        P(("seq", "batch")),
        P(("seq", "batch")),
    )
    out_specs = (
        P("batch", "seq", None),
        P("batch", "seq", None),
        P(("seq", "batch"), None),
        P(("seq", "batch"), None),
        P(("seq", "batch"), None),
        P(("seq", "batch"), None),
        P(("seq", "batch")),
        P(("seq", "batch")),
        P(("seq", "batch")),
    )
    small_slice = mesh.shape["seq"] == 2 and mesh.shape["batch"] == 4 * LINE
    body = split_device if small_slice else general_device
    return jax.shard_map(body, mesh=mesh, in_specs=in_specs, out_specs=out_specs, check_vma=False)
```
